32 devices in a mesh: grp: 2 (over x), tile: 16 (over z, y, core).
Axes of the slice: x: 2, y: 2, z: 4, core: 2. Of those that a mesh axis runs over, the one named last changes fastest.
Arguments:
- visibility: bfloat16 [32, 16, 2, 256, 256], P('tile', 'grp'), parts along dimension 1, may hold values from -12 to 12
- station_beam: bfloat16 [16, 2, 512, 2048], P('grp', None, 'tile'), parts along dimension 0, may hold values from -4.1875 to 4.1875
- antenna_uvw: float32 [16, 3, 2048], P('grp'), parts along dimension 0, may hold values from -40 to 40
- source_dirs: float32 [2, 4096], P(None, 'tile'), may hold values from -0.4 to 0.4
- source_flux: bfloat16 [8192], P(('grp', 'tile')), parts along dimension 0, may hold values from 0.0029907227 to 0.029907227
- visible_list: int32 [8, 512], P(None, 'tile'), may hold values from 0 to 255
- antenna_flags: int32 [16, 2048], P('grp'), parts along dimension 0, may hold values 0 or 1
Outputs:
- residual: bfloat16 [32, 16, 2, 256, 256], P('tile', 'grp'), parts along dimension 1
- flux_grad: float32 [16, 512], P('grp', 'tile'), parts along dimension 0
The draws below stay inside these ranges and needn't reach their ends.
There are 2 independent parts, one for each index of `grp`. The reference program is written for one: setup_inputs(seed, part) draws one part's arguments, and reference() takes and returns one part's arrays. A program takes and returns all parts, laid end to end along the dimension named above; an argument that names none is the same for every part. Nothing has to cross between parts.
Inputs may be any that keep to these rules, and one draw needn't show every extreme that they name: `visible_list`: entry k of a slot names pool source 256 * (k // 32) + value, a source of its own group. `antenna_flags`: 1 marks a flagged antenna.
All inputs are finite; a program needn't handle non-finite values.
Results may differ from the reference program's by a relative error of at most 0.0034.
Values may be sent and summed in bfloat16 or wider, within the bound.
No kernel may reach another device: no remote copies, remote signals or barrier semaphores. Data moves between devices by JAX's collectives and lax.ppermute only.
A program may use at most 192 MiB of HBM per device.

```python
import math
import jax
import jax.numpy as jnp
import numpy as np
from jax import lax

ANTENNAS = 2048
VISIBLE = 512
SLOTS = 8
POOL_DEV = 256
BLOCKS = 8
SPAN = 256
UNITS = 32
PER_GROUP = 32
POOL = 4096


def place_ends(values, stream_key, smallest, top_value):
    longest = values.shape.index(max(values.shape))
    spots = []
    for shift in (0, 1):
        where = [jax.random.randint(jax.random.fold_in(stream_key, axis), (), 0, length) for axis, length in enumerate(values.shape)]
        where[longest] = (where[longest] + shift) % values.shape[longest]
        spots.append(tuple(where))
    return values.at[spots[0]].set(smallest).at[spots[1]].set(top_value)


def level_of(rng, shape, cuts, low, high):
    level = 1.0
    for dim, shards_of in cuts:
        draws = jax.random.uniform(jax.random.fold_in(jax.random.fold_in(rng, 6), dim), (shards_of,), jnp.float32, low / len(cuts), high / len(cuts))
        level = level * jnp.repeat(jnp.exp(draws), shape[dim] // shards_of).reshape((-1,) + (1,) * (len(shape) - 1 - dim))
    return level


def centred(stream_key, shape, scale, most, shards=(), held_as=jnp.bfloat16):
    drawn = scale * jax.random.normal(stream_key, shape, jnp.float32)
    if shards:
        drawn = drawn * level_of(stream_key, shape, shards, -0.22, 0.18)
    return jnp.clip(drawn, -most, most).astype(held_as)


def setup_inputs(seed: int = 0, part: int = 0) -> dict:
    arg_keys = jax.random.split(jax.random.key(seed), 8)
    part_keys = jax.random.split(jax.random.fold_in(arg_keys[7], part), 8)
    visibility = centred(part_keys[0], (UNITS, SLOTS, 2, SPAN, SPAN), 2.0, 12.0, ((0, 16),))
    station_beam = centred(part_keys[1], (SLOTS, 2, VISIBLE, ANTENNAS), 0.7, 4.1875, ((2, 16),))
    antenna_uvw = jnp.clip(jax.random.uniform(part_keys[2], (SLOTS, 3, ANTENNAS), jnp.float32, -40.0, 40.0), -40.0, 40.0)
    source_dirs = jnp.clip(jax.random.uniform(arg_keys[3], (2, POOL), jnp.float32, -0.4, 0.4) * level_of(arg_keys[3], (2, POOL), ((1, 16),), -0.4, 0.0), -0.4, 0.4)
    source_flux = jnp.clip(jnp.exp(math.log(0.029907227) - 2.3025851 * jax.random.uniform(part_keys[4], (POOL,), jnp.float32) ** level_of(part_keys[4], (POOL,), ((0, 16),), -0.2, 0.2)), 0.0029907227, 0.029907227).astype(jnp.bfloat16)
    visible_list = place_ends(jax.random.randint(arg_keys[5], (SLOTS, VISIBLE), 0, POOL_DEV), jax.random.fold_in(arg_keys[5], 1), 0, POOL_DEV - 1).astype(jnp.int32)
    antenna_flags = place_ends((jax.random.randint(part_keys[6], (SLOTS, ANTENNAS), 0, 10) < 1).astype(jnp.int32), jax.random.fold_in(part_keys[6], 1), 0, 1)
    return {"visibility": visibility, "station_beam": station_beam, "antenna_uvw": antenna_uvw, "source_dirs": source_dirs, "source_flux": source_flux, "visible_list": visible_list, "antenna_flags": antenna_flags}


two_pi = 2.0 * math.pi

def unit_table(block_count):
    first_list = []
    second_list = []
    diag_list = []
    for row_block in range(block_count):
        for col_block in range(row_block + 1, block_count):
            first_list.append(row_block)
            second_list.append(col_block)
            diag_list.append(0)
    for pair_index in range(block_count // 2):
        first_list.append(2 * pair_index)
        second_list.append(2 * pair_index + 1)
        diag_list.append(1)
    return (np.array(first_list, np.int32), np.array(second_list, np.int32), np.array(diag_list, np.int32))

def make_factors(station_beam, antenna_uvw, coord_east, coord_north):
    depth_term = jnp.sqrt(1.0 - coord_east * coord_east - coord_north * coord_north) - 1.0
    delay_sum = antenna_uvw[:, 0, None, :] * coord_east[:, :, None] + antenna_uvw[:, 1, None, :] * coord_north[:, :, None] + antenna_uvw[:, 2, None, :] * depth_term[:, :, None]
    phases = two_pi * delay_sum
    cosine = jnp.cos(phases)
    sine = jnp.sin(phases)
    beam_f = station_beam.astype(jnp.float32)
    real_part = beam_f[:, 0] * cosine + beam_f[:, 1] * sine
    imag_part = beam_f[:, 1] * cosine - beam_f[:, 0] * sine
    return jnp.stack([real_part, imag_part], 1).astype(jnp.bfloat16)

def predict(rows_f, cols_f, brightness):
    scaled = (rows_f.astype(jnp.float32) * brightness.astype(jnp.float32)[:, None, :, None]).astype(jnp.bfloat16)
    turned = jnp.stack([scaled[:, 1], -scaled[:, 0]], 1)
    stacked = jnp.stack([scaled, turned], 1).astype(jnp.float32)
    return jnp.einsum('tdckr,tckq->tdrq', stacked, cols_f.astype(jnp.float32))

def pull_back(resid, rows_f, cols_f):
    rstack = jnp.stack([jnp.stack([resid[:, 0], -resid[:, 1]], 1), jnp.stack([resid[:, 1], resid[:, 0]], 1)], 1).astype(jnp.float32)
    pulled = jnp.einsum('tdcrq,tckq->tdkr', rstack, cols_f.astype(jnp.float32))
    return lax.optimization_barrier(jnp.sum(rows_f.astype(jnp.float32) * pulled, axis=(1, 3)))

def reference(visibility, station_beam, antenna_uvw, source_dirs, source_flux, visible_list, antenna_flags):
    group_base = jnp.arange(VISIBLE, dtype=jnp.int32) // PER_GROUP * POOL_DEV
    pool_index = (group_base[None, :] + visible_list).astype(jnp.int32)
    coord_east = jnp.take(source_dirs[0], pool_index)
    coord_north = jnp.take(source_dirs[1], pool_index)
    brightness = jnp.take(source_flux, pool_index)
    factors = make_factors(station_beam, antenna_uvw, coord_east, coord_north)
    keep_all = 1.0 - antenna_flags.astype(jnp.float32)
    first_tab, second_tab, diag_tab = unit_table(BLOCKS)
    first_arr = jnp.asarray(first_tab)
    second_arr = jnp.asarray(second_tab)
    diag_arr = jnp.asarray(diag_tab)
    local_ids = jnp.arange(SPAN, dtype=jnp.int32)
    upper_part = local_ids[:, None] < local_ids[None, :]
    lower_part = local_ids[:, None] > local_ids[None, :]

    def one_unit(unit_id):
        start_one = (first_arr[unit_id] * SPAN).astype(jnp.int32)
        start_two = (second_arr[unit_id] * SPAN).astype(jnp.int32)
        diag_tile = diag_arr[unit_id] == 1
        block_one = lax.dynamic_slice_in_dim(factors, start_one, SPAN, 3)
        block_two = lax.dynamic_slice_in_dim(factors, start_two, SPAN, 3)
        cols_one = jnp.where(diag_tile, block_one, block_two)
        first_pred = predict(block_one, cols_one, brightness)
        second_pred = predict(block_two, block_two, brightness)
        first_mask = jnp.logical_or(jnp.logical_not(diag_tile), upper_part)
        predicted = jnp.where(first_mask[None, None], first_pred, jnp.swapaxes(second_pred, 2, 3))
        keep_one = lax.dynamic_slice_in_dim(keep_all, start_one, SPAN, 1)
        keep_two = lax.dynamic_slice_in_dim(keep_all, start_two, SPAN, 1)
        upper_f = upper_part.astype(jnp.float32)
        lower_f = lower_part.astype(jnp.float32)
        off_weight = keep_one[:, :, None] * keep_two[:, None, :]
        diag_weight = upper_f[None] * keep_one[:, :, None] * keep_one[:, None, :] + lower_f[None] * keep_two[:, :, None] * keep_two[:, None, :]
        weights = jnp.where(diag_tile, diag_weight, off_weight)
        vis_unit = lax.dynamic_index_in_dim(visibility, unit_id, 0, keepdims=False)
        residual = (weights[:, None] * (vis_unit.astype(jnp.float32) - predicted)).astype(jnp.bfloat16)
        zero_res = jnp.zeros_like(residual)
        first_res = jnp.where(first_mask[None, None], residual, zero_res)
        second_sel = jnp.logical_and(diag_tile, lower_part)
        second_res = jnp.swapaxes(jnp.where(second_sel[None, None], residual, zero_res), 2, 3)
        partial_value = pull_back(first_res, block_one, cols_one) + pull_back(second_res, block_two, block_two)
        return (residual, partial_value)
    residual, partial_value = lax.map(one_unit, jnp.arange(UNITS, dtype=jnp.int32))
    flux_grad = lax.optimization_barrier(jnp.sum(partial_value, 0)) * (-1.0 / (8.0 * ANTENNAS))
    return (residual, flux_grad)
```

```python
import functools
import math

import jax
import jax.numpy as jnp
import numpy as np
from jax import lax
from jax.experimental import pallas as pl
from jax.experimental.pallas import tpu as pltpu
from jax.sharding import PartitionSpec as P

BLOCKS = 8
CHUNKS = 4


def unit_table(block_count):
    first_list = []
    second_list = []
    diag_list = []
    for row_block in range(block_count):
        for col_block in range(row_block + 1, block_count):
            first_list.append(row_block)
            second_list.append(col_block)
            diag_list.append(0)
    for pair_index in range(block_count // 2):
        first_list.append(2 * pair_index)
        second_list.append(2 * pair_index + 1)
        diag_list.append(1)
    return np.stack([first_list, second_list, diag_list], 1).astype(np.int32)


def turn_polynomials():
    nodes = 0.125 + 0.125 * np.cos(np.pi * (np.arange(64) + 0.5) / 64)
    root = np.sqrt(nodes)
    fit = np.polynomial.Polynomial.fit
    sine = fit(nodes, np.sin(2 * np.pi * root) / root, 7, domain=[0, 0.25]).convert()
    cosine = fit(nodes, np.cos(2 * np.pi * root), 8, domain=[0, 0.25]).convert()
    return [float(c) for c in sine.coef], [float(c) for c in cosine.coef]


def horner(coefs, x):
    total = coefs[-1]
    for coef in coefs[-2::-1]:
        total = total * x + coef
    return total


def build_kernel(first_slot, beam_ref, uvw_ref, dirs_ref, list_ref, out_ref):
    slot = first_slot + pl.program_id(0)
    pool = dirs_ref.shape[1]
    slots = list_ref.shape[1]
    picked = lax.broadcasted_iota(jnp.int32, list_ref.shape, 1) == slot
    chosen_id = jnp.sum(jnp.where(picked, list_ref[...], 0), axis=1, keepdims=True)
    chosen = chosen_id == lax.broadcasted_iota(jnp.int32, (list_ref.shape[0], pool), 1)
    east = jnp.sum(jnp.where(chosen, dirs_ref[0:1, :], 0.0), axis=1, keepdims=True)
    north = jnp.sum(jnp.where(chosen, dirs_ref[1:2, :], 0.0), axis=1, keepdims=True)
    depth = jnp.sqrt(1.0 - east * east - north * north) - 1.0
    sin_coefs, cos_coefs = turn_polynomials()
    width = 512
    for start in range(0, beam_ref.shape[3], width):
        cols = pl.ds(start, width)
        delay = (
            uvw_ref[0, 0:1, cols] * east
            + uvw_ref[0, 1:2, cols] * north
            + uvw_ref[0, 2:3, cols] * depth
        )
        turn = delay - jnp.floor(delay + 0.5)
        square = turn * turn
        sine = horner(sin_coefs, square) * turn
        cosine = horner(cos_coefs, square)
        real = beam_ref[0, 0, :, cols].astype(jnp.float32)
        imag = beam_ref[0, 1, :, cols].astype(jnp.float32)
        out_ref[0, 0, :, cols] = (real * cosine + imag * sine).astype(jnp.bfloat16)
        out_ref[0, 1, :, cols] = (imag * cosine - real * sine).astype(jnp.bfloat16)


def build_factors(first_slot, slot_count, station_beam, antenna_uvw, source_dirs, list_cols):
    _, _, per_group, antennas = station_beam.shape
    return pl.pallas_call(
        functools.partial(build_kernel, first_slot),
        grid=(slot_count,),
        in_specs=[
            pl.BlockSpec((1, 2, per_group, antennas), lambda t: (first_slot + t, 0, 0, 0)),
            pl.BlockSpec((1, 3, antennas), lambda t: (first_slot + t, 0, 0)),
            pl.BlockSpec(source_dirs.shape, lambda t: (0, 0)),
            pl.BlockSpec(list_cols.shape, lambda t: (0, 0)),
        ],
        out_specs=pl.BlockSpec((1, 2, per_group, antennas), lambda t: (t, 0, 0, 0)),
        out_shape=jax.ShapeDtypeStruct((slot_count, 2, per_group, antennas), jnp.bfloat16),
        compiler_params=pltpu.CompilerParams(vmem_limit_bytes=32 * 1024 * 1024),
        name="build_factors",
    )(station_beam, antenna_uvw, source_dirs, list_cols)


def flat(parts, real, imag):
    groups, per_group, span = real.shape
    return jnp.stack([real, imag], 1).reshape(groups * 2 * per_group, span)


def unit_kernel(first_slot, tab_ref, one_ref, two_ref, vis_ref, keep_one_ref, keep_two_ref, bright_ref, *rest):
    res_ref, grad_ref, total_ref = rest[-3:]
    unit = pl.program_id(1)
    slot = first_slot + pl.program_id(0)
    groups, _, _, per_group, span = one_ref.shape
    rows = groups * 2 * per_group

    def dot(a, b):
        return lax.dot_general(a, b, (((1,), (0,)), ((), ())), preferred_element_type=jnp.float32)

    bright = jnp.broadcast_to(bright_ref[pl.ds(slot, 1), :], (128, groups * per_group)).T
    bright = jnp.concatenate([bright] * (span // 128), 1).reshape(groups, 1, per_group, span)

    def scaled_of(factors):
        return (factors.astype(jnp.float32) * bright).astype(jnp.bfloat16)

    def turned_of(factors):
        return jnp.stack([factors[:, 1], -factors[:, 0]], 1)

    def flat_of(factors):
        return factors.reshape(rows, span)

    def outer(a, b):
        row_ids = lax.broadcasted_iota(jnp.int32, a.shape, 0)
        a = jnp.where(row_ids == slot, a, 0.0)
        return lax.dot_general(a, b, (((0,), (0,)), ((), ())), preferred_element_type=jnp.float32)

    def pull(factors, res_re, res_im):
        flat_f = flat_of(factors)
        with_re = dot(flat_f, res_re).reshape(groups, 2, per_group, span)
        with_im = dot(flat_f, res_im).reshape(groups, 2, per_group, span)
        return with_re, with_im

    def add_grad(value):
        value = value.reshape(groups * per_group, span)
        folded = value[:, :128]
        for start in range(128, span, 128):
            folded = folded + value[:, start : start + 128]

        @pl.when(unit == 0)
        def _():
            total_ref[...] = folded

        @pl.when(unit > 0)
        def _():
            total_ref[...] += folded

    vis_re = vis_ref[0, 0, 0].astype(jnp.float32)
    vis_im = vis_ref[0, 0, 1].astype(jnp.float32)

    @pl.when(tab_ref[unit, 2] == 0)
    def _():
        one = one_ref[:, 0]
        two = two_ref[:, 0]
        lhs = flat_of(scaled_of(one)).T
        pred_re = dot(lhs, flat_of(two))
        pred_im = -dot(lhs, flat_of(turned_of(two)))
        weights = outer(keep_one_ref[...], keep_two_ref[...])
        res_re = (weights * (vis_re - pred_re)).astype(jnp.bfloat16)
        res_im = (weights * (vis_im - pred_im)).astype(jnp.bfloat16)
        res_ref[0, 0, 0] = res_re
        res_ref[0, 0, 1] = res_im
        with_re, with_im = pull(one, res_re, res_im)
        sum_re = with_re[:, 0] + with_im[:, 1]
        sum_im = with_im[:, 0] - with_re[:, 1]
        add_grad(sum_re * two[:, 0].astype(jnp.float32) - sum_im * two[:, 1].astype(jnp.float32))

    @pl.when(tab_ref[unit, 2] == 1)
    def _():
        one = one_ref[:, 0]
        two = two_ref[:, 0]
        row_ids = lax.broadcasted_iota(jnp.int32, (span, span), 0)
        col_ids = lax.broadcasted_iota(jnp.int32, (span, span), 1)
        upper = row_ids < col_ids
        lower = row_ids > col_ids
        lhs = flat_of(scaled_of(one)).T
        first_re = dot(lhs, flat_of(one))
        first_im = -dot(lhs, flat_of(turned_of(one)))
        scaled = scaled_of(two)
        lhs = flat_of(two).T
        second_re = dot(lhs, flat_of(scaled))
        second_im = dot(lhs, flat_of(turned_of(scaled)))
        keep_one = keep_one_ref[...]
        keep_two = keep_two_ref[...]
        weights = jnp.where(upper, outer(keep_one, keep_one), 0.0) + jnp.where(
            lower, outer(keep_two, keep_two), 0.0
        )
        res_re = (weights * (vis_re - jnp.where(upper, first_re, second_re))).astype(jnp.bfloat16)
        res_im = (weights * (vis_im - jnp.where(upper, first_im, second_im))).astype(jnp.bfloat16)
        res_ref[0, 0, 0] = res_re
        res_ref[0, 0, 1] = res_im
        none = jnp.zeros_like(res_re)
        with_re, with_im = pull(one, jnp.where(upper, res_re, none), jnp.where(upper, res_im, none))
        sum_re = with_re[:, 0] + with_im[:, 1]
        sum_im = with_im[:, 0] - with_re[:, 1]
        value = sum_re * one[:, 0].astype(jnp.float32) - sum_im * one[:, 1].astype(jnp.float32)
        with_re, with_im = pull(two, jnp.where(lower, res_re, none), jnp.where(lower, res_im, none))
        sum_re = with_re[:, 0] - with_im[:, 1]
        sum_im = with_im[:, 0] + with_re[:, 1]
        value += sum_re * two[:, 0].astype(jnp.float32) + sum_im * two[:, 1].astype(jnp.float32)
        add_grad(value)

    @pl.when(unit == pl.num_programs(1) - 1)
    def _():
        grad_ref[0] = jnp.sum(total_ref[...].T, axis=0, keepdims=True)


def unit_work(first_slot, slot_count, table, gathered, visibility, keep, bright, residual):
    units_dev, slots, _, span, _ = visibility.shape
    groups, _, _, per_group, _ = gathered.shape
    in_specs = [
        pl.BlockSpec((groups, 1, 2, per_group, span), lambda t, u, tab: (0, t, 0, 0, tab[u, 0])),
        pl.BlockSpec((groups, 1, 2, per_group, span), lambda t, u, tab: (0, t, 0, 0, tab[u, 1])),
        pl.BlockSpec((1, 1, 2, span, span), lambda t, u, tab: (u, first_slot + t, 0, 0, 0)),
        pl.BlockSpec((slots, span), lambda t, u, tab: (0, tab[u, 0])),
        pl.BlockSpec((slots, span), lambda t, u, tab: (0, tab[u, 1])),
        pl.BlockSpec(bright.shape, lambda t, u, tab: (0, 0)),
    ]
    operands = [table, gathered, gathered, visibility, keep, keep, bright]
    aliases = {}
    if residual is not None:
        in_specs.append(pl.BlockSpec(memory_space=pl.ANY))
        operands.append(residual)
        aliases = {7: 0}
    flops = 16 * slot_count * units_dev * groups * per_group * span * span
    return pl.pallas_call(
        functools.partial(unit_kernel, first_slot),
        grid_spec=pltpu.PrefetchScalarGridSpec(
            num_scalar_prefetch=1,
            grid=(slot_count, units_dev),
            in_specs=in_specs,
            out_specs=[
                pl.BlockSpec((1, 1, 2, span, span), lambda t, u, tab: (u, first_slot + t, 0, 0, 0)),
                pl.BlockSpec((1, 1, groups * per_group), lambda t, u, tab: (t, 0, 0)),
            ],
            scratch_shapes=[pltpu.VMEM((groups * per_group, 128), jnp.float32)],
        ),
        out_shape=[
            jax.ShapeDtypeStruct(visibility.shape, jnp.bfloat16),
            jax.ShapeDtypeStruct((slot_count, 1, groups * per_group), jnp.float32),
        ],
        input_output_aliases=aliases,
        compiler_params=pltpu.CompilerParams(vmem_limit_bytes=48 * 1024 * 1024),
        cost_estimate=pl.CostEstimate(flops=flops, bytes_accessed=flops // 128, transcendentals=0),
        name="unit_work",
    )(*operands)


def per_device(
    visibility, station_beam, antenna_uvw, source_dirs, source_flux, visible_list, antenna_flags
):
    units_dev = visibility.shape[0]
    slot_count, _, per_group, antennas = station_beam.shape
    chunk = slot_count // CHUNKS
    tile_index = lax.axis_index("tile")
    table = lax.dynamic_slice_in_dim(
        jnp.asarray(unit_table(BLOCKS)), tile_index * units_dev, units_dev, 0
    )
    list_cols = visible_list.T
    gathered = []
    for first_slot in range(0, slot_count, chunk):
        owned = build_factors(first_slot, chunk, station_beam, antenna_uvw, source_dirs, list_cols)
        gathered.append(lax.all_gather(owned, "tile", axis=0))
    chosen = visible_list[:, :, None] == jnp.arange(source_flux.shape[0], dtype=jnp.int32)
    brightness = jnp.sum(jnp.where(chosen, source_flux.astype(jnp.float32), 0.0), axis=2)
    bright_all = lax.all_gather(brightness, "tile", axis=1, tiled=True)
    keep = 1.0 - antenna_flags.astype(jnp.float32)
    residual = None
    grads = []
    for index, first_slot in enumerate(range(0, slot_count, chunk)):
        residual, grad = unit_work(
            first_slot, chunk, table, gathered[index], visibility, keep, bright_all, residual
        )
        grads.append(grad)
    partial_total = jnp.concatenate(grads, 0)[:, 0]
    summed = lax.psum_scatter(partial_total, "tile", scatter_dimension=1, tiled=True)
    flux_grad = summed * (-1.0 / (8.0 * antennas))
    return (residual, flux_grad)


def solution(mesh):
    return jax.shard_map(
        per_device,
        mesh=mesh,
        in_specs=(
            P("tile", "grp", None, None, None),
            P("grp", None, "tile", None),
            P("grp", None, None),
            P(None, "tile"),
            P(("grp", "tile")),
            P(None, "tile"),
            P("grp", None),
        ),
        out_specs=(P("tile", "grp", None, None, None), P("grp", "tile")),
        check_vma=False,
    )
```

```python
import functools
import math

import jax
import jax.numpy as jnp
import numpy as np
from jax import lax
from jax.experimental import pallas as pl
from jax.experimental.pallas import tpu as pltpu
from jax.sharding import PartitionSpec as P


def unit_table(block_count):
    first_list = []
    second_list = []
    diag_list = []
    for row_block in range(block_count):
        for col_block in range(row_block + 1, block_count):
            first_list.append(row_block)
            second_list.append(col_block)
            diag_list.append(0)
    for pair_index in range(block_count // 2):
        first_list.append(2 * pair_index)
        second_list.append(2 * pair_index + 1)
        diag_list.append(1)
    return np.stack([first_list, second_list, diag_list], 1).astype(np.int32)


def turn_polynomials():
    nodes = 0.125 + 0.125 * np.cos(np.pi * (np.arange(64) + 0.5) / 64)
    root = np.sqrt(nodes)
    fit = np.polynomial.Polynomial.fit
    sine = fit(nodes, np.sin(2 * np.pi * root) / root, 7, domain=[0, 0.25]).convert()
    cosine = fit(nodes, np.cos(2 * np.pi * root), 8, domain=[0, 0.25]).convert()
    return [float(c) for c in sine.coef], [float(c) for c in cosine.coef]


def horner(coefs, x):
    total = coefs[-1]
    for coef in coefs[-2::-1]:
        total = total * x + coef
    return total


def build_kernel(slot, beam_ref, uvw_ref, dirs_ref, list_ref, picks_ref, out_ref, pick_ref):
    pool = dirs_ref.shape[1]
    picked = lax.broadcasted_iota(jnp.int32, list_ref.shape, 1) == slot
    chosen_id = jnp.sum(jnp.where(picked, list_ref[...], 0), axis=1, keepdims=True)
    chosen = chosen_id == lax.broadcasted_iota(jnp.int32, (list_ref.shape[0], pool), 1)
    east = jnp.sum(jnp.where(chosen, dirs_ref[0:1, :], 0.0), axis=1, keepdims=True)
    north = jnp.sum(jnp.where(chosen, dirs_ref[1:2, :], 0.0), axis=1, keepdims=True)
    depth = jnp.sqrt(1.0 - east * east - north * north) - 1.0
    sin_coefs, cos_coefs = turn_polynomials()
    span = out_ref.shape[3]
    for block in range(out_ref.shape[1]):
        cols = pl.ds(block * span, span)
        delay = (
            uvw_ref[0, 0:1, cols] * east
            + uvw_ref[0, 1:2, cols] * north
            + uvw_ref[0, 2:3, cols] * depth
        )
        turn = delay - jnp.floor(delay + 0.5)
        square = turn * turn
        sine = horner(sin_coefs, square) * turn
        cosine = horner(cos_coefs, square)
        real = beam_ref[0, 0, :, cols].astype(jnp.float32)
        imag = beam_ref[0, 1, :, cols].astype(jnp.float32)
        out_ref[0, block] = (real * cosine + imag * sine).astype(jnp.bfloat16)
        out_ref[1, block] = (imag * cosine - real * sine).astype(jnp.bfloat16)
    for place in range(pick_ref.shape[1]):
        block = picks_ref[place]
        pick_ref[0, place] = out_ref[0, block]
        pick_ref[1, place] = out_ref[1, block]


def build_factors(slot, span, station_beam, antenna_uvw, source_dirs, list_cols, picks):
    _, _, per_group, antennas = station_beam.shape
    blocks = antennas // span
    return pl.pallas_call(
        functools.partial(build_kernel, slot),
        grid=(1,),
        in_specs=[
            pl.BlockSpec((1, 2, per_group, antennas), lambda t: (slot, 0, 0, 0)),
            pl.BlockSpec((1, 3, antennas), lambda t: (slot, 0, 0)),
            pl.BlockSpec(source_dirs.shape, lambda t: (0, 0)),
            pl.BlockSpec(list_cols.shape, lambda t: (0, 0)),
            pl.BlockSpec(memory_space=pltpu.SMEM),
        ],
        out_specs=[
            pl.BlockSpec((2, blocks, per_group, span), lambda t: (0, 0, 0, 0)),
            pl.BlockSpec((2, picks.shape[0], per_group, span), lambda t: (0, 0, 0, 0)),
        ],
        out_shape=[
            jax.ShapeDtypeStruct((2, blocks, per_group, span), jnp.bfloat16),
            jax.ShapeDtypeStruct((2, picks.shape[0], per_group, span), jnp.bfloat16),
        ],
        compiler_params=pltpu.CompilerParams(vmem_limit_bytes=32 * 1024 * 1024),
        name="build_factors",
    )(station_beam, antenna_uvw, source_dirs, list_cols, picks)


def read_block(payload, block):
    if isinstance(payload, tuple):
        return jnp.stack([part[block] for part in payload], 0)
    return payload[:, block]


def pick_side_kernel(extra_count, tab_ref, *refs):
    own, before, after, far_re, far_im, far_out, extra_out = refs
    columns = [own, before, after, (far_re, far_im)]
    for place in range(far_out.shape[1]):
        far_out[:, place] = read_block(columns[3], tab_ref[SIDE_ROW, place])
    for lead, payload in enumerate(columns):
        for place in range(extra_count):
            extra_out[lead, :, place] = read_block(payload, tab_ref[EXTRA_ROW, place])


def pick_near_kernel(tab_ref, before, after, near_out):
    for lead, payload in enumerate((before, after)):
        for place in range(near_out.shape[2]):
            near_out[lead, :, place] = read_block(payload, tab_ref[SIDE_ROW, place])


def pick_core_kernel(tab_ref, *refs):
    own, before, after, far_re, far_im, side_own, side_near, side_far, extra, send_out, mine_out = refs
    columns = [own, before, after, (far_re, far_im)]
    sides = [side_own, side_near.at[0], side_near.at[1], side_far]
    main = side_own.shape[1]
    for out_ref, row in ((send_out, SEND_ROW), (mine_out, MINE_ROW)):
        for place in range(out_ref.shape[2]):
            block = tab_ref[row, place]
            at = tab_ref[row + 1, place]
            for lead, payload in enumerate(columns):
                out_ref[lead, :, place] = read_block(payload, block)

            @pl.when(at < main)
            def _(out_ref=out_ref, place=place, at=at):
                for lead, payload in enumerate(sides):
                    out_ref[4 + lead, :, place] = payload[:, at]

            @pl.when(at >= main)
            def _(out_ref=out_ref, place=place, at=at):
                for lead in range(len(sides)):
                    out_ref[4 + lead, :, place] = extra[lead, :, at - main]


def pick_blocks(kernel, out_shapes, table, *arrays):
    whole = pl.BlockSpec(memory_space=pltpu.VMEM)
    return pl.pallas_call(
        kernel,
        in_specs=[pl.BlockSpec(memory_space=pltpu.SMEM)] + [whole] * len(arrays),
        out_specs=[whole] * len(out_shapes),
        out_shape=[jax.ShapeDtypeStruct(shape, jnp.bfloat16) for shape in out_shapes],
        compiler_params=pltpu.CompilerParams(vmem_limit_bytes=32 * 1024 * 1024),
        name="pick_blocks",
    )(table, *arrays)


def flat(parts, real, imag):
    groups, per_group, span = real.shape
    return jnp.stack([real, imag], 1).reshape(groups * 2 * per_group, span)


def unit_kernel(slot, parts, tab_ref, *refs):
    one_refs, two_refs, refs = refs[:parts], refs[parts : 2 * parts], refs[2 * parts :]
    vis_ref, keep_one_ref, keep_two_ref, bright_ref = refs[:4]
    res_ref, grad_ref, total_ref = refs[-3:]
    unit = pl.program_id(0)
    groups = sum(ref.shape[0] for ref in one_refs)
    per_group, span = one_refs[0].shape[3:]
    rows = groups * 2 * per_group

    def dot(a, b):
        return lax.dot_general(a, b, (((1,), (0,)), ((), ())), preferred_element_type=jnp.float32)

    bright = jnp.broadcast_to(bright_ref[pl.ds(slot, 1), :], (128, groups * per_group)).T
    bright = jnp.concatenate([bright] * (span // 128), 1).reshape(groups, 1, per_group, span)

    def scaled_of(factors):
        return (factors.astype(jnp.float32) * bright).astype(jnp.bfloat16)

    def turned_of(factors):
        return jnp.stack([factors[:, 1], -factors[:, 0]], 1)

    def flat_of(factors):
        return factors.reshape(rows, span)

    def outer(a, b):
        row_ids = lax.broadcasted_iota(jnp.int32, a.shape, 0)
        a = jnp.where(row_ids == slot, a, 0.0)
        return lax.dot_general(a, b, (((0,), (0,)), ((), ())), preferred_element_type=jnp.float32)

    def pull(factors, res_re, res_im):
        flat_f = flat_of(factors)
        with_re = dot(flat_f, res_re).reshape(groups, 2, per_group, span)
        with_im = dot(flat_f, res_im).reshape(groups, 2, per_group, span)
        return with_re, with_im

    def add_grad(value):
        value = value.reshape(groups * per_group, span)
        folded = value[:, :128]
        for start in range(128, span, 128):
            folded = folded + value[:, start : start + 128]

        @pl.when(unit == 0)
        def _():
            total_ref[...] = folded

        @pl.when(unit > 0)
        def _():
            total_ref[...] += folded

    vis_re = vis_ref[0, 0, 0].astype(jnp.float32)
    vis_im = vis_ref[0, 0, 1].astype(jnp.float32)

    @pl.when(tab_ref[unit, 2] == 0)
    def _():
        one = jnp.concatenate([ref[:, :, 0] for ref in one_refs], 0)
        two = jnp.concatenate([ref[:, :, 0] for ref in two_refs], 0)
        lhs = flat_of(scaled_of(one)).T
        pred_re = dot(lhs, flat_of(two))
        pred_im = -dot(lhs, flat_of(turned_of(two)))
        weights = outer(keep_one_ref[...], keep_two_ref[...])
        res_re = (weights * (vis_re - pred_re)).astype(jnp.bfloat16)
        res_im = (weights * (vis_im - pred_im)).astype(jnp.bfloat16)
        res_ref[0, 0, 0] = res_re
        res_ref[0, 0, 1] = res_im
        with_re, with_im = pull(one, res_re, res_im)
        sum_re = with_re[:, 0] + with_im[:, 1]
        sum_im = with_im[:, 0] - with_re[:, 1]
        add_grad(sum_re * two[:, 0].astype(jnp.float32) - sum_im * two[:, 1].astype(jnp.float32))

    @pl.when(tab_ref[unit, 2] == 1)
    def _():
        one = jnp.concatenate([ref[:, :, 0] for ref in one_refs], 0)
        two = jnp.concatenate([ref[:, :, 0] for ref in two_refs], 0)
        row_ids = lax.broadcasted_iota(jnp.int32, (span, span), 0)
        col_ids = lax.broadcasted_iota(jnp.int32, (span, span), 1)
        upper = row_ids < col_ids
        lower = row_ids > col_ids
        lhs = flat_of(scaled_of(one)).T
        first_re = dot(lhs, flat_of(one))
        first_im = -dot(lhs, flat_of(turned_of(one)))
        scaled = scaled_of(two)
        lhs = flat_of(two).T
        second_re = dot(lhs, flat_of(scaled))
        second_im = dot(lhs, flat_of(turned_of(scaled)))
        keep_one = keep_one_ref[...]
        keep_two = keep_two_ref[...]
        weights = jnp.where(upper, outer(keep_one, keep_one), 0.0) + jnp.where(
            lower, outer(keep_two, keep_two), 0.0
        )
        res_re = (weights * (vis_re - jnp.where(upper, first_re, second_re))).astype(jnp.bfloat16)
        res_im = (weights * (vis_im - jnp.where(upper, first_im, second_im))).astype(jnp.bfloat16)
        res_ref[0, 0, 0] = res_re
        res_ref[0, 0, 1] = res_im
        none = jnp.zeros_like(res_re)
        with_re, with_im = pull(one, jnp.where(upper, res_re, none), jnp.where(upper, res_im, none))
        sum_re = with_re[:, 0] + with_im[:, 1]
        sum_im = with_im[:, 0] - with_re[:, 1]
        value = sum_re * one[:, 0].astype(jnp.float32) - sum_im * one[:, 1].astype(jnp.float32)
        with_re, with_im = pull(two, jnp.where(lower, res_re, none), jnp.where(lower, res_im, none))
        sum_re = with_re[:, 0] - with_im[:, 1]
        sum_im = with_im[:, 0] + with_re[:, 1]
        value += sum_re * two[:, 0].astype(jnp.float32) + sum_im * two[:, 1].astype(jnp.float32)
        add_grad(value)

    @pl.when(unit == pl.num_programs(0) - 1)
    def _():
        grad_ref[...] = jnp.sum(total_ref[...].T, axis=0, keepdims=True)


def unit_work(slot, table, factors, visibility, keep, bright, residual):
    units_dev, slots, _, span, _ = visibility.shape
    per_group = factors[0].shape[3]
    groups = sum(array.shape[0] for array in factors)
    in_specs = []
    for column in (3, 4):
        for array in factors:
            in_specs.append(
                pl.BlockSpec(
                    (array.shape[0], 2, 1, per_group, span),
                    lambda u, tab, column=column: (0, 0, tab[u, column], 0, 0),
                )
            )
    in_specs += [
        pl.BlockSpec((1, 1, 2, span, span), lambda u, tab: (u, slot, 0, 0, 0)),
        pl.BlockSpec((slots, span), lambda u, tab: (0, tab[u, 0])),
        pl.BlockSpec((slots, span), lambda u, tab: (0, tab[u, 1])),
        pl.BlockSpec(bright.shape, lambda u, tab: (0, 0)),
    ]
    operands = [table, *factors, *factors, visibility, keep, keep, bright]
    aliases = {}
    if residual is not None:
        in_specs.append(pl.BlockSpec(memory_space=pl.ANY))
        aliases = {len(operands): 0}
        operands.append(residual)
    flops = 16 * units_dev * groups * per_group * span * span
    return pl.pallas_call(
        functools.partial(unit_kernel, slot, len(factors)),
        grid_spec=pltpu.PrefetchScalarGridSpec(
            num_scalar_prefetch=1,
            grid=(units_dev,),
            in_specs=in_specs,
            out_specs=[
                pl.BlockSpec((1, 1, 2, span, span), lambda u, tab: (u, slot, 0, 0, 0)),
                pl.BlockSpec((1, groups * per_group), lambda u, tab: (0, 0)),
            ],
            scratch_shapes=[pltpu.VMEM((groups * per_group, 128), jnp.float32)],
        ),
        out_shape=[
            jax.ShapeDtypeStruct(visibility.shape, jnp.bfloat16),
            jax.ShapeDtypeStruct((1, groups * per_group), jnp.float32),
        ],
        input_output_aliases=aliases,
        compiler_params=pltpu.CompilerParams(vmem_limit_bytes=48 * 1024 * 1024),
        cost_estimate=pl.CostEstimate(flops=flops, bytes_accessed=flops // 128, transcendentals=0),
        name="unit_work",
    )(*operands)


SIDE_ROW = 0
EXTRA_ROW = 1
SEND_ROW = 2
MINE_ROW = 4
MAIN_PLACES = 6
CORE_PLACES = 4


class Routes:
    def __init__(self, planes, chips, cores, units):
        ring = [0] + list(range(1, planes, 2)) + list(range(planes - 2, 0, -2))
        count = planes * chips * cores
        units_dev = units.shape[0] // count

        def tile_of(plane, chip, core):
            return (plane * chips + chip) * cores + core

        places = [(t // (chips * cores), t // cores % chips, t % cores) for t in range(count)]

        def along(step):
            at = {plane: ring[(n + step) % planes] for n, plane in enumerate(ring)}
            return [(t, tile_of(at[z], y, c)) for t, (z, y, c) in enumerate(places)]

        self.onward = along(1)
        self.backward = along(-1)
        self.opposite = along(2)
        self.side = [(t, tile_of(z, 1 - y, c)) for t, (z, y, c) in enumerate(places)]
        self.core = [(t, tile_of(z, y, 1 - c)) for t, (z, y, c) in enumerate(places)]
        need = []
        for t in range(count):
            mine = units[t * units_dev : (t + 1) * units_dev, :2]
            need.append(sorted(set(mine.reshape(-1).tolist())))
        chip_need = []
        for t, (z, y, _) in enumerate(places):
            whole = set()
            for core in range(cores):
                whole |= set(need[tile_of(z, y, core)])
            chip_need.append(sorted(whole))

        def padded(values, length):
            return (list(values) + [values[0] if values else 0] * length)[:length]

        self.extra_places = max(0, max(len(n) for n in chip_need) - MAIN_PLACES)
        self.extra = [(a, b) for a, b in self.side if len(chip_need[b]) > MAIN_PLACES]
        width = 8
        table = np.zeros((count, 6, width), np.int32)
        unit_places = np.zeros((units.shape[0], 2), np.int32)
        for t in range(count):
            side, core = self.side[t][1], self.core[t][1]
            table[t, SIDE_ROW] = padded(chip_need[side][:MAIN_PLACES], width)
            table[t, EXTRA_ROW] = padded(chip_need[side][MAIN_PLACES:], width)
            for row, other in ((SEND_ROW, core), (MINE_ROW, t)):
                blocks = padded(need[other], width)
                table[t, row] = blocks
                table[t, row + 1] = [chip_need[t].index(b) for b in blocks]
            for u in range(t * units_dev, (t + 1) * units_dev):
                unit_places[u] = [need[t].index(b) for b in units[u, :2]]
        self.table = table
        self.unit_places = unit_places
        assert max(len(n) for n in need) <= CORE_PLACES


def ship(value, pairs):
    return lax.ppermute(value, "tile", pairs)


def in_order(values, *earlier):
    earlier = tuple(value for value in earlier if value is not None)
    return lax.optimization_barrier(values + earlier)[: len(values)]


def spread(routes, value):
    column = jnp.stack(
        [
            value,
            ship(value, routes.onward),
            ship(value, routes.backward),
            ship(value, routes.opposite),
        ],
        0,
    )
    half = jnp.concatenate([column, ship(column, routes.side)], 0)
    return jnp.concatenate([half, ship(half, routes.core)], 0)


def collect(routes, value):
    count = value.shape[0]
    value = value[: count // 2] + ship(value[count // 2 :], routes.core)
    value = value[: count // 4] + ship(value[count // 4 :], routes.side)
    return (
        (value[0] + ship(value[3], routes.opposite))
        + (ship(value[1], routes.backward) + ship(value[2], routes.onward))
    )


def per_device(
    visibility, station_beam, antenna_uvw, source_dirs, source_flux, visible_list, antenna_flags
):
    units_dev = visibility.shape[0]
    span = visibility.shape[4]
    slots, _, per_group, antennas = station_beam.shape
    tile_count = lax.axis_size("tile")
    tile_index = lax.axis_index("tile")
    units = unit_table(antennas // span)
    list_cols = visible_list.T
    chosen = visible_list[:, :, None] == jnp.arange(source_flux.shape[0], dtype=jnp.int32)
    brightness = jnp.sum(jnp.where(chosen, source_flux.astype(jnp.float32), 0.0), axis=2)
    keep = 1.0 - antenna_flags.astype(jnp.float32)
    scale = -1.0 / (8.0 * antennas)

    if tile_count != 16:
        unit_tab = np.concatenate([units, units[:, :2]], 1)
        unit_tab = lax.dynamic_slice_in_dim(
            jnp.asarray(unit_tab), tile_index * units_dev, units_dev, 0
        )
        picks = jnp.zeros((1,), jnp.int32)
        bright_all = lax.all_gather(brightness, "tile", axis=1, tiled=True)
        residual = None
        grads = []
        for slot in range(slots):
            owned, _ = build_factors(
                slot, span, station_beam, antenna_uvw, source_dirs, list_cols, picks
            )
            factors = lax.all_gather(owned, "tile", axis=0)
            residual, grad = unit_work(
                slot, unit_tab, [factors], visibility, keep, bright_all, residual
            )
            grads.append(grad)
        summed = lax.psum_scatter(
            jnp.concatenate(grads, 0), "tile", scatter_dimension=1, tiled=True
        )
        return (residual, summed * scale)

    routes = Routes(4, 2, 2, units)
    table = lax.dynamic_index_in_dim(jnp.asarray(routes.table), tile_index, 0, keepdims=False)
    unit_tab = lax.dynamic_slice_in_dim(
        jnp.asarray(np.concatenate([units, routes.unit_places], 1)),
        tile_index * units_dev,
        units_dev,
        0,
    )
    side_picks = table[SIDE_ROW, :MAIN_PLACES]
    bright_all = spread(routes, brightness)
    bright_all = jnp.swapaxes(bright_all, 0, 1).reshape(slots, tile_count * per_group)

    block_shape = (per_group, span)
    own, before, later, side_own = {}, {}, {}, {}
    far_re, far_im, side_near, side_far, extra = {}, {}, {}, {}, {}
    mine, other, sent, grads = {}, {}, {}, {}
    residual = None

    def near_step(slot):
        owned, picked = build_factors(
            slot, span, station_beam, antenna_uvw, source_dirs, list_cols, side_picks
        )
        owned, picked = in_order(
            (owned, picked), before.get(slot - 2), sent.get(slot - 3), grads.get(slot - 5)
        )
        own[slot] = owned
        before[slot] = ship(owned, routes.onward)
        later[slot] = ship(owned, routes.backward)
        side_own[slot] = ship(picked, routes.side)

    def far_step(slot):
        far_re[slot] = ship(before[slot][0], routes.onward)
        far_im[slot] = ship(later[slot][1], routes.backward)
        near = pick_blocks(
            pick_near_kernel, [(2, 2, MAIN_PLACES) + block_shape], table, before[slot], later[slot]
        )[0]
        side_near[slot] = ship(near, routes.side)

    def side_step(slot):
        far, rest = pick_blocks(
            functools.partial(pick_side_kernel, routes.extra_places),
            [(2, MAIN_PLACES) + block_shape, (4, 2, max(1, routes.extra_places)) + block_shape],
            table,
            own[slot],
            before[slot],
            later[slot],
            far_re[slot],
            far_im[slot],
        )
        far, rest = in_order((far, rest), grads.get(slot - 3))
        side_far[slot] = ship(far, routes.side)
        extra[slot] = ship(rest, routes.extra) if routes.extra_places else rest

    def core_step(slot):
        send, mine[slot] = pick_blocks(
            pick_core_kernel,
            [(8, 2, CORE_PLACES) + block_shape] * 2,
            table,
            own[slot],
            before[slot],
            later[slot],
            far_re[slot],
            far_im[slot],
            side_own[slot],
            side_near[slot],
            side_far[slot],
            extra[slot],
        )
        (sent[slot],) = in_order((send,), grads.get(slot - 2))
        other[slot] = ship(sent[slot], routes.core)

    for tick in range(slots + 4):
        for lag, step in ((0, near_step), (1, far_step), (2, side_step), (3, core_step)):
            if 0 <= tick - lag < slots:
                step(tick - lag)
        slot = tick - 4
        if 0 <= slot < slots:
            residual, grads[slot] = unit_work(
                slot, unit_tab, [mine[slot], other[slot]], visibility, keep, bright_all, residual
            )
    partial = jnp.concatenate([grads[slot] for slot in range(slots)], 0).reshape(slots, tile_count, per_group)
    return (residual, collect(routes, jnp.swapaxes(partial, 0, 1)) * scale)


def solution(mesh):
    return jax.shard_map(
        per_device,
        mesh=mesh,
        in_specs=(
            P("tile", "grp", None, None, None),
            P("grp", None, "tile", None),
            P("grp", None, None),
            P(None, "tile"),
            P(("grp", "tile")),
            P(None, "tile"),
            P("grp", None),
        ),
        out_specs=(P("tile", "grp", None, None, None), P("grp", "tile")),
        check_vma=False,
    )
```

```python
import functools
import math

import jax
import jax.numpy as jnp
import numpy as np
from jax import lax
from jax.experimental import pallas as pl
from jax.experimental.pallas import tpu as pltpu
from jax.sharding import PartitionSpec as P


def unit_table(block_count):
    first_list = []
    second_list = []
    diag_list = []
    for row_block in range(block_count):
        for col_block in range(row_block + 1, block_count):
            first_list.append(row_block)
            second_list.append(col_block)
            diag_list.append(0)
    for pair_index in range(block_count // 2):
        first_list.append(2 * pair_index)
        second_list.append(2 * pair_index + 1)
        diag_list.append(1)
    return np.stack([first_list, second_list, diag_list], 1).astype(np.int32)


def turn_polynomials():
    nodes = 0.125 + 0.125 * np.cos(np.pi * (np.arange(64) + 0.5) / 64)
    root = np.sqrt(nodes)
    fit = np.polynomial.Polynomial.fit
    sine = fit(nodes, np.sin(2 * np.pi * root) / root, 7, domain=[0, 0.25]).convert()
    cosine = fit(nodes, np.cos(2 * np.pi * root), 8, domain=[0, 0.25]).convert()
    return [float(c) for c in sine.coef], [float(c) for c in cosine.coef]


def horner(coefs, x):
    total = coefs[-1]
    for coef in coefs[-2::-1]:
        total = total * x + coef
    return total


def build_kernel(chunk, parts, picks_ref, *refs):
    sets, refs = refs[: 4 * parts], refs[4 * parts :]
    uvw_ref, out_ref, pick_ref = refs
    first, count, with_bright = chunk
    per_group, span = out_ref.shape[2:]
    blocks = uvw_ref.shape[2] // span
    places = pick_ref.shape[0] // (2 * count)
    sin_coefs, cos_coefs = turn_polynomials()
    for part in range(parts):
        beam_ref, dirs_ref, flux_ref, list_ref = sets[4 * part : 4 * part + 4]
        pool = dirs_ref.shape[1]
        slots = list_ref.shape[1]
        pool_ids = lax.broadcasted_iota(jnp.int32, (per_group, pool), 1)
        lanes = lax.broadcasted_iota(jnp.int32, (per_group, span), 1)
        if with_bright:
            bright = jnp.zeros((per_group, span), jnp.float32)
            for slot in range(slots):
                chosen = list_ref[:, slot : slot + 1] == pool_ids
                flux = jnp.sum(jnp.where(chosen, flux_ref[...], 0.0), axis=1, keepdims=True)
                bright = jnp.where(lanes == slot, flux, bright)
            out_ref[part, 2 * count * blocks] = bright.astype(jnp.bfloat16)
        for index in range(count):
            slot = first + index
            chosen = list_ref[:, slot : slot + 1] == pool_ids
            east = jnp.sum(jnp.where(chosen, dirs_ref[0:1, :], 0.0), axis=1, keepdims=True)
            north = jnp.sum(jnp.where(chosen, dirs_ref[1:2, :], 0.0), axis=1, keepdims=True)
            depth = jnp.sqrt(1.0 - east * east - north * north) - 1.0
            for block in range(blocks):
                cols = pl.ds(block * span, span)
                delay = (
                    uvw_ref[slot, 0:1, cols] * east
                    + uvw_ref[slot, 1:2, cols] * north
                    + uvw_ref[slot, 2:3, cols] * depth
                )
                turn = delay - jnp.floor(delay + 0.5)
                square = turn * turn
                sine = horner(sin_coefs, square) * turn
                cosine = horner(cos_coefs, square)
                real = beam_ref[index, 0, :, cols].astype(jnp.float32)
                imag = beam_ref[index, 1, :, cols].astype(jnp.float32)
                row = 2 * index * blocks + block
                out_ref[part, row] = (real * cosine + imag * sine).astype(jnp.bfloat16)
                out_ref[part, row + blocks] = (imag * cosine - real * sine).astype(jnp.bfloat16)
    copy_blocks(out_ref.at[0], pick_ref, 0, count, blocks, places, lambda place: picks_ref[place])
    if with_bright:
        pick_ref[2 * count * places] = out_ref[0, 2 * count * blocks]


def copy_blocks(source, target, start, count, blocks, places, block_at):
    for place in range(places):
        block = block_at(place)
        for row in range(2 * count):
            target[start + row * places + place] = source[row * blocks + block]


def chunk_rows(chunk, places):
    return 2 * chunk[1] * places + chunk[2]


def build_factors(chunk, span, sets, antenna_uvw, picks):
    first, count, _ = chunk
    _, _, per_group, antennas = sets[0][0].shape
    blocks = antennas // span
    whole = pl.BlockSpec(memory_space=pltpu.VMEM)
    assert first % count == 0
    in_specs = [pl.BlockSpec(memory_space=pltpu.SMEM)]
    operands = [picks]
    for beam, *small in sets:
        in_specs.append(
            pl.BlockSpec((count, 2, per_group, antennas), lambda t: (first // count, 0, 0, 0))
        )
        in_specs += [pl.BlockSpec(array.shape, lambda t: (0, 0)) for array in small]
        operands += [beam, *small]
    in_specs.append(pl.BlockSpec(antenna_uvw.shape, lambda t: (0, 0, 0)))
    out_shapes = [
        (len(sets), chunk_rows(chunk, blocks), per_group, span),
        (chunk_rows(chunk, picks.shape[0]), per_group, span),
    ]
    return pl.pallas_call(
        functools.partial(build_kernel, chunk, len(sets)),
        grid=(1,),
        in_specs=in_specs,
        out_specs=[
            pl.BlockSpec(out_shapes[0], lambda t: (0, 0, 0, 0)),
            pl.BlockSpec(out_shapes[1], lambda t: (0, 0, 0)),
        ],
        out_shape=[jax.ShapeDtypeStruct(shape, jnp.bfloat16) for shape in out_shapes],
        compiler_params=pltpu.CompilerParams(vmem_limit_bytes=40 * 1024 * 1024),
        name="build_factors",
    )(*operands, antenna_uvw)


def pick_side_kernel(items, blocks, tab_ref, *refs):
    out_ref = refs[-1]
    start = 0
    for ref, (chunk, lead) in zip(refs, items):
        source = ref if lead is None else ref.at[lead]
        copy_blocks(
            source, out_ref, start, chunk[1], blocks, SIDE_PLACES, lambda n: tab_ref[SIDE_ROW, n]
        )
        start += chunk_rows(chunk, SIDE_PLACES)
        if chunk[2]:
            out_ref[start - 1] = source[2 * chunk[1] * blocks]


def pick_core_kernel(chunk, starts, blocks, tab_ref, chip, near, far, *refs):
    sides, (send_out, mine_out) = refs[:-2], refs[-2:]
    columns = [chip.at[0], near.at[0], near.at[1], far]
    count = chunk[1]
    for out_ref, row in ((send_out, SEND_ROW), (mine_out, MINE_ROW)):
        for lead, source in enumerate(columns):
            copy_blocks(
                source, out_ref.at[lead], 0, count, blocks, CORE_PLACES, lambda n: tab_ref[row, n]
            )
            if chunk[2]:
                out_ref[lead, 2 * count * CORE_PLACES] = source[2 * count * blocks]
        for lead, (source, start) in enumerate(zip(sides, starts)):
            copy_blocks(
                source,
                out_ref.at[len(columns) + lead],
                0,
                count,
                SIDE_PLACES,
                CORE_PLACES,
                lambda n: start + tab_ref[row + 1, n],
            )
            if chunk[2]:
                bright = source[start + 2 * count * SIDE_PLACES]
                out_ref[len(columns) + lead, 2 * count * CORE_PLACES] = bright


def pick_blocks(kernel, out_shapes, table, *arrays):
    whole = pl.BlockSpec(memory_space=pltpu.VMEM)
    return pl.pallas_call(
        kernel,
        in_specs=[pl.BlockSpec(memory_space=pltpu.SMEM)] + [whole] * len(arrays),
        out_specs=[whole] * len(out_shapes),
        out_shape=[jax.ShapeDtypeStruct(shape, jnp.bfloat16) for shape in out_shapes],
        compiler_params=pltpu.CompilerParams(vmem_limit_bytes=40 * 1024 * 1024),
        name="pick_blocks",
    )(table, *arrays)


def unit_kernel(chunk, layers, guest, tab_ref, *refs):
    factors, refs = refs[: 4 * layers], refs[4 * layers :]
    brights, refs = refs[:layers], refs[layers:]
    vis_ref, keep_one_ref, keep_two_ref = refs[:3]
    guest_ref = refs[3] if guest else None
    out_refs = refs[-4 if guest else -3 :]
    res_ref, grad_ref, total_ref = out_refs[0], out_refs[-2], out_refs[-1]
    unit = pl.program_id(1)
    slot = chunk[0] + pl.program_id(0)
    per_group, span = factors[0].shape[2:]

    def joined(which):
        parts = [ref[:, 0] for ref in factors[which * layers : (which + 1) * layers]]
        return jnp.concatenate(parts, 0).reshape(-1, span)

    def dot(a, b):
        return lax.dot_general(a, b, (((1,), (0,)), ((), ())), preferred_element_type=jnp.float32)

    def scaled_of(re, im):
        lanes = lax.broadcasted_iota(jnp.int32, (re.shape[0], brights[0].shape[3]), 1)
        rows = jnp.concatenate([ref[:, 0] for ref in brights], 0).reshape(lanes.shape)
        column = jnp.where(lanes == slot, rows.astype(jnp.float32), 0.0)
        column = jnp.sum(column, axis=1, keepdims=True)
        return (
            (re.astype(jnp.float32) * column).astype(jnp.bfloat16),
            (im.astype(jnp.float32) * column).astype(jnp.bfloat16),
        )

    def outer(a, b):
        row_ids = lax.broadcasted_iota(jnp.int32, a.shape, 0)
        a = jnp.where(row_ids == slot, a, 0.0)
        return lax.dot_general(a, b, (((0,), (0,)), ((), ())), preferred_element_type=jnp.float32)

    def cross(a_re, a_im, b_re, b_im):
        lhs = jnp.concatenate([a_re, a_im], 0).T
        rhs = jnp.concatenate(
            [jnp.concatenate([b_re, -b_im], 1), jnp.concatenate([b_im, b_re], 1)], 0
        )
        both = dot(lhs, rhs)
        return both[:, :span], both[:, span:]

    def pull(re, im, res_re, res_im, sign):
        lhs = jnp.concatenate([re, im], 1)
        rhs = jnp.concatenate(
            [
                jnp.concatenate([res_re, res_im], 1),
                jnp.concatenate([res_im, -res_re] if sign == 1 else [-res_im, res_re], 1),
            ],
            0,
        )
        both = dot(lhs, rhs)
        return both[:, :span], both[:, span:]

    def add_grad(value):
        folded = value[:, :128]
        for start in range(128, span, 128):
            folded = folded + value[:, start : start + 128]
        total_ref[...] += folded

    def put(res_re, res_im):
        if guest:

            @pl.when(unit < 2)
            def _():
                res_ref[0, 0, 0] = res_re
                res_ref[0, 0, 1] = res_im

            @pl.when(unit == 2)
            def _():
                out_refs[1][0, 0] = res_re
                out_refs[1][0, 1] = res_im
        else:
            res_ref[0, 0, 0] = res_re
            res_ref[0, 0, 1] = res_im

    def vis(part):
        if guest:
            return jnp.where(unit == 2, guest_ref[0, part], vis_ref[0, 0, part]).astype(jnp.float32)
        return vis_ref[0, 0, part].astype(jnp.float32)

    @pl.when(unit == 0)
    def _():
        total_ref[...] = jnp.zeros_like(total_ref)

    @pl.when(tab_ref[unit, 2] == 0)
    def _():
        one_re, one_im, two_re, two_im = [joined(n) for n in range(4)]
        pred_re, pred_im = cross(*scaled_of(one_re, one_im), two_re, two_im)
        weights = outer(keep_one_ref[...], keep_two_ref[...])
        res_re = (weights * (vis(0) - pred_re)).astype(jnp.bfloat16)
        res_im = (weights * (vis(1) - pred_im)).astype(jnp.bfloat16)
        put(res_re, res_im)
        sum_re, sum_im = pull(one_re, one_im, res_re, res_im, 1)
        add_grad(sum_re * two_re.astype(jnp.float32) - sum_im * two_im.astype(jnp.float32))

    @pl.when(tab_ref[unit, 2] == 1)
    def _():
        one_re, one_im, two_re, two_im = [joined(n) for n in range(4)]
        row_ids = lax.broadcasted_iota(jnp.int32, (span, span), 0)
        col_ids = lax.broadcasted_iota(jnp.int32, (span, span), 1)
        upper = row_ids < col_ids
        lower = row_ids > col_ids
        first_re, first_im = cross(*scaled_of(one_re, one_im), one_re, one_im)
        second_re, second_im = cross(two_re, two_im, *scaled_of(two_re, two_im))
        keep_one = keep_one_ref[...]
        keep_two = keep_two_ref[...]
        weights = jnp.where(upper, outer(keep_one, keep_one), 0.0) + jnp.where(
            lower, outer(keep_two, keep_two), 0.0
        )
        res_re = (weights * (vis(0) - jnp.where(upper, first_re, second_re))).astype(jnp.bfloat16)
        res_im = (weights * (vis(1) - jnp.where(upper, first_im, -second_im))).astype(jnp.bfloat16)
        put(res_re, res_im)
        none = jnp.zeros_like(res_re)
        sum_re, sum_im = pull(
            one_re, one_im, jnp.where(upper, res_re, none), jnp.where(upper, res_im, none), 1
        )
        add_grad(sum_re * one_re.astype(jnp.float32) - sum_im * one_im.astype(jnp.float32))
        sum_re, sum_im = pull(
            two_re, two_im, jnp.where(lower, res_re, none), jnp.where(lower, res_im, none), -1
        )
        add_grad(sum_re * two_re.astype(jnp.float32) + sum_im * two_im.astype(jnp.float32))

    @pl.when(unit == pl.num_programs(1) - 1)
    def _():
        grad_ref[0] = jnp.sum(total_ref[...].T, axis=0, keepdims=True)


def unit_work(chunk, table, factors, places, bright, visibility, keep, guest, residual):
    first, count, _ = chunk
    units_dev, slots, _, span, _ = visibility.shape
    steps = table.shape[0]
    per_group = factors[0].shape[2]
    groups = sum(array.shape[0] for array in factors)
    in_specs = []
    for column in (3, 4):
        for part in (0, 1):
            for array in factors:
                in_specs.append(
                    pl.BlockSpec(
                        (array.shape[0], 1, per_group, span),
                        lambda t, u, tab, column=column, part=part: (
                            0,
                            (2 * t + part) * places + tab[u, column],
                            0,
                            0,
                        ),
                    )
                )
    for array in bright:
        in_specs.append(
            pl.BlockSpec(
                (array.shape[0], 1, per_group, 128),
                lambda t, u, tab, row=array.shape[1] - 1: (0, row, 0, 0),
            )
        )
    vis_spec = pl.BlockSpec(
        (1, 1, 2, span, span),
        lambda t, u, tab: (jnp.minimum(u, units_dev - 1), first + t, 0, 0, 0),
    )
    in_specs += [
        vis_spec,
        pl.BlockSpec((slots, span), lambda t, u, tab: (0, tab[u, 0])),
        pl.BlockSpec((slots, span), lambda t, u, tab: (0, tab[u, 1])),
    ]
    operands = [table, *factors * 4, *bright, visibility, keep, keep]
    out_specs = [vis_spec]
    out_shapes = [jax.ShapeDtypeStruct(visibility.shape, jnp.bfloat16)]
    if guest is not None:
        in_specs.append(
            pl.BlockSpec((1, 2, span, span), lambda t, u, tab: (first + t, 0, 0, 0))
        )
        operands.append(guest)
        out_specs.append(pl.BlockSpec((1, 2, span, span), lambda t, u, tab: (t, 0, 0, 0)))
        out_shapes.append(jax.ShapeDtypeStruct((count, 2, span, span), jnp.bfloat16))
    out_specs.append(pl.BlockSpec((1, 1, groups * per_group), lambda t, u, tab: (t, 0, 0)))
    out_shapes.append(jax.ShapeDtypeStruct((count, 1, groups * per_group), jnp.float32))
    aliases = {}
    if residual is not None:
        in_specs.append(pl.BlockSpec(memory_space=pl.ANY))
        aliases = {len(operands): 0}
        operands.append(residual)
    flops = 16 * count * units_dev * groups * per_group * span * span
    return pl.pallas_call(
        functools.partial(unit_kernel, chunk, len(factors), guest is not None),
        grid_spec=pltpu.PrefetchScalarGridSpec(
            num_scalar_prefetch=1,
            grid=(count, steps),
            in_specs=in_specs,
            out_specs=out_specs,
            scratch_shapes=[pltpu.VMEM((groups * per_group, 128), jnp.float32)],
        ),
        out_shape=out_shapes,
        input_output_aliases=aliases,
        compiler_params=pltpu.CompilerParams(vmem_limit_bytes=48 * 1024 * 1024),
        cost_estimate=pl.CostEstimate(flops=flops, bytes_accessed=flops // 128, transcendentals=0),
        name="unit_work",
    )(*operands)


def return_kernel(moves, tab_ref, *refs):
    arrays, res_ref, sem = refs[: len(moves)], refs[-2], refs[-1]

    @pl.when(tab_ref[0] >= 0)
    def _():
        for array, (first, count) in zip(arrays, moves):
            copy = pltpu.make_async_copy(
                array, res_ref.at[tab_ref[0], pl.ds(first, count)], sem.at[0]
            )
            copy.start()
            copy.wait()


def put_returned(chunks, place, returned, residual):
    moves = [chunk[:2] for chunk in chunks]
    anywhere = pl.BlockSpec(memory_space=pl.ANY)
    return pl.pallas_call(
        functools.partial(return_kernel, moves),
        in_specs=[pl.BlockSpec(memory_space=pltpu.SMEM)] + [anywhere] * (len(moves) + 1),
        out_specs=anywhere,
        out_shape=jax.ShapeDtypeStruct(residual.shape, residual.dtype),
        scratch_shapes=[pltpu.SemaphoreType.DMA((1,))],
        input_output_aliases={len(moves) + 1: 0},
        name="put_returned",
    )(place, *returned, residual)


SIDE_ROW = 0
SEND_ROW = 1
MINE_ROW = 3
SIDE_PLACES = 6
CORE_PLACES = 4


class Routes:
    def __init__(self, planes, chips, cores, units):
        ring = [0] + list(range(1, planes, 2)) + list(range(planes - 2, 0, -2))
        count = planes * chips * cores
        units_dev = units.shape[0] // count

        def tile_of(plane, chip, core):
            return (plane * chips + chip) * cores + core

        places = [(t // (chips * cores), t // cores % chips, t % cores) for t in range(count)]

        def along(plane, step):
            return ring[(ring.index(plane) + step) % planes]

        self.near = [(t, tile_of(along(z, 1 - 2 * c), y, c)) for t, (z, y, c) in enumerate(places)]
        self.near_back = [(b, a) for a, b in self.near]
        self.near_cross = [
            (t, tile_of(along(z, 2 * c - 1), y, 1 - c)) for t, (z, y, c) in enumerate(places)
        ]
        self.far = [(t, tile_of(along(z, 2), y, c)) for t, (z, y, c) in enumerate(places)]
        self.side = [(t, tile_of(z, 1 - y, c)) for t, (z, y, c) in enumerate(places)]
        self.core = [(t, tile_of(z, y, 1 - c)) for t, (z, y, c) in enumerate(places)]
        work = [list(range(t * units_dev, (t + 1) * units_dev)) for t in range(count)]
        self.move = (14, 1, 10)
        home, index, host = self.move
        moved = work[home][index]
        work[home][index] = None
        work[host].append(moved)
        need = []
        for t in range(count):
            need.append(sorted({b for u in work[t] if u is not None for b in units[u, :2].tolist()}))
        chip_need = []
        for z, y, _ in places:
            chip_need.append(
                sorted({b for core in range(cores) for b in need[tile_of(z, y, core)]})
            )
        assert max(len(n) for n in need) <= CORE_PLACES
        assert max(len(n) for n in chip_need) <= SIDE_PLACES

        def padded(values, length=8):
            return (values + values[:1] * length)[:length]

        self.table = np.zeros((count, 5, 8), np.int32)
        self.units = np.zeros((count, units_dev + 1, 5), np.int32)
        self.returns = np.full((count, 1), -1, np.int32)
        self.returns[home] = index
        for t in range(count):
            self.table[t, SIDE_ROW] = padded(chip_need[self.side[t][1]])
            for row, other in ((SEND_ROW, self.core[t][1]), (MINE_ROW, t)):
                blocks = padded(need[other])
                self.table[t, row] = blocks
                self.table[t, row + 1] = [chip_need[t].index(b) for b in blocks]
            rows = work[t] + [None] * (units_dev + 1 - len(work[t]))
            held = [u for u in rows if u is not None]
            for step, u in enumerate(rows):
                known = u if u is not None else held[0 if step == 0 else -1]
                one, two, kind = units[known]
                kind = 2 if u is None else kind
                self.units[t, step] = [one, two, kind, need[t].index(one), need[t].index(two)]


def ship(value, pairs):
    return lax.ppermute(value, "tile", pairs)


def in_order(values, *earlier):
    earlier = tuple(value for value in earlier if value is not None)
    return lax.optimization_barrier(values + earlier)[: len(values)]


def collect(routes, value):
    count = value.shape[0]
    value = value[: count // 2] + ship(value[count // 2 :], routes.core)
    value = value[: count // 4] + ship(value[count // 4 :], routes.side)
    return (value[0] + ship(value[3], routes.far)) + (
        ship(value[1], routes.near_back) + ship(value[2], routes.near_cross)
    )


def plain_program(
    visibility, beam, antenna_uvw, source_dirs, flux, list_cols, keep
):
    units_dev, slots, _, span, _ = visibility.shape
    _, _, per_group, antennas = beam.shape
    blocks = antennas // span
    tile_index = lax.axis_index("tile")
    units = unit_table(blocks)
    unit_tab = lax.dynamic_slice_in_dim(
        jnp.asarray(np.concatenate([units, units[:, :2]], 1)), tile_index * units_dev, units_dev, 0
    )
    picks = jnp.zeros((1,), jnp.int32)
    residual = bright = None
    grads = []
    for slot in range(slots):
        chunk = (slot, 1, int(slot == 0))
        owned, _ = build_factors(
            chunk, span, [(beam, source_dirs, flux, list_cols)], antenna_uvw, picks
        )
        factors = lax.all_gather(owned[0], "tile", axis=0)
        bright = factors if bright is None else bright
        residual, grad = unit_work(
            chunk, unit_tab, [factors], blocks, [bright], visibility, keep, None, residual
        )
        grads.append(grad)
    partial = jnp.concatenate(grads, 0)[:, 0]
    return residual, lax.psum_scatter(partial, "tile", scatter_dimension=1, tiled=True)


CHUNK_SLOTS = (1, 1, 2, 2, 1, 1)


def ring_program(routes, visibility, beam, antenna_uvw, source_dirs, flux, list_cols, keep):
    units_dev, slots, _, span, _ = visibility.shape
    _, _, per_group, antennas = beam.shape
    blocks = antennas // span
    tile_index = lax.axis_index("tile")

    def mine_of(rows):
        return lax.dynamic_index_in_dim(jnp.asarray(rows), tile_index, 0, keepdims=False)

    table = mine_of(routes.table)
    unit_tab = mine_of(routes.units)
    returns = mine_of(routes.returns)
    side_picks = table[SIDE_ROW, :SIDE_PLACES]
    home, home_unit, host = routes.move

    chunks = []
    for count in CHUNK_SLOTS:
        first = sum(chunk[1] for chunk in chunks)
        chunks.append((first, count, int(first == 0)))
    last = len(chunks)

    small = jnp.concatenate(
        [source_dirs, flux, list_cols.T.reshape(1, -1).astype(jnp.float32)], 0
    )
    other_beam = ship(beam, routes.core)
    small = ship(small, routes.core)
    sets = [
        (beam, source_dirs, flux, list_cols),
        (
            other_beam,
            small[:2],
            small[2:3],
            small[3].reshape(slots, per_group).T.astype(jnp.int32),
        ),
    ]
    guest = None

    chip, owned_side, near, far, sides, mine, other, sent, grads, back = ({} for _ in range(10))
    side_at = {}
    residual = None

    def build(c):
        chip[c], owned_side[c] = build_factors(chunks[c], span, sets, antenna_uvw, side_picks)

    def side_message(stage):
        items, arrays, keys = [], [], []
        own = [0, 1] if stage == 0 else [stage + 1]
        for c in own:
            if c < last:
                keys.append(("own", c))
                items.append((chunks[c], 0))
                arrays.append(chip[c])
        c = stage - 1
        if 0 <= c < last:
            for lead in (0, 1):
                keys.append(("near", c, lead))
                items.append((chunks[c], lead))
                arrays.append(near[c])
        c = stage - 2
        if 0 <= c < last:
            keys.append(("far", c))
            items.append((chunks[c], None))
            arrays.append(far[c])
        rows = [chunk_rows(chunk, SIDE_PLACES) for chunk, _ in items]
        (message,) = pick_blocks(
            functools.partial(pick_side_kernel, items, blocks),
            [(sum(rows), per_group, span)],
            table,
            *arrays,
        )
        (message,) = in_order((message,), grads.get(stage - 5))
        sides[stage] = ship(message, routes.side)
        for n, key in enumerate(keys):
            side_at[key] = (stage, sum(rows[:n]))

    def core_message(c):
        keys = [("own", c), ("near", c, 0), ("near", c, 1), ("far", c)]
        rows = chunk_rows(chunks[c], CORE_PLACES)
        send, mine[c] = pick_blocks(
            functools.partial(pick_core_kernel, chunks[c], [side_at[k][1] for k in keys], blocks),
            [(8, rows, per_group, span)] * 2,
            table,
            chip[c],
            near[c],
            far[c],
            *[sides[side_at[k][0]] for k in keys],
        )
        (sent[c],) = in_order((send,), grads.get(c - 2))
        other[c] = ship(sent[c], routes.core)

    build(0)
    build(1)
    for stage in range(last + 5):
        if stage < last:
            (chip[stage],) = in_order(
                (chip[stage],), near.get(stage - 2), sent.get(stage - 4), grads.get(stage - 6)
            )
            near[stage] = ship(chip[stage], routes.near)
        if stage == 0:
            guest = ship(visibility[home_unit], [(home, host)])
        c = stage - 1
        if 0 <= c < last:
            far[c] = ship(near[c][0], routes.near)
        if stage + 2 < last:
            build(stage + 2)
        if stage < last + 2:
            side_message(stage)
        c = stage - 3
        if 0 <= c < last:
            core_message(c)
        c = stage - 4
        if 0 <= c < last:
            residual, guest_res, grads[c] = unit_work(
                chunks[c],
                unit_tab,
                [mine[c], other[c]],
                CORE_PLACES,
                [mine[0], other[0]],
                visibility,
                keep,
                guest,
                residual,
            )
            back[c] = ship(guest_res, [(host, home)])
    residual = put_returned(chunks, returns, [back[c] for c in range(last)], residual)
    partial = jnp.concatenate([grads[c] for c in range(last)], 0)
    partial = jnp.swapaxes(partial.reshape(slots, -1, per_group), 0, 1)
    return residual, collect(routes, partial)


def per_device(
    visibility, station_beam, antenna_uvw, source_dirs, source_flux, visible_list, antenna_flags
):
    span = visibility.shape[4]
    antennas = station_beam.shape[3]
    list_cols = visible_list.T
    flux = source_flux.astype(jnp.float32)[None]
    keep = 1.0 - antenna_flags.astype(jnp.float32)
    arguments = (visibility, station_beam, antenna_uvw, source_dirs, flux, list_cols, keep)
    if lax.axis_size("tile") == 16:
        routes = Routes(4, 2, 2, unit_table(antennas // span))
        residual, summed = ring_program(routes, *arguments)
    else:
        residual, summed = plain_program(*arguments)
    return (residual, summed * (-1.0 / (8.0 * antennas)))


def solution(mesh):
    return jax.shard_map(
        per_device,
        mesh=mesh,
        in_specs=(
            P("tile", "grp", None, None, None),
            P("grp", None, "tile", None),
            P("grp", None, None),
            P(None, "tile"),
            P(("grp", "tile")),
            P(None, "tile"),
            P("grp", None),
        ),
        out_specs=(P("tile", "grp", None, None, None), P("grp", "tile")),
        check_vma=False,
    )
```

```python
import functools
import itertools

import jax
import jax.numpy as jnp
import numpy as np
from jax import lax
from jax.experimental import pallas as pl
from jax.experimental.pallas import tpu as pltpu
from jax.sharding import PartitionSpec as P


def unit_table(block_count):
    first_list = []
    second_list = []
    diag_list = []
    for row_block in range(block_count):
        for col_block in range(row_block + 1, block_count):
            first_list.append(row_block)
            second_list.append(col_block)
            diag_list.append(0)
    for pair_index in range(block_count // 2):
        first_list.append(2 * pair_index)
        second_list.append(2 * pair_index + 1)
        diag_list.append(1)
    return np.stack([first_list, second_list, diag_list], 1).astype(np.int32)


def turn_polynomials():
    nodes = 0.125 + 0.125 * np.cos(np.pi * (np.arange(64) + 0.5) / 64)
    root = np.sqrt(nodes)
    fit = np.polynomial.Polynomial.fit
    sine = fit(nodes, np.sin(2 * np.pi * root) / root, 7, domain=[0, 0.25]).convert()
    cosine = fit(nodes, np.cos(2 * np.pi * root), 8, domain=[0, 0.25]).convert()
    return [float(c) for c in sine.coef], [float(c) for c in cosine.coef]


def horner(coefs, x):
    total = coefs[-1]
    for coef in coefs[-2::-1]:
        total = total * x + coef
    return total


def build_kernel(sets, slot_ids, pieces, place_ref, *refs):
    beams, smalls, refs = refs[:sets], refs[sets : 2 * sets], refs[2 * sets :]
    uvw_ref, outs, bright_ref = refs[0], refs[1 : 1 + len(pieces)], refs[-1]
    per_group = outs[0].shape[2] // sets
    span = outs[0].shape[3]
    width = smalls[0].shape[1]
    lanes = lax.broadcasted_iota(jnp.int32, (per_group, width), 1)
    rows = lax.broadcasted_iota(jnp.int32, (per_group, width), 0)
    bright_lanes = lax.broadcasted_iota(jnp.int32, (per_group, 128), 1)
    sin_coefs, cos_coefs = turn_polynomials()
    brights = []
    for part, small in enumerate(smalls):
        group = pl.ds(part * per_group, per_group)

        def pick(chosen, row):
            return jnp.sum(jnp.where(chosen, small[row : row + 1, :], 0.0), axis=1, keepdims=True)

        def chosen_at(index):
            listed = pick(lanes == (place_ref[0] + index) * per_group + rows, 3)
            return listed.astype(jnp.int32) == lanes

        bright = jnp.zeros((per_group, 128), jnp.float32)
        for index in range(slot_ids[1]):
            bright = jnp.where(bright_lanes == index, pick(chosen_at(index), 2), bright)
        brights.append(bright)
        chosen = chosen_at(slot_ids[0])
        east = pick(chosen, 0)
        north = pick(chosen, 1)
        depth = jnp.sqrt(1.0 - east * east - north * north) - 1.0
        for out_ref, piece in zip(outs, pieces):
            for place, block in enumerate(piece):
                cols = pl.ds(block * span, span)
                delay = (
                    uvw_ref[0, 0:1, cols] * east
                    + uvw_ref[0, 1:2, cols] * north
                    + uvw_ref[0, 2:3, cols] * depth
                )
                turn = delay - jnp.floor(delay + 0.5)
                square = turn * turn
                sine = horner(sin_coefs, square) * turn
                cosine = horner(cos_coefs, square)
                real = beams[part][0, 0, :, cols].astype(jnp.float32)
                imag = beams[part][0, 1, :, cols].astype(jnp.float32)
                out_ref[0, place, group] = (real * cosine + imag * sine).astype(jnp.bfloat16)
                out_ref[1, place, group] = (imag * cosine - real * sine).astype(jnp.bfloat16)
    missing = -len(brights) * per_group % 128
    if missing:
        brights.append(jnp.zeros((missing, 128), jnp.float32))
    turned = jnp.concatenate(brights, 0).T
    bright_ref[...] = turned[: bright_ref.shape[0], : bright_ref.shape[1]]


def build_factors(slot_ids, place, beam, other_beams, antenna_uvw, smalls, pieces, span):
    _, _, per_group, antennas = beam.shape
    sets = 1 + len(other_beams)
    index = slot_ids[0]
    whole = pl.BlockSpec(memory_space=pltpu.VMEM)
    shapes = [(2, len(piece), sets * per_group, span) for piece in pieces]
    return pl.pallas_call(
        functools.partial(build_kernel, sets, slot_ids, pieces),
        grid_spec=pltpu.PrefetchScalarGridSpec(
            num_scalar_prefetch=1,
            grid=(1,),
            in_specs=[
                pl.BlockSpec((1, 2, per_group, antennas), lambda n, at: (at[0] + index, 0, 0, 0)),
                *[whole] * (len(other_beams) + sets),
                pl.BlockSpec((1, 3, antennas), lambda n, at: (at[0] + index, 0, 0)),
            ],
            out_specs=[whole] * (len(pieces) + 1),
        ),
        out_shape=[jax.ShapeDtypeStruct(shape, jnp.bfloat16) for shape in shapes]
        + [jax.ShapeDtypeStruct((8, sets * per_group), jnp.float32)],
        compiler_params=pltpu.CompilerParams(vmem_limit_bytes=40 * 1024 * 1024),
        name="build_factors",
    )(place, beam, *other_beams, *smalls, antenna_uvw)


KIND, ONE, TWO, ONE_AT, TWO_AT, OUT_ROWS, VIS_AT = 0, 1, 2, 3, 5, 7, 9
COLUMNS = 11


def unit_kernel(index, pieces, outs, aliased, tab_ref, place_ref, *refs):
    arrays = []
    for both, single in pieces:
        entries = [(ref.at[0], ref.at[1]) for ref in refs[:both]]
        if single:
            entries.append((refs[both], refs[both + 1]))
        arrays.append(entries)
        refs = refs[both + 2 * single :]
    vis_ref, keep_one_ref, keep_two_ref, bright_ref = refs[:4]
    refs = refs[4 + aliased :]
    out_refs, grad_ref = refs[:outs], refs[outs]
    total_ref, column_ref, one_ref, two_ref = refs[outs + 1 :]
    step = pl.program_id(0)
    slot = place_ref[0] + index
    sources, span = one_ref.shape[1:]

    def load(target, at):
        for n, entries in enumerate(arrays):

            @pl.when(tab_ref[step, at] == n)
            def _(entries=entries):
                place = tab_ref[step, at + 1]
                start = 0
                for entry in entries:
                    count = entry[0].shape[1]
                    for part in (0, 1):
                        target[part, pl.ds(start, count)] = entry[part][place]
                    start += count

    def dot(a, b):
        return lax.dot_general(a, b, (((1,), (0,)), ((), ())), preferred_element_type=jnp.float32)

    def scaled_of(re, im):
        column = jnp.concatenate([column_ref[...]] * (span // 128), 1)
        return (
            (re.astype(jnp.float32) * column).astype(jnp.bfloat16),
            (im.astype(jnp.float32) * column).astype(jnp.bfloat16),
        )

    def outer(a, b):
        row_ids = lax.broadcasted_iota(jnp.int32, a.shape, 0)
        a = jnp.where(row_ids == slot, a, 0.0)
        return lax.dot_general(a, b, (((0,), (0,)), ((), ())), preferred_element_type=jnp.float32)

    def cross(a_re, a_im, b_re, b_im):
        lhs = jnp.concatenate([a_re, a_im], 0).T
        rhs = jnp.concatenate(
            [jnp.concatenate([b_re, -b_im], 1), jnp.concatenate([b_im, b_re], 1)], 0
        )
        both = dot(lhs, rhs)
        return both[:, :span], both[:, span:]

    def pull(re, im, res_re, res_im, sign):
        lhs = jnp.concatenate([re, im], 1)
        rhs = jnp.concatenate(
            [
                jnp.concatenate([res_re, res_im], 1),
                jnp.concatenate([res_im, -res_re] if sign == 1 else [-res_im, res_re], 1),
            ],
            0,
        )
        both = dot(lhs, rhs)
        return both[:, :span], both[:, span:]

    def add_grad(value):
        folded = value[:, :128]
        for start in range(128, span, 128):
            folded = folded + value[:, start : start + 128]
        total_ref[...] += folded

    def put(res_re, res_im):
        for out_ref in out_refs:
            out_ref[0, 0] = res_re
            out_ref[0, 1] = res_im

    @pl.when(step == 0)
    def _():
        total_ref[...] = jnp.zeros_like(total_ref)
        for start in range(0, sources, 128):
            row = bright_ref[pl.ds(index, 1), pl.ds(start, 128)]
            column_ref[pl.ds(start, 128)] = jnp.broadcast_to(row, (128, 128)).T

    @pl.when(tab_ref[step, KIND] != 2)
    def _():
        load(one_ref, ONE_AT)
        load(two_ref, TWO_AT)

    @pl.when(tab_ref[step, KIND] == 0)
    def _():
        one_re, one_im, two_re, two_im = one_ref[0], one_ref[1], two_ref[0], two_ref[1]
        pred_re, pred_im = cross(*scaled_of(one_re, one_im), two_re, two_im)
        weights = outer(keep_one_ref[...], keep_two_ref[...])
        res_re = (weights * (vis_ref[0, 0, 0, 0].astype(jnp.float32) - pred_re)).astype(jnp.bfloat16)
        res_im = (weights * (vis_ref[0, 0, 0, 1].astype(jnp.float32) - pred_im)).astype(jnp.bfloat16)
        put(res_re, res_im)
        sum_re, sum_im = pull(one_re, one_im, res_re, res_im, 1)
        add_grad(sum_re * two_re.astype(jnp.float32) - sum_im * two_im.astype(jnp.float32))

    @pl.when(tab_ref[step, KIND] == 1)
    def _():
        one_re, one_im, two_re, two_im = one_ref[0], one_ref[1], two_ref[0], two_ref[1]
        row_ids = lax.broadcasted_iota(jnp.int32, (span, span), 0)
        col_ids = lax.broadcasted_iota(jnp.int32, (span, span), 1)
        upper = row_ids < col_ids
        lower = row_ids > col_ids
        first_re, first_im = cross(*scaled_of(one_re, one_im), one_re, one_im)
        second_re, second_im = cross(two_re, two_im, *scaled_of(two_re, two_im))
        keep_one = keep_one_ref[...]
        keep_two = keep_two_ref[...]
        weights = jnp.where(upper, outer(keep_one, keep_one), 0.0) + jnp.where(
            lower, outer(keep_two, keep_two), 0.0
        )
        vis_re = vis_ref[0, 0, 0, 0].astype(jnp.float32)
        vis_im = vis_ref[0, 0, 0, 1].astype(jnp.float32)
        res_re = (weights * (vis_re - jnp.where(upper, first_re, second_re))).astype(jnp.bfloat16)
        res_im = (weights * (vis_im - jnp.where(upper, first_im, -second_im))).astype(jnp.bfloat16)
        put(res_re, res_im)
        none = jnp.zeros_like(res_re)
        sum_re, sum_im = pull(
            one_re, one_im, jnp.where(upper, res_re, none), jnp.where(upper, res_im, none), 1
        )
        add_grad(sum_re * one_re.astype(jnp.float32) - sum_im * one_im.astype(jnp.float32))
        sum_re, sum_im = pull(
            two_re, two_im, jnp.where(lower, res_re, none), jnp.where(lower, res_im, none), -1
        )
        add_grad(sum_re * two_re.astype(jnp.float32) + sum_im * two_im.astype(jnp.float32))

    @pl.when(step == pl.num_programs(0) - 1)
    def _():
        grad_ref[...] = jnp.sum(total_ref[...].T, axis=0, keepdims=True)


def unit_work(index, table, place, pieces, vis, keep, bright, outs):
    span = vis.shape[5]
    slots = keep.shape[0]
    sources = sum(array.shape[-2] for array in pieces[0][0]) + (
        pieces[0][1][0].shape[-2] if pieces[0][1] else 0
    )
    whole = pl.BlockSpec(memory_space=pltpu.VMEM)
    arrays = [array for both, single in pieces for array in (*both, *single)]
    in_specs = [whole] * len(arrays) + [
        pl.BlockSpec(
            (1, 1, 1, 2, span, span),
            lambda u, tab, at: (tab[u, VIS_AT], tab[u, VIS_AT + 1], index, 0, 0, 0),
        ),
        pl.BlockSpec((slots, span), lambda u, tab, at: (0, tab[u, ONE])),
        pl.BlockSpec((slots, span), lambda u, tab, at: (0, tab[u, TWO])),
        whole,
    ]
    operands = [table, place, *arrays, vis, keep, keep, bright]
    aliases = {}
    out_specs, out_shapes = [], []
    for n, out in enumerate(outs):
        rows = out
        if not isinstance(out, int):
            rows = out.shape[0]
            aliases[len(operands)] = n
            operands.append(out)
            in_specs.append(pl.BlockSpec(memory_space=pl.ANY))
        out_specs.append(
            pl.BlockSpec((1, 2, span, span), lambda u, tab, at, n=n: (tab[u, OUT_ROWS + n], 0, 0, 0))
        )
        out_shapes.append(jax.ShapeDtypeStruct((rows, 2, span, span), jnp.bfloat16))
    out_specs.append(pl.BlockSpec((1, sources), lambda u, tab, at: (0, 0)))
    out_shapes.append(jax.ShapeDtypeStruct((1, sources), jnp.float32))
    steps = table.shape[0]
    flops = 16 * steps * sources * span * span
    kinds = [(len(both), int(bool(single))) for both, single in pieces]
    return pl.pallas_call(
        functools.partial(unit_kernel, index, kinds, len(outs), len(aliases)),
        grid_spec=pltpu.PrefetchScalarGridSpec(
            num_scalar_prefetch=2,
            grid=(steps,),
            in_specs=in_specs,
            out_specs=out_specs,
            scratch_shapes=[
                pltpu.VMEM((sources, 128), jnp.float32),
                pltpu.VMEM((sources, 128), jnp.float32),
                pltpu.VMEM((2, sources, span), jnp.bfloat16),
                pltpu.VMEM((2, sources, span), jnp.bfloat16),
            ],
        ),
        out_shape=out_shapes,
        input_output_aliases=aliases,
        compiler_params=pltpu.CompilerParams(vmem_limit_bytes=48 * 1024 * 1024),
        cost_estimate=pl.CostEstimate(flops=flops, bytes_accessed=flops // 128, transcendentals=0),
        name="unit_work",
    )(*operands)


def put_kernel(sources, tab_ref, *refs):
    out_ref = refs[-1]
    for step, (which, row) in enumerate(sources):

        @pl.when(pl.program_id(0) == step)
        def _(which=which, row=row):
            out_ref[0, 0] = refs[which][...] if row is None else refs[which][row]


def put_residuals(sources, arrays, targets, shape, residual):
    span = shape[-1]
    whole = pl.BlockSpec(memory_space=pltpu.VMEM)
    operands = [targets, *arrays]
    in_specs = [whole] * len(arrays)
    aliases = {}
    if residual is not None:
        aliases = {len(operands): 0}
        operands.append(residual)
        in_specs.append(pl.BlockSpec(memory_space=pl.ANY))
    return pl.pallas_call(
        functools.partial(put_kernel, sources),
        grid_spec=pltpu.PrefetchScalarGridSpec(
            num_scalar_prefetch=1,
            grid=(len(sources),),
            in_specs=in_specs,
            out_specs=pl.BlockSpec(
                (1, 1, 2, span, span), lambda n, tab: (tab[n, 0], tab[n, 1], 0, 0, 0)
            ),
        ),
        out_shape=jax.ShapeDtypeStruct(shape, jnp.bfloat16),
        input_output_aliases=aliases,
        compiler_params=pltpu.CompilerParams(vmem_limit_bytes=32 * 1024 * 1024),
        name="put_residuals",
    )(*operands)


class Routes:
    def __init__(self, planes, width, units):
        count = planes * width
        blocks = int(units[:, :2].max()) + 1
        self.width = width
        self.units_dev = units_dev = units.shape[0] // count
        ring = [0] + list(range(1, planes, 2)) + list(range(planes - 2, 0, -2))

        def along(step):
            at = {plane: ring[(n + step) % planes] for n, plane in enumerate(ring)}
            return [(t, at[t // width] * width + t % width) for t in range(count)]

        self.onward = along(1)
        self.backward = along(-1)
        self.opposite = along(2)
        self.partner = [[(t, t ^ m) for t in range(count)] for m in range(width)]

        touched = [set(units[u, :2].tolist()) for u in range(units.shape[0])]
        home = [list(range(t * units_dev, (t + 1) * units_dev)) for t in range(count)]
        of_plane = [range(z * width * units_dev, (z + 1) * width * units_dev) for z in range(planes)]

        def most(wanted):
            return max(sum(bool(wanted(touched[u])) for u in plane) for plane in of_plane)

        def stuck(block):
            return sum(all(block in touched[u] for u in mine) for mine in home)

        end = min(range(blocks), key=lambda b: (stuck(b), most(lambda t: b in t)))
        rest = [b for b in range(blocks) if b != end]
        start = min(
            itertools.combinations(rest, blocks // 2),
            key=lambda c: most(lambda t: end not in t and not t <= set(c)),
        )
        self.pieces = [list(start), [b for b in rest if b not in start], [end]]
        events = []
        for blocks_of in touched:
            events.append(max(n for n, piece in enumerate(self.pieces) if blocks_of & set(piece)))
        order = [sorted(mine, key=lambda u: events[u]) for mine in home]
        self.full = [list(range(blocks))]

        def rows_of(t, pieces, wanted, row_of, trash):
            rows = []
            for m in range(width):
                for phase, u in enumerate(order[t ^ m]):
                    if not wanted(u):
                        continue
                    one, two, kind = units[u].tolist()
                    at = [
                        (n, piece.index(b))
                        for b in (one, two)
                        for n, piece in enumerate(pieces)
                        if b in piece
                    ]
                    rows.append(
                        [kind, one, two, *at[0], *at[1], *row_of(m, phase), m, u % units_dev]
                    )
            return rows

        def table_of(pieces, wanted, row_of, trash):
            tables = [rows_of(t, pieces, wanted, row_of, trash) for t in range(count)]
            steps = max(len(rows) for rows in tables)
            for rows in tables:
                while len(rows) < steps:
                    rows.append([2] + (rows[-1][1:] if rows else [0] * (COLUMNS - 1)))
                    rows[-1][OUT_ROWS : OUT_ROWS + 2] = [trash, trash]
            return np.array(tables, np.int32)

        self.first_table = table_of(
            self.full, lambda u: True, lambda m, phase: (m * units_dev + phase, 0), 0
        )
        self.tables = [
            table_of(
                self.pieces,
                lambda u, n=n: events[u] == n,
                lambda m, phase: (m, width) if phase == 0 else (width, m + width * (phase - 1)),
                width,
            )
            for n in range(len(self.pieces))
        ]
        assert units_dev == 2
        assert all(events[order[t][0]] < len(self.pieces) - 1 for t in range(count))
        self.unit_of = np.array([[u % units_dev for u in order[t]] for t in range(count)], np.int32)


def ship(value, pairs):
    return lax.ppermute(value, "tile", pairs)


def in_order(value, *earlier):
    return lax.optimization_barrier((value, *earlier))[0]


def packed_small(source_dirs, source_flux, visible_list):
    listed = visible_list.astype(jnp.float32).reshape(1, -1)
    rows = [source_dirs, source_flux.astype(jnp.float32)[None], listed]
    width = max(row.shape[1] for row in rows)
    return jnp.concatenate([jnp.pad(row, ((0, 0), (0, width - row.shape[1]))) for row in rows], 0)


def plain_program(visibility, beam, antenna_uvw, small, keep):
    units_dev, slots, _, span, _ = visibility.shape
    blocks = beam.shape[3] // span
    tile_index = lax.axis_index("tile")
    units = unit_table(blocks)
    own_rows = np.tile(np.arange(units_dev), units.shape[0] // units_dev)
    none = np.zeros_like(own_rows)
    table = np.stack(
        [units[:, 2], units[:, 0], units[:, 1], none, units[:, 0], none, units[:, 1]]
        + [own_rows, none, none, own_rows],
        1,
    )
    table = lax.dynamic_slice_in_dim(
        jnp.asarray(table.astype(np.int32)), tile_index * units_dev, units_dev, 0
    )
    place = jnp.zeros((1,), jnp.int32)
    bright = None
    residuals, grads = [], []
    for slot in range(slots):
        owned, shine = build_factors(
            (slot, slots), place, beam, [], antenna_uvw, [small], [list(range(blocks))], span
        )
        factors = lax.all_gather(owned, "tile", axis=2, tiled=True)
        if bright is None:
            bright = lax.all_gather(shine, "tile", axis=1, tiled=True)
        residual, grad = unit_work(
            slot, table, place, [([factors], [])], visibility[None], keep, bright, [units_dev]
        )
        residuals.append(residual)
        grads.append(grad)
    summed = lax.psum_scatter(jnp.concatenate(grads, 0), "tile", scatter_dimension=1, tiled=True)
    return jnp.stack(residuals, 1), summed


def plane_program(routes, visibility, beam, antenna_uvw, small, keep):
    units_dev, slots, _, span, _ = visibility.shape
    width = routes.width
    share = slots // width
    tile_index = lax.axis_index("tile")
    mine = tile_index % width
    others = range(1, width)

    def mine_of(rows):
        return lax.dynamic_index_in_dim(jnp.asarray(rows), tile_index, 0, keepdims=False)

    def slots_of(m):
        return jnp.bitwise_xor(mine, m) * share

    place = slots_of(0).astype(jnp.int32).reshape(1)

    smalls = [small] + [ship(small, routes.partner[m]) for m in others]

    def beams_of(index):
        return [
            lax.dynamic_slice_in_dim(beam, slots_of(m) + index, 1, 0)
            for m in others
        ]

    beams = [ship(part, routes.partner[m]) for m, part in zip(others, beams_of(0))]
    (first, bright) = build_factors(
        (0, share), place, beam, beams, antenna_uvw, smalls, routes.full, span
    )

    def near(piece):
        return [ship(piece, routes.onward), ship(piece, routes.backward)]

    def far(piece, sides):
        halves = [ship(sides[0][0], routes.onward), ship(sides[1][1], routes.backward)]
        return ([piece, *sides], halves)

    sides_first = near(first)

    link = first
    later_beams = []
    for m, part in zip(others, beams_of(1)):
        later_beams.append(ship(in_order(part, link), routes.partner[m]))
    link = later_beams[-1]
    *later, _ = build_factors(
        (1, share), place, beam, later_beams, antenna_uvw, smalls, routes.pieces, span
    )
    brights = [
        bright,
        ship(bright, routes.onward),
        ship(bright, routes.backward),
        ship(bright, routes.opposite),
    ]
    vis = []
    for m in range(width):
        part = lax.dynamic_slice_in_dim(visibility, slots_of(m), share, 1)
        if m:
            part = ship(in_order(part, link), routes.partner[m])
            link = part
        vis.append(part)
    vis = jnp.stack(vis, 0)
    bright = jnp.concatenate(brights, 1)

    held = []
    sides = sides_first
    ready = [far(first, sides_first)]
    for n, piece in enumerate(later):
        if n == len(later) - 1:
            first_res, first_grad = unit_work(
                0,
                mine_of(routes.first_table),
                place,
                [ready[0]],
                vis,
                keep,
                bright,
                [width * units_dev],
            )
            piece = in_order(piece, first_grad)
        piece = in_order(piece, *sides)
        sides = near(piece)
        held.append((piece, sides))
        ready.append(far(piece, sides))

    residual = None
    unit_of = mine_of(routes.unit_of)

    def targets_of(pairs, index):
        return jnp.stack(
            [jnp.stack([unit_of[phase], slots_of(m).astype(jnp.int32) + index]) for m, phase in pairs]
        ).astype(jnp.int32)

    returned = []
    for m in others:
        rows = first_res[m * units_dev : (m + 1) * units_dev]
        returned.append(ship(in_order(rows, link), routes.partner[m]))
        link = returned[-1]
    pairs = [(m, phase) for m in range(width) for phase in range(units_dev)]
    residual = put_residuals(
        [(m, phase) for m, phase in pairs],
        [first_res, *returned],
        targets_of(pairs, 0),
        visibility.shape,
        None,
    )

    grads = []
    outs = [width + 1, width + 1]
    for n in range(len(later)):
        last = n == len(later) - 1
        if last:
            outs = outs[1:]
        table = mine_of(routes.tables[n])
        if last:
            table = jnp.concatenate(
                [table[:, :OUT_ROWS], table[:, OUT_ROWS + 1 :][:, :1], table[:, OUT_ROWS + 1 :]], 1
            )
        *outs, grad = unit_work(1, table, place, ready[1 : n + 2], vis, keep, bright, outs)
        grads.append(grad)
        if n >= len(later) - 2:
            back = [ship(outs[0][m], routes.partner[m]) for m in others]
            phase = 1 if last else 0
            pairs = [(m, phase) for m in range(width)]
            residual = put_residuals(
                [(0, 0)] + [(m, None) for m in others],
                [outs[0], *back],
                targets_of(pairs, 1),
                visibility.shape,
                residual,
            )

    partial = jnp.concatenate([first_grad, sum(grads[1:], grads[0])], 0)
    group = partial.shape[1] // 4
    parts = [partial[:, n * group : (n + 1) * group] for n in range(4)]
    plane_sum = (parts[0] + ship(parts[3], routes.opposite)) + (
        ship(parts[1], routes.backward) + ship(parts[2], routes.onward)
    )
    per_group = group // width
    own = [plane_sum[:, m * per_group : (m + 1) * per_group] for m in range(width)]
    own = jnp.stack([own[0]] + [ship(own[m], routes.partner[m]) for m in others], 0)
    ids = jnp.arange(width, dtype=jnp.int32)
    here = jnp.bitwise_xor(ids[:, None], mine) == ids[None, :]
    summed = jnp.sum(jnp.where(here[:, :, None, None], own[None], 0.0), axis=1)
    return residual, summed.reshape(slots, per_group)


def per_device(
    visibility, station_beam, antenna_uvw, source_dirs, source_flux, visible_list, antenna_flags
):
    span = visibility.shape[4]
    antennas = station_beam.shape[3]
    small = packed_small(source_dirs, source_flux, visible_list)
    keep = 1.0 - antenna_flags.astype(jnp.float32)
    arguments = (visibility, station_beam, antenna_uvw, small, keep)
    if lax.axis_size("tile") == 16:
        routes = Routes(4, 4, unit_table(antennas // span))
        residual, summed = plane_program(routes, *arguments)
    else:
        residual, summed = plain_program(*arguments)
    return (residual, summed * (-1.0 / (8.0 * antennas)))


def solution(mesh):
    return jax.shard_map(
        per_device,
        mesh=mesh,
        in_specs=(
            P("tile", "grp", None, None, None),
            P("grp", None, "tile", None),
            P("grp", None, None),
            P(None, "tile"),
            P(("grp", "tile")),
            P(None, "tile"),
            P("grp", None),
        ),
        out_specs=(P("tile", "grp", None, None, None), P("grp", "tile")),
        check_vma=False,
    )
```

```python
import functools
import itertools

import jax
import jax.numpy as jnp
import numpy as np
from jax import lax
from jax.experimental import pallas as pl
from jax.experimental.pallas import tpu as pltpu
from jax.sharding import PartitionSpec as P


def unit_table(block_count):
    first_list = []
    second_list = []
    diag_list = []
    for row_block in range(block_count):
        for col_block in range(row_block + 1, block_count):
            first_list.append(row_block)
            second_list.append(col_block)
            diag_list.append(0)
    for pair_index in range(block_count // 2):
        first_list.append(2 * pair_index)
        second_list.append(2 * pair_index + 1)
        diag_list.append(1)
    return np.stack([first_list, second_list, diag_list], 1).astype(np.int32)


def turn_polynomials():
    nodes = 0.125 + 0.125 * np.cos(np.pi * (np.arange(64) + 0.5) / 64)
    root = np.sqrt(nodes)
    fit = np.polynomial.Polynomial.fit
    sine = fit(nodes, np.sin(2 * np.pi * root) / root, 7, domain=[0, 0.25]).convert()
    cosine = fit(nodes, np.cos(2 * np.pi * root), 8, domain=[0, 0.25]).convert()
    return [float(c) for c in sine.coef], [float(c) for c in cosine.coef]


def horner(coefs, x):
    total = coefs[-1]
    for coef in coefs[-2::-1]:
        total = total * x + coef
    return total


def build_kernel(sets, small_count, slot_ids, pieces, tab_ref, *refs):
    beams, smalls, refs = refs[:sets], refs[sets : sets + small_count], refs[sets + small_count :]
    beams = (None,) * (small_count - sets) + beams
    uvw_ref, outs, bright_ref = refs[0], refs[1 : 1 + len(pieces)], refs[-1]
    per_group = outs[0].shape[2] // sets
    span = outs[0].shape[3]
    width = smalls[0].shape[1]
    lanes = lax.broadcasted_iota(jnp.int32, (per_group, width), 1)
    rows = lax.broadcasted_iota(jnp.int32, (per_group, width), 0)
    bright_lanes = lax.broadcasted_iota(jnp.int32, (per_group, 128), 1)
    sin_coefs, cos_coefs = turn_polynomials()
    brights = []
    for part, small in enumerate(smalls):

        def pick(chosen, row):
            return jnp.sum(jnp.where(chosen, small[row : row + 1, :], 0.0), axis=1, keepdims=True)

        def chosen_at(index):
            listed = pick(lanes == (tab_ref[0] + index) * per_group + rows, 3)
            return listed.astype(jnp.int32) == lanes

        bright = jnp.zeros((per_group, 128), jnp.float32)
        for index in range(slot_ids[1]):
            bright = jnp.where(bright_lanes == index, pick(chosen_at(index), 2), bright)
        brights.append(bright)
        if beams[part] is None:
            continue
        group = pl.ds((part - small_count + sets) * per_group, per_group)
        chosen = chosen_at(slot_ids[0])
        east = pick(chosen, 0)
        north = pick(chosen, 1)
        depth = jnp.sqrt(1.0 - east * east - north * north) - 1.0
        for out_ref, piece in zip(outs, pieces):
            for place, block in enumerate(piece):
                cols = pl.ds(block * span, span)
                delay = (
                    uvw_ref[0, 0:1, cols] * east
                    + uvw_ref[0, 1:2, cols] * north
                    + uvw_ref[0, 2:3, cols] * depth
                )
                turn = delay - jnp.floor(delay + 0.5)
                square = turn * turn
                sine = horner(sin_coefs, square) * turn
                cosine = horner(cos_coefs, square)
                real = beams[part][0, 0, :, cols].astype(jnp.float32)
                imag = beams[part][0, 1, :, cols].astype(jnp.float32)
                out_ref[0, place, group] = (real * cosine + imag * sine).astype(jnp.bfloat16)
                out_ref[1, place, group] = (imag * cosine - real * sine).astype(jnp.bfloat16)
    missing = -len(brights) * per_group % 128
    if missing:
        brights.append(jnp.zeros((missing, 128), jnp.float32))
    turned = jnp.concatenate(brights, 0).T
    bright_ref[...] = turned[: bright_ref.shape[0], : bright_ref.shape[1]]


def build_factors(slot_ids, table, beam, other_beams, antenna_uvw, smalls, pieces, span):
    _, _, per_group, antennas = (other_beams or [beam])[0].shape
    sets = (beam is not None) + len(other_beams)
    index = slot_ids[0]
    whole = pl.BlockSpec(memory_space=pltpu.VMEM)
    shapes = [(2, len(piece), sets * per_group, span) for piece in pieces]
    own = []
    if beam is not None:
        own.append(
            pl.BlockSpec((1, 2, per_group, antennas), lambda n, tab: (tab[0] + index, 0, 0, 0))
        )
    return pl.pallas_call(
        functools.partial(build_kernel, sets, len(smalls), slot_ids, pieces),
        grid_spec=pltpu.PrefetchScalarGridSpec(
            num_scalar_prefetch=1,
            grid=(1,),
            in_specs=[
                *own,
                *[whole] * (len(other_beams) + len(smalls)),
                pl.BlockSpec((1, 3, antennas), lambda n, tab: (tab[0] + index, 0, 0)),
            ],
            out_specs=[whole] * (len(pieces) + 1),
        ),
        out_shape=[jax.ShapeDtypeStruct(shape, jnp.bfloat16) for shape in shapes]
        + [jax.ShapeDtypeStruct((8, len(smalls) * per_group), jnp.float32)],
        compiler_params=pltpu.CompilerParams(vmem_limit_bytes=40 * 1024 * 1024),
        name="build_factors",
    )(table, *([beam] if own else []), *other_beams, *smalls, antenna_uvw)


def slice_kernel(count, tab_ref, *refs):
    for source, target in zip(refs[:count], refs[count:]):
        target[...] = source[...]


def slices_for(array, axis, size, starts, table):
    lead = axis > 0
    shape = array.shape[:axis] + (size,) + array.shape[axis + 1 :]
    block = (1,) + shape[1:] if lead else shape
    rest = (0,) * (array.ndim - axis - 1)
    return pl.pallas_call(
        functools.partial(slice_kernel, len(starts)),
        grid_spec=pltpu.PrefetchScalarGridSpec(
            num_scalar_prefetch=1,
            grid=(shape[0] if lead else 1,),
            in_specs=[
                pl.BlockSpec(
                    block,
                    lambda n, tab, start=start, shift=shift: (
                        *((n,) if lead else ()),
                        tab[start] // size + shift,
                        *rest,
                    ),
                )
                for start, shift in starts
            ],
            out_specs=[
                pl.BlockSpec(block, lambda n, tab: (n,) + (0,) * (array.ndim - 1)) for _ in starts
            ],
        ),
        out_shape=[jax.ShapeDtypeStruct(shape, array.dtype) for _ in starts],
        name="slices_for",
    )(table, *[array] * len(starts))


KIND, ONE, TWO, ONE_AT, TWO_AT, OUT_ROWS, VIS_AT = 0, 1, 2, 3, 5, 7, 9
COLUMNS = 11


def unit_kernel(index, offset, pieces, outs, aliased, tab_ref, *refs):
    arrays = []
    for entries in pieces:
        found = []
        for count, start in entries:
            parts = (refs[0].at[0], refs[0].at[1]) if count == 1 else refs[:2]
            found.append((parts, start))
            refs = refs[count:]
        arrays.append(found)
    vis_ref, keep_one_ref, keep_two_ref, bright_ref = refs[:4]
    refs = refs[4 + aliased :]
    out_refs, grad_ref = refs[:outs], refs[outs]
    total_ref, column_ref, one_ref, two_ref = refs[outs + 1 :]
    step = pl.program_id(0)
    slot = tab_ref[0] + index
    sources, span = one_ref.shape[1:]

    def entry(column):
        return tab_ref[offset + step * COLUMNS + column]

    def load(target, at):
        for n, found in enumerate(arrays):

            @pl.when(entry(at) == n)
            def _(found=found):
                place = entry(at + 1)
                for parts, start in found:
                    for part in (0, 1):
                        target[part, pl.ds(start, parts[0].shape[1])] = parts[part][place]

    def dot(a, b):
        return lax.dot_general(a, b, (((1,), (0,)), ((), ())), preferred_element_type=jnp.float32)

    def scaled_of(re, im):
        column = jnp.concatenate([column_ref[...]] * (span // 128), 1)
        return (
            (re.astype(jnp.float32) * column).astype(jnp.bfloat16),
            (im.astype(jnp.float32) * column).astype(jnp.bfloat16),
        )

    def outer(a, b):
        row_ids = lax.broadcasted_iota(jnp.int32, a.shape, 0)
        a = jnp.where(row_ids == slot, a, 0.0)
        return lax.dot_general(a, b, (((0,), (0,)), ((), ())), preferred_element_type=jnp.float32)

    def cross(a_re, a_im, b_re, b_im):
        lhs = jnp.concatenate([a_re, a_im], 0).T
        rhs = jnp.concatenate(
            [jnp.concatenate([b_re, -b_im], 1), jnp.concatenate([b_im, b_re], 1)], 0
        )
        both = dot(lhs, rhs)
        return both[:, :span], both[:, span:]

    def pull(re, im, res_re, res_im, sign):
        lhs = jnp.concatenate([re, im], 1)
        rhs = jnp.concatenate(
            [
                jnp.concatenate([res_re, res_im], 1),
                jnp.concatenate([res_im, -res_re] if sign == 1 else [-res_im, res_re], 1),
            ],
            0,
        )
        both = dot(lhs, rhs)
        return both[:, :span], both[:, span:]

    def add_grad(value):
        folded = value[:, :128]
        for start in range(128, span, 128):
            folded = folded + value[:, start : start + 128]
        total_ref[...] += folded

    def put(res_re, res_im):
        for out_ref in out_refs:
            out_ref[0, 0] = res_re
            out_ref[0, 1] = res_im

    @pl.when(step == 0)
    def _():
        total_ref[...] = jnp.zeros_like(total_ref)
        for start in range(0, sources, 128):
            row = bright_ref[pl.ds(index, 1), pl.ds(start, 128)]
            column_ref[pl.ds(start, 128)] = jnp.broadcast_to(row, (128, 128)).T

    @pl.when(entry(KIND) != 2)
    def _():
        load(one_ref, ONE_AT)
        load(two_ref, TWO_AT)

    @pl.when(entry(KIND) == 0)
    def _():
        one_re, one_im, two_re, two_im = one_ref[0], one_ref[1], two_ref[0], two_ref[1]
        pred_re, pred_im = cross(*scaled_of(one_re, one_im), two_re, two_im)
        weights = outer(keep_one_ref[...], keep_two_ref[...])
        res_re = (weights * (vis_ref[0, 0, 0, 0].astype(jnp.float32) - pred_re)).astype(jnp.bfloat16)
        res_im = (weights * (vis_ref[0, 0, 0, 1].astype(jnp.float32) - pred_im)).astype(jnp.bfloat16)
        put(res_re, res_im)
        sum_re, sum_im = pull(one_re, one_im, res_re, res_im, 1)
        add_grad(sum_re * two_re.astype(jnp.float32) - sum_im * two_im.astype(jnp.float32))

    @pl.when(entry(KIND) == 1)
    def _():
        one_re, one_im, two_re, two_im = one_ref[0], one_ref[1], two_ref[0], two_ref[1]
        row_ids = lax.broadcasted_iota(jnp.int32, (span, span), 0)
        col_ids = lax.broadcasted_iota(jnp.int32, (span, span), 1)
        upper = row_ids < col_ids
        lower = row_ids > col_ids
        first_re, first_im = cross(*scaled_of(one_re, one_im), one_re, one_im)
        second_re, second_im = cross(two_re, two_im, *scaled_of(two_re, two_im))
        keep_one = keep_one_ref[...]
        keep_two = keep_two_ref[...]
        weights = jnp.where(upper, outer(keep_one, keep_one), 0.0) + jnp.where(
            lower, outer(keep_two, keep_two), 0.0
        )
        vis_re = vis_ref[0, 0, 0, 0].astype(jnp.float32)
        vis_im = vis_ref[0, 0, 0, 1].astype(jnp.float32)
        res_re = (weights * (vis_re - jnp.where(upper, first_re, second_re))).astype(jnp.bfloat16)
        res_im = (weights * (vis_im - jnp.where(upper, first_im, -second_im))).astype(jnp.bfloat16)
        put(res_re, res_im)
        none = jnp.zeros_like(res_re)
        sum_re, sum_im = pull(
            one_re, one_im, jnp.where(upper, res_re, none), jnp.where(upper, res_im, none), 1
        )
        add_grad(sum_re * one_re.astype(jnp.float32) - sum_im * one_im.astype(jnp.float32))
        sum_re, sum_im = pull(
            two_re, two_im, jnp.where(lower, res_re, none), jnp.where(lower, res_im, none), -1
        )
        add_grad(sum_re * two_re.astype(jnp.float32) + sum_im * two_im.astype(jnp.float32))

    @pl.when(step == pl.num_programs(0) - 1)
    def _():
        grad_ref[...] = jnp.sum(total_ref[...].T, axis=0, keepdims=True)


def unit_work(index, steps, table, pieces, vis, keep, bright, outs):
    span = vis.shape[5]
    slots = keep.shape[0]
    sources = sum(arrays[0].shape[-2] for arrays, _ in pieces[0])
    offset, count = steps
    whole = pl.BlockSpec(memory_space=pltpu.VMEM)
    arrays = [array for piece in pieces for entry, _ in piece for array in entry]

    def at(tab, step, column):
        return tab[offset + step * COLUMNS + column]

    in_specs = [whole] * len(arrays) + [
        pl.BlockSpec(
            (1, 1, 1, 2, span, span),
            lambda u, tab: (at(tab, u, VIS_AT), at(tab, u, VIS_AT + 1), index, 0, 0, 0),
        ),
        pl.BlockSpec((slots, span), lambda u, tab: (0, at(tab, u, ONE))),
        pl.BlockSpec((slots, span), lambda u, tab: (0, at(tab, u, TWO))),
        whole,
    ]
    operands = [table, *arrays, vis, keep, keep, bright]
    aliases = {}
    out_specs, out_shapes = [], []
    for which, out in outs:
        rows = out
        if not isinstance(out, int):
            rows = out.shape[0]
            aliases[len(operands)] = len(out_specs)
            operands.append(out)
            in_specs.append(pl.BlockSpec(memory_space=pl.ANY))
        out_specs.append(
            pl.BlockSpec(
                (1, 2, span, span),
                lambda u, tab, which=which: (at(tab, u, OUT_ROWS + which), 0, 0, 0),
            )
        )
        out_shapes.append(jax.ShapeDtypeStruct((rows, 2, span, span), jnp.bfloat16))
    out_specs.append(pl.BlockSpec((1, sources), lambda u, tab: (0, 0)))
    out_shapes.append(jax.ShapeDtypeStruct((1, sources), jnp.float32))
    flops = 16 * count * sources * span * span
    kinds = [[(len(entry), start) for entry, start in piece] for piece in pieces]
    return pl.pallas_call(
        functools.partial(unit_kernel, index, offset, kinds, len(outs), len(aliases)),
        grid_spec=pltpu.PrefetchScalarGridSpec(
            num_scalar_prefetch=1,
            grid=(count,),
            in_specs=in_specs,
            out_specs=out_specs,
            scratch_shapes=[
                pltpu.VMEM((sources, 128), jnp.float32),
                pltpu.VMEM((sources, 128), jnp.float32),
                pltpu.VMEM((2, sources, span), jnp.bfloat16),
                pltpu.VMEM((2, sources, span), jnp.bfloat16),
            ],
        ),
        out_shape=out_shapes,
        input_output_aliases=aliases,
        compiler_params=pltpu.CompilerParams(vmem_limit_bytes=48 * 1024 * 1024),
        cost_estimate=pl.CostEstimate(flops=flops, bytes_accessed=flops // 128, transcendentals=0),
        name="unit_work",
    )(*operands)


def put_kernel(sources, tab_ref, *refs):
    out_ref = refs[-1]
    for step, (which, row) in enumerate(sources):

        @pl.when(pl.program_id(0) == step)
        def _(which=which, row=row):
            out_ref[0, 0] = refs[which][...] if row is None else refs[which][row]


def put_residuals(sources, arrays, offset, table, shape, residual):
    span = shape[-1]
    whole = pl.BlockSpec(memory_space=pltpu.VMEM)
    operands = [table, *arrays]
    in_specs = [whole] * len(arrays)
    aliases = {}
    if residual is not None:
        aliases = {len(operands): 0}
        operands.append(residual)
        in_specs.append(pl.BlockSpec(memory_space=pl.ANY))
    return pl.pallas_call(
        functools.partial(put_kernel, sources),
        grid_spec=pltpu.PrefetchScalarGridSpec(
            num_scalar_prefetch=1,
            grid=(len(sources),),
            in_specs=in_specs,
            out_specs=pl.BlockSpec(
                (1, 1, 2, span, span),
                lambda n, tab: (tab[offset + 2 * n], tab[offset + 2 * n + 1], 0, 0, 0),
            ),
        ),
        out_shape=jax.ShapeDtypeStruct(shape, jnp.bfloat16),
        input_output_aliases=aliases,
        compiler_params=pltpu.CompilerParams(vmem_limit_bytes=32 * 1024 * 1024),
        name="put_residuals",
    )(*operands)


class Routes:
    def __init__(self, planes, width, units, share):
        count = planes * width
        blocks = int(units[:, :2].max()) + 1
        self.width = width
        self.units_dev = units_dev = units.shape[0] // count
        ring = [0] + list(range(1, planes, 2)) + list(range(planes - 2, 0, -2))

        def along(step):
            at = {plane: ring[(n + step) % planes] for n, plane in enumerate(ring)}
            return [(t, at[t // width] * width + t % width) for t in range(count)]

        self.onward = along(1)
        self.backward = along(-1)
        self.opposite = along(2)
        self.partner = [[(t, t ^ m) for t in range(count)] for m in range(width)]

        touched = [set(units[u, :2].tolist()) for u in range(units.shape[0])]
        home = [list(range(t * units_dev, (t + 1) * units_dev)) for t in range(count)]
        of_plane = [range(z * width * units_dev, (z + 1) * width * units_dev) for z in range(planes)]

        def most(wanted):
            return max(sum(bool(wanted(touched[u])) for u in plane) for plane in of_plane)

        def stuck(block):
            return sum(all(block in touched[u] for u in mine) for mine in home)

        end = min(range(blocks), key=lambda b: (stuck(b), most(lambda t: b in t)))
        rest = [b for b in range(blocks) if b != end]
        start = min(
            itertools.combinations(rest, blocks // 2),
            key=lambda c: most(lambda t: end not in t and not t <= set(c)),
        )
        self.pieces = [list(start), [b for b in rest if b not in start], [end]]
        events = []
        for blocks_of in touched:
            events.append(max(n for n, piece in enumerate(self.pieces) if blocks_of & set(piece)))
        order = [sorted(mine, key=lambda u: events[u]) for mine in home]
        self.full = [list(range(blocks))]

        def rows_of(t, pieces, wanted, row_of, trash):
            rows = []
            for m in range(width):
                for phase, u in enumerate(order[t ^ m]):
                    if not wanted(u):
                        continue
                    one, two, kind = units[u].tolist()
                    at = [
                        (n, piece.index(b))
                        for b in (one, two)
                        for n, piece in enumerate(pieces)
                        if b in piece
                    ]
                    rows.append(
                        [kind, one, two, *at[0], *at[1], *row_of(m, phase), m, u % units_dev]
                    )
            return rows

        def table_of(pieces, wanted, row_of, trash):
            tables = [rows_of(t, pieces, wanted, row_of, trash) for t in range(count)]
            steps = max(len(rows) for rows in tables)
            for rows in tables:
                while len(rows) < steps:
                    rows.append([2] + (rows[-1][1:] if rows else [0] * (COLUMNS - 1)))
                    rows[-1][OUT_ROWS : OUT_ROWS + 2] = [trash, trash]
            return np.array(tables, np.int32)

        first_table = table_of(
            self.full, lambda u: True, lambda m, phase: (m * units_dev + phase, 0), 0
        )
        tables = [
            table_of(
                self.pieces,
                lambda u, n=n: events[u] == n,
                lambda m, phase: (m, width) if phase == 0 else (width, m + width * (phase - 1)),
                width,
            )
            for n in range(len(self.pieces))
        ]
        assert units_dev == 2
        assert all(events[order[t][0]] < len(self.pieces) - 1 for t in range(count))

        def targets(phases, index):
            rows = np.zeros((count, width, len(phases), 2), np.int32)
            for t in range(count):
                for m in range(width):
                    for n, phase in enumerate(phases):
                        rows[t, m, n] = order[t][phase] % units_dev, (t % width ^ m) * share + index
            return rows

        starts = np.array([[(t % width ^ m) * share for m in range(width)] for t in range(count)])
        parts = [starts, first_table, *tables, targets([0, 1], 0), targets([0], 1), targets([1], 1)]
        parts = [part.reshape(count, -1).astype(np.int32) for part in parts]
        ends = np.cumsum([part.shape[1] for part in parts]).tolist()
        self.table = np.concatenate(parts, 1)
        self.first_steps = (ends[0], first_table.shape[1])
        self.steps = [(ends[1 + n], table.shape[1]) for n, table in enumerate(tables)]
        self.targets = ends[1 + len(tables) : 4 + len(tables)]


def ship(value, pairs):
    return lax.ppermute(value, "tile", pairs)


def in_order(value, *earlier):
    return lax.optimization_barrier((value, *earlier))[0]


def packed_small(source_dirs, source_flux, visible_list):
    listed = visible_list.astype(jnp.float32).reshape(1, -1)
    rows = [source_dirs, source_flux.astype(jnp.float32)[None], listed]
    width = max(row.shape[1] for row in rows)
    return jnp.concatenate([jnp.pad(row, ((0, 0), (0, width - row.shape[1]))) for row in rows], 0)


def plain_program(visibility, beam, antenna_uvw, small, keep):
    units_dev, slots, _, span, _ = visibility.shape
    blocks = beam.shape[3] // span
    tile_index = lax.axis_index("tile")
    units = unit_table(blocks)
    own_rows = np.tile(np.arange(units_dev), units.shape[0] // units_dev)
    none = np.zeros_like(own_rows)
    table = np.stack(
        [units[:, 2], units[:, 0], units[:, 1], none, units[:, 0], none, units[:, 1]]
        + [own_rows, none, none, own_rows],
        1,
    )
    table = table.astype(np.int32).reshape(-1, units_dev * COLUMNS)
    table = np.pad(table, ((0, 0), (1, 0)))
    table = lax.dynamic_index_in_dim(jnp.asarray(table), tile_index, 0, keepdims=False)
    bright = None
    residuals, grads = [], []
    for slot in range(slots):
        owned, shine = build_factors(
            (slot, slots), table, beam, [], antenna_uvw, [small], [list(range(blocks))], span
        )
        factors = lax.all_gather(owned, "tile", axis=2, tiled=True)
        if bright is None:
            bright = lax.all_gather(shine, "tile", axis=1, tiled=True)
        residual, grad = unit_work(
            slot,
            (1, units_dev),
            table,
            [[((factors,), 0)]],
            visibility[None],
            keep,
            bright,
            [(0, units_dev)],
        )
        residuals.append(residual)
        grads.append(grad)
    summed = lax.psum_scatter(jnp.concatenate(grads, 0), "tile", scatter_dimension=1, tiled=True)
    return jnp.stack(residuals, 1), summed


def plane_program(routes, visibility, beam, antenna_uvw, small, keep):
    units_dev, slots, _, span, _ = visibility.shape
    width = routes.width
    share = slots // width
    tile_index = lax.axis_index("tile")
    mine = tile_index % width
    others = range(1, width)
    table = lax.dynamic_index_in_dim(jnp.asarray(routes.table), tile_index, 0, keepdims=False)

    def near(piece):
        return [ship(piece, routes.onward), ship(piece, routes.backward)]

    def far(sides):
        return ship(sides[0][0], routes.onward), ship(sides[1][1], routes.backward)

    def entries(piece, sides, halves, first=0):
        found = [(piece,), (sides[0],), (sides[1],), halves]
        return [(arrays, n * group + first) for n, arrays in enumerate(found)]

    per_group = beam.shape[2]
    group = width * per_group

    smalls = [small] + [ship(small, routes.partner[m]) for m in others]
    beams = slices_for(beam, 0, 1, [(m, 0) for m in others], table)
    beams = [ship(part, routes.partner[m]) for m, part in zip(others, beams)]
    first_a, _ = build_factors(
        (0, share), table, beam, [], antenna_uvw, [small], routes.full, span
    )
    sides_a = near(first_a)
    first_b, bright = build_factors(
        (0, share), table, None, beams, antenna_uvw, smalls, routes.full, span
    )
    bright = [
        bright,
        ship(bright, routes.onward),
        ship(bright, routes.backward),
        ship(bright, routes.opposite),
    ]
    bright = jnp.concatenate(bright, 1)
    sides_b = near(first_b)
    far_a = far(sides_a)

    waiting = in_order(beam, *sides_a)
    later_beams = slices_for(waiting, 0, 1, [(m, 1) for m in others], table)
    later_beams = [ship(part, routes.partner[m]) for m, part in zip(others, later_beams)]
    later = build_factors(
        (1, share), table, beam, later_beams, antenna_uvw, smalls, routes.pieces, span
    )[:-1]
    vis = list(
        slices_for(
            in_order(visibility, *later_beams), 1, share, [(m, 0) for m in range(width)], table
        )
    )
    link = later[0]
    for m in others:
        vis[m] = link = ship(in_order(vis[m], link), routes.partner[m])
    vis = jnp.stack(vis, 0)

    far_b = far(sides_b)
    pieces = [entries(first_a, sides_a, far_a) + entries(first_b, sides_b, far_b, per_group)]
    before = [tuple(sides_b), far_b]
    ready = []
    for piece in later:
        piece = in_order(piece, *before[0])
        before = before[1:]
        sides = near(piece)
        halves = far(sides)
        before.append(halves)
        ready.append(entries(piece, sides, halves))

    first_res, first_grad = unit_work(
        0, routes.first_steps, table, pieces, vis, keep, bright, [(0, width * units_dev)]
    )
    returned = []
    for m in others:
        rows = first_res[m * units_dev : (m + 1) * units_dev]
        returned.append(ship(rows, routes.partner[m]))
    pairs = [(m, phase) for m in range(width) for phase in range(units_dev)]
    residual = put_residuals(
        pairs, [first_res, *returned], routes.targets[0], table, visibility.shape, None
    )

    grads = []
    outs = [(0, width + 1), (1, width + 1)]
    waits = [returned[:1], returned[1:], [residual]]
    for n, wait in enumerate(waits):
        last = n == len(waits) - 1
        if last:
            outs = outs[1:]
        *found, grad = unit_work(
            1, routes.steps[n], in_order(table, *wait), ready[: n + 1], vis, keep, bright, outs
        )
        outs = [(which, out) for (which, _), out in zip(outs, found)]
        grads.append(grad)
        if n >= len(waits) - 2:
            back = [ship(found[0][m], routes.partner[m]) for m in others]
            residual = put_residuals(
                [(0, 0)] + [(m, None) for m in others],
                [found[0], *back],
                routes.targets[2 if last else 1],
                table,
                visibility.shape,
                residual,
            )

    partial = jnp.concatenate([first_grad, sum(grads[1:], grads[0])], 0)
    parts = [partial[:, n * group : (n + 1) * group] for n in range(4)]
    plane_sum = (parts[0] + ship(parts[3], routes.opposite)) + (
        ship(parts[1], routes.backward) + ship(parts[2], routes.onward)
    )
    own = [plane_sum[:, m * per_group : (m + 1) * per_group] for m in range(width)]
    own = jnp.stack([own[0]] + [ship(own[m], routes.partner[m]) for m in others], 0)
    ids = jnp.arange(width, dtype=jnp.int32)
    here = jnp.bitwise_xor(ids[:, None], mine) == ids[None, :]
    summed = jnp.sum(jnp.where(here[:, :, None, None], own[None], 0.0), axis=1)
    return residual, summed.reshape(slots, per_group)


def per_device(
    visibility, station_beam, antenna_uvw, source_dirs, source_flux, visible_list, antenna_flags
):
    span = visibility.shape[4]
    antennas = station_beam.shape[3]
    small = packed_small(source_dirs, source_flux, visible_list)
    keep = 1.0 - antenna_flags.astype(jnp.float32)
    arguments = (visibility, station_beam, antenna_uvw, small, keep)
    if lax.axis_size("tile") == 16:
        routes = Routes(4, 4, unit_table(antennas // span), visibility.shape[1] // 4)
        residual, summed = plane_program(routes, *arguments)
    else:
        residual, summed = plain_program(*arguments)
    return (residual, summed * (-1.0 / (8.0 * antennas)))


def solution(mesh):
    return jax.shard_map(
        per_device,
        mesh=mesh,
        in_specs=(
            P("tile", "grp", None, None, None),
            P("grp", None, "tile", None),
            P("grp", None, None),
            P(None, "tile"),
            P(("grp", "tile")),
            P(None, "tile"),
            P("grp", None),
        ),
        out_specs=(P("tile", "grp", None, None, None), P("grp", "tile")),
        check_vma=False,
    )
```

```python
import functools
import itertools

import jax
import jax.numpy as jnp
import numpy as np
from jax import lax
from jax.experimental import pallas as pl
from jax.experimental.pallas import tpu as pltpu
from jax.sharding import PartitionSpec as P


def unit_table(block_count):
    first_list = []
    second_list = []
    diag_list = []
    for row_block in range(block_count):
        for col_block in range(row_block + 1, block_count):
            first_list.append(row_block)
            second_list.append(col_block)
            diag_list.append(0)
    for pair_index in range(block_count // 2):
        first_list.append(2 * pair_index)
        second_list.append(2 * pair_index + 1)
        diag_list.append(1)
    return np.stack([first_list, second_list, diag_list], 1).astype(np.int32)


def turn_polynomials():
    nodes = 0.125 + 0.125 * np.cos(np.pi * (np.arange(64) + 0.5) / 64)
    root = np.sqrt(nodes)
    fit = np.polynomial.Polynomial.fit
    sine = fit(nodes, np.sin(2 * np.pi * root) / root, 7, domain=[0, 0.25]).convert()
    cosine = fit(nodes, np.cos(2 * np.pi * root), 8, domain=[0, 0.25]).convert()
    return [float(c) for c in sine.coef], [float(c) for c in cosine.coef]


def horner(coefs, x):
    total = coefs[-1]
    for coef in coefs[-2::-1]:
        total = total * x + coef
    return total


def build_kernel(sets, slot_ids, pieces, bright_rows, width, tab_ref, *refs):
    uvw_ref, outs = refs[-1 - len(pieces)], refs[-len(pieces) :]
    per_group = sets[0][0]
    span = outs[0].shape[2]
    count = len(sets) * per_group
    sin_coefs, cos_coefs = turn_polynomials()
    brights = []
    for part, (_, beam_at, small_at) in enumerate(sets):
        beam_ref = refs[beam_at]
        if beam_ref.shape[0] == 1:
            beam = [beam_ref.at[0, 0], beam_ref.at[0, 1]]
        else:
            beam = [beam_ref.at[pl.ds(n * per_group, per_group)] for n in (0, 1)]
        small_ref = refs[small_at]
        if small_ref.dtype == jnp.float32:
            small = small_ref[...]
        else:
            small = unsplit(small_ref, 2 * per_group, width)
        lanes = lax.broadcasted_iota(jnp.int32, (per_group, width), 1)
        rows = lax.broadcasted_iota(jnp.int32, (per_group, width), 0)

        def pick(chosen, row):
            return jnp.sum(jnp.where(chosen, small[row : row + 1, :], 0.0), axis=1, keepdims=True)

        def chosen_at(index):
            listed = pick(lanes == (tab_ref[0] + index) * per_group + rows, 3)
            return listed.astype(jnp.int32) == lanes

        group = part * per_group
        if bright_rows:
            columns = lax.broadcasted_iota(jnp.int32, (per_group, span), 1)
            numbers = lax.broadcasted_iota(jnp.int32, (per_group, span), 0) + group
            for index in range(slot_ids[1]):
                flux = pick(chosen_at(index), 2)
                line = jnp.sum(jnp.where(columns == numbers, flux, 0.0), axis=0, keepdims=True)
                if part == 0:
                    brights.append(line)
                else:
                    brights[index] += line
        chosen = chosen_at(slot_ids[0])
        east = pick(chosen, 0)
        north = pick(chosen, 1)
        depth = jnp.sqrt(1.0 - east * east - north * north) - 1.0
        for out_ref, piece in zip(outs, pieces):
            for place, block in enumerate(piece):
                cols = pl.ds(block * span, span)
                delay = (
                    uvw_ref[0, 0:1, cols] * east
                    + uvw_ref[0, 1:2, cols] * north
                    + uvw_ref[0, 2:3, cols] * depth
                )
                turn = delay - jnp.floor(delay + 0.5)
                square = turn * turn
                sine = horner(sin_coefs, square) * turn
                cosine = horner(cos_coefs, square)
                real = beam[0][:, cols].astype(jnp.float32)
                imag = beam[1][:, cols].astype(jnp.float32)
                at = pl.ds(place * count + group, per_group)
                out_ref[0, at] = (real * cosine + imag * sine).astype(jnp.bfloat16)
                out_ref[1, at] = (imag * cosine - real * sine).astype(jnp.bfloat16)
    if bright_rows:
        padding = jnp.zeros((bright_rows - len(brights), span), jnp.float32)
        block = jnp.concatenate(brights + [padding], 0).astype(jnp.bfloat16)
        for part in (0, 1):
            outs[0][part, pl.ds(len(pieces[0]) * count, bright_rows)] = block


def unsplit(message_ref, start, width):
    terms = [message_ref[pl.ds(start, 16), pl.ds(n * width, width)].astype(jnp.float32) for n in range(3)]
    return (terms[0] + terms[1]) + terms[2]


BRIGHT_ROWS = 16


def build_factors(
    slot_ids, table, beam, messages, antenna_uvw, smalls, pieces, span, bright_rows, small_width
):
    slots, _, antennas = antenna_uvw.shape
    per_group = slot_ids[2]
    index = slot_ids[0]
    whole = pl.BlockSpec(memory_space=pltpu.VMEM)
    operands, in_specs, sets = [], [], []
    if beam is not None:
        operands.append(beam)
        in_specs.append(
            pl.BlockSpec((1, 2, per_group, antennas), lambda n, tab: (tab[0] + index, 0, 0, 0))
        )
    operands += messages
    beams = len(operands)
    for n, small in enumerate(smalls):
        at = next((k for k, known in enumerate(operands) if known is small), len(operands))
        if at == len(operands):
            operands.append(small)
        sets.append((per_group, n, at))
    in_specs += [whole] * (len(operands) - len(in_specs))
    in_specs.append(pl.BlockSpec((1, 3, antennas), lambda n, tab: (tab[0] + index, 0, 0)))
    count = beams * per_group
    shapes = [
        (2, len(piece) * count + (0 if n else bright_rows), span) for n, piece in enumerate(pieces)
    ]
    return pl.pallas_call(
        functools.partial(build_kernel, sets, slot_ids, pieces, bright_rows, small_width),
        grid_spec=pltpu.PrefetchScalarGridSpec(
            num_scalar_prefetch=1,
            grid=(1,),
            in_specs=in_specs,
            out_specs=[whole] * len(pieces),
        ),
        out_shape=[jax.ShapeDtypeStruct(shape, jnp.bfloat16) for shape in shapes],
        compiler_params=pltpu.CompilerParams(vmem_limit_bytes=40 * 1024 * 1024),
        cost_estimate=LITTLE,
        name="build_factors",
    )(table, *operands, antenna_uvw)


LITTLE = pl.CostEstimate(flops=1, bytes_accessed=1, transcendentals=0)


def message_kernel(per_group, tab_ref, *refs):
    outs = [ref for ref in refs if ref.dtype == jnp.bfloat16 and len(ref.shape) == 2]
    small_ref = refs[len(outs)] if len(refs) > 2 * len(outs) else None
    for beam_ref, out_ref in zip(refs, outs):
        for part in (0, 1):
            out_ref[pl.ds(part * per_group, per_group)] = beam_ref[0, part]
        if small_ref is not None:
            count, width = small_ref.shape
            rest = jnp.concatenate([small_ref[...], jnp.zeros((16 - count, width), jnp.float32)], 0)
            out_ref[pl.ds(2 * per_group, 16)] = jnp.zeros((16, out_ref.shape[1]), jnp.bfloat16)
            for n in range(3):
                term = rest.astype(jnp.bfloat16)
                out_ref[pl.ds(2 * per_group, 16), pl.ds(n * width, width)] = term
                rest = rest - term.astype(jnp.float32)


def messages_for(beam, index, others, small, table):
    _, _, per_group, antennas = beam.shape
    rows = 2 * per_group + (0 if small is None else 16)
    whole = pl.BlockSpec(memory_space=pltpu.VMEM)
    return pl.pallas_call(
        functools.partial(message_kernel, per_group),
        grid_spec=pltpu.PrefetchScalarGridSpec(
            num_scalar_prefetch=1,
            grid=(1,),
            in_specs=[
                pl.BlockSpec(
                    (1, 2, per_group, antennas), lambda n, tab, m=m: (tab[m] + index, 0, 0, 0)
                )
                for m in others
            ]
            + ([] if small is None else [whole]),
            out_specs=[whole for _ in others],
        ),
        out_shape=[jax.ShapeDtypeStruct((rows, antennas), jnp.bfloat16) for _ in others],
        cost_estimate=LITTLE,
        name="messages_for",
    )(table, *[beam] * len(others), *([] if small is None else [small]))


def slice_kernel(count, tab_ref, *refs):
    for source, target in zip(refs[:count], refs[count:]):
        target[...] = source[...]


def slices_for(array, axis, size, starts, table):
    lead = axis > 0
    shape = array.shape[:axis] + (size,) + array.shape[axis + 1 :]
    block = (1,) + shape[1:] if lead else shape
    rest = (0,) * (array.ndim - axis - 1)
    return pl.pallas_call(
        functools.partial(slice_kernel, len(starts)),
        grid_spec=pltpu.PrefetchScalarGridSpec(
            num_scalar_prefetch=1,
            grid=(shape[0] if lead else 1,),
            in_specs=[
                pl.BlockSpec(
                    block,
                    lambda n, tab, start=start, shift=shift: (
                        *((n,) if lead else ()),
                        tab[start] // size + shift,
                        *rest,
                    ),
                )
                for start, shift in starts
            ],
            out_specs=[
                pl.BlockSpec(block, lambda n, tab: (n,) + (0,) * (array.ndim - 1)) for _ in starts
            ],
        ),
        out_shape=[jax.ShapeDtypeStruct(shape, array.dtype) for _ in starts],
        cost_estimate=LITTLE,
        name="slices_for",
    )(table, *[array] * len(starts))


KIND, ONE, TWO, ONE_AT, TWO_AT, OUT_ROW, VIS_AT = 0, 1, 2, 3, 5, 7, 8
COLUMNS = 10


def unit_kernel(index, offset, pieces, bright_at, outs, aliased, tab_ref, *refs):
    arrays = []
    for entries in pieces:
        found = []
        for count, start, number in entries:
            parts = (refs[0].at[0], refs[0].at[1]) if count == 1 else refs[:2]
            found.append((parts, start, number))
            refs = refs[count:]
        arrays.append(found)
    vis_ref, keep_one_ref, keep_two_ref = refs[:3]
    refs = refs[3:]
    columns_ref = None
    if bright_at is None:
        columns_ref, refs = refs[0], refs[1:]
    refs = refs[aliased:]
    out_refs, grad_ref = refs[:outs], refs[outs]
    refs = refs[outs + 1 :]
    if bright_at is not None:
        columns_ref, refs = refs[0], refs[1:]
    total_ref, one_ref, two_ref = refs
    step = pl.program_id(0)
    slot = tab_ref[0] + index
    sources, span = one_ref.shape[1:]

    def entry(column):
        return tab_ref[offset + step * COLUMNS + column]

    def load(target, at):
        for n, found in enumerate(arrays):

            @pl.when(entry(at) == n)
            def _(found=found):
                place = entry(at + 1)
                for parts, start, number in found:
                    rows = pl.ds(pl.multiple_of(place * number, number), number)
                    for part in (0, 1):
                        target[part, pl.ds(start, number)] = parts[part][rows]

    if bright_at is not None:

        @pl.when(step == 0)
        def _():
            for parts, start, number in arrays[0]:
                lines = parts[0][pl.ds(bright_at * number, BRIGHT_ROWS)].astype(jnp.float32)
                lanes = lax.broadcasted_iota(jnp.int32, (number, span), 1)
                rows = lax.broadcasted_iota(jnp.int32, (number, span), 0)
                for n in range(columns_ref.shape[0]):
                    line = jnp.where(lanes == rows, lines[n : n + 1, :], 0.0)
                    column = jnp.sum(line, axis=1, keepdims=True)
                    columns_ref[n, pl.ds(start, number)] = jnp.broadcast_to(column, (number, 128))

    def dot(a, b):
        return lax.dot_general(a, b, (((1,), (0,)), ((), ())), preferred_element_type=jnp.float32)

    def scaled_of(re, im):
        column = jnp.concatenate([columns_ref[index]] * (span // 128), 1)
        return (
            (re.astype(jnp.float32) * column).astype(jnp.bfloat16),
            (im.astype(jnp.float32) * column).astype(jnp.bfloat16),
        )

    def outer(a, b):
        row_ids = lax.broadcasted_iota(jnp.int32, a.shape, 0)
        a = jnp.where(row_ids == slot, a, 0.0)
        return lax.dot_general(a, b, (((0,), (0,)), ((), ())), preferred_element_type=jnp.float32)

    def cross(a_re, a_im, b_re, b_im):
        lhs = jnp.concatenate([a_re, a_im], 0).T
        rhs = jnp.concatenate(
            [jnp.concatenate([b_re, -b_im], 1), jnp.concatenate([b_im, b_re], 1)], 0
        )
        both = dot(lhs, rhs)
        return both[:, :span], both[:, span:]

    def pull(re, im, res_re, res_im, sign):
        lhs = jnp.concatenate([re, im], 1)
        rhs = jnp.concatenate(
            [
                jnp.concatenate([res_re, res_im], 1),
                jnp.concatenate([res_im, -res_re] if sign == 1 else [-res_im, res_re], 1),
            ],
            0,
        )
        both = dot(lhs, rhs)
        return both[:, :span], both[:, span:]

    def add_grad(value):
        folded = value[:, :128]
        for start in range(128, span, 128):
            folded = folded + value[:, start : start + 128]
        total_ref[...] += folded

    def put(res_re, res_im):
        for out_ref in out_refs:
            out_ref[0, 0] = res_re
            out_ref[0, 1] = res_im

    @pl.when(step == 0)
    def _():
        total_ref[...] = jnp.zeros_like(total_ref)

    @pl.when(entry(KIND) != 2)
    def _():
        load(one_ref, ONE_AT)
        load(two_ref, TWO_AT)

    @pl.when(entry(KIND) == 0)
    def _():
        one_re, one_im, two_re, two_im = one_ref[0], one_ref[1], two_ref[0], two_ref[1]
        pred_re, pred_im = cross(*scaled_of(one_re, one_im), two_re, two_im)
        weights = outer(keep_one_ref[...], keep_two_ref[...])
        res_re = (weights * (vis_ref[0, 0, 0, 0].astype(jnp.float32) - pred_re)).astype(jnp.bfloat16)
        res_im = (weights * (vis_ref[0, 0, 0, 1].astype(jnp.float32) - pred_im)).astype(jnp.bfloat16)
        put(res_re, res_im)
        sum_re, sum_im = pull(one_re, one_im, res_re, res_im, 1)
        add_grad(sum_re * two_re.astype(jnp.float32) - sum_im * two_im.astype(jnp.float32))

    @pl.when(entry(KIND) == 1)
    def _():
        one_re, one_im, two_re, two_im = one_ref[0], one_ref[1], two_ref[0], two_ref[1]
        row_ids = lax.broadcasted_iota(jnp.int32, (span, span), 0)
        col_ids = lax.broadcasted_iota(jnp.int32, (span, span), 1)
        upper = row_ids < col_ids
        lower = row_ids > col_ids
        first_re, first_im = cross(*scaled_of(one_re, one_im), one_re, one_im)
        second_re, second_im = cross(two_re, two_im, *scaled_of(two_re, two_im))
        keep_one = keep_one_ref[...]
        keep_two = keep_two_ref[...]
        weights = jnp.where(upper, outer(keep_one, keep_one), 0.0) + jnp.where(
            lower, outer(keep_two, keep_two), 0.0
        )
        vis_re = vis_ref[0, 0, 0, 0].astype(jnp.float32)
        vis_im = vis_ref[0, 0, 0, 1].astype(jnp.float32)
        res_re = (weights * (vis_re - jnp.where(upper, first_re, second_re))).astype(jnp.bfloat16)
        res_im = (weights * (vis_im - jnp.where(upper, first_im, -second_im))).astype(jnp.bfloat16)
        put(res_re, res_im)
        none = jnp.zeros_like(res_re)
        sum_re, sum_im = pull(
            one_re, one_im, jnp.where(upper, res_re, none), jnp.where(upper, res_im, none), 1
        )
        add_grad(sum_re * one_re.astype(jnp.float32) - sum_im * one_im.astype(jnp.float32))
        sum_re, sum_im = pull(
            two_re, two_im, jnp.where(lower, res_re, none), jnp.where(lower, res_im, none), -1
        )
        add_grad(sum_re * two_re.astype(jnp.float32) + sum_im * two_im.astype(jnp.float32))

    @pl.when(step == pl.num_programs(0) - 1)
    def _():
        grad_ref[...] = jnp.sum(total_ref[...].T, axis=0, keepdims=True)


def unit_work(index, steps, table, pieces, vis, keep, bright, outs):
    span = vis.shape[5]
    slots = keep.shape[0]
    sources = sum(number for _, _, number in pieces[0])
    offset, count = steps
    whole = pl.BlockSpec(memory_space=pltpu.VMEM)
    arrays = [array for piece in pieces for entry, _, _ in piece for array in entry]

    def at(tab, step, column):
        return tab[offset + step * COLUMNS + column]

    in_specs = [whole] * len(arrays) + [
        pl.BlockSpec(
            (1, 1, 1, 2, span, span),
            lambda u, tab: (at(tab, u, VIS_AT), at(tab, u, VIS_AT + 1), index, 0, 0, 0),
        ),
        pl.BlockSpec((slots, span), lambda u, tab: (0, at(tab, u, ONE))),
        pl.BlockSpec((slots, span), lambda u, tab: (0, at(tab, u, TWO))),
    ]
    operands = [table, *arrays, vis, keep, keep]
    bright_at = None
    if isinstance(bright, int):
        first = pieces[0][0]
        bright_at = (first[0][0].shape[1] - BRIGHT_ROWS) // first[2]
    else:
        in_specs.append(whole)
        operands.append(bright)
    aliases = {}
    out_specs, out_shapes = [], []
    for out in outs:
        rows = out
        if not isinstance(out, int):
            rows = out.shape[0]
            aliases[len(operands)] = len(out_specs)
            operands.append(out)
            in_specs.append(pl.BlockSpec(memory_space=pl.ANY))
        out_specs.append(
            pl.BlockSpec((1, 2, span, span), lambda u, tab: (at(tab, u, OUT_ROW), 0, 0, 0))
        )
        out_shapes.append(jax.ShapeDtypeStruct((rows, 2, span, span), jnp.bfloat16))
    out_specs.append(pl.BlockSpec((1, sources), lambda u, tab: (0, 0)))
    out_shapes.append(jax.ShapeDtypeStruct((1, sources), jnp.float32))
    if bright_at is not None:
        out_specs.append(pl.BlockSpec((bright, sources, 128), lambda u, tab: (0, 0, 0)))
        out_shapes.append(jax.ShapeDtypeStruct((bright, sources, 128), jnp.float32))
    kinds = [[(len(entry), start, number) for entry, start, number in piece] for piece in pieces]
    return pl.pallas_call(
        functools.partial(unit_kernel, index, offset, kinds, bright_at, len(outs), len(aliases)),
        grid_spec=pltpu.PrefetchScalarGridSpec(
            num_scalar_prefetch=1,
            grid=(count,),
            in_specs=in_specs,
            out_specs=out_specs,
            scratch_shapes=[
                pltpu.VMEM((sources, 128), jnp.float32),
                pltpu.VMEM((2, sources, span), jnp.bfloat16),
                pltpu.VMEM((2, sources, span), jnp.bfloat16),
            ],
        ),
        out_shape=out_shapes,
        input_output_aliases=aliases,
        compiler_params=pltpu.CompilerParams(vmem_limit_bytes=48 * 1024 * 1024),
        cost_estimate=LITTLE,
        name="unit_work",
    )(*operands)


def put_kernel(sources, tab_ref, *refs):
    out_ref = refs[-1]
    for step, (which, row) in enumerate(sources):

        @pl.when(pl.program_id(0) == step)
        def _(which=which, row=row):
            out_ref[0, 0] = refs[which][...] if row is None else refs[which][row]


def put_residuals(sources, arrays, offset, table, shape, residual):
    span = shape[-1]
    whole = pl.BlockSpec(memory_space=pltpu.VMEM)
    operands = [table, *arrays]
    in_specs = [whole] * len(arrays)
    aliases = {}
    if residual is not None:
        aliases = {len(operands): 0}
        operands.append(residual)
        in_specs.append(pl.BlockSpec(memory_space=pl.ANY))
    return pl.pallas_call(
        functools.partial(put_kernel, sources),
        grid_spec=pltpu.PrefetchScalarGridSpec(
            num_scalar_prefetch=1,
            grid=(len(sources),),
            in_specs=in_specs,
            out_specs=pl.BlockSpec(
                (1, 1, 2, span, span),
                lambda n, tab: (tab[offset + 2 * n], tab[offset + 2 * n + 1], 0, 0, 0),
            ),
        ),
        out_shape=jax.ShapeDtypeStruct(shape, jnp.bfloat16),
        input_output_aliases=aliases,
        compiler_params=pltpu.CompilerParams(vmem_limit_bytes=32 * 1024 * 1024),
        cost_estimate=LITTLE,
        name="put_residuals",
    )(*operands)


class Routes:
    def __init__(self, planes, width, units, share):
        count = planes * width
        blocks = int(units[:, :2].max()) + 1
        self.width = width
        self.units_dev = units_dev = units.shape[0] // count
        ring = [0] + list(range(1, planes, 2)) + list(range(planes - 2, 0, -2))

        def along(step):
            at = {plane: ring[(n + step) % planes] for n, plane in enumerate(ring)}
            return [(t, at[t // width] * width + t % width) for t in range(count)]

        self.onward = along(1)
        self.backward = along(-1)
        self.opposite = along(2)
        self.partner = [[(t, t ^ m) for t in range(count)] for m in range(width)]

        touched = [set(units[u, :2].tolist()) for u in range(units.shape[0])]
        home = [list(range(t * units_dev, (t + 1) * units_dev)) for t in range(count)]
        of_plane = [range(z * width * units_dev, (z + 1) * width * units_dev) for z in range(planes)]

        def most(wanted):
            return max(sum(bool(wanted(touched[u])) for u in plane) for plane in of_plane)

        def stuck(block):
            return sum(all(block in touched[u] for u in mine) for mine in home)

        end = min(range(blocks), key=lambda b: most(lambda t: b in t))
        rest = [b for b in range(blocks) if b != end]
        start = min(
            itertools.combinations(rest, blocks * FIRST_PART // 8),
            key=lambda c: most(lambda t: end not in t and not t <= set(c)),
        )
        self.pieces = [list(start), [b for b in rest if b not in start], [end]]
        self.full = [list(range(blocks))]
        events = []
        for blocks_of in touched:
            events.append(max(n for n, piece in enumerate(self.pieces) if blocks_of & set(piece)))

        def rows_of(t, pieces, wanted):
            rows = []
            for m in range(width):
                for n, u in enumerate(home[t ^ m]):
                    if not wanted(u):
                        continue
                    one, two, kind = units[u].tolist()
                    at = [
                        (k, piece.index(b))
                        for b in (one, two)
                        for k, piece in enumerate(pieces)
                        if b in piece
                    ]
                    rows.append([kind, one, two, *at[0], *at[1], m * units_dev + n, m, n])
            return rows

        def table_of(pieces, wanted):
            tables = [rows_of(t, pieces, wanted) for t in range(count)]
            steps = max(len(rows) for rows in tables)
            for rows in tables:
                while len(rows) < steps:
                    rows.append([2] + (rows[-1][1:] if rows else [0] * (COLUMNS - 1)))
                    rows[-1][OUT_ROW] = width * units_dev
            return np.array(tables, np.int32)

        first_table = table_of(self.full, lambda u: True)
        tables = [
            table_of(self.pieces, lambda u, n=n: events[u] == n) for n in range(len(self.pieces))
        ]

        def targets(index):
            rows = np.zeros((count, width, units_dev, 2), np.int32)
            for t in range(count):
                for m in range(width):
                    for n in range(units_dev):
                        rows[t, m, n] = n, (t % width ^ m) * share + index
            return rows

        starts = np.array([[(t % width ^ m) * share for m in range(width)] for t in range(count)])
        parts = [starts, first_table, *tables, *[targets(n) for n in range(share)]]
        parts = [part.reshape(count, -1).astype(np.int32) for part in parts]
        ends = np.cumsum([part.shape[1] for part in parts]).tolist()
        self.table = np.concatenate(parts, 1)
        self.first_steps = (ends[0], first_table.shape[1])
        self.steps = [(ends[1 + n], table.shape[1]) for n, table in enumerate(tables)]
        self.targets = ends[1 + len(tables) :]


FIRST_PART = 4


def packed_small(source_dirs, source_flux, visible_list):
    listed = visible_list.astype(jnp.float32).reshape(1, -1)
    rows = [source_dirs, source_flux.astype(jnp.float32)[None], listed]
    width = max(row.shape[1] for row in rows)
    rows = [jnp.pad(row, ((0, 0), (0, width - row.shape[1]))) for row in rows]
    return jnp.concatenate(rows, 0)


def plain_program(visibility, beam, antenna_uvw, small, keep):
    units_dev, slots, _, span, _ = visibility.shape
    _, _, per_group, antennas = beam.shape
    blocks = antennas // span
    tile_index = lax.axis_index("tile")
    units = unit_table(blocks)
    own_rows = np.tile(np.arange(units_dev), units.shape[0] // units_dev)
    none = np.zeros_like(own_rows)
    table = np.stack(
        [units[:, 2], units[:, 0], units[:, 1], none, units[:, 0], none, units[:, 1]]
        + [own_rows, none, own_rows],
        1,
    )
    table = table.astype(np.int32).reshape(-1, units_dev * COLUMNS)
    table = np.pad(table, ((0, 0), (1, 0)))
    table = lax.dynamic_index_in_dim(jnp.asarray(table), tile_index, 0, keepdims=False)
    columns = None
    residuals, grads = [], []
    for slot in range(slots):
        (owned,) = build_factors(
            (slot, slots, per_group),
            table,
            beam,
            [],
            antenna_uvw,
            [small],
            [list(range(blocks))],
            span,
            0 if slot else BRIGHT_ROWS,
            small.shape[1],
        )
        everyone = lax.all_gather(owned, "tile", axis=0)
        rows = blocks * per_group
        if columns is None:
            bright = everyone[:, 0, rows : rows + slots, :per_group].astype(jnp.float32)
            bright = jnp.swapaxes(bright, 0, 1).reshape(slots, -1, 1)
            columns = jnp.broadcast_to(bright, bright.shape[:2] + (128,))
        factors = everyone[:, :, :rows].reshape(-1, 2, blocks, per_group, span)
        number = factors.shape[0] * per_group
        factors = factors.transpose(1, 2, 0, 3, 4).reshape(2, blocks * number, span)
        residual, grad = unit_work(
            slot,
            (1, units_dev),
            table,
            [[((factors,), 0, number)]],
            visibility[None],
            keep,
            columns,
            [units_dev],
        )
        residuals.append(residual)
        grads.append(grad)
    summed = lax.psum_scatter(jnp.concatenate(grads, 0), "tile", scatter_dimension=1, tiled=True)
    return jnp.stack(residuals, 1), summed


GATES = {
    "own": (),
}


def plane_program(routes, visibility, beam, antenna_uvw, small, keep):
    units_dev, slots, _, span, _ = visibility.shape
    per_group = beam.shape[2]
    width = routes.width
    share = slots // width
    group = width * per_group
    tile_index = lax.axis_index("tile")
    mine = tile_index % width
    others = range(1, width)
    table = lax.dynamic_index_in_dim(jnp.asarray(routes.table), tile_index, 0, keepdims=False)
    done = {}

    def gated(name, value):
        earlier = [done[gate] for gate in GATES.get(name, ())]
        return lax.optimization_barrier((value, *earlier))[0] if earlier else value

    def send(name, value, pairs):
        done[name] = lax.ppermute(gated(name, value), "tile", pairs)
        return done[name]

    def near(name, piece):
        return [
            send(name + " onward", piece, routes.onward),
            send(name + " backward", piece, routes.backward),
        ]

    def far(name, sides):
        return [
            send(name + " onward", sides[0][0], routes.onward),
            send(name + " backward", sides[1][1], routes.backward),
        ]

    def entries(piece, sides, halves, first, number):
        found = [(piece,), (sides[0],), (sides[1],), tuple(halves)]
        return [(arrays, n * group + first, number) for n, arrays in enumerate(found)]

    def sent_home(name, results):
        parts = [results[m * units_dev : (m + 1) * units_dev] for m in others]
        return [send(f"{name} {m}", part, routes.partner[m]) for m, part in zip(others, parts)]

    first_slot = (0, share, per_group)
    (own,) = build_factors(
        first_slot,
        gated("own", table),
        beam,
        [],
        antenna_uvw,
        [small],
        routes.full,
        span,
        BRIGHT_ROWS,
        small.shape[1],
    )
    done["own"] = own
    own_sides = near("own near", own)
    messages = messages_for(beam, 0, others, small, gated("beams", table))
    messages = [send(f"beams {m}", messages[m - 1], routes.partner[m]) for m in others]
    own_far = far("own far", own_sides)
    (rest,) = build_factors(
        first_slot,
        gated("rest", table),
        None,
        messages,
        antenna_uvw,
        messages,
        routes.full,
        span,
        BRIGHT_ROWS,
        small.shape[1],
    )
    done["rest"] = rest
    rest_sides = near("rest near", rest)

    later = messages_for(beam, 1, others, None, gated("later beams", table))
    later = [send(f"later beams {m}", later[m - 1], routes.partner[m]) for m in others]
    vis = slices_for(
        visibility, 1, share, [(m, 0) for m in range(width)], gated("vis", table)
    )
    vis = [vis[0]] + [send(f"vis {m}", vis[m], routes.partner[m]) for m in others]
    later_pieces = build_factors(
        (1, share, per_group),
        gated("later", table),
        beam,
        later,
        antenna_uvw,
        [small, *messages],
        routes.pieces,
        span,
        0,
        small.shape[1],
    )
    rest_far = far("rest far", rest_sides)
    near_0 = near("piece 0 near", later_pieces[0])
    near_1 = near("piece 1 near", later_pieces[1])
    far_0 = far("piece 0 far", near_0)

    vis = jnp.stack(vis, 0)
    pieces = entries(own, own_sides, own_far, 0, per_group)
    pieces += entries(rest, rest_sides, rest_far, per_group, group - per_group)
    results, grad, columns = unit_work(
        0,
        routes.first_steps,
        gated("work", table),
        [pieces],
        vis,
        keep,
        share,
        [width * units_dev],
    )
    done["work"] = grad
    grads = [grad]
    home = sent_home("home", results)
    far_1 = far("piece 1 far", near_1)
    near_2 = near("piece 2 near", later_pieces[2])
    far_2 = far("piece 2 far", near_2)
    ready = [
        entries(piece, sides, halves, 0, group)
        for piece, sides, halves in zip(
            later_pieces, (near_0, near_1, near_2), (far_0, far_1, far_2)
        )
    ]
    pairs = [(m, n) for m in range(width) for n in range(units_dev)]
    residual = put_residuals(
        pairs, [results, *home], routes.targets[0], gated("put", table), visibility.shape, None
    )
    done["put"] = residual

    results = width * units_dev + 1
    for n, steps in enumerate(routes.steps):
        results, grad = unit_work(
            1,
            steps,
            gated(f"work {n}", table),
            ready[: n + 1],
            vis,
            keep,
            columns,
            [results],
        )
        done[f"work {n}"] = grad
        grads.append(grad)
    returned = sent_home("later home", results)

    partial = jnp.concatenate([grads[0], sum(grads[2:], grads[1])], 0)
    parts = [partial[:, n * group : (n + 1) * group] for n in range(4)]
    plane_sum = (parts[0] + send("sum opposite", parts[3], routes.opposite)) + (
        send("sum backward", parts[1], routes.backward)
        + send("sum onward", parts[2], routes.onward)
    )
    sums = [plane_sum[:, m * per_group : (m + 1) * per_group] for m in range(width)]
    sums = [sums[0]] + [send(f"sum {m}", sums[m], routes.partner[m]) for m in others]
    sums = jnp.stack(sums, 0)
    ids = jnp.arange(width, dtype=jnp.int32)
    here = jnp.bitwise_xor(ids[:, None], mine) == ids[None, :]
    summed = jnp.sum(jnp.where(here[:, :, None, None], sums[None], 0.0), axis=1)
    summed = summed.reshape(slots, per_group)

    residual = put_residuals(
        pairs,
        [results, *returned],
        routes.targets[1],
        gated("later put", table),
        visibility.shape,
        residual,
    )
    return residual, summed


def per_device(
    visibility, station_beam, antenna_uvw, source_dirs, source_flux, visible_list, antenna_flags
):
    span = visibility.shape[4]
    antennas = station_beam.shape[3]
    small = packed_small(source_dirs, source_flux, visible_list)
    keep = 1.0 - antenna_flags.astype(jnp.float32)
    arguments = (visibility, station_beam, antenna_uvw, small, keep)
    if lax.axis_size("tile") == 16:
        routes = Routes(4, 4, unit_table(antennas // span), visibility.shape[1] // 4)
        residual, summed = plane_program(routes, *arguments)
    else:
        residual, summed = plain_program(*arguments)
    return (residual, summed * (-1.0 / (8.0 * antennas)))


def solution(mesh):
    return jax.shard_map(
        per_device,
        mesh=mesh,
        in_specs=(
            P("tile", "grp", None, None, None),
            P("grp", None, "tile", None),
            P("grp", None, None),
            P(None, "tile"),
            P(("grp", "tile")),
            P(None, "tile"),
            P("grp", None),
        ),
        out_specs=(P("tile", "grp", None, None, None), P("grp", "tile")),
        check_vma=False,
    )
```

```python
import functools

import jax
import jax.numpy as jnp
import numpy as np
from jax import lax
from jax.experimental import pallas as pl
from jax.experimental.pallas import tpu as pltpu
from jax.sharding import PartitionSpec as P


def unit_table(block_count):
    first_list = []
    second_list = []
    diag_list = []
    for row_block in range(block_count):
        for col_block in range(row_block + 1, block_count):
            first_list.append(row_block)
            second_list.append(col_block)
            diag_list.append(0)
    for pair_index in range(block_count // 2):
        first_list.append(2 * pair_index)
        second_list.append(2 * pair_index + 1)
        diag_list.append(1)
    return np.stack([first_list, second_list, diag_list], 1).astype(np.int32)


def turn_polynomials():
    nodes = 0.125 + 0.125 * np.cos(np.pi * (np.arange(64) + 0.5) / 64)
    root = np.sqrt(nodes)
    fit = np.polynomial.Polynomial.fit
    sine = fit(nodes, np.sin(2 * np.pi * root) / root, 7, domain=[0, 0.25]).convert()
    cosine = fit(nodes, np.cos(2 * np.pi * root), 8, domain=[0, 0.25]).convert()
    return [float(c) for c in sine.coef], [float(c) for c in cosine.coef]


def horner(coefs, x):
    total = coefs[-1]
    for coef in coefs[-2::-1]:
        total = total * x + coef
    return total


def build_kernel(sets, slot_ids, pieces, bright_rows, width, tab_ref, *refs):
    uvw_ref, outs = refs[-1 - len(pieces)], refs[-len(pieces) :]
    per_group = sets[0][0]
    span = outs[0].shape[2]
    count = len(sets) * per_group
    sin_coefs, cos_coefs = turn_polynomials()
    brights = []
    for part, (_, beam_at, small_at) in enumerate(sets):
        beam_ref = refs[beam_at]
        if beam_ref.shape[0] == 1:
            beam = [beam_ref.at[0, 0], beam_ref.at[0, 1]]
        else:
            beam = [beam_ref.at[pl.ds(n * per_group, per_group)] for n in (0, 1)]
        small_ref = refs[small_at]
        if small_ref.dtype == jnp.float32:
            small = small_ref[...]
        else:
            small = unsplit(small_ref, 2 * per_group, width)
        lanes = lax.broadcasted_iota(jnp.int32, (per_group, width), 1)
        rows = lax.broadcasted_iota(jnp.int32, (per_group, width), 0)

        def pick(chosen, row):
            return jnp.sum(jnp.where(chosen, small[row : row + 1, :], 0.0), axis=1, keepdims=True)

        def chosen_at(index):
            listed = pick(lanes == (tab_ref[0] + index) * per_group + rows, 3)
            return listed.astype(jnp.int32) == lanes

        group = part * per_group
        if bright_rows:
            columns = lax.broadcasted_iota(jnp.int32, (per_group, span), 1)
            numbers = lax.broadcasted_iota(jnp.int32, (per_group, span), 0) + group
            for index in range(slot_ids[1]):
                flux = pick(chosen_at(index), 2)
                line = jnp.sum(jnp.where(columns == numbers, flux, 0.0), axis=0, keepdims=True)
                if part == 0:
                    brights.append(line)
                else:
                    brights[index] += line
        chosen = chosen_at(slot_ids[0])
        east = pick(chosen, 0)
        north = pick(chosen, 1)
        depth = jnp.sqrt(1.0 - east * east - north * north) - 1.0
        for out_ref, piece in zip(outs, pieces):
            for place, block in enumerate(piece):
                cols = pl.ds(block * span, span)
                delay = (
                    uvw_ref[0, 0:1, cols] * east
                    + uvw_ref[0, 1:2, cols] * north
                    + uvw_ref[0, 2:3, cols] * depth
                )
                turn = delay - jnp.floor(delay + 0.5)
                square = turn * turn
                sine = horner(sin_coefs, square) * turn
                cosine = horner(cos_coefs, square)
                real = beam[0][:, cols].astype(jnp.float32)
                imag = beam[1][:, cols].astype(jnp.float32)
                at = pl.ds(place * count + group, per_group)
                out_ref[0, at] = (real * cosine + imag * sine).astype(jnp.bfloat16)
                out_ref[1, at] = (imag * cosine - real * sine).astype(jnp.bfloat16)
    if bright_rows:
        padding = jnp.zeros((bright_rows - len(brights), span), jnp.float32)
        block = jnp.concatenate(brights + [padding], 0).astype(jnp.bfloat16)
        for part in (0, 1):
            outs[0][part, pl.ds(len(pieces[0]) * count, bright_rows)] = block


def unsplit(message_ref, start, width):
    terms = [message_ref[pl.ds(start, 16), pl.ds(n * width, width)].astype(jnp.float32) for n in range(3)]
    return (terms[0] + terms[1]) + terms[2]


BRIGHT_ROWS = 16


def build_factors(
    slot_ids, table, beam, messages, antenna_uvw, smalls, pieces, span, bright_rows, small_width
):
    slots, _, antennas = antenna_uvw.shape
    per_group = slot_ids[2]
    index = slot_ids[0]
    whole = pl.BlockSpec(memory_space=pltpu.VMEM)
    operands, in_specs, sets = [], [], []
    if beam is not None:
        operands.append(beam)
        in_specs.append(
            pl.BlockSpec((1, 2, per_group, antennas), lambda n, tab: (tab[0] + index, 0, 0, 0))
        )
    operands += messages
    beams = len(operands)
    for n, small in enumerate(smalls):
        at = next((k for k, known in enumerate(operands) if known is small), len(operands))
        if at == len(operands):
            operands.append(small)
        sets.append((per_group, n, at))
    in_specs += [whole] * (len(operands) - len(in_specs))
    in_specs.append(pl.BlockSpec((1, 3, antennas), lambda n, tab: (tab[0] + index, 0, 0)))
    count = beams * per_group
    shapes = [
        (2, len(piece) * count + (0 if n else bright_rows), span) for n, piece in enumerate(pieces)
    ]
    return pl.pallas_call(
        functools.partial(build_kernel, sets, slot_ids, pieces, bright_rows, small_width),
        grid_spec=pltpu.PrefetchScalarGridSpec(
            num_scalar_prefetch=1,
            grid=(1,),
            in_specs=in_specs,
            out_specs=[whole] * len(pieces),
        ),
        out_shape=[jax.ShapeDtypeStruct(shape, jnp.bfloat16) for shape in shapes],
        compiler_params=pltpu.CompilerParams(vmem_limit_bytes=40 * 1024 * 1024),
        cost_estimate=LITTLE,
        name="build_factors",
    )(table, *operands, antenna_uvw)


LITTLE = pl.CostEstimate(flops=1, bytes_accessed=1, transcendentals=0)


def message_kernel(per_group, tab_ref, *refs):
    outs = [ref for ref in refs if ref.dtype == jnp.bfloat16 and len(ref.shape) == 2]
    small_ref = refs[len(outs)] if len(refs) > 2 * len(outs) else None
    for beam_ref, out_ref in zip(refs, outs):
        for part in (0, 1):
            out_ref[pl.ds(part * per_group, per_group)] = beam_ref[0, part]
        if small_ref is not None:
            count, width = small_ref.shape
            rest = jnp.concatenate([small_ref[...], jnp.zeros((16 - count, width), jnp.float32)], 0)
            out_ref[pl.ds(2 * per_group, 16)] = jnp.zeros((16, out_ref.shape[1]), jnp.bfloat16)
            for n in range(3):
                term = rest.astype(jnp.bfloat16)
                out_ref[pl.ds(2 * per_group, 16), pl.ds(n * width, width)] = term
                rest = rest - term.astype(jnp.float32)


def messages_for(beam, index, others, small, table):
    _, _, per_group, antennas = beam.shape
    rows = 2 * per_group + (0 if small is None else 16)
    whole = pl.BlockSpec(memory_space=pltpu.VMEM)
    return pl.pallas_call(
        functools.partial(message_kernel, per_group),
        grid_spec=pltpu.PrefetchScalarGridSpec(
            num_scalar_prefetch=1,
            grid=(1,),
            in_specs=[
                pl.BlockSpec(
                    (1, 2, per_group, antennas), lambda n, tab, m=m: (tab[m] + index, 0, 0, 0)
                )
                for m in others
            ]
            + ([] if small is None else [whole]),
            out_specs=[whole for _ in others],
        ),
        out_shape=[jax.ShapeDtypeStruct((rows, antennas), jnp.bfloat16) for _ in others],
        cost_estimate=LITTLE,
        name="messages_for",
    )(table, *[beam] * len(others), *([] if small is None else [small]))


def slice_kernel(count, tab_ref, *refs):
    for source, target in zip(refs[:count], refs[count:]):
        target[...] = source[...]


def slices_for(array, axis, size, starts, table):
    lead = axis > 0
    shape = array.shape[:axis] + (size,) + array.shape[axis + 1 :]
    block = (1,) + shape[1:] if lead else shape
    rest = (0,) * (array.ndim - axis - 1)
    return pl.pallas_call(
        functools.partial(slice_kernel, len(starts)),
        grid_spec=pltpu.PrefetchScalarGridSpec(
            num_scalar_prefetch=1,
            grid=(shape[0] if lead else 1,),
            in_specs=[
                pl.BlockSpec(
                    block,
                    lambda n, tab, start=start, shift=shift: (
                        *((n,) if lead else ()),
                        tab[start] // size + shift,
                        *rest,
                    ),
                )
                for start, shift in starts
            ],
            out_specs=[
                pl.BlockSpec(block, lambda n, tab: (n,) + (0,) * (array.ndim - 1)) for _ in starts
            ],
        ),
        out_shape=[jax.ShapeDtypeStruct(shape, array.dtype) for _ in starts],
        cost_estimate=LITTLE,
        name="slices_for",
    )(table, *[array] * len(starts))


KIND, ONE, TWO, ONE_AT, TWO_AT = 0, 1, 2, 3, 5
COLUMNS = 7


def unit_kernel(index, offset, pieces, bright_at, homes, tab_ref, *refs):
    arrays = []
    for entries in pieces:
        found = []
        for count, start, number in entries:
            parts = (refs[0].at[0], refs[0].at[1]) if count == 1 else refs[:2]
            found.append((parts, start, number))
            refs = refs[count:]
        arrays.append(found)
    vis_refs, (keep_one_ref, keep_two_ref) = refs[:homes], refs[homes : homes + 2]
    refs = refs[homes + 2 :]
    columns_ref = None
    if bright_at is None:
        columns_ref, refs = refs[0], refs[1:]
    out_refs, grad_ref = refs[:homes], refs[homes]
    refs = refs[homes + 1 :]
    if bright_at is not None:
        columns_ref, refs = refs[0], refs[1:]
    total_ref, one_ref, two_ref, vis_ref = refs
    step = pl.program_id(0)
    slot = tab_ref[0] + index
    sources, span = one_ref.shape[1:]

    def entry(column):
        return tab_ref[offset + step * COLUMNS + column]

    def load(target, at):
        for n, found in enumerate(arrays):

            @pl.when(entry(at) == n)
            def _(found=found):
                place = entry(at + 1)
                for parts, start, number in found:
                    rows = pl.ds(pl.multiple_of(place * number, number), number)
                    for part in (0, 1):
                        target[part, pl.ds(start, number)] = parts[part][rows]

    if bright_at is not None:

        @pl.when(step == 0)
        def _():
            for parts, start, number in arrays[0]:
                lines = parts[0][pl.ds(bright_at * number, BRIGHT_ROWS)].astype(jnp.float32)
                lanes = lax.broadcasted_iota(jnp.int32, (number, span), 1)
                rows = lax.broadcasted_iota(jnp.int32, (number, span), 0)
                for n in range(columns_ref.shape[0]):
                    line = jnp.where(lanes == rows, lines[n : n + 1, :], 0.0)
                    column = jnp.sum(line, axis=1, keepdims=True)
                    columns_ref[n, pl.ds(start, number)] = jnp.broadcast_to(column, (number, 128))

    def dot(a, b):
        return lax.dot_general(a, b, (((1,), (0,)), ((), ())), preferred_element_type=jnp.float32)

    def scaled_of(re, im):
        column = jnp.concatenate([columns_ref[index]] * (span // 128), 1)
        return (
            (re.astype(jnp.float32) * column).astype(jnp.bfloat16),
            (im.astype(jnp.float32) * column).astype(jnp.bfloat16),
        )

    def outer(a, b):
        row_ids = lax.broadcasted_iota(jnp.int32, a.shape, 0)
        a = jnp.where(row_ids == slot, a, 0.0)
        return lax.dot_general(a, b, (((0,), (0,)), ((), ())), preferred_element_type=jnp.float32)

    def cross(a_re, a_im, b_re, b_im):
        lhs = jnp.concatenate([a_re, a_im], 0).T
        rhs = jnp.concatenate(
            [jnp.concatenate([b_re, -b_im], 1), jnp.concatenate([b_im, b_re], 1)], 0
        )
        both = dot(lhs, rhs)
        return both[:, :span], both[:, span:]

    def pull(re, im, res_re, res_im, sign):
        lhs = jnp.concatenate([re, im], 1)
        rhs = jnp.concatenate(
            [
                jnp.concatenate([res_re, res_im], 1),
                jnp.concatenate([res_im, -res_re] if sign == 1 else [-res_im, res_re], 1),
            ],
            0,
        )
        both = dot(lhs, rhs)
        return both[:, :span], both[:, span:]

    def add_grad(value):
        folded = value[:, :128]
        for start in range(128, span, 128):
            folded = folded + value[:, start : start + 128]
        total_ref[...] += folded

    each = pl.num_programs(0) // homes

    def put(res_re, res_im):
        for home, out_ref in enumerate(out_refs):

            @pl.when(step // each == home)
            def _(out_ref=out_ref):
                out_ref[0, 0] = res_re
                out_ref[0, 1] = res_im

    @pl.when(step == 0)
    def _():
        total_ref[...] = jnp.zeros_like(total_ref)

    load(one_ref, ONE_AT)
    load(two_ref, TWO_AT)
    for home, home_ref in enumerate(vis_refs):

        @pl.when(step // each == home)
        def _(home_ref=home_ref):
            vis_ref[...] = home_ref[0, 0]

    @pl.when(entry(KIND) == 0)
    def _():
        one_re, one_im, two_re, two_im = one_ref[0], one_ref[1], two_ref[0], two_ref[1]
        pred_re, pred_im = cross(*scaled_of(one_re, one_im), two_re, two_im)
        weights = outer(keep_one_ref[...], keep_two_ref[...])
        res_re = (weights * (vis_ref[0].astype(jnp.float32) - pred_re)).astype(jnp.bfloat16)
        res_im = (weights * (vis_ref[1].astype(jnp.float32) - pred_im)).astype(jnp.bfloat16)
        put(res_re, res_im)
        sum_re, sum_im = pull(one_re, one_im, res_re, res_im, 1)
        add_grad(sum_re * two_re.astype(jnp.float32) - sum_im * two_im.astype(jnp.float32))

    @pl.when(entry(KIND) == 1)
    def _():
        one_re, one_im, two_re, two_im = one_ref[0], one_ref[1], two_ref[0], two_ref[1]
        row_ids = lax.broadcasted_iota(jnp.int32, (span, span), 0)
        col_ids = lax.broadcasted_iota(jnp.int32, (span, span), 1)
        upper = row_ids < col_ids
        lower = row_ids > col_ids
        first_re, first_im = cross(*scaled_of(one_re, one_im), one_re, one_im)
        second_re, second_im = cross(two_re, two_im, *scaled_of(two_re, two_im))
        keep_one = keep_one_ref[...]
        keep_two = keep_two_ref[...]
        weights = jnp.where(upper, outer(keep_one, keep_one), 0.0) + jnp.where(
            lower, outer(keep_two, keep_two), 0.0
        )
        vis_re = vis_ref[0].astype(jnp.float32)
        vis_im = vis_ref[1].astype(jnp.float32)
        res_re = (weights * (vis_re - jnp.where(upper, first_re, second_re))).astype(jnp.bfloat16)
        res_im = (weights * (vis_im - jnp.where(upper, first_im, -second_im))).astype(jnp.bfloat16)
        put(res_re, res_im)
        none = jnp.zeros_like(res_re)
        sum_re, sum_im = pull(
            one_re, one_im, jnp.where(upper, res_re, none), jnp.where(upper, res_im, none), 1
        )
        add_grad(sum_re * one_re.astype(jnp.float32) - sum_im * one_im.astype(jnp.float32))
        sum_re, sum_im = pull(
            two_re, two_im, jnp.where(lower, res_re, none), jnp.where(lower, res_im, none), -1
        )
        add_grad(sum_re * two_re.astype(jnp.float32) + sum_im * two_im.astype(jnp.float32))

    @pl.when(step == pl.num_programs(0) - 1)
    def _():
        grad_ref[...] = jnp.sum(total_ref[...].T, axis=0, keepdims=True)


def unit_work(index, offset, table, pieces, vis, keep, bright):
    units_dev, _, _, span, _ = vis[0].shape
    slots = keep.shape[0]
    sources = sum(number for _, _, number in pieces[0])
    count = units_dev * len(vis)
    whole = pl.BlockSpec(memory_space=pltpu.VMEM)
    arrays = [array for piece in pieces for entry, _, _ in piece for array in entry]

    def at(tab, step, column):
        return tab[offset + step * COLUMNS + column]

    def unit(step, home):
        return jnp.clip(step - home * units_dev, 0, units_dev - 1)

    in_specs = [whole] * len(arrays)
    for home, array in enumerate(vis):
        if array.shape[1] == slots:
            slot = lambda tab: tab[0] + index
        else:
            slot = lambda tab: index
        in_specs.append(
            pl.BlockSpec(
                (1, 1, 2, span, span),
                lambda u, tab, home=home, slot=slot: (unit(u, home), slot(tab), 0, 0, 0),
            )
        )
    in_specs += [
        pl.BlockSpec((slots, span), lambda u, tab: (0, at(tab, u, ONE))),
        pl.BlockSpec((slots, span), lambda u, tab: (0, at(tab, u, TWO))),
    ]
    operands = [table, *arrays, *vis, keep, keep]
    bright_at = None
    if isinstance(bright, int):
        first = pieces[0][0]
        bright_at = (first[0][0].shape[1] - BRIGHT_ROWS) // first[2]
    else:
        in_specs.append(whole)
        operands.append(bright)
    out_specs = [
        pl.BlockSpec((1, 2, span, span), lambda u, tab, home=home: (unit(u, home), 0, 0, 0))
        for home in range(len(vis))
    ]
    out_shapes = [jax.ShapeDtypeStruct((units_dev, 2, span, span), jnp.bfloat16) for _ in vis]
    out_specs.append(pl.BlockSpec((1, sources), lambda u, tab: (0, 0)))
    out_shapes.append(jax.ShapeDtypeStruct((1, sources), jnp.float32))
    if bright_at is not None:
        out_specs.append(pl.BlockSpec((bright, sources, 128), lambda u, tab: (0, 0, 0)))
        out_shapes.append(jax.ShapeDtypeStruct((bright, sources, 128), jnp.float32))
    kinds = [[(len(entry), start, number) for entry, start, number in piece] for piece in pieces]
    return pl.pallas_call(
        functools.partial(unit_kernel, index, offset, kinds, bright_at, len(vis)),
        grid_spec=pltpu.PrefetchScalarGridSpec(
            num_scalar_prefetch=1,
            grid=(count,),
            in_specs=in_specs,
            out_specs=out_specs,
            scratch_shapes=[
                pltpu.VMEM((sources, 128), jnp.float32),
                pltpu.VMEM((2, sources, span), jnp.bfloat16),
                pltpu.VMEM((2, sources, span), jnp.bfloat16),
                pltpu.VMEM((2, span, span), jnp.bfloat16),
            ],
        ),
        out_shape=out_shapes,
        compiler_params=pltpu.CompilerParams(vmem_limit_bytes=48 * 1024 * 1024),
        cost_estimate=LITTLE,
        name="unit_work",
    )(*operands)


def put_kernel(sources, tab_ref, *refs):
    out_ref = refs[-1]
    for step, (which, row) in enumerate(sources):

        @pl.when(pl.program_id(0) == step)
        def _(which=which, row=row):
            out_ref[0, 0] = refs[which][...] if row is None else refs[which][row]


def put_residuals(sources, arrays, offset, table, shape, residual):
    span = shape[-1]
    whole = pl.BlockSpec(memory_space=pltpu.VMEM)
    operands = [table, *arrays]
    in_specs = [whole] * len(arrays)
    aliases = {}
    if residual is not None:
        aliases = {len(operands): 0}
        operands.append(residual)
        in_specs.append(pl.BlockSpec(memory_space=pl.ANY))
    return pl.pallas_call(
        functools.partial(put_kernel, sources),
        grid_spec=pltpu.PrefetchScalarGridSpec(
            num_scalar_prefetch=1,
            grid=(len(sources),),
            in_specs=in_specs,
            out_specs=pl.BlockSpec(
                (1, 1, 2, span, span),
                lambda n, tab: (tab[offset + 2 * n], tab[offset + 2 * n + 1], 0, 0, 0),
            ),
        ),
        out_shape=jax.ShapeDtypeStruct(shape, jnp.bfloat16),
        input_output_aliases=aliases,
        compiler_params=pltpu.CompilerParams(vmem_limit_bytes=32 * 1024 * 1024),
        cost_estimate=LITTLE,
        name="put_residuals",
    )(*operands)


class Routes:
    def __init__(self, planes, width, units, share):
        count = planes * width
        blocks = int(units[:, :2].max()) + 1
        self.width = width
        self.units_dev = units_dev = units.shape[0] // count
        ring = [0] + list(range(1, planes, 2)) + list(range(planes - 2, 0, -2))

        def along(step):
            at = {plane: ring[(n + step) % planes] for n, plane in enumerate(ring)}
            return [(t, at[t // width] * width + t % width) for t in range(count)]

        self.onward = along(1)
        self.backward = along(-1)
        self.opposite = along(2)
        self.partner = [[(t, t ^ m) for t in range(count)] for m in range(width)]

        half = blocks // 2
        self.full = [list(range(blocks))]
        self.pieces = [list(range(half)), list(range(half, blocks))]

        def table_of(pieces, order):
            rows = np.zeros((count, len(order), units_dev, COLUMNS), np.int32)
            for t in range(count):
                for n, m in enumerate(order):
                    for k in range(units_dev):
                        one, two, kind = units[(t ^ m) * units_dev + k].tolist()
                        at = [
                            (p, piece.index(b))
                            for b in (one, two)
                            for p, piece in enumerate(pieces)
                            if b in piece
                        ]
                        rows[t, n, k] = [kind, one, two, *at[0], *at[1]]
            return rows

        def targets(index):
            rows = np.zeros((count, len(self.order), units_dev, 2), np.int32)
            for t in range(count):
                for n, m in enumerate(self.order):
                    for k in range(units_dev):
                        rows[t, n, k] = k, (t % width ^ m) * share + index
            return rows

        self.order = list(range(width // 2, width)) + list(range(width // 2 - 1, -1, -1))
        starts = np.array([[(t % width ^ m) * share for m in range(width)] for t in range(count)])
        parts = [starts, table_of(self.full, self.order), table_of(self.pieces, self.order)]
        parts += [targets(n) for n in range(share)]
        parts = [part.reshape(count, -1) for part in parts]
        ends = np.cumsum([part.shape[1] for part in parts]).tolist()
        self.table = np.concatenate(parts, 1).astype(np.int32)
        self.steps = ends[:2]
        self.targets = ends[2:]
        self.steps_per_home = units_dev * COLUMNS
        self.targets_per_home = units_dev * 2


def packed_small(source_dirs, source_flux, visible_list):
    listed = visible_list.astype(jnp.float32).reshape(1, -1)
    rows = [source_dirs, source_flux.astype(jnp.float32)[None], listed]
    width = max(row.shape[1] for row in rows)
    rows = [jnp.pad(row, ((0, 0), (0, width - row.shape[1]))) for row in rows]
    return jnp.concatenate(rows, 0)


def plain_program(visibility, beam, antenna_uvw, small, keep):
    units_dev, slots, _, span, _ = visibility.shape
    _, _, per_group, antennas = beam.shape
    blocks = antennas // span
    tile_index = lax.axis_index("tile")
    units = unit_table(blocks)
    none = np.zeros_like(units[:, 0])
    table = np.stack([units[:, 2], units[:, 0], units[:, 1], none, units[:, 0], none, units[:, 1]], 1)
    table = table.astype(np.int32).reshape(-1, units_dev * COLUMNS)
    table = np.pad(table, ((0, 0), (1, 0)))
    table = lax.dynamic_index_in_dim(jnp.asarray(table), tile_index, 0, keepdims=False)
    columns = None
    residuals, grads = [], []
    for slot in range(slots):
        (owned,) = build_factors(
            (slot, slots, per_group),
            table,
            beam,
            [],
            antenna_uvw,
            [small],
            [list(range(blocks))],
            span,
            0 if slot else BRIGHT_ROWS,
            small.shape[1],
        )
        everyone = lax.all_gather(owned, "tile", axis=0)
        rows = blocks * per_group
        if columns is None:
            bright = everyone[:, 0, rows : rows + slots, :per_group].astype(jnp.float32)
            bright = jnp.swapaxes(bright, 0, 1).reshape(slots, -1, 1)
            columns = jnp.broadcast_to(bright, bright.shape[:2] + (128,))
        factors = everyone[:, :, :rows].reshape(-1, 2, blocks, per_group, span)
        number = factors.shape[0] * per_group
        factors = factors.transpose(1, 2, 0, 3, 4).reshape(2, blocks * number, span)
        residual, grad = unit_work(
            slot, 1, table, [[((factors,), 0, number)]], [visibility], keep, columns
        )
        residuals.append(residual)
        grads.append(grad)
    summed = lax.psum_scatter(jnp.concatenate(grads, 0), "tile", scatter_dimension=1, tiled=True)
    return jnp.stack(residuals, 1), summed


OWN, OWN_NEAR, OWN_FAR, REST, REST_NEAR, REST_FAR = 0, 1, 3, 5, 6, 8
BEAM, SIDE_BEAMS, LATER_BEAMS, VIS, LATER = 10, 12, 15, 19, 23
PIECE_NEAR, PIECE_FAR = (24, 26), (28, 30)
WORK, HOME, PUT, LATER_WORK, LATER_HOME, PUT_NEAR, PUT_LAST = 32, 35, 38, 40, 43, 46, 47
SUM_PLANES, SUM_PLANE = 48, 51
GATES = {
    1: (0,),
    5: (0, 1, 2, 11),
    6: (0, 11, 13),
    12: (11,),
    15: (13,),
    19: (3, 4, 18),
    20: (4, 6),
    21: (3, 5, 14, 17),
    22: (13, 21),
    23: (18,),
    24: (6, 16),
    25: (6, 7, 23),
    26: (9,),
    27: (8, 23),
    30: (26,),
    31: (26,),
    34: (28,),
    35: (28,),
    36: (9,),
    37: (26, 27),
    40: (36, 37),
    43: (30,),
    45: (44,),
    46: (38, 43),
    48: (35,),
    51: (31, 45),
}


def plane_program(routes, visibility, beam, antenna_uvw, small, keep):
    units_dev, slots, _, span, _ = visibility.shape
    per_group = beam.shape[2]
    width = routes.width
    share = slots // width
    group = width * per_group
    tile_index = lax.axis_index("tile")
    mine = tile_index % width
    table = lax.dynamic_index_in_dim(jnp.asarray(routes.table), tile_index, 0, keepdims=False)
    done = {}

    def gated(step, value):
        earlier = [done[gate] for gate in GATES.get(step, ())]
        return lax.optimization_barrier((value, *earlier))[0] if earlier else value

    def send(step, value, pairs):
        done[step] = lax.ppermute(gated(step, value), "tile", pairs)
        return done[step]

    def near(step, piece):
        return [send(step, piece, routes.onward), send(step + 1, piece, routes.backward)]

    def far(step, sides):
        return [
            send(step, sides[0][0], routes.onward),
            send(step + 1, sides[1][1], routes.backward),
        ]

    def entries(piece, sides, halves, first, number):
        found = [(piece,), (sides[0],), (sides[1],), tuple(halves)]
        return [(arrays, n * group + first, number) for n, arrays in enumerate(found)]

    def build(step, index, own_beam, messages, smalls, pieces, bright_rows):
        built = build_factors(
            (index, share, per_group),
            gated(step, table),
            own_beam,
            messages,
            antenna_uvw,
            smalls,
            pieces,
            span,
            bright_rows,
            small.shape[1],
        )
        done[step] = built[0]
        return built

    core, *side = range(1, width)
    (message,) = messages_for(beam, 0, [core], small, gated(BEAM, table))
    message = send(BEAM + 1, message, routes.partner[core])
    (own,) = build(OWN, 0, beam, [message], [small, message], routes.full, BRIGHT_ROWS)
    own_sides = near(OWN_NEAR, own)
    messages = messages_for(beam, 0, side, small, gated(SIDE_BEAMS, table))
    messages = [
        send(SIDE_BEAMS + 1 + n, messages[n], routes.partner[m]) for n, m in enumerate(side)
    ]
    own_far = far(OWN_FAR, own_sides)
    (rest,) = build(REST, 0, None, messages, messages, routes.full, BRIGHT_ROWS)
    rest_sides = near(REST_NEAR, rest)

    later = messages_for(beam, 1, [core, *side], None, gated(LATER_BEAMS, table))
    later = [send(LATER_BEAMS + m, later[m - 1], routes.partner[m]) for m in (core, *side)]
    vis = slices_for(
        visibility, 1, share, [(m, 0) for m in (core, *side)], gated(VIS, table)
    )
    vis = [visibility] + [send(VIS + m, vis[m - 1], routes.partner[m]) for m in (core, *side)]
    later_pieces = build(
        LATER, 1, beam, later, [small, message, *messages], routes.pieces, 0
    )
    rest_far = far(REST_FAR, rest_sides)
    near_0 = near(PIECE_NEAR[0], later_pieces[0])
    near_1 = near(PIECE_NEAR[1], later_pieces[1])
    far_0 = far(PIECE_FAR[0], near_0)

    grads = []

    def work(index, step, home_step, ready, bright):
        arrived, total = [], None
        for n, homes in enumerate([routes.order[:1], routes.order[1:2], routes.order[2:]]):
            made = unit_work(
                index,
                routes.steps[index] + len(arrived) * routes.steps_per_home,
                gated(step + n, table),
                ready,
                [vis[m] for m in homes],
                keep,
                bright,
            )
            results, grad = made[: len(homes)], made[len(homes)]
            if isinstance(bright, int):
                bright = made[-1]
            done[step + n] = grad
            total = grad if total is None else total + grad
            arrived += [
                send(home_step - 1 + m, part, routes.partner[m]) if m else part
                for m, part in zip(homes, results)
            ]
        grads.append(total)
        return arrived, bright

    def put(step, homes, arrays, index, residual):
        rows = [(n, k) for n in range(len(arrays)) for k in range(units_dev)]
        offset = routes.targets[index] + homes * routes.targets_per_home
        done[step] = put_residuals(
            rows, arrays, offset, gated(step, table), visibility.shape, residual
        )
        return done[step]

    number = group // 2
    pieces = entries(own, own_sides, own_far, 0, number)
    pieces += entries(rest, rest_sides, rest_far, number, number)
    arrived, columns = work(0, WORK, HOME, [pieces], share)
    far_1 = far(PIECE_FAR[1], near_1)
    residual = put(PUT, 0, arrived, 0, None)
    ready = [
        entries(piece, sides, halves, 0, group)
        for piece, sides, halves in zip(later_pieces, (near_0, near_1), (far_0, far_1))
    ]
    arrived, _ = work(1, LATER_WORK, LATER_HOME, ready, columns)

    partial = jnp.concatenate(grads, 0)
    parts = [partial[:, n * group : (n + 1) * group] for n in range(4)]
    plane_sum = (parts[0] + send(SUM_PLANES, parts[3], routes.opposite)) + (
        send(SUM_PLANES + 1, parts[1], routes.backward)
        + send(SUM_PLANES + 2, parts[2], routes.onward)
    )
    sums = [plane_sum[:, m * per_group : (m + 1) * per_group] for m in range(width)]
    sums = [sums[0]] + [
        send(SUM_PLANE - 1 + m, sums[m], routes.partner[m]) for m in (core, *side)
    ]
    sums = jnp.stack(sums, 0)
    ids = jnp.arange(width, dtype=jnp.int32)
    here = jnp.bitwise_xor(ids[:, None], mine) == ids[None, :]
    summed = jnp.sum(jnp.where(here[:, :, None, None], sums[None], 0.0), axis=1)
    summed = summed.reshape(slots, per_group)

    residual = put(PUT_NEAR, 2, arrived[2:], 1, residual)
    residual = put(PUT_LAST, 0, arrived[:2], 1, residual)
    return residual, summed


def per_device(
    visibility, station_beam, antenna_uvw, source_dirs, source_flux, visible_list, antenna_flags
):
    span = visibility.shape[4]
    antennas = station_beam.shape[3]
    small = packed_small(source_dirs, source_flux, visible_list)
    keep = 1.0 - antenna_flags.astype(jnp.float32)
    arguments = (visibility, station_beam, antenna_uvw, small, keep)
    if lax.axis_size("tile") == 16:
        routes = Routes(4, 4, unit_table(antennas // span), visibility.shape[1] // 4)
        residual, summed = plane_program(routes, *arguments)
    else:
        residual, summed = plain_program(*arguments)
    return (residual, summed * (-1.0 / (8.0 * antennas)))


def solution(mesh):
    return jax.shard_map(
        per_device,
        mesh=mesh,
        in_specs=(
            P("tile", "grp", None, None, None),
            P("grp", None, "tile", None),
            P("grp", None, None),
            P(None, "tile"),
            P(("grp", "tile")),
            P(None, "tile"),
            P("grp", None),
        ),
        out_specs=(P("tile", "grp", None, None, None), P("grp", "tile")),
        check_vma=False,
    )
```

```python
import functools

import jax
import jax.numpy as jnp
import numpy as np
from jax import lax
from jax.experimental import pallas as pl
from jax.experimental.pallas import tpu as pltpu
from jax.sharding import PartitionSpec as P


def unit_table(block_count):
    first_list = []
    second_list = []
    diag_list = []
    for row_block in range(block_count):
        for col_block in range(row_block + 1, block_count):
            first_list.append(row_block)
            second_list.append(col_block)
            diag_list.append(0)
    for pair_index in range(block_count // 2):
        first_list.append(2 * pair_index)
        second_list.append(2 * pair_index + 1)
        diag_list.append(1)
    return np.stack([first_list, second_list, diag_list], 1).astype(np.int32)


def turn_polynomials():
    nodes = 0.125 + 0.125 * np.cos(np.pi * (np.arange(64) + 0.5) / 64)
    root = np.sqrt(nodes)
    fit = np.polynomial.Polynomial.fit
    sine = fit(nodes, np.sin(2 * np.pi * root) / root, 7, domain=[0, 0.25]).convert()
    cosine = fit(nodes, np.cos(2 * np.pi * root), 8, domain=[0, 0.25]).convert()
    return [float(c) for c in sine.coef], [float(c) for c in cosine.coef]


def horner(coefs, x):
    total = coefs[-1]
    for coef in coefs[-2::-1]:
        total = total * x + coef
    return total


def build_kernel(sets, slot_ids, pieces, bright_rows, width, tab_ref, *refs):
    refs, scratch_ref = refs[:-1], refs[-1]
    uvw_ref, outs = refs[-1 - len(pieces)], refs[-len(pieces) :]
    per_group = sets[0][0]
    span = outs[0].shape[2]
    count = len(sets) * per_group
    sin_coefs, cos_coefs = turn_polynomials()
    brights = []
    for part, (_, beam_at, small_at) in enumerate(sets):
        beam_ref = refs[beam_at]
        if beam_ref.shape[0] == 1:
            beam = [beam_ref.at[0, 0], beam_ref.at[0, 1]]
        else:
            beam = [beam_ref.at[pl.ds(n * per_group, per_group)] for n in (0, 1)]
        if refs[small_at].dtype == jnp.float32:
            small = small_rows(scratch_ref, *refs[small_at : small_at + 3])
        else:
            small = unsplit(refs[small_at], 2 * per_group, width)
        lanes = lax.broadcasted_iota(jnp.int32, (per_group, width), 1)
        rows = lax.broadcasted_iota(jnp.int32, (per_group, width), 0)

        def pick(chosen, row):
            return jnp.sum(jnp.where(chosen, small[row : row + 1, :], 0.0), axis=1, keepdims=True)

        def chosen_at(index):
            here = lax.broadcasted_iota(jnp.int32, small.shape, 0) == LIST_ROW + tab_ref[0] + index
            line = jnp.sum(jnp.where(here, small, 0.0), axis=0, keepdims=True)
            listed = jnp.sum(jnp.where(lanes == rows, line, 0.0), axis=1, keepdims=True)
            return listed.astype(jnp.int32) == lanes

        group = part * per_group
        if bright_rows:
            columns = lax.broadcasted_iota(jnp.int32, (per_group, span), 1)
            numbers = lax.broadcasted_iota(jnp.int32, (per_group, span), 0) + group
            for index in range(slot_ids[1]):
                flux = pick(chosen_at(index), 2)
                line = jnp.sum(jnp.where(columns == numbers, flux, 0.0), axis=0, keepdims=True)
                if part == 0:
                    brights.append(line)
                else:
                    brights[index] += line
        chosen = chosen_at(slot_ids[0])
        east = pick(chosen, 0)
        north = pick(chosen, 1)
        depth = jnp.sqrt(1.0 - east * east - north * north) - 1.0
        for out_ref, piece in zip(outs, pieces):
            for place, block in enumerate(piece):
                cols = pl.ds(block * span, span)
                delay = (
                    uvw_ref[0, 0:1, cols] * east
                    + uvw_ref[0, 1:2, cols] * north
                    + uvw_ref[0, 2:3, cols] * depth
                )
                turn = delay - jnp.floor(delay + 0.5)
                square = turn * turn
                sine = horner(sin_coefs, square) * turn
                cosine = horner(cos_coefs, square)
                real = beam[0][:, cols].astype(jnp.float32)
                imag = beam[1][:, cols].astype(jnp.float32)
                at = pl.ds(place * count + group, per_group)
                out_ref[0, at] = (real * cosine + imag * sine).astype(jnp.bfloat16)
                out_ref[1, at] = (imag * cosine - real * sine).astype(jnp.bfloat16)
    if bright_rows:
        padding = jnp.zeros((bright_rows - len(brights), span), jnp.float32)
        block = jnp.concatenate(brights + [padding], 0).astype(jnp.bfloat16)
        for part in (0, 1):
            outs[0][part, pl.ds(len(pieces[0]) * count, bright_rows)] = block


def small_rows(rows_ref, dirs_ref, flux_ref, list_ref):
    rows_ref[...] = jnp.zeros_like(rows_ref)
    rows_ref[0:2, 0 : dirs_ref.shape[1]] = dirs_ref[...]
    rows_ref[2:3, 0 : flux_ref.shape[1]] = flux_ref[...]
    slots, count = list_ref.shape
    rows_ref[LIST_ROW : LIST_ROW + slots, 0:count] = list_ref[...].astype(jnp.float32)
    return rows_ref[...]


LIST_ROW = 8
SMALL_ROWS = 16


def unsplit(message_ref, start, width):
    rows = pl.ds(start, SMALL_ROWS)
    terms = [message_ref[rows, pl.ds(n * width, width)].astype(jnp.float32) for n in range(3)]
    return (terms[0] + terms[1]) + terms[2]


BRIGHT_ROWS = 16


def build_factors(
    slot_ids, table, beam, messages, antenna_uvw, smalls, pieces, span, bright_rows, small_width
):
    slots, _, antennas = antenna_uvw.shape
    per_group = slot_ids[2]
    index = slot_ids[0]
    whole = pl.BlockSpec(memory_space=pltpu.VMEM)
    operands, in_specs, sets = [], [], []
    if beam is not None:
        operands.append(beam)
        in_specs.append(
            pl.BlockSpec((1, 2, per_group, antennas), lambda n, tab: (tab[0] + index, 0, 0, 0))
        )
    operands += messages
    beams = len(operands)
    for n, small in enumerate(smalls):
        at = next((k for k, known in enumerate(operands) if known is small), len(operands))
        if at == len(operands):
            operands += small if isinstance(small, tuple) else [small]
        sets.append((per_group, n, at))
    in_specs += [whole] * (len(operands) - len(in_specs))
    in_specs.append(pl.BlockSpec((1, 3, antennas), lambda n, tab: (tab[0] + index, 0, 0)))
    count = beams * per_group
    shapes = [
        (2, len(piece) * count + (0 if n else bright_rows), span) for n, piece in enumerate(pieces)
    ]
    return pl.pallas_call(
        functools.partial(build_kernel, sets, slot_ids, pieces, bright_rows, small_width),
        grid_spec=pltpu.PrefetchScalarGridSpec(
            num_scalar_prefetch=1,
            grid=(1,),
            in_specs=in_specs,
            out_specs=[whole] * len(pieces),
            scratch_shapes=[pltpu.VMEM((SMALL_ROWS, small_width), jnp.float32)],
        ),
        out_shape=[jax.ShapeDtypeStruct(shape, jnp.bfloat16) for shape in shapes],
        compiler_params=pltpu.CompilerParams(vmem_limit_bytes=40 * 1024 * 1024),
        cost_estimate=LITTLE,
        name="build_factors",
    )(table, *operands, antenna_uvw)


LITTLE = pl.CostEstimate(flops=1, bytes_accessed=1, transcendentals=0)


def message_kernel(count, with_small, tab_ref, *refs):
    beams, refs = refs[:count], refs[count:]
    if with_small:
        smalls, outs, scratch_ref = refs[:3], refs[3:-1], refs[-1]
        terms = []
        rest = small_rows(scratch_ref, *smalls)
        width = rest.shape[1]
        for _ in range(3):
            terms.append(rest.astype(jnp.bfloat16))
            rest = rest - terms[-1].astype(jnp.float32)
    else:
        outs = refs
    for beam_ref, out_ref in zip(beams, outs):
        per_group = beam_ref.shape[2]
        for part in (0, 1):
            out_ref[pl.ds(part * per_group, per_group)] = beam_ref[0, part]
        if with_small:
            rows = pl.ds(2 * per_group, SMALL_ROWS)
            out_ref[rows] = jnp.zeros((SMALL_ROWS, out_ref.shape[1]), jnp.bfloat16)
            for n, term in enumerate(terms):
                out_ref[rows, pl.ds(n * width, width)] = term


def messages_for(beam, index, others, small, table):
    _, _, per_group, antennas = beam.shape
    smalls = small or ()
    rows = 2 * per_group + (SMALL_ROWS if smalls else 0)
    whole = pl.BlockSpec(memory_space=pltpu.VMEM)
    scratch = []
    if smalls:
        scratch.append(pltpu.VMEM((SMALL_ROWS, smalls[0].shape[1]), jnp.float32))
    return pl.pallas_call(
        functools.partial(message_kernel, len(others), bool(smalls)),
        grid_spec=pltpu.PrefetchScalarGridSpec(
            num_scalar_prefetch=1,
            grid=(1,),
            in_specs=[
                pl.BlockSpec(
                    (1, 2, per_group, antennas), lambda n, tab, m=m: (tab[m] + index, 0, 0, 0)
                )
                for m in others
            ]
            + [whole for _ in smalls],
            out_specs=[whole for _ in others],
            scratch_shapes=scratch,
        ),
        out_shape=[jax.ShapeDtypeStruct((rows, antennas), jnp.bfloat16) for _ in others],
        cost_estimate=LITTLE,
        name="messages_for",
    )(table, *[beam] * len(others), *smalls)


def slice_kernel(count, tab_ref, *refs):
    for source, target in zip(refs[:count], refs[count:]):
        target[...] = source[...]


def slices_for(array, axis, size, starts, table):
    lead = axis > 0
    shape = array.shape[:axis] + (size,) + array.shape[axis + 1 :]
    block = (1,) + shape[1:] if lead else shape
    rest = (0,) * (array.ndim - axis - 1)
    return pl.pallas_call(
        functools.partial(slice_kernel, len(starts)),
        grid_spec=pltpu.PrefetchScalarGridSpec(
            num_scalar_prefetch=1,
            grid=(shape[0] if lead else 1,),
            in_specs=[
                pl.BlockSpec(
                    block,
                    lambda n, tab, start=start, shift=shift: (
                        *((n,) if lead else ()),
                        tab[start] // size + shift,
                        *rest,
                    ),
                )
                for start, shift in starts
            ],
            out_specs=[
                pl.BlockSpec(block, lambda n, tab: (n,) + (0,) * (array.ndim - 1)) for _ in starts
            ],
        ),
        out_shape=[jax.ShapeDtypeStruct(shape, array.dtype) for _ in starts],
        cost_estimate=LITTLE,
        name="slices_for",
    )(table, *[array] * len(starts))


KIND, ONE, TWO, ONE_AT, TWO_AT = 0, 1, 2, 3, 5
COLUMNS = 7


def unit_kernel(index, offset, pieces, bright_at, homes, tab_ref, *refs):
    arrays = []
    for entries in pieces:
        found = []
        for count, start, number in entries:
            parts = (refs[0].at[0], refs[0].at[1]) if count == 1 else refs[:2]
            found.append((parts, start, number))
            refs = refs[count:]
        arrays.append(found)
    vis_refs, (keep_one_ref, keep_two_ref) = refs[:homes], refs[homes : homes + 2]
    refs = refs[homes + 2 :]
    columns_ref = None
    if bright_at is None:
        columns_ref, refs = refs[0], refs[1:]
    out_refs, grad_ref = refs[:homes], refs[homes]
    refs = refs[homes + 1 :]
    if bright_at is not None:
        columns_ref, refs = refs[0], refs[1:]
    total_ref, one_ref, two_ref, vis_ref = refs
    step = pl.program_id(0)
    slot = tab_ref[0] + index
    sources, span = one_ref.shape[1:]

    def entry(column):
        return tab_ref[offset + step * COLUMNS + column]

    def load(target, at):
        for n, found in enumerate(arrays):

            @pl.when(entry(at) == n)
            def _(found=found):
                place = entry(at + 1)
                for parts, start, number in found:
                    rows = pl.ds(pl.multiple_of(place * number, number), number)
                    for part in (0, 1):
                        target[part, pl.ds(start, number)] = parts[part][rows]

    if bright_at is not None:

        @pl.when(step == 0)
        def _():
            for parts, start, number in arrays[0]:
                lines = parts[0][pl.ds(bright_at * number, BRIGHT_ROWS)].astype(jnp.float32)
                lanes = lax.broadcasted_iota(jnp.int32, (number, span), 1)
                rows = lax.broadcasted_iota(jnp.int32, (number, span), 0)
                for n in range(columns_ref.shape[0]):
                    line = jnp.where(lanes == rows, lines[n : n + 1, :], 0.0)
                    column = jnp.sum(line, axis=1, keepdims=True)
                    columns_ref[n, pl.ds(start, number)] = jnp.broadcast_to(column, (number, 128))

    def dot(a, b):
        return lax.dot_general(a, b, (((1,), (0,)), ((), ())), preferred_element_type=jnp.float32)

    def scaled_of(re, im):
        column = jnp.concatenate([columns_ref[index]] * (span // 128), 1)
        return (
            (re.astype(jnp.float32) * column).astype(jnp.bfloat16),
            (im.astype(jnp.float32) * column).astype(jnp.bfloat16),
        )

    def outer(a, b):
        row_ids = lax.broadcasted_iota(jnp.int32, a.shape, 0)
        a = jnp.where(row_ids == slot, a, 0.0)
        return lax.dot_general(a, b, (((0,), (0,)), ((), ())), preferred_element_type=jnp.float32)

    def cross(a_re, a_im, b_re, b_im):
        lhs = jnp.concatenate([a_re, a_im], 0).T
        rhs = jnp.concatenate(
            [jnp.concatenate([b_re, -b_im], 1), jnp.concatenate([b_im, b_re], 1)], 0
        )
        both = dot(lhs, rhs)
        return both[:, :span], both[:, span:]

    def pull(re, im, res_re, res_im, sign):
        lhs = jnp.concatenate([re, im], 1)
        rhs = jnp.concatenate(
            [
                jnp.concatenate([res_re, res_im], 1),
                jnp.concatenate([res_im, -res_re] if sign == 1 else [-res_im, res_re], 1),
            ],
            0,
        )
        both = dot(lhs, rhs)
        return both[:, :span], both[:, span:]

    def add_grad(value):
        folded = value[:, :128]
        for start in range(128, span, 128):
            folded = folded + value[:, start : start + 128]
        total_ref[...] += folded

    each = pl.num_programs(0) // homes

    def put(res_re, res_im):
        for home, out_ref in enumerate(out_refs):

            @pl.when(step // each == home)
            def _(out_ref=out_ref):
                out_ref[0, 0] = res_re
                out_ref[0, 1] = res_im

    @pl.when(step == 0)
    def _():
        total_ref[...] = jnp.zeros_like(total_ref)

    load(one_ref, ONE_AT)
    load(two_ref, TWO_AT)
    for home, home_ref in enumerate(vis_refs):

        @pl.when(step // each == home)
        def _(home_ref=home_ref):
            vis_ref[...] = home_ref[0, 0]

    @pl.when(entry(KIND) == 0)
    def _():
        one_re, one_im, two_re, two_im = one_ref[0], one_ref[1], two_ref[0], two_ref[1]
        pred_re, pred_im = cross(*scaled_of(one_re, one_im), two_re, two_im)
        weights = outer(keep_one_ref[...], keep_two_ref[...])
        res_re = (weights * (vis_ref[0].astype(jnp.float32) - pred_re)).astype(jnp.bfloat16)
        res_im = (weights * (vis_ref[1].astype(jnp.float32) - pred_im)).astype(jnp.bfloat16)
        put(res_re, res_im)
        sum_re, sum_im = pull(one_re, one_im, res_re, res_im, 1)
        add_grad(sum_re * two_re.astype(jnp.float32) - sum_im * two_im.astype(jnp.float32))

    @pl.when(entry(KIND) == 1)
    def _():
        one_re, one_im, two_re, two_im = one_ref[0], one_ref[1], two_ref[0], two_ref[1]
        row_ids = lax.broadcasted_iota(jnp.int32, (span, span), 0)
        col_ids = lax.broadcasted_iota(jnp.int32, (span, span), 1)
        upper = row_ids < col_ids
        lower = row_ids > col_ids
        first_re, first_im = cross(*scaled_of(one_re, one_im), one_re, one_im)
        second_re, second_im = cross(two_re, two_im, *scaled_of(two_re, two_im))
        keep_one = keep_one_ref[...]
        keep_two = keep_two_ref[...]
        weights = jnp.where(upper, outer(keep_one, keep_one), 0.0) + jnp.where(
            lower, outer(keep_two, keep_two), 0.0
        )
        vis_re = vis_ref[0].astype(jnp.float32)
        vis_im = vis_ref[1].astype(jnp.float32)
        res_re = (weights * (vis_re - jnp.where(upper, first_re, second_re))).astype(jnp.bfloat16)
        res_im = (weights * (vis_im - jnp.where(upper, first_im, -second_im))).astype(jnp.bfloat16)
        put(res_re, res_im)
        none = jnp.zeros_like(res_re)
        sum_re, sum_im = pull(
            one_re, one_im, jnp.where(upper, res_re, none), jnp.where(upper, res_im, none), 1
        )
        add_grad(sum_re * one_re.astype(jnp.float32) - sum_im * one_im.astype(jnp.float32))
        sum_re, sum_im = pull(
            two_re, two_im, jnp.where(lower, res_re, none), jnp.where(lower, res_im, none), -1
        )
        add_grad(sum_re * two_re.astype(jnp.float32) + sum_im * two_im.astype(jnp.float32))

    @pl.when(step == pl.num_programs(0) - 1)
    def _():
        grad_ref[...] = jnp.sum(total_ref[...].T, axis=0, keepdims=True)


def unit_work(index, offset, table, pieces, vis, keep, bright):
    units_dev, _, _, span, _ = vis[0].shape
    slots = keep.shape[0]
    sources = sum(number for _, _, number in pieces[0])
    count = units_dev * len(vis)
    whole = pl.BlockSpec(memory_space=pltpu.VMEM)
    arrays = [array for piece in pieces for entry, _, _ in piece for array in entry]

    def at(tab, step, column):
        return tab[offset + step * COLUMNS + column]

    def unit(step, home):
        return jnp.clip(step - home * units_dev, 0, units_dev - 1)

    in_specs = [whole] * len(arrays)
    for home, array in enumerate(vis):
        if array.shape[1] == slots:
            slot = lambda tab: tab[0] + index
        else:
            slot = lambda tab: index
        in_specs.append(
            pl.BlockSpec(
                (1, 1, 2, span, span),
                lambda u, tab, home=home, slot=slot: (unit(u, home), slot(tab), 0, 0, 0),
            )
        )
    in_specs += [
        pl.BlockSpec((slots, span), lambda u, tab: (0, at(tab, u, ONE))),
        pl.BlockSpec((slots, span), lambda u, tab: (0, at(tab, u, TWO))),
    ]
    operands = [table, *arrays, *vis, keep, keep]
    bright_at = None
    if isinstance(bright, int):
        first = pieces[0][0]
        bright_at = (first[0][0].shape[1] - BRIGHT_ROWS) // first[2]
    else:
        in_specs.append(whole)
        operands.append(bright)
    out_specs = [
        pl.BlockSpec((1, 2, span, span), lambda u, tab, home=home: (unit(u, home), 0, 0, 0))
        for home in range(len(vis))
    ]
    out_shapes = [jax.ShapeDtypeStruct((units_dev, 2, span, span), jnp.bfloat16) for _ in vis]
    out_specs.append(pl.BlockSpec((1, sources), lambda u, tab: (0, 0)))
    out_shapes.append(jax.ShapeDtypeStruct((1, sources), jnp.float32))
    if bright_at is not None:
        out_specs.append(pl.BlockSpec((bright, sources, 128), lambda u, tab: (0, 0, 0)))
        out_shapes.append(jax.ShapeDtypeStruct((bright, sources, 128), jnp.float32))
    kinds = [[(len(entry), start, number) for entry, start, number in piece] for piece in pieces]
    return pl.pallas_call(
        functools.partial(unit_kernel, index, offset, kinds, bright_at, len(vis)),
        grid_spec=pltpu.PrefetchScalarGridSpec(
            num_scalar_prefetch=1,
            grid=(count,),
            in_specs=in_specs,
            out_specs=out_specs,
            scratch_shapes=[
                pltpu.VMEM((sources, 128), jnp.float32),
                pltpu.VMEM((2, sources, span), jnp.bfloat16),
                pltpu.VMEM((2, sources, span), jnp.bfloat16),
                pltpu.VMEM((2, span, span), jnp.bfloat16),
            ],
        ),
        out_shape=out_shapes,
        compiler_params=pltpu.CompilerParams(vmem_limit_bytes=48 * 1024 * 1024),
        cost_estimate=LITTLE,
        name="unit_work",
    )(*operands)


def put_kernel(sources, tab_ref, *refs):
    out_ref = refs[-1]
    for step, (which, row) in enumerate(sources):

        @pl.when(pl.program_id(0) == step)
        def _(which=which, row=row):
            out_ref[0, 0] = refs[which][...] if row is None else refs[which][row]


def put_residuals(sources, arrays, offset, table, shape, residual):
    span = shape[-1]
    whole = pl.BlockSpec(memory_space=pltpu.VMEM)
    operands = [table, *arrays]
    in_specs = [whole] * len(arrays)
    aliases = {}
    if residual is not None:
        aliases = {len(operands): 0}
        operands.append(residual)
        in_specs.append(pl.BlockSpec(memory_space=pl.ANY))
    return pl.pallas_call(
        functools.partial(put_kernel, sources),
        grid_spec=pltpu.PrefetchScalarGridSpec(
            num_scalar_prefetch=1,
            grid=(len(sources),),
            in_specs=in_specs,
            out_specs=pl.BlockSpec(
                (1, 1, 2, span, span),
                lambda n, tab: (tab[offset + 2 * n], tab[offset + 2 * n + 1], 0, 0, 0),
            ),
        ),
        out_shape=jax.ShapeDtypeStruct(shape, jnp.bfloat16),
        input_output_aliases=aliases,
        compiler_params=pltpu.CompilerParams(vmem_limit_bytes=32 * 1024 * 1024),
        cost_estimate=LITTLE,
        name="put_residuals",
    )(*operands)


class Routes:
    def __init__(self, planes, width, units, share):
        count = planes * width
        blocks = int(units[:, :2].max()) + 1
        self.width = width
        self.units_dev = units_dev = units.shape[0] // count
        ring = [0] + list(range(1, planes, 2)) + list(range(planes - 2, 0, -2))

        def along(step):
            at = {plane: ring[(n + step) % planes] for n, plane in enumerate(ring)}
            return [(t, at[t // width] * width + t % width) for t in range(count)]

        self.onward = along(1)
        self.backward = along(-1)
        self.opposite = along(2)
        self.partner = [[(t, t ^ m) for t in range(count)] for m in range(width)]

        half = blocks // 2
        self.full = [list(range(blocks))]
        self.pieces = [list(range(half)), list(range(half, blocks))]

        def table_of(pieces, order):
            rows = np.zeros((count, len(order), units_dev, COLUMNS), np.int32)
            for t in range(count):
                for n, m in enumerate(order):
                    for k in range(units_dev):
                        one, two, kind = units[(t ^ m) * units_dev + k].tolist()
                        at = [
                            (p, piece.index(b))
                            for b in (one, two)
                            for p, piece in enumerate(pieces)
                            if b in piece
                        ]
                        rows[t, n, k] = [kind, one, two, *at[0], *at[1]]
            return rows

        def targets(index):
            rows = np.zeros((count, len(self.order), units_dev, 2), np.int32)
            for t in range(count):
                for n, m in enumerate(self.order):
                    for k in range(units_dev):
                        rows[t, n, k] = k, (t % width ^ m) * share + index
            return rows

        self.order = list(range(width // 2, width)) + list(range(width // 2 - 1, -1, -1))
        starts = np.array([[(t % width ^ m) * share for m in range(width)] for t in range(count)])
        parts = [starts, table_of(self.full, self.order), table_of(self.pieces, self.order)]
        parts += [targets(n) for n in range(share)]
        parts = [part.reshape(count, -1) for part in parts]
        ends = np.cumsum([part.shape[1] for part in parts]).tolist()
        self.table = np.concatenate(parts, 1).astype(np.int32)
        self.steps = ends[:2]
        self.targets = ends[2:]
        self.steps_per_home = units_dev * COLUMNS
        self.targets_per_home = units_dev * 2


def plain_program(visibility, beam, antenna_uvw, small, keep):
    units_dev, slots, _, span, _ = visibility.shape
    _, _, per_group, antennas = beam.shape
    blocks = antennas // span
    tile_index = lax.axis_index("tile")
    units = unit_table(blocks)
    none = np.zeros_like(units[:, 0])
    table = np.stack([units[:, 2], units[:, 0], units[:, 1], none, units[:, 0], none, units[:, 1]], 1)
    table = table.astype(np.int32).reshape(-1, units_dev * COLUMNS)
    table = np.pad(table, ((0, 0), (1, 0)))
    table = lax.dynamic_index_in_dim(jnp.asarray(table), tile_index, 0, keepdims=False)
    columns = None
    residuals, grads = [], []
    for slot in range(slots):
        (owned,) = build_factors(
            (slot, slots, per_group),
            table,
            beam,
            [],
            antenna_uvw,
            [small],
            [list(range(blocks))],
            span,
            0 if slot else BRIGHT_ROWS,
            small[0].shape[1],
        )
        everyone = lax.all_gather(owned, "tile", axis=0)
        rows = blocks * per_group
        if columns is None:
            bright = everyone[:, 0, rows : rows + slots, :per_group].astype(jnp.float32)
            bright = jnp.swapaxes(bright, 0, 1).reshape(slots, -1, 1)
            columns = jnp.broadcast_to(bright, bright.shape[:2] + (128,))
        factors = everyone[:, :, :rows].reshape(-1, 2, blocks, per_group, span)
        number = factors.shape[0] * per_group
        factors = factors.transpose(1, 2, 0, 3, 4).reshape(2, blocks * number, span)
        residual, grad = unit_work(
            slot, 1, table, [[((factors,), 0, number)]], [visibility], keep, columns
        )
        residuals.append(residual)
        grads.append(grad)
    summed = lax.psum_scatter(jnp.concatenate(grads, 0), "tile", scatter_dimension=1, tiled=True)
    return jnp.stack(residuals, 1), summed


OWN, OWN_NEAR, OWN_FAR, REST, REST_NEAR, REST_FAR = 0, 1, 3, 5, 6, 8
BEAM, SIDE_BEAMS, LATER_BEAMS, VIS, LATER = 10, 12, 15, 19, 23
PIECE_NEAR, PIECE_FAR = (24, 26), (28, 30)
WORK, HOME, PUT, LATER_WORK, LATER_HOME, PUT_NEAR, PUT_LAST = 32, 35, 38, 40, 43, 46, 47
SUM_PLANES, SUM_PLANE = 48, 51
GATES = {
    1: (0,),
    3: (0, 1),
    5: (0, 2, 13),
    6: (1, 2, 11),
    7: (1, 2),
    14: (13,),
    16: (2,),
    17: (1,),
    19: (18,),
    20: (3, 4, 6, 7, 17),
    21: (3, 4, 5, 13, 14, 16, 17),
    23: (4, 17),
    24: (6, 9, 17),
    25: (6, 9, 17, 23),
    26: (9,),
    27: (8,),
    28: (22,),
    31: (25, 27),
    33: (23, 32),
    34: (33,),
    35: (8, 9, 24, 25),
    40: (28, 34, 36, 37),
    41: (40,),
    42: (29, 41),
    43: (41,),
    45: (28, 32),
    48: (35,),
    49: (44,),
    51: (34,),
    52: (38,),
}


def plane_program(routes, visibility, beam, antenna_uvw, small, keep):
    units_dev, slots, _, span, _ = visibility.shape
    per_group = beam.shape[2]
    width = routes.width
    share = slots // width
    group = width * per_group
    tile_index = lax.axis_index("tile")
    mine = tile_index % width
    table = lax.dynamic_index_in_dim(jnp.asarray(routes.table), tile_index, 0, keepdims=False)
    done = {}

    def gated(step, value):
        earlier = [done[gate] for gate in GATES.get(step, ())]
        return lax.optimization_barrier((value, *earlier))[0] if earlier else value

    def send(step, value, pairs):
        done[step] = lax.ppermute(gated(step, value), "tile", pairs)
        return done[step]

    def near(step, piece):
        return [send(step, piece, routes.onward), send(step + 1, piece, routes.backward)]

    def far(step, sides):
        return [
            send(step, sides[0][0], routes.onward),
            send(step + 1, sides[1][1], routes.backward),
        ]

    def entries(piece, sides, halves, first, number):
        found = [(piece,), (sides[0],), (sides[1],), tuple(halves)]
        return [(arrays, n * group + first, number) for n, arrays in enumerate(found)]

    def build(step, index, own_beam, messages, smalls, pieces, bright_rows):
        built = build_factors(
            (index, share, per_group),
            gated(step, table),
            own_beam,
            messages,
            antenna_uvw,
            smalls,
            pieces,
            span,
            bright_rows,
            small[0].shape[1],
        )
        done[step] = built[0]
        return built

    core, *side = range(1, width)
    (message,) = messages_for(beam, 0, [core], small, gated(BEAM, table))
    message = send(BEAM + 1, message, routes.partner[core])
    (own,) = build(OWN, 0, beam, [message], [small, message], routes.full, BRIGHT_ROWS)
    own_sides = near(OWN_NEAR, own)
    messages = messages_for(beam, 0, side, small, gated(SIDE_BEAMS, table))
    messages = [
        send(SIDE_BEAMS + 1 + n, messages[n], routes.partner[m]) for n, m in enumerate(side)
    ]
    own_far = far(OWN_FAR, own_sides)
    (rest,) = build(REST, 0, None, messages, messages, routes.full, BRIGHT_ROWS)
    rest_sides = near(REST_NEAR, rest)

    later = messages_for(beam, 1, [core, *side], None, gated(LATER_BEAMS, table))
    later = [send(LATER_BEAMS + m, later[m - 1], routes.partner[m]) for m in (core, *side)]
    vis = slices_for(
        visibility, 1, share, [(m, 0) for m in (core, *side)], gated(VIS, table)
    )
    vis = [visibility] + [send(VIS + m, vis[m - 1], routes.partner[m]) for m in (core, *side)]
    later_pieces = build(
        LATER, 1, beam, later, [small, message, *messages], routes.pieces, 0
    )
    rest_far = far(REST_FAR, rest_sides)
    near_0 = near(PIECE_NEAR[0], later_pieces[0])
    near_1 = near(PIECE_NEAR[1], later_pieces[1])
    far_0 = far(PIECE_FAR[0], near_0)

    grads = []

    def work(index, step, home_step, ready, bright):
        arrived, total = [], None
        for n, homes in enumerate([routes.order[:1], routes.order[1:2], routes.order[2:]]):
            made = unit_work(
                index,
                routes.steps[index] + len(arrived) * routes.steps_per_home,
                gated(step + n, table),
                ready,
                [vis[m] for m in homes],
                keep,
                bright,
            )
            results, grad = made[: len(homes)], made[len(homes)]
            if isinstance(bright, int):
                bright = made[-1]
            done[step + n] = grad
            total = grad if total is None else total + grad
            arrived += [
                send(home_step - 1 + m, part, routes.partner[m]) if m else part
                for m, part in zip(homes, results)
            ]
        grads.append(total)
        return arrived, bright

    def put(step, homes, arrays, index, residual):
        rows = [(n, k) for n in range(len(arrays)) for k in range(units_dev)]
        offset = routes.targets[index] + homes * routes.targets_per_home
        done[step] = put_residuals(
            rows, arrays, offset, gated(step, table), visibility.shape, residual
        )
        return done[step]

    number = group // 2
    pieces = entries(own, own_sides, own_far, 0, number)
    pieces += entries(rest, rest_sides, rest_far, number, number)
    arrived, columns = work(0, WORK, HOME, [pieces], share)
    far_1 = far(PIECE_FAR[1], near_1)
    residual = put(PUT, 0, arrived, 0, None)
    ready = [
        entries(piece, sides, halves, 0, group)
        for piece, sides, halves in zip(later_pieces, (near_0, near_1), (far_0, far_1))
    ]
    arrived, _ = work(1, LATER_WORK, LATER_HOME, ready, columns)

    partial = jnp.concatenate(grads, 0)
    parts = [partial[:, n * group : (n + 1) * group] for n in range(4)]
    plane_sum = (parts[0] + send(SUM_PLANES, parts[3], routes.opposite)) + (
        send(SUM_PLANES + 1, parts[1], routes.backward)
        + send(SUM_PLANES + 2, parts[2], routes.onward)
    )
    sums = [plane_sum[:, m * per_group : (m + 1) * per_group] for m in range(width)]
    sums = [sums[0]] + [
        send(SUM_PLANE - 1 + m, sums[m], routes.partner[m]) for m in (core, *side)
    ]
    sums = jnp.stack(sums, 0)
    ids = jnp.arange(width, dtype=jnp.int32)
    here = jnp.bitwise_xor(ids[:, None], mine) == ids[None, :]
    summed = jnp.sum(jnp.where(here[:, :, None, None], sums[None], 0.0), axis=1)
    summed = summed.reshape(slots, per_group)

    residual = put(PUT_NEAR, 2, arrived[2:], 1, residual)
    residual = put(PUT_LAST, 0, arrived[:2], 1, residual)
    return residual, summed


def per_device(
    visibility, station_beam, antenna_uvw, source_dirs, source_flux, visible_list, antenna_flags
):
    span = visibility.shape[4]
    antennas = station_beam.shape[3]
    small = (source_dirs, source_flux.astype(jnp.float32)[None], visible_list)
    keep = 1.0 - antenna_flags.astype(jnp.float32)
    arguments = (visibility, station_beam, antenna_uvw, small, keep)
    if lax.axis_size("tile") == 16:
        routes = Routes(4, 4, unit_table(antennas // span), visibility.shape[1] // 4)
        residual, summed = plane_program(routes, *arguments)
    else:
        residual, summed = plain_program(*arguments)
    return (residual, summed * (-1.0 / (8.0 * antennas)))


def solution(mesh):
    return jax.shard_map(
        per_device,
        mesh=mesh,
        in_specs=(
            P("tile", "grp", None, None, None),
            P("grp", None, "tile", None),
            P("grp", None, None),
            P(None, "tile"),
            P(("grp", "tile")),
            P(None, "tile"),
            P("grp", None),
        ),
        out_specs=(P("tile", "grp", None, None, None), P("grp", "tile")),
        check_vma=False,
    )
```

```python
import functools

import jax
import jax.numpy as jnp
import numpy as np
from jax import lax
from jax.experimental import pallas as pl
from jax.experimental.pallas import tpu as pltpu
from jax.sharding import PartitionSpec as P


def unit_table(block_count):
    first_list = []
    second_list = []
    diag_list = []
    for row_block in range(block_count):
        for col_block in range(row_block + 1, block_count):
            first_list.append(row_block)
            second_list.append(col_block)
            diag_list.append(0)
    for pair_index in range(block_count // 2):
        first_list.append(2 * pair_index)
        second_list.append(2 * pair_index + 1)
        diag_list.append(1)
    return np.stack([first_list, second_list, diag_list], 1).astype(np.int32)


def turn_polynomials():
    nodes = 0.125 + 0.125 * np.cos(np.pi * (np.arange(64) + 0.5) / 64)
    root = np.sqrt(nodes)
    fit = np.polynomial.Polynomial.fit
    sine = fit(nodes, np.sin(2 * np.pi * root) / root, 7, domain=[0, 0.25]).convert()
    cosine = fit(nodes, np.cos(2 * np.pi * root), 8, domain=[0, 0.25]).convert()
    return [float(c) for c in sine.coef], [float(c) for c in cosine.coef]


def horner(coefs, x):
    total = coefs[-1]
    for coef in coefs[-2::-1]:
        total = total * x + coef
    return total


def build_kernel(sets, slot_ids, pieces, bright_rows, width, tab_ref, *refs):
    refs, scratch_ref = refs[:-1], refs[-1]
    uvw_ref, outs = refs[-1 - len(pieces)], refs[-len(pieces) :]
    per_group = sets[0][0]
    span = outs[0].shape[2]
    count = len(sets) * per_group
    sin_coefs, cos_coefs = turn_polynomials()
    brights = []
    for part, (_, beam_at, small_at) in enumerate(sets):
        beam_ref = refs[beam_at]
        if beam_ref.shape[0] == 1:
            beam = [beam_ref.at[0, 0], beam_ref.at[0, 1]]
        else:
            beam = [beam_ref.at[pl.ds(n * per_group, per_group)] for n in (0, 1)]
        if refs[small_at].dtype == jnp.float32:
            small = small_rows(scratch_ref, *refs[small_at : small_at + 3])
        else:
            small = unsplit(refs[small_at], 2 * per_group, width)
        lanes = lax.broadcasted_iota(jnp.int32, (per_group, width), 1)
        rows = lax.broadcasted_iota(jnp.int32, (per_group, width), 0)

        def pick(chosen, row):
            return jnp.sum(jnp.where(chosen, small[row : row + 1, :], 0.0), axis=1, keepdims=True)

        def chosen_at(index):
            here = lax.broadcasted_iota(jnp.int32, small.shape, 0) == LIST_ROW + tab_ref[0] + index
            line = jnp.sum(jnp.where(here, small, 0.0), axis=0, keepdims=True)
            listed = jnp.sum(jnp.where(lanes == rows, line, 0.0), axis=1, keepdims=True)
            return listed.astype(jnp.int32) == lanes

        group = part * per_group
        if bright_rows:
            columns = lax.broadcasted_iota(jnp.int32, (per_group, span), 1)
            numbers = lax.broadcasted_iota(jnp.int32, (per_group, span), 0) + group
            for index in range(slot_ids[1]):
                flux = pick(chosen_at(index), 2)
                line = jnp.sum(jnp.where(columns == numbers, flux, 0.0), axis=0, keepdims=True)
                if part == 0:
                    brights.append(line)
                else:
                    brights[index] += line
        chosen = chosen_at(slot_ids[0])
        east = pick(chosen, 0)
        north = pick(chosen, 1)
        depth = jnp.sqrt(1.0 - east * east - north * north) - 1.0
        for out_ref, piece in zip(outs, pieces):
            for place, block in enumerate(piece):
                cols = pl.ds(block * span, span)
                delay = (
                    uvw_ref[0, 0:1, cols] * east
                    + uvw_ref[0, 1:2, cols] * north
                    + uvw_ref[0, 2:3, cols] * depth
                )
                turn = delay - jnp.floor(delay + 0.5)
                square = turn * turn
                sine = horner(sin_coefs, square) * turn
                cosine = horner(cos_coefs, square)
                real = beam[0][:, cols].astype(jnp.float32)
                imag = beam[1][:, cols].astype(jnp.float32)
                at = pl.ds(place * count + group, per_group)
                out_ref[0, at] = (real * cosine + imag * sine).astype(jnp.bfloat16)
                out_ref[1, at] = (imag * cosine - real * sine).astype(jnp.bfloat16)
    if bright_rows:
        padding = jnp.zeros((bright_rows - len(brights), span), jnp.float32)
        block = jnp.concatenate(brights + [padding], 0).astype(jnp.bfloat16)
        for part in (0, 1):
            outs[0][part, pl.ds(len(pieces[0]) * count, bright_rows)] = block


def small_rows(rows_ref, dirs_ref, flux_ref, list_ref):
    rows_ref[...] = jnp.zeros_like(rows_ref)
    rows_ref[0:2, 0 : dirs_ref.shape[1]] = dirs_ref[...]
    rows_ref[2:3, 0 : flux_ref.shape[1]] = flux_ref[...]
    slots, count = list_ref.shape
    rows_ref[LIST_ROW : LIST_ROW + slots, 0:count] = list_ref[...].astype(jnp.float32)
    return rows_ref[...]


LIST_ROW = 8
SMALL_ROWS = 16


def unsplit(message_ref, start, width):
    rows = pl.ds(start, SMALL_ROWS)
    terms = [message_ref[rows, pl.ds(n * width, width)].astype(jnp.float32) for n in range(3)]
    return (terms[0] + terms[1]) + terms[2]


BRIGHT_ROWS = 16


def build_factors(
    slot_ids, table, beam, messages, antenna_uvw, smalls, pieces, span, bright_rows, small_width
):
    slots, _, antennas = antenna_uvw.shape
    per_group = slot_ids[2]
    index = slot_ids[0]
    whole = pl.BlockSpec(memory_space=pltpu.VMEM)
    operands, in_specs, sets = [], [], []
    if beam is not None:
        operands.append(beam)
        in_specs.append(
            pl.BlockSpec((1, 2, per_group, antennas), lambda n, tab: (tab[0] + index, 0, 0, 0))
        )
    operands += messages
    beams = len(operands)
    for n, small in enumerate(smalls):
        at = next((k for k, known in enumerate(operands) if known is small), len(operands))
        if at == len(operands):
            operands += small if isinstance(small, tuple) else [small]
        sets.append((per_group, n, at))
    in_specs += [whole] * (len(operands) - len(in_specs))
    in_specs.append(pl.BlockSpec((1, 3, antennas), lambda n, tab: (tab[0] + index, 0, 0)))
    count = beams * per_group
    shapes = [
        (2, len(piece) * count + (0 if n else bright_rows), span) for n, piece in enumerate(pieces)
    ]
    return pl.pallas_call(
        functools.partial(build_kernel, sets, slot_ids, pieces, bright_rows, small_width),
        grid_spec=pltpu.PrefetchScalarGridSpec(
            num_scalar_prefetch=1,
            grid=(1,),
            in_specs=in_specs,
            out_specs=[whole] * len(pieces),
            scratch_shapes=[pltpu.VMEM((SMALL_ROWS, small_width), jnp.float32)],
        ),
        out_shape=[jax.ShapeDtypeStruct(shape, jnp.bfloat16) for shape in shapes],
        compiler_params=pltpu.CompilerParams(vmem_limit_bytes=40 * 1024 * 1024),
        cost_estimate=LITTLE,
        name="build_factors",
    )(table, *operands, antenna_uvw)


LITTLE = pl.CostEstimate(flops=1, bytes_accessed=1, transcendentals=0)


def message_kernel(count, with_small, tab_ref, *refs):
    beams, refs = refs[:count], refs[count:]
    if with_small:
        smalls, outs, scratch_ref = refs[:3], refs[3:-1], refs[-1]
        terms = []
        rest = small_rows(scratch_ref, *smalls)
        width = rest.shape[1]
        for _ in range(3):
            terms.append(rest.astype(jnp.bfloat16))
            rest = rest - terms[-1].astype(jnp.float32)
    else:
        outs = refs
    for beam_ref, out_ref in zip(beams, outs):
        per_group = beam_ref.shape[2]
        for part in (0, 1):
            out_ref[pl.ds(part * per_group, per_group)] = beam_ref[0, part]
        if with_small:
            rows = pl.ds(2 * per_group, SMALL_ROWS)
            out_ref[rows] = jnp.zeros((SMALL_ROWS, out_ref.shape[1]), jnp.bfloat16)
            for n, term in enumerate(terms):
                out_ref[rows, pl.ds(n * width, width)] = term


def messages_for(beam, index, others, small, table):
    _, _, per_group, antennas = beam.shape
    smalls = small or ()
    rows = 2 * per_group + (SMALL_ROWS if smalls else 0)
    whole = pl.BlockSpec(memory_space=pltpu.VMEM)
    scratch = []
    if smalls:
        scratch.append(pltpu.VMEM((SMALL_ROWS, smalls[0].shape[1]), jnp.float32))
    return pl.pallas_call(
        functools.partial(message_kernel, len(others), bool(smalls)),
        grid_spec=pltpu.PrefetchScalarGridSpec(
            num_scalar_prefetch=1,
            grid=(1,),
            in_specs=[
                pl.BlockSpec(
                    (1, 2, per_group, antennas), lambda n, tab, m=m: (tab[m] + index, 0, 0, 0)
                )
                for m in others
            ]
            + [whole for _ in smalls],
            out_specs=[whole for _ in others],
            scratch_shapes=scratch,
        ),
        out_shape=[jax.ShapeDtypeStruct((rows, antennas), jnp.bfloat16) for _ in others],
        cost_estimate=LITTLE,
        name="messages_for",
    )(table, *[beam] * len(others), *smalls)


def slice_kernel(count, tab_ref, *refs):
    for source, target in zip(refs[:count], refs[count:]):
        target[...] = source[...]


def slices_for(array, axis, size, starts, table):
    lead = axis > 0
    shape = array.shape[:axis] + (size,) + array.shape[axis + 1 :]
    block = (1,) + shape[1:] if lead else shape
    rest = (0,) * (array.ndim - axis - 1)
    return pl.pallas_call(
        functools.partial(slice_kernel, len(starts)),
        grid_spec=pltpu.PrefetchScalarGridSpec(
            num_scalar_prefetch=1,
            grid=(shape[0] if lead else 1,),
            in_specs=[
                pl.BlockSpec(
                    block,
                    lambda n, tab, start=start, shift=shift: (
                        *((n,) if lead else ()),
                        tab[start] // size + shift,
                        *rest,
                    ),
                )
                for start, shift in starts
            ],
            out_specs=[
                pl.BlockSpec(block, lambda n, tab: (n,) + (0,) * (array.ndim - 1)) for _ in starts
            ],
        ),
        out_shape=[jax.ShapeDtypeStruct(shape, array.dtype) for _ in starts],
        cost_estimate=LITTLE,
        name="slices_for",
    )(table, *[array] * len(starts))


KIND, ONE, TWO, ONE_AT, TWO_AT = 0, 1, 2, 3, 5
COLUMNS = 7


def unit_kernel(index, offset, pieces, bright_at, homes, tab_ref, *refs):
    arrays = []
    for entries in pieces:
        found = []
        for count, start, number in entries:
            parts = (refs[0].at[0], refs[0].at[1]) if count == 1 else refs[:2]
            found.append((parts, start, number))
            refs = refs[count:]
        arrays.append(found)
    vis_refs, (keep_one_ref, keep_two_ref) = refs[:homes], refs[homes : homes + 2]
    refs = refs[homes + 2 :]
    columns_ref = None
    if bright_at is None:
        columns_ref, refs = refs[0], refs[1:]
    out_refs, grad_ref = refs[:homes], refs[homes]
    refs = refs[homes + 1 :]
    if bright_at is not None:
        columns_ref, refs = refs[0], refs[1:]
    total_ref, one_ref, two_ref, vis_ref = refs
    step = pl.program_id(0)
    slot = tab_ref[0] + index
    sources, span = one_ref.shape[1:]

    def entry(column):
        return tab_ref[offset + step * COLUMNS + column]

    def load(target, at):
        for n, found in enumerate(arrays):

            @pl.when(entry(at) == n)
            def _(found=found):
                place = entry(at + 1)
                for parts, start, number in found:
                    rows = pl.ds(pl.multiple_of(place * number, number), number)
                    for part in (0, 1):
                        target[part, pl.ds(start, number)] = parts[part][rows]

    if bright_at is not None:

        @pl.when(step == 0)
        def _():
            for parts, start, number in arrays[0]:
                lines = parts[0][pl.ds(bright_at * number, BRIGHT_ROWS)].astype(jnp.float32)
                lanes = lax.broadcasted_iota(jnp.int32, (number, span), 1)
                rows = lax.broadcasted_iota(jnp.int32, (number, span), 0)
                for n in range(columns_ref.shape[0]):
                    line = jnp.where(lanes == rows, lines[n : n + 1, :], 0.0)
                    column = jnp.sum(line, axis=1, keepdims=True)
                    columns_ref[n, pl.ds(start, number)] = jnp.broadcast_to(column, (number, 128))

    def dot(a, b):
        return lax.dot_general(a, b, (((1,), (0,)), ((), ())), preferred_element_type=jnp.float32)

    def scaled_of(re, im):
        column = jnp.concatenate([columns_ref[index].astype(jnp.bfloat16)] * (span // 128), 1)
        return re * column, im * column

    def outer(a, b):
        row_ids = lax.broadcasted_iota(jnp.int32, a.shape, 0)
        a = jnp.where(row_ids == slot, a, 0.0)
        return lax.dot_general(a, b, (((0,), (0,)), ((), ())), preferred_element_type=jnp.float32)

    def cross(a_re, a_im, b_re, b_im):
        lhs = jnp.concatenate([a_re, a_im], 0).T
        rhs = jnp.concatenate(
            [jnp.concatenate([b_re, -b_im], 1), jnp.concatenate([b_im, b_re], 1)], 0
        )
        both = dot(lhs, rhs)
        return both[:, :span], both[:, span:]

    def pull(re, im, res_re, res_im, sign):
        lhs = jnp.concatenate([re, im], 1)
        rhs = jnp.concatenate(
            [
                jnp.concatenate([res_re, res_im], 1),
                jnp.concatenate([res_im, -res_re] if sign == 1 else [-res_im, res_re], 1),
            ],
            0,
        )
        both = dot(lhs, rhs)
        return both[:, :span], both[:, span:]

    def add_grad(value):
        folded = value[:, :128]
        for start in range(128, span, 128):
            folded = folded + value[:, start : start + 128]
        total_ref[...] += folded

    each = pl.num_programs(0) // homes

    def put(res_re, res_im):
        for home, out_ref in enumerate(out_refs):

            @pl.when(step // each == home)
            def _(out_ref=out_ref):
                out_ref[0, 0] = res_re
                out_ref[0, 1] = res_im

    @pl.when(step == 0)
    def _():
        total_ref[...] = jnp.zeros_like(total_ref)

    load(one_ref, ONE_AT)
    load(two_ref, TWO_AT)
    for home, home_ref in enumerate(vis_refs):

        @pl.when(step // each == home)
        def _(home_ref=home_ref):
            vis_ref[...] = home_ref[0, 0]

    @pl.when(entry(KIND) == 0)
    def _():
        one_re, one_im, two_re, two_im = one_ref[0], one_ref[1], two_ref[0], two_ref[1]
        pred_re, pred_im = cross(*scaled_of(one_re, one_im), two_re, two_im)
        weights = outer(keep_one_ref[...], keep_two_ref[...])
        res_re = (weights * (vis_ref[0].astype(jnp.float32) - pred_re)).astype(jnp.bfloat16)
        res_im = (weights * (vis_ref[1].astype(jnp.float32) - pred_im)).astype(jnp.bfloat16)
        put(res_re, res_im)
        sum_re, sum_im = pull(one_re, one_im, res_re, res_im, 1)
        add_grad(sum_re * two_re.astype(jnp.float32) - sum_im * two_im.astype(jnp.float32))

    @pl.when(entry(KIND) == 1)
    def _():
        one_re, one_im, two_re, two_im = one_ref[0], one_ref[1], two_ref[0], two_ref[1]
        row_ids = lax.broadcasted_iota(jnp.int32, (span, span), 0)
        col_ids = lax.broadcasted_iota(jnp.int32, (span, span), 1)
        upper = row_ids < col_ids
        lower = row_ids > col_ids
        first_re, first_im = cross(*scaled_of(one_re, one_im), one_re, one_im)
        second_re, second_im = cross(two_re, two_im, *scaled_of(two_re, two_im))
        keep_one = keep_one_ref[...]
        keep_two = keep_two_ref[...]
        weights = jnp.where(upper, outer(keep_one, keep_one), 0.0) + jnp.where(
            lower, outer(keep_two, keep_two), 0.0
        )
        vis_re = vis_ref[0].astype(jnp.float32)
        vis_im = vis_ref[1].astype(jnp.float32)
        res_re = (weights * (vis_re - jnp.where(upper, first_re, second_re))).astype(jnp.bfloat16)
        res_im = (weights * (vis_im - jnp.where(upper, first_im, -second_im))).astype(jnp.bfloat16)
        put(res_re, res_im)
        none = jnp.zeros_like(res_re)
        sum_re, sum_im = pull(
            one_re, one_im, jnp.where(upper, res_re, none), jnp.where(upper, res_im, none), 1
        )
        add_grad(sum_re * one_re.astype(jnp.float32) - sum_im * one_im.astype(jnp.float32))
        sum_re, sum_im = pull(
            two_re, two_im, jnp.where(lower, res_re, none), jnp.where(lower, res_im, none), -1
        )
        add_grad(sum_re * two_re.astype(jnp.float32) + sum_im * two_im.astype(jnp.float32))

    @pl.when(step == pl.num_programs(0) - 1)
    def _():
        grad_ref[...] = jnp.sum(total_ref[...].T, axis=0, keepdims=True)


def unit_work(index, offset, table, pieces, vis, keep, bright):
    units_dev, _, _, span, _ = vis[0].shape
    slots = keep.shape[0]
    sources = sum(number for _, _, number in pieces[0])
    count = units_dev * len(vis)
    whole = pl.BlockSpec(memory_space=pltpu.VMEM)
    arrays = [array for piece in pieces for entry, _, _ in piece for array in entry]

    def at(tab, step, column):
        return tab[offset + step * COLUMNS + column]

    def unit(step, home):
        return jnp.clip(step - home * units_dev, 0, units_dev - 1)

    in_specs = [whole] * len(arrays)
    for home, array in enumerate(vis):
        if array.shape[1] == slots:
            slot = lambda tab: tab[0] + index
        else:
            slot = lambda tab: index
        in_specs.append(
            pl.BlockSpec(
                (1, 1, 2, span, span),
                lambda u, tab, home=home, slot=slot: (unit(u, home), slot(tab), 0, 0, 0),
            )
        )
    in_specs += [
        pl.BlockSpec((slots, span), lambda u, tab: (0, at(tab, u, ONE))),
        pl.BlockSpec((slots, span), lambda u, tab: (0, at(tab, u, TWO))),
    ]
    operands = [table, *arrays, *vis, keep, keep]
    bright_at = None
    if isinstance(bright, int):
        first = pieces[0][0]
        bright_at = (first[0][0].shape[1] - BRIGHT_ROWS) // first[2]
    else:
        in_specs.append(whole)
        operands.append(bright)
    out_specs = [
        pl.BlockSpec((1, 2, span, span), lambda u, tab, home=home: (unit(u, home), 0, 0, 0))
        for home in range(len(vis))
    ]
    out_shapes = [jax.ShapeDtypeStruct((units_dev, 2, span, span), jnp.bfloat16) for _ in vis]
    out_specs.append(pl.BlockSpec((1, sources), lambda u, tab: (0, 0)))
    out_shapes.append(jax.ShapeDtypeStruct((1, sources), jnp.float32))
    if bright_at is not None:
        out_specs.append(pl.BlockSpec((bright, sources, 128), lambda u, tab: (0, 0, 0)))
        out_shapes.append(jax.ShapeDtypeStruct((bright, sources, 128), jnp.float32))
    kinds = [[(len(entry), start, number) for entry, start, number in piece] for piece in pieces]
    return pl.pallas_call(
        functools.partial(unit_kernel, index, offset, kinds, bright_at, len(vis)),
        grid_spec=pltpu.PrefetchScalarGridSpec(
            num_scalar_prefetch=1,
            grid=(count,),
            in_specs=in_specs,
            out_specs=out_specs,
            scratch_shapes=[
                pltpu.VMEM((sources, 128), jnp.float32),
                pltpu.VMEM((2, sources, span), jnp.bfloat16),
                pltpu.VMEM((2, sources, span), jnp.bfloat16),
                pltpu.VMEM((2, span, span), jnp.bfloat16),
            ],
        ),
        out_shape=out_shapes,
        compiler_params=pltpu.CompilerParams(vmem_limit_bytes=48 * 1024 * 1024),
        cost_estimate=LITTLE,
        name="unit_work",
    )(*operands)


def put_kernel(sources, tab_ref, *refs):
    out_ref = refs[-1]
    for step, (which, row) in enumerate(sources):

        @pl.when(pl.program_id(0) == step)
        def _(which=which, row=row):
            out_ref[0, 0] = refs[which][...] if row is None else refs[which][row]


def put_residuals(sources, arrays, offset, table, shape, residual):
    span = shape[-1]
    whole = pl.BlockSpec(memory_space=pltpu.VMEM)
    operands = [table, *arrays]
    in_specs = [whole] * len(arrays)
    aliases = {}
    if residual is not None:
        aliases = {len(operands): 0}
        operands.append(residual)
        in_specs.append(pl.BlockSpec(memory_space=pl.ANY))
    return pl.pallas_call(
        functools.partial(put_kernel, sources),
        grid_spec=pltpu.PrefetchScalarGridSpec(
            num_scalar_prefetch=1,
            grid=(len(sources),),
            in_specs=in_specs,
            out_specs=pl.BlockSpec(
                (1, 1, 2, span, span),
                lambda n, tab: (tab[offset + 2 * n], tab[offset + 2 * n + 1], 0, 0, 0),
            ),
        ),
        out_shape=jax.ShapeDtypeStruct(shape, jnp.bfloat16),
        input_output_aliases=aliases,
        compiler_params=pltpu.CompilerParams(vmem_limit_bytes=32 * 1024 * 1024),
        cost_estimate=LITTLE,
        name="put_residuals",
    )(*operands)


class Routes:
    def __init__(self, planes, width, units, share):
        count = planes * width
        blocks = int(units[:, :2].max()) + 1
        self.width = width
        self.units_dev = units_dev = units.shape[0] // count
        ring = [0] + list(range(1, planes, 2)) + list(range(planes - 2, 0, -2))

        def along(step):
            at = {plane: ring[(n + step) % planes] for n, plane in enumerate(ring)}
            return [(t, at[t // width] * width + t % width) for t in range(count)]

        self.onward = along(1)
        self.backward = along(-1)
        self.opposite = along(2)
        self.partner = [[(t, t ^ m) for t in range(count)] for m in range(width)]

        half = blocks // 2
        self.full = [list(range(blocks))]
        self.pieces = [list(range(half)), list(range(half, blocks))]

        def table_of(pieces, order):
            rows = np.zeros((count, len(order), units_dev, COLUMNS), np.int32)
            for t in range(count):
                for n, m in enumerate(order):
                    for k in range(units_dev):
                        one, two, kind = units[(t ^ m) * units_dev + k].tolist()
                        at = [
                            (p, piece.index(b))
                            for b in (one, two)
                            for p, piece in enumerate(pieces)
                            if b in piece
                        ]
                        rows[t, n, k] = [kind, one, two, *at[0], *at[1]]
            return rows

        def targets(index):
            rows = np.zeros((count, len(self.order), units_dev, 2), np.int32)
            for t in range(count):
                for n, m in enumerate(self.order):
                    for k in range(units_dev):
                        rows[t, n, k] = k, (t % width ^ m) * share + index
            return rows

        self.order = list(range(width // 2, width)) + list(range(width // 2 - 1, -1, -1))
        starts = np.array([[(t % width ^ m) * share for m in range(width)] for t in range(count)])
        parts = [starts, table_of(self.full, self.order), table_of(self.pieces, self.order)]
        parts += [targets(n) for n in range(share)]
        parts = [part.reshape(count, -1) for part in parts]
        ends = np.cumsum([part.shape[1] for part in parts]).tolist()
        self.table = np.concatenate(parts, 1).astype(np.int32)
        self.steps = ends[:2]
        self.targets = ends[2:]
        self.steps_per_home = units_dev * COLUMNS
        self.targets_per_home = units_dev * 2


def plain_program(visibility, beam, antenna_uvw, small, keep):
    units_dev, slots, _, span, _ = visibility.shape
    _, _, per_group, antennas = beam.shape
    blocks = antennas // span
    tile_index = lax.axis_index("tile")
    units = unit_table(blocks)
    none = np.zeros_like(units[:, 0])
    table = np.stack([units[:, 2], units[:, 0], units[:, 1], none, units[:, 0], none, units[:, 1]], 1)
    table = table.astype(np.int32).reshape(-1, units_dev * COLUMNS)
    table = np.pad(table, ((0, 0), (1, 0)))
    table = lax.dynamic_index_in_dim(jnp.asarray(table), tile_index, 0, keepdims=False)
    columns = None
    residuals, grads = [], []
    for slot in range(slots):
        (owned,) = build_factors(
            (slot, slots, per_group),
            table,
            beam,
            [],
            antenna_uvw,
            [small],
            [list(range(blocks))],
            span,
            0 if slot else BRIGHT_ROWS,
            small[0].shape[1],
        )
        everyone = lax.all_gather(owned, "tile", axis=0)
        rows = blocks * per_group
        if columns is None:
            bright = everyone[:, 0, rows : rows + slots, :per_group].astype(jnp.float32)
            bright = jnp.swapaxes(bright, 0, 1).reshape(slots, -1, 1)
            columns = jnp.broadcast_to(bright, bright.shape[:2] + (128,))
        factors = everyone[:, :, :rows].reshape(-1, 2, blocks, per_group, span)
        number = factors.shape[0] * per_group
        factors = factors.transpose(1, 2, 0, 3, 4).reshape(2, blocks * number, span)
        residual, grad = unit_work(
            slot, 1, table, [[((factors,), 0, number)]], [visibility], keep, columns
        )
        residuals.append(residual)
        grads.append(grad)
    summed = lax.psum_scatter(jnp.concatenate(grads, 0), "tile", scatter_dimension=1, tiled=True)
    return jnp.stack(residuals, 1), summed


OWN, OWN_NEAR, OWN_FAR, REST, REST_NEAR, REST_FAR = 0, 1, 3, 5, 6, 8
BEAM, SIDE_BEAMS, LATER_BEAMS, VIS, LATER = 10, 12, 15, 19, 23
PIECE_NEAR, PIECE_FAR = (24, 26), (28, 30)
WORK, HOME, PUT, LATER_WORK, LATER_HOME, PUT_NEAR, PUT_LAST = 32, 35, 38, 40, 43, 46, 47
SUM_PLANES, SUM_PLANE = 48, 51
GATES = {
    1: (0, 11),
    2: (0, 11),
    3: (0,),
    4: (0, 13),
    5: (0, 2, 13),
    6: (13,),
    7: (1, 2),
    14: (13,),
    16: (0, 2),
    17: (0, 1),
    18: (0,),
    19: (3, 4, 18),
    20: (3, 4, 6, 17),
    21: (3, 4, 13, 14, 16, 17),
    24: (6, 7, 16, 17, 21),
    25: (7, 9, 17, 21, 23),
    27: (8,),
    28: (22, 25),
    29: (25,),
    31: (27, 28, 37),
    33: (32,),
    35: (8, 9, 24, 25, 36),
    37: (24,),
    38: (25,),
    40: (24, 33, 36, 37),
    41: (28, 31, 40),
    44: (28, 30),
    45: (28, 32, 35),
    46: (40,),
    48: (35,),
    49: (44,),
    51: (33,),
    52: (38, 40, 44),
    53: (49,),
}


def plane_program(routes, visibility, beam, antenna_uvw, small, keep):
    units_dev, slots, _, span, _ = visibility.shape
    per_group = beam.shape[2]
    width = routes.width
    share = slots // width
    group = width * per_group
    tile_index = lax.axis_index("tile")
    mine = tile_index % width
    table = lax.dynamic_index_in_dim(jnp.asarray(routes.table), tile_index, 0, keepdims=False)
    done = {}

    def gated(step, value):
        earlier = [done[gate] for gate in GATES.get(step, ())]
        return lax.optimization_barrier((value, *earlier))[0] if earlier else value

    def send(step, value, pairs):
        done[step] = lax.ppermute(gated(step, value), "tile", pairs)
        return done[step]

    def near(step, piece):
        return [send(step, piece, routes.onward), send(step + 1, piece, routes.backward)]

    def far(step, sides):
        return [
            send(step, sides[0][0], routes.onward),
            send(step + 1, sides[1][1], routes.backward),
        ]

    def entries(piece, sides, halves, first, number):
        found = [(piece,), (sides[0],), (sides[1],), tuple(halves)]
        return [(arrays, n * group + first, number) for n, arrays in enumerate(found)]

    def build(step, index, own_beam, messages, smalls, pieces, bright_rows):
        built = build_factors(
            (index, share, per_group),
            gated(step, table),
            own_beam,
            messages,
            antenna_uvw,
            smalls,
            pieces,
            span,
            bright_rows,
            small[0].shape[1],
        )
        done[step] = built[0]
        return built

    core, *side = range(1, width)
    (message,) = messages_for(beam, 0, [core], small, gated(BEAM, table))
    message = send(BEAM + 1, message, routes.partner[core])
    (own,) = build(OWN, 0, beam, [message], [small, message], routes.full, BRIGHT_ROWS)
    own_sides = near(OWN_NEAR, own)
    messages = messages_for(beam, 0, side, small, gated(SIDE_BEAMS, table))
    messages = [
        send(SIDE_BEAMS + 1 + n, messages[n], routes.partner[m]) for n, m in enumerate(side)
    ]
    own_far = far(OWN_FAR, own_sides)
    (rest,) = build(REST, 0, None, messages, messages, routes.full, BRIGHT_ROWS)
    rest_sides = near(REST_NEAR, rest)

    later = messages_for(beam, 1, [core, *side], None, gated(LATER_BEAMS, table))
    later = [send(LATER_BEAMS + m, later[m - 1], routes.partner[m]) for m in (core, *side)]
    vis = slices_for(
        visibility, 1, share, [(m, 0) for m in (core, *side)], gated(VIS, table)
    )
    vis = [visibility] + [send(VIS + m, vis[m - 1], routes.partner[m]) for m in (core, *side)]
    later_pieces = build(
        LATER, 1, beam, later, [small, message, *messages], routes.pieces, 0
    )
    rest_far = far(REST_FAR, rest_sides)
    near_0 = near(PIECE_NEAR[0], later_pieces[0])
    near_1 = near(PIECE_NEAR[1], later_pieces[1])
    far_0 = far(PIECE_FAR[0], near_0)

    grads = []

    def work(index, step, home_step, ready, bright):
        arrived, total = [], None
        for n, homes in enumerate([routes.order[:1], routes.order[1:]]):
            made = unit_work(
                index,
                routes.steps[index] + len(arrived) * routes.steps_per_home,
                gated(step + n, table),
                ready,
                [vis[m] for m in homes],
                keep,
                bright,
            )
            results, grad = made[: len(homes)], made[len(homes)]
            if isinstance(bright, int):
                bright = made[-1]
            done[step + n] = grad
            total = grad if total is None else total + grad
            arrived += [
                send(home_step - 1 + m, part, routes.partner[m]) if m else part
                for m, part in zip(homes, results)
            ]
        grads.append(total)
        return arrived, bright

    def put(step, homes, arrays, index, residual):
        rows = [(n, k) for n in range(len(arrays)) for k in range(units_dev)]
        offset = routes.targets[index] + homes * routes.targets_per_home
        done[step] = put_residuals(
            rows, arrays, offset, gated(step, table), visibility.shape, residual
        )
        return done[step]

    number = group // 2
    pieces = entries(own, own_sides, own_far, 0, number)
    pieces += entries(rest, rest_sides, rest_far, number, number)
    arrived, columns = work(0, WORK, HOME, [pieces], share)
    far_1 = far(PIECE_FAR[1], near_1)
    residual = put(PUT, 0, arrived, 0, None)
    ready = [
        entries(piece, sides, halves, 0, group)
        for piece, sides, halves in zip(later_pieces, (near_0, near_1), (far_0, far_1))
    ]
    arrived, _ = work(1, LATER_WORK, LATER_HOME, ready, columns)

    partial = jnp.concatenate(grads, 0)
    parts = [partial[:, n * group : (n + 1) * group] for n in range(4)]
    plane_sum = (parts[0] + send(SUM_PLANES, parts[3], routes.opposite)) + (
        send(SUM_PLANES + 1, parts[1], routes.backward)
        + send(SUM_PLANES + 2, parts[2], routes.onward)
    )
    sums = [plane_sum[:, m * per_group : (m + 1) * per_group] for m in range(width)]
    sums = [sums[0]] + [
        send(SUM_PLANE - 1 + m, sums[m], routes.partner[m]) for m in (core, *side)
    ]
    sums = jnp.stack(sums, 0)
    ids = jnp.arange(width, dtype=jnp.int32)
    here = jnp.bitwise_xor(ids[:, None], mine) == ids[None, :]
    summed = jnp.sum(jnp.where(here[:, :, None, None], sums[None], 0.0), axis=1)
    summed = summed.reshape(slots, per_group)

    residual = put(PUT_NEAR, 2, arrived[2:], 1, residual)
    residual = put(PUT_LAST, 0, arrived[:2], 1, residual)
    return residual, summed


def per_device(
    visibility, station_beam, antenna_uvw, source_dirs, source_flux, visible_list, antenna_flags
):
    span = visibility.shape[4]
    antennas = station_beam.shape[3]
    small = (source_dirs, source_flux.astype(jnp.float32)[None], visible_list)
    keep = 1.0 - antenna_flags.astype(jnp.float32)
    arguments = (visibility, station_beam, antenna_uvw, small, keep)
    if lax.axis_size("tile") == 16:
        routes = Routes(4, 4, unit_table(antennas // span), visibility.shape[1] // 4)
        residual, summed = plane_program(routes, *arguments)
    else:
        residual, summed = plain_program(*arguments)
    return (residual, summed * (-1.0 / (8.0 * antennas)))


def solution(mesh):
    return jax.shard_map(
        per_device,
        mesh=mesh,
        in_specs=(
            P("tile", "grp", None, None, None),
            P("grp", None, "tile", None),
            P("grp", None, None),
            P(None, "tile"),
            P(("grp", "tile")),
            P(None, "tile"),
            P("grp", None),
        ),
        out_specs=(P("tile", "grp", None, None, None), P("grp", "tile")),
        check_vma=False,
    )
```

```python
import functools

import jax
import jax.numpy as jnp
import numpy as np
from jax import lax
from jax.experimental import pallas as pl
from jax.experimental.pallas import tpu as pltpu
from jax.sharding import PartitionSpec as P


def unit_table(block_count):
    first_list = []
    second_list = []
    diag_list = []
    for row_block in range(block_count):
        for col_block in range(row_block + 1, block_count):
            first_list.append(row_block)
            second_list.append(col_block)
            diag_list.append(0)
    for pair_index in range(block_count // 2):
        first_list.append(2 * pair_index)
        second_list.append(2 * pair_index + 1)
        diag_list.append(1)
    return np.stack([first_list, second_list, diag_list], 1).astype(np.int32)


def turn_polynomials():
    nodes = 0.125 + 0.125 * np.cos(np.pi * (np.arange(64) + 0.5) / 64)
    root = np.sqrt(nodes)
    fit = np.polynomial.Polynomial.fit
    sine = fit(nodes, np.sin(2 * np.pi * root) / root, 7, domain=[0, 0.25]).convert()
    cosine = fit(nodes, np.cos(2 * np.pi * root), 8, domain=[0, 0.25]).convert()
    return [float(c) for c in sine.coef], [float(c) for c in cosine.coef]


def horner(coefs, x):
    total = coefs[-1]
    for coef in coefs[-2::-1]:
        total = total * x + coef
    return total


def build_kernel(sets, slot_ids, pieces, bright_rows, width, tab_ref, *refs):
    refs, scratch_ref = refs[:-1], refs[-1]
    uvw_ref, outs = refs[-1 - len(pieces)], refs[-len(pieces) :]
    per_group = sets[0][0]
    span = outs[0].shape[2]
    count = len(sets) * per_group
    sin_coefs, cos_coefs = turn_polynomials()
    brights = []
    for part, (_, beam_at, small_at) in enumerate(sets):
        beam_ref = refs[beam_at]
        if beam_ref.shape[0] == 1:
            beam = [beam_ref.at[0, 0], beam_ref.at[0, 1]]
        else:
            beam = [beam_ref.at[pl.ds(n * per_group, per_group)] for n in (0, 1)]
        if refs[small_at].dtype == jnp.float32:
            small = small_rows(scratch_ref, *refs[small_at : small_at + 3])
        else:
            small = unsplit(refs[small_at], 2 * per_group, width)
        lanes = lax.broadcasted_iota(jnp.int32, (per_group, width), 1)
        rows = lax.broadcasted_iota(jnp.int32, (per_group, width), 0)

        def pick(chosen, row):
            return jnp.sum(jnp.where(chosen, small[row : row + 1, :], 0.0), axis=1, keepdims=True)

        def chosen_at(index):
            here = lax.broadcasted_iota(jnp.int32, small.shape, 0) == LIST_ROW + tab_ref[0] + index
            line = jnp.sum(jnp.where(here, small, 0.0), axis=0, keepdims=True)
            listed = jnp.sum(jnp.where(lanes == rows, line, 0.0), axis=1, keepdims=True)
            return listed.astype(jnp.int32) == lanes

        group = part * per_group
        if bright_rows:
            columns = lax.broadcasted_iota(jnp.int32, (per_group, span), 1)
            numbers = lax.broadcasted_iota(jnp.int32, (per_group, span), 0) + group
            for index in range(slot_ids[1]):
                flux = pick(chosen_at(index), 2)
                line = jnp.sum(jnp.where(columns == numbers, flux, 0.0), axis=0, keepdims=True)
                if part == 0:
                    brights.append(line)
                else:
                    brights[index] += line
        chosen = chosen_at(slot_ids[0])
        east = pick(chosen, 0)
        north = pick(chosen, 1)
        depth = jnp.sqrt(1.0 - east * east - north * north) - 1.0
        for out_ref, piece in zip(outs, pieces):
            for place, block in enumerate(piece):
                cols = pl.ds(block * span, span)
                delay = (
                    uvw_ref[0, 0:1, cols] * east
                    + uvw_ref[0, 1:2, cols] * north
                    + uvw_ref[0, 2:3, cols] * depth
                )
                turn = delay - jnp.floor(delay + 0.5)
                square = turn * turn
                sine = horner(sin_coefs, square) * turn
                cosine = horner(cos_coefs, square)
                real = beam[0][:, cols].astype(jnp.float32)
                imag = beam[1][:, cols].astype(jnp.float32)
                at = pl.ds(place * count + group, per_group)
                out_ref[0, at] = (real * cosine + imag * sine).astype(jnp.bfloat16)
                out_ref[1, at] = (imag * cosine - real * sine).astype(jnp.bfloat16)
    if bright_rows:
        padding = jnp.zeros((bright_rows - len(brights), span), jnp.float32)
        block = jnp.concatenate(brights + [padding], 0).astype(jnp.bfloat16)
        for part in (0, 1):
            outs[0][part, pl.ds(len(pieces[0]) * count, bright_rows)] = block


def small_rows(rows_ref, dirs_ref, flux_ref, list_ref):
    rows_ref[...] = jnp.zeros_like(rows_ref)
    rows_ref[0:2, 0 : dirs_ref.shape[1]] = dirs_ref[...]
    rows_ref[2:3, 0 : flux_ref.shape[1]] = flux_ref[...]
    slots, count = list_ref.shape
    rows_ref[LIST_ROW : LIST_ROW + slots, 0:count] = list_ref[...].astype(jnp.float32)
    return rows_ref[...]


LIST_ROW = 8
SMALL_ROWS = 16


def unsplit(message_ref, start, width):
    rows = pl.ds(start, SMALL_ROWS)
    terms = [message_ref[rows, pl.ds(n * width, width)].astype(jnp.float32) for n in range(3)]
    return (terms[0] + terms[1]) + terms[2]


BRIGHT_ROWS = 16


def full(array):
    return pl.BlockSpec(array.shape, lambda *_: (0,) * array.ndim)


def build_factors(
    slot_ids, table, beam, messages, antenna_uvw, smalls, pieces, span, bright_rows, small_width
):
    slots, _, antennas = antenna_uvw.shape
    per_group = slot_ids[2]
    index = slot_ids[0]
    whole = pl.BlockSpec(memory_space=pltpu.VMEM)
    operands, in_specs, sets = [], [], []
    if beam is not None:
        operands.append(beam)
        in_specs.append(
            pl.BlockSpec((1, 2, per_group, antennas), lambda n, tab: (tab[0] + index, 0, 0, 0))
        )
    operands += messages
    beams = len(operands)
    for n, small in enumerate(smalls):
        at = next((k for k, known in enumerate(operands) if known is small), len(operands))
        if at == len(operands):
            operands += small if isinstance(small, tuple) else [small]
        sets.append((per_group, n, at))
    in_specs += [full(array) for array in operands[len(in_specs) :]]
    in_specs.append(pl.BlockSpec((1, 3, antennas), lambda n, tab: (tab[0] + index, 0, 0)))
    count = beams * per_group
    shapes = [
        (2, len(piece) * count + (0 if n else bright_rows), span) for n, piece in enumerate(pieces)
    ]
    return pl.pallas_call(
        functools.partial(build_kernel, sets, slot_ids, pieces, bright_rows, small_width),
        grid_spec=pltpu.PrefetchScalarGridSpec(
            num_scalar_prefetch=1,
            grid=(1,),
            in_specs=in_specs,
            out_specs=[whole] * len(pieces),
            scratch_shapes=[pltpu.VMEM((SMALL_ROWS, small_width), jnp.float32)],
        ),
        out_shape=[jax.ShapeDtypeStruct(shape, jnp.bfloat16) for shape in shapes],
        compiler_params=pltpu.CompilerParams(vmem_limit_bytes=40 * 1024 * 1024),
        cost_estimate=LITTLE,
        name="build_factors",
    )(table, *operands, antenna_uvw)


LITTLE = pl.CostEstimate(flops=1, bytes_accessed=1, transcendentals=0)


def message_kernel(count, with_small, tab_ref, *refs):
    beams, refs = refs[:count], refs[count:]
    if with_small:
        smalls, outs, scratch_ref = refs[:3], refs[3:-1], refs[-1]
        terms = []
        rest = small_rows(scratch_ref, *smalls)
        width = rest.shape[1]
        for _ in range(3):
            terms.append(rest.astype(jnp.bfloat16))
            rest = rest - terms[-1].astype(jnp.float32)
    else:
        outs = refs
    for beam_ref, out_ref in zip(beams, outs):
        per_group = beam_ref.shape[2]
        for part in (0, 1):
            out_ref[pl.ds(part * per_group, per_group)] = beam_ref[0, part]
        if with_small:
            rows = pl.ds(2 * per_group, SMALL_ROWS)
            out_ref[rows] = jnp.zeros((SMALL_ROWS, out_ref.shape[1]), jnp.bfloat16)
            for n, term in enumerate(terms):
                out_ref[rows, pl.ds(n * width, width)] = term


def messages_for(beam, index, others, small, table):
    _, _, per_group, antennas = beam.shape
    smalls = small or ()
    rows = 2 * per_group + (SMALL_ROWS if smalls else 0)
    whole = pl.BlockSpec(memory_space=pltpu.VMEM)
    scratch = []
    if smalls:
        scratch.append(pltpu.VMEM((SMALL_ROWS, smalls[0].shape[1]), jnp.float32))
    return pl.pallas_call(
        functools.partial(message_kernel, len(others), bool(smalls)),
        grid_spec=pltpu.PrefetchScalarGridSpec(
            num_scalar_prefetch=1,
            grid=(1,),
            in_specs=[
                pl.BlockSpec(
                    (1, 2, per_group, antennas), lambda n, tab, m=m: (tab[m] + index, 0, 0, 0)
                )
                for m in others
            ]
            + [full(array) for array in smalls],
            out_specs=[whole for _ in others],
            scratch_shapes=scratch,
        ),
        out_shape=[jax.ShapeDtypeStruct((rows, antennas), jnp.bfloat16) for _ in others],
        cost_estimate=LITTLE,
        name="messages_for",
    )(table, *[beam] * len(others), *smalls)


def slice_kernel(count, tab_ref, *refs):
    for source, target in zip(refs[:count], refs[count:]):
        target[...] = source[...]


def slices_for(array, axis, size, starts, table):
    lead = axis > 0
    shape = array.shape[:axis] + (size,) + array.shape[axis + 1 :]
    block = (1,) + shape[1:] if lead else shape
    rest = (0,) * (array.ndim - axis - 1)
    return pl.pallas_call(
        functools.partial(slice_kernel, len(starts)),
        grid_spec=pltpu.PrefetchScalarGridSpec(
            num_scalar_prefetch=1,
            grid=(shape[0] if lead else 1,),
            in_specs=[
                pl.BlockSpec(
                    block,
                    lambda n, tab, start=start, shift=shift: (
                        *((n,) if lead else ()),
                        tab[start] // size + shift,
                        *rest,
                    ),
                )
                for start, shift in starts
            ],
            out_specs=[
                pl.BlockSpec(block, lambda n, tab: (n,) + (0,) * (array.ndim - 1)) for _ in starts
            ],
        ),
        out_shape=[jax.ShapeDtypeStruct(shape, array.dtype) for _ in starts],
        cost_estimate=LITTLE,
        name="slices_for",
    )(table, *[array] * len(starts))


KIND, ONE, TWO, ONE_AT, TWO_AT = 0, 1, 2, 3, 5
COLUMNS = 7


def unit_kernel(index, offset, pieces, bright_at, homes, tab_ref, *refs):
    arrays = []
    for entries in pieces:
        found = []
        for count, start, number in entries:
            parts = (refs[0].at[0], refs[0].at[1]) if count == 1 else refs[:2]
            found.append((parts, start, number))
            refs = refs[count:]
        arrays.append(found)
    vis_refs, (keep_one_ref, keep_two_ref) = refs[:homes], refs[homes : homes + 2]
    refs = refs[homes + 2 :]
    columns_ref = None
    if bright_at is None:
        columns_ref, refs = refs[0], refs[1:]
    out_refs, grad_ref = refs[:homes], refs[homes]
    refs = refs[homes + 1 :]
    if bright_at is not None:
        columns_ref, refs = refs[0], refs[1:]
    total_ref, one_ref, two_ref, vis_ref = refs
    step = pl.program_id(0)
    slot = tab_ref[0] + index
    sources, span = one_ref.shape[1:]

    def entry(column):
        return tab_ref[offset + step * COLUMNS + column]

    def load(target, at):
        for n, found in enumerate(arrays):

            @pl.when(entry(at) == n)
            def _(found=found):
                place = entry(at + 1)
                for parts, start, number in found:
                    rows = pl.ds(pl.multiple_of(place * number, number), number)
                    for part in (0, 1):
                        target[part, pl.ds(start, number)] = parts[part][rows]

    if bright_at is not None:

        @pl.when(step == 0)
        def _():
            for parts, start, number in arrays[0]:
                lines = parts[0][pl.ds(bright_at * number, BRIGHT_ROWS)].astype(jnp.float32)
                lanes = lax.broadcasted_iota(jnp.int32, (number, span), 1)
                rows = lax.broadcasted_iota(jnp.int32, (number, span), 0)
                for n in range(columns_ref.shape[0]):
                    line = jnp.where(lanes == rows, lines[n : n + 1, :], 0.0)
                    column = jnp.sum(line, axis=1, keepdims=True)
                    columns_ref[n, pl.ds(start, number)] = jnp.broadcast_to(column, (number, 128))

    def dot(a, b):
        return lax.dot_general(a, b, (((1,), (0,)), ((), ())), preferred_element_type=jnp.float32)

    def scaled_of(re, im):
        column = jnp.concatenate([columns_ref[index].astype(jnp.bfloat16)] * (span // 128), 1)
        return re * column, im * column

    def outer(a, b):
        row_ids = lax.broadcasted_iota(jnp.int32, a.shape, 0)
        a = jnp.where(row_ids == slot, a, 0.0)
        return lax.dot_general(a, b, (((0,), (0,)), ((), ())), preferred_element_type=jnp.float32)

    def cross(a_re, a_im, b_re, b_im):
        lhs = jnp.concatenate([a_re, a_im], 0).T
        rhs = jnp.concatenate(
            [jnp.concatenate([b_re, -b_im], 1), jnp.concatenate([b_im, b_re], 1)], 0
        )
        both = dot(lhs, rhs)
        return both[:, :span], both[:, span:]

    def pull(re, im, res_re, res_im, sign):
        lhs = jnp.concatenate([re, im], 1)
        rhs = jnp.concatenate(
            [
                jnp.concatenate([res_re, res_im], 1),
                jnp.concatenate([res_im, -res_re] if sign == 1 else [-res_im, res_re], 1),
            ],
            0,
        )
        both = dot(lhs, rhs)
        return both[:, :span], both[:, span:]

    def add_grad(value):
        folded = value[:, :128]
        for start in range(128, span, 128):
            folded = folded + value[:, start : start + 128]
        total_ref[...] += folded

    each = pl.num_programs(0) // homes

    def put(res_re, res_im):
        for home, out_ref in enumerate(out_refs):

            @pl.when(step // each == home)
            def _(out_ref=out_ref):
                out_ref[0, 0] = res_re
                out_ref[0, 1] = res_im

    @pl.when(step == 0)
    def _():
        total_ref[...] = jnp.zeros_like(total_ref)

    load(one_ref, ONE_AT)
    load(two_ref, TWO_AT)
    for home, home_ref in enumerate(vis_refs):

        @pl.when(step // each == home)
        def _(home_ref=home_ref):
            vis_ref[...] = home_ref[0, 0]

    @pl.when(entry(KIND) == 0)
    def _():
        one_re, one_im, two_re, two_im = one_ref[0], one_ref[1], two_ref[0], two_ref[1]
        pred_re, pred_im = cross(*scaled_of(one_re, one_im), two_re, two_im)
        weights = outer(keep_one_ref[...], keep_two_ref[...])
        res_re = (weights * (vis_ref[0].astype(jnp.float32) - pred_re)).astype(jnp.bfloat16)
        res_im = (weights * (vis_ref[1].astype(jnp.float32) - pred_im)).astype(jnp.bfloat16)
        put(res_re, res_im)
        sum_re, sum_im = pull(one_re, one_im, res_re, res_im, 1)
        add_grad(sum_re * two_re.astype(jnp.float32) - sum_im * two_im.astype(jnp.float32))

    @pl.when(entry(KIND) == 1)
    def _():
        one_re, one_im, two_re, two_im = one_ref[0], one_ref[1], two_ref[0], two_ref[1]
        row_ids = lax.broadcasted_iota(jnp.int32, (span, span), 0)
        col_ids = lax.broadcasted_iota(jnp.int32, (span, span), 1)
        upper = row_ids < col_ids
        lower = row_ids > col_ids
        first_re, first_im = cross(*scaled_of(one_re, one_im), one_re, one_im)
        second_re, second_im = cross(two_re, two_im, *scaled_of(two_re, two_im))
        keep_one = keep_one_ref[...]
        keep_two = keep_two_ref[...]
        weights = jnp.where(upper, outer(keep_one, keep_one), 0.0) + jnp.where(
            lower, outer(keep_two, keep_two), 0.0
        )
        vis_re = vis_ref[0].astype(jnp.float32)
        vis_im = vis_ref[1].astype(jnp.float32)
        res_re = (weights * (vis_re - jnp.where(upper, first_re, second_re))).astype(jnp.bfloat16)
        res_im = (weights * (vis_im - jnp.where(upper, first_im, -second_im))).astype(jnp.bfloat16)
        put(res_re, res_im)
        none = jnp.zeros_like(res_re)
        sum_re, sum_im = pull(
            one_re, one_im, jnp.where(upper, res_re, none), jnp.where(upper, res_im, none), 1
        )
        add_grad(sum_re * one_re.astype(jnp.float32) - sum_im * one_im.astype(jnp.float32))
        sum_re, sum_im = pull(
            two_re, two_im, jnp.where(lower, res_re, none), jnp.where(lower, res_im, none), -1
        )
        add_grad(sum_re * two_re.astype(jnp.float32) + sum_im * two_im.astype(jnp.float32))

    @pl.when(step == pl.num_programs(0) - 1)
    def _():
        grad_ref[...] = jnp.sum(total_ref[...].T, axis=0, keepdims=True)


def unit_work(index, offset, table, pieces, vis, keep, bright):
    units_dev, _, _, span, _ = vis[0].shape
    slots = keep.shape[0]
    sources = sum(number for _, _, number in pieces[0])
    count = units_dev * len(vis)
    arrays = [array for piece in pieces for entry, _, _ in piece for array in entry]

    def at(tab, step, column):
        return tab[offset + step * COLUMNS + column]

    def unit(step, home):
        return jnp.clip(step - home * units_dev, 0, units_dev - 1)

    in_specs = [full(array) for array in arrays]
    for home, array in enumerate(vis):
        if array.shape[1] == slots:
            slot = lambda tab: tab[0] + index
        else:
            slot = lambda tab: index
        in_specs.append(
            pl.BlockSpec(
                (1, 1, 2, span, span),
                lambda u, tab, home=home, slot=slot: (unit(u, home), slot(tab), 0, 0, 0),
            )
        )
    in_specs += [
        pl.BlockSpec((slots, span), lambda u, tab: (0, at(tab, u, ONE))),
        pl.BlockSpec((slots, span), lambda u, tab: (0, at(tab, u, TWO))),
    ]
    operands = [table, *arrays, *vis, keep, keep]
    bright_at = None
    if isinstance(bright, int):
        first = pieces[0][0]
        bright_at = (first[0][0].shape[1] - BRIGHT_ROWS) // first[2]
    else:
        in_specs.append(full(bright))
        operands.append(bright)
    out_specs = [
        pl.BlockSpec((1, 2, span, span), lambda u, tab, home=home: (unit(u, home), 0, 0, 0))
        for home in range(len(vis))
    ]
    out_shapes = [jax.ShapeDtypeStruct((units_dev, 2, span, span), jnp.bfloat16) for _ in vis]
    out_specs.append(pl.BlockSpec((1, sources), lambda u, tab: (0, 0)))
    out_shapes.append(jax.ShapeDtypeStruct((1, sources), jnp.float32))
    if bright_at is not None:
        out_specs.append(pl.BlockSpec((bright, sources, 128), lambda u, tab: (0, 0, 0)))
        out_shapes.append(jax.ShapeDtypeStruct((bright, sources, 128), jnp.float32))
    kinds = [[(len(entry), start, number) for entry, start, number in piece] for piece in pieces]
    return pl.pallas_call(
        functools.partial(unit_kernel, index, offset, kinds, bright_at, len(vis)),
        grid_spec=pltpu.PrefetchScalarGridSpec(
            num_scalar_prefetch=1,
            grid=(count,),
            in_specs=in_specs,
            out_specs=out_specs,
            scratch_shapes=[
                pltpu.VMEM((sources, 128), jnp.float32),
                pltpu.VMEM((2, sources, span), jnp.bfloat16),
                pltpu.VMEM((2, sources, span), jnp.bfloat16),
                pltpu.VMEM((2, span, span), jnp.bfloat16),
            ],
        ),
        out_shape=out_shapes,
        compiler_params=pltpu.CompilerParams(vmem_limit_bytes=48 * 1024 * 1024),
        cost_estimate=LITTLE,
        name="unit_work",
    )(*operands)


def put_kernel(sources, tab_ref, *refs):
    out_ref = refs[-1]
    for step, (which, row) in enumerate(sources):

        @pl.when(pl.program_id(0) == step)
        def _(which=which, row=row):
            out_ref[0, 0] = refs[which][...] if row is None else refs[which][row]


def put_residuals(sources, arrays, offset, table, shape, residual):
    span = shape[-1]
    operands = [table, *arrays]
    in_specs = [full(array) for array in arrays]
    aliases = {}
    if residual is not None:
        aliases = {len(operands): 0}
        operands.append(residual)
        in_specs.append(pl.BlockSpec(memory_space=pl.ANY))
    return pl.pallas_call(
        functools.partial(put_kernel, sources),
        grid_spec=pltpu.PrefetchScalarGridSpec(
            num_scalar_prefetch=1,
            grid=(len(sources),),
            in_specs=in_specs,
            out_specs=pl.BlockSpec(
                (1, 1, 2, span, span),
                lambda n, tab: (tab[offset + 2 * n], tab[offset + 2 * n + 1], 0, 0, 0),
            ),
        ),
        out_shape=jax.ShapeDtypeStruct(shape, jnp.bfloat16),
        input_output_aliases=aliases,
        compiler_params=pltpu.CompilerParams(vmem_limit_bytes=32 * 1024 * 1024),
        cost_estimate=LITTLE,
        name="put_residuals",
    )(*operands)


class Routes:
    def __init__(self, planes, width, units, share):
        count = planes * width
        blocks = int(units[:, :2].max()) + 1
        self.width = width
        self.units_dev = units_dev = units.shape[0] // count
        ring = [0] + list(range(1, planes, 2)) + list(range(planes - 2, 0, -2))

        def along(step):
            at = {plane: ring[(n + step) % planes] for n, plane in enumerate(ring)}
            return [(t, at[t // width] * width + t % width) for t in range(count)]

        self.onward = along(1)
        self.backward = along(-1)
        self.opposite = along(2)
        self.partner = [[(t, t ^ m) for t in range(count)] for m in range(width)]

        half = blocks // 2
        self.full = [list(range(blocks))]
        self.pieces = [list(range(half)), list(range(half, blocks))]

        def table_of(pieces, order):
            rows = np.zeros((count, len(order), units_dev, COLUMNS), np.int32)
            for t in range(count):
                for n, m in enumerate(order):
                    for k in range(units_dev):
                        one, two, kind = units[(t ^ m) * units_dev + k].tolist()
                        at = [
                            (p, piece.index(b))
                            for b in (one, two)
                            for p, piece in enumerate(pieces)
                            if b in piece
                        ]
                        rows[t, n, k] = [kind, one, two, *at[0], *at[1]]
            return rows

        def targets(index):
            rows = np.zeros((count, len(self.order), units_dev, 2), np.int32)
            for t in range(count):
                for n, m in enumerate(self.order):
                    for k in range(units_dev):
                        rows[t, n, k] = k, (t % width ^ m) * share + index
            return rows

        self.order = list(range(width // 2, width)) + list(range(width // 2 - 1, -1, -1))
        starts = np.array([[(t % width ^ m) * share for m in range(width)] for t in range(count)])
        parts = [starts, table_of(self.full, self.order), table_of(self.pieces, self.order)]
        parts += [targets(n) for n in range(share)]
        parts = [part.reshape(count, -1) for part in parts]
        ends = np.cumsum([part.shape[1] for part in parts]).tolist()
        self.table = np.concatenate(parts, 1).astype(np.int32)
        self.steps = ends[:2]
        self.targets = ends[2:]
        self.steps_per_home = units_dev * COLUMNS
        self.targets_per_home = units_dev * 2


def plain_program(visibility, beam, antenna_uvw, small, keep):
    units_dev, slots, _, span, _ = visibility.shape
    _, _, per_group, antennas = beam.shape
    blocks = antennas // span
    tile_index = lax.axis_index("tile")
    units = unit_table(blocks)
    none = np.zeros_like(units[:, 0])
    table = np.stack([units[:, 2], units[:, 0], units[:, 1], none, units[:, 0], none, units[:, 1]], 1)
    table = table.astype(np.int32).reshape(-1, units_dev * COLUMNS)
    table = np.pad(table, ((0, 0), (1, 0)))
    table = lax.dynamic_index_in_dim(jnp.asarray(table), tile_index, 0, keepdims=False)
    columns = None
    residuals, grads = [], []
    for slot in range(slots):
        (owned,) = build_factors(
            (slot, slots, per_group),
            table,
            beam,
            [],
            antenna_uvw,
            [small],
            [list(range(blocks))],
            span,
            0 if slot else BRIGHT_ROWS,
            small[0].shape[1],
        )
        everyone = lax.all_gather(owned, "tile", axis=0)
        rows = blocks * per_group
        if columns is None:
            bright = everyone[:, 0, rows : rows + slots, :per_group].astype(jnp.float32)
            bright = jnp.swapaxes(bright, 0, 1).reshape(slots, -1, 1)
            columns = jnp.broadcast_to(bright, bright.shape[:2] + (128,))
        factors = everyone[:, :, :rows].reshape(-1, 2, blocks, per_group, span)
        number = factors.shape[0] * per_group
        factors = factors.transpose(1, 2, 0, 3, 4).reshape(2, blocks * number, span)
        residual, grad = unit_work(
            slot, 1, table, [[((factors,), 0, number)]], [visibility], keep, columns
        )
        residuals.append(residual)
        grads.append(grad)
    summed = lax.psum_scatter(jnp.concatenate(grads, 0), "tile", scatter_dimension=1, tiled=True)
    return jnp.stack(residuals, 1), summed


OWN, OWN_NEAR, OWN_FAR, REST, REST_NEAR, REST_FAR = 0, 1, 3, 5, 6, 8
BEAM, SIDE_BEAMS, LATER_BEAMS, VIS, LATER = 10, 12, 15, 19, 23
PIECE_NEAR, PIECE_FAR = (24, 26), (28, 30)
WORK, HOME, PUT, LATER_WORK, LATER_HOME, PUT_NEAR, PUT_LAST = 32, 35, 38, 40, 43, 46, 47
SUM_PLANES, SUM_PLANE = 48, 51
GATES = {
    3: (0, 1),
    5: (0, 2),
    6: (1, 11),
    7: (1, 2),
    14: (11, 13),
    17: (1,),
    19: (2, 18),
    20: (3, 4, 7, 16, 17),
    21: (3, 4, 5, 13, 14, 16, 17),
    23: (17, 4),
    24: (9, 17),
    25: (9, 23, 6, 17),
    26: (9,),
    27: (8,),
    28: (22,),
    31: (25, 26, 27, 37),
    33: (32, 25, 23),
    35: (8, 9, 22, 24, 25, 26, 28, 29),
    40: (33, 36, 37, 28, 29, 30, 31),
    49: (44,),
    53: (35,),
    46: (30, 31),
    37: (32, 9),
    38: (25,),
    30: (26,),
    43: (32,),
    44: (26, 27, 30, 31),
    36: (8, 9),
    4: (0,),
    16: (0,),
    13: (0,),
    41: (40,),
}


def plane_program(routes, visibility, beam, antenna_uvw, small, keep):
    units_dev, slots, _, span, _ = visibility.shape
    per_group = beam.shape[2]
    width = routes.width
    share = slots // width
    group = width * per_group
    tile_index = lax.axis_index("tile")
    mine = tile_index % width
    table = lax.dynamic_index_in_dim(jnp.asarray(routes.table), tile_index, 0, keepdims=False)
    done = {}

    def gated(step, value):
        earlier = [done[gate] for gate in GATES.get(step, ())]
        return lax.optimization_barrier((value, *earlier))[0] if earlier else value

    def send(step, value, pairs):
        done[step] = lax.ppermute(gated(step, value), "tile", pairs)
        return done[step]

    def near(step, piece):
        return [send(step, piece, routes.onward), send(step + 1, piece, routes.backward)]

    def far(step, sides):
        return [
            send(step, sides[0][0], routes.onward),
            send(step + 1, sides[1][1], routes.backward),
        ]

    def entries(piece, sides, halves, first, number):
        found = [(piece,), (sides[0],), (sides[1],), tuple(halves)]
        return [(arrays, n * group + first, number) for n, arrays in enumerate(found)]

    def build(step, index, own_beam, messages, smalls, pieces, bright_rows):
        built = build_factors(
            (index, share, per_group),
            gated(step, table),
            own_beam,
            messages,
            antenna_uvw,
            smalls,
            pieces,
            span,
            bright_rows,
            small[0].shape[1],
        )
        done[step] = built[0]
        return built

    core, *side = range(1, width)
    (message,) = messages_for(beam, 0, [core], small, gated(BEAM, table))
    message = send(BEAM + 1, message, routes.partner[core])
    (own,) = build(OWN, 0, beam, [message], [small, message], routes.full, BRIGHT_ROWS)
    own_sides = near(OWN_NEAR, own)
    messages = messages_for(beam, 0, side, small, gated(SIDE_BEAMS, table))
    messages = [
        send(SIDE_BEAMS + 1 + n, messages[n], routes.partner[m]) for n, m in enumerate(side)
    ]
    own_far = far(OWN_FAR, own_sides)
    (rest,) = build(REST, 0, None, messages, messages, routes.full, BRIGHT_ROWS)
    rest_sides = near(REST_NEAR, rest)

    later = messages_for(beam, 1, [core, *side], None, gated(LATER_BEAMS, table))
    later = [send(LATER_BEAMS + m, later[m - 1], routes.partner[m]) for m in (core, *side)]
    vis = slices_for(
        visibility, 1, share, [(m, 0) for m in (core, *side)], gated(VIS, table)
    )
    vis = [visibility] + [send(VIS + m, vis[m - 1], routes.partner[m]) for m in (core, *side)]
    later_pieces = build(
        LATER, 1, beam, later, [small, message, *messages], routes.pieces, 0
    )
    rest_far = far(REST_FAR, rest_sides)
    near_0 = near(PIECE_NEAR[0], later_pieces[0])
    near_1 = near(PIECE_NEAR[1], later_pieces[1])
    far_0 = far(PIECE_FAR[0], near_0)

    grads = []

    def work(index, step, home_step, ready, bright):
        arrived, total = [], None
        for n, homes in enumerate([routes.order[:1], routes.order[1:]]):
            made = unit_work(
                index,
                routes.steps[index] + len(arrived) * routes.steps_per_home,
                gated(step + n, table),
                ready,
                [vis[m] for m in homes],
                keep,
                bright,
            )
            results, grad = made[: len(homes)], made[len(homes)]
            if isinstance(bright, int):
                bright = made[-1]
            done[step + n] = grad
            total = grad if total is None else total + grad
            arrived += [
                send(home_step - 1 + m, part, routes.partner[m]) if m else part
                for m, part in zip(homes, results)
            ]
        grads.append(total)
        return arrived, bright

    def put(step, homes, arrays, index, residual):
        rows = [(n, k) for n in range(len(arrays)) for k in range(units_dev)]
        offset = routes.targets[index] + homes * routes.targets_per_home
        done[step] = put_residuals(
            rows, arrays, offset, gated(step, table), visibility.shape, residual
        )
        return done[step]

    number = group // 2
    pieces = entries(own, own_sides, own_far, 0, number)
    pieces += entries(rest, rest_sides, rest_far, number, number)
    arrived, columns = work(0, WORK, HOME, [pieces], share)
    far_1 = far(PIECE_FAR[1], near_1)
    residual = put(PUT, 0, arrived, 0, None)
    ready = [
        entries(piece, sides, halves, 0, group)
        for piece, sides, halves in zip(later_pieces, (near_0, near_1), (far_0, far_1))
    ]
    arrived, _ = work(1, LATER_WORK, LATER_HOME, ready, columns)

    partial = jnp.concatenate(grads, 0)
    parts = [partial[:, n * group : (n + 1) * group] for n in range(4)]
    plane_sum = (parts[0] + send(SUM_PLANES, parts[3], routes.opposite)) + (
        send(SUM_PLANES + 1, parts[1], routes.backward)
        + send(SUM_PLANES + 2, parts[2], routes.onward)
    )
    sums = [plane_sum[:, m * per_group : (m + 1) * per_group] for m in range(width)]
    sums = [sums[0]] + [
        send(SUM_PLANE - 1 + m, sums[m], routes.partner[m]) for m in (core, *side)
    ]
    sums = jnp.stack(sums, 0)
    ids = jnp.arange(width, dtype=jnp.int32)
    here = jnp.bitwise_xor(ids[:, None], mine) == ids[None, :]
    summed = jnp.sum(jnp.where(here[:, :, None, None], sums[None], 0.0), axis=1)
    summed = summed.reshape(slots, per_group)

    residual = put(PUT_NEAR, 2, arrived[2:], 1, residual)
    residual = put(PUT_LAST, 0, arrived[:2], 1, residual)
    return residual, summed


def per_device(
    visibility, station_beam, antenna_uvw, source_dirs, source_flux, visible_list, antenna_flags
):
    span = visibility.shape[4]
    antennas = station_beam.shape[3]
    small = (source_dirs, source_flux.astype(jnp.float32)[None], visible_list)
    keep = 1.0 - antenna_flags.astype(jnp.float32)
    arguments = (visibility, station_beam, antenna_uvw, small, keep)
    if lax.axis_size("tile") == 16:
        routes = Routes(4, 4, unit_table(antennas // span), visibility.shape[1] // 4)
        residual, summed = plane_program(routes, *arguments)
    else:
        residual, summed = plain_program(*arguments)
    return (residual, summed * (-1.0 / (8.0 * antennas)))


def solution(mesh):
    return jax.shard_map(
        per_device,
        mesh=mesh,
        in_specs=(
            P("tile", "grp", None, None, None),
            P("grp", None, "tile", None),
            P("grp", None, None),
            P(None, "tile"),
            P(("grp", "tile")),
            P(None, "tile"),
            P("grp", None),
        ),
        out_specs=(P("tile", "grp", None, None, None), P("grp", "tile")),
        check_vma=False,
    )
```

```python
import functools

import jax
import jax.numpy as jnp
import numpy as np
from jax import lax
from jax.experimental import pallas as pl
from jax.experimental.pallas import tpu as pltpu
from jax.sharding import PartitionSpec as P


def unit_table(block_count):
    first_list = []
    second_list = []
    diag_list = []
    for row_block in range(block_count):
        for col_block in range(row_block + 1, block_count):
            first_list.append(row_block)
            second_list.append(col_block)
            diag_list.append(0)
    for pair_index in range(block_count // 2):
        first_list.append(2 * pair_index)
        second_list.append(2 * pair_index + 1)
        diag_list.append(1)
    return np.stack([first_list, second_list, diag_list], 1).astype(np.int32)


def turn_polynomials():
    nodes = 0.125 + 0.125 * np.cos(np.pi * (np.arange(64) + 0.5) / 64)
    root = np.sqrt(nodes)
    fit = np.polynomial.Polynomial.fit
    sine = fit(nodes, np.sin(2 * np.pi * root) / root, 7, domain=[0, 0.25]).convert()
    cosine = fit(nodes, np.cos(2 * np.pi * root), 8, domain=[0, 0.25]).convert()
    return [float(c) for c in sine.coef], [float(c) for c in cosine.coef]


def horner(coefs, x):
    total = coefs[-1]
    for coef in coefs[-2::-1]:
        total = total * x + coef
    return total


def build_kernel(sets, slot_ids, pieces, bright_rows, width, tab_ref, *refs):
    refs, scratch_ref = refs[:-1], refs[-1]
    uvw_ref, outs = refs[-1 - len(pieces)], refs[-len(pieces) :]
    per_group = sets[0][0]
    span = outs[0].shape[2]
    count = len(sets) * per_group
    sin_coefs, cos_coefs = turn_polynomials()
    brights = []
    for part, (_, beam_at, small_at) in enumerate(sets):
        beam_ref = refs[beam_at]
        if beam_ref.shape[0] == 1:
            beam = [beam_ref.at[0, 0], beam_ref.at[0, 1]]
        else:
            beam = [beam_ref.at[pl.ds(n * per_group, per_group)] for n in (0, 1)]
        if refs[small_at].dtype == jnp.float32:
            small = small_rows(scratch_ref, *refs[small_at : small_at + 3])
        else:
            small = unsplit(refs[small_at], 2 * per_group, width)
        lanes = lax.broadcasted_iota(jnp.int32, (per_group, width), 1)
        rows = lax.broadcasted_iota(jnp.int32, (per_group, width), 0)

        def pick(chosen, row):
            return jnp.sum(jnp.where(chosen, small[row : row + 1, :], 0.0), axis=1, keepdims=True)

        def chosen_at(index):
            here = lax.broadcasted_iota(jnp.int32, small.shape, 0) == LIST_ROW + tab_ref[0] + index
            line = jnp.sum(jnp.where(here, small, 0.0), axis=0, keepdims=True)
            listed = jnp.sum(jnp.where(lanes == rows, line, 0.0), axis=1, keepdims=True)
            return listed.astype(jnp.int32) == lanes

        group = part * per_group
        if bright_rows:
            columns = lax.broadcasted_iota(jnp.int32, (per_group, span), 1)
            numbers = lax.broadcasted_iota(jnp.int32, (per_group, span), 0) + group
            for index in range(slot_ids[1]):
                flux = pick(chosen_at(index), 2)
                line = jnp.sum(jnp.where(columns == numbers, flux, 0.0), axis=0, keepdims=True)
                if part == 0:
                    brights.append(line)
                else:
                    brights[index] += line
        chosen = chosen_at(slot_ids[0])
        east = pick(chosen, 0)
        north = pick(chosen, 1)
        depth = jnp.sqrt(1.0 - east * east - north * north) - 1.0
        for out_ref, piece in zip(outs, pieces):
            for place, block in enumerate(piece):
                cols = pl.ds(block * span, span)
                delay = (
                    uvw_ref[0, 0:1, cols] * east
                    + uvw_ref[0, 1:2, cols] * north
                    + uvw_ref[0, 2:3, cols] * depth
                )
                turn = delay - jnp.floor(delay + 0.5)
                square = turn * turn
                sine = horner(sin_coefs, square) * turn
                cosine = horner(cos_coefs, square)
                real = beam[0][:, cols].astype(jnp.float32)
                imag = beam[1][:, cols].astype(jnp.float32)
                at = pl.ds(place * count + group, per_group)
                out_ref[0, at] = (real * cosine + imag * sine).astype(jnp.bfloat16)
                out_ref[1, at] = (imag * cosine - real * sine).astype(jnp.bfloat16)
    if bright_rows:
        padding = jnp.zeros((bright_rows - len(brights), span), jnp.float32)
        block = jnp.concatenate(brights + [padding], 0).astype(jnp.bfloat16)
        for part in (0, 1):
            outs[0][part, pl.ds(len(pieces[0]) * count, bright_rows)] = block


def small_rows(rows_ref, dirs_ref, flux_ref, list_ref):
    rows_ref[...] = jnp.zeros_like(rows_ref)
    rows_ref[0:2, 0 : dirs_ref.shape[1]] = dirs_ref[...]
    rows_ref[2:3, 0 : flux_ref.shape[1]] = flux_ref[...]
    slots, count = list_ref.shape
    rows_ref[LIST_ROW : LIST_ROW + slots, 0:count] = list_ref[...].astype(jnp.float32)
    return rows_ref[...]


LIST_ROW = 8
SMALL_ROWS = 16


def unsplit(message_ref, start, width):
    rows = pl.ds(start, SMALL_ROWS)
    terms = [message_ref[rows, pl.ds(n * width, width)].astype(jnp.float32) for n in range(3)]
    return (terms[0] + terms[1]) + terms[2]


BRIGHT_ROWS = 16


def build_factors(
    slot_ids, table, beam, messages, antenna_uvw, smalls, pieces, span, bright_rows, small_width
):
    slots, _, antennas = antenna_uvw.shape
    per_group = slot_ids[2]
    index = slot_ids[0]
    whole = pl.BlockSpec(memory_space=pltpu.VMEM)
    operands, in_specs, sets = [], [], []
    if beam is not None:
        operands.append(beam)
        in_specs.append(
            pl.BlockSpec((1, 2, per_group, antennas), lambda n, tab: (tab[0] + index, 0, 0, 0))
        )
    operands += messages
    beams = len(operands)
    for n, small in enumerate(smalls):
        at = next((k for k, known in enumerate(operands) if known is small), len(operands))
        if at == len(operands):
            operands += small if isinstance(small, tuple) else [small]
        sets.append((per_group, n, at))
    in_specs += [whole] * (len(operands) - len(in_specs))
    in_specs.append(pl.BlockSpec((1, 3, antennas), lambda n, tab: (tab[0] + index, 0, 0)))
    count = beams * per_group
    shapes = [
        (2, len(piece) * count + (0 if n else bright_rows), span) for n, piece in enumerate(pieces)
    ]
    return pl.pallas_call(
        functools.partial(build_kernel, sets, slot_ids, pieces, bright_rows, small_width),
        grid_spec=pltpu.PrefetchScalarGridSpec(
            num_scalar_prefetch=1,
            grid=(1,),
            in_specs=in_specs,
            out_specs=[whole] * len(pieces),
            scratch_shapes=[pltpu.VMEM((SMALL_ROWS, small_width), jnp.float32)],
        ),
        out_shape=[jax.ShapeDtypeStruct(shape, jnp.bfloat16) for shape in shapes],
        compiler_params=pltpu.CompilerParams(vmem_limit_bytes=16 * 1024 * 1024),
        cost_estimate=LITTLE,
        name="build_factors",
    )(table, *operands, antenna_uvw)


LITTLE = pl.CostEstimate(flops=1, bytes_accessed=1, transcendentals=0)


def message_kernel(count, with_small, tab_ref, *refs):
    beams, refs = refs[:count], refs[count:]
    if with_small:
        smalls, outs, scratch_ref = refs[:3], refs[3:-1], refs[-1]
        terms = []
        rest = small_rows(scratch_ref, *smalls)
        width = rest.shape[1]
        for _ in range(3):
            terms.append(rest.astype(jnp.bfloat16))
            rest = rest - terms[-1].astype(jnp.float32)
    else:
        outs = refs
    for beam_ref, out_ref in zip(beams, outs):
        per_group = beam_ref.shape[2]
        for part in (0, 1):
            out_ref[pl.ds(part * per_group, per_group)] = beam_ref[0, part]
        if with_small:
            rows = pl.ds(2 * per_group, SMALL_ROWS)
            out_ref[rows] = jnp.zeros((SMALL_ROWS, out_ref.shape[1]), jnp.bfloat16)
            for n, term in enumerate(terms):
                out_ref[rows, pl.ds(n * width, width)] = term


def messages_for(beam, index, others, small, table):
    _, _, per_group, antennas = beam.shape
    smalls = small or ()
    rows = 2 * per_group + (SMALL_ROWS if smalls else 0)
    whole = pl.BlockSpec(memory_space=pltpu.VMEM)
    scratch = []
    if smalls:
        scratch.append(pltpu.VMEM((SMALL_ROWS, smalls[0].shape[1]), jnp.float32))
    return pl.pallas_call(
        functools.partial(message_kernel, len(others), bool(smalls)),
        grid_spec=pltpu.PrefetchScalarGridSpec(
            num_scalar_prefetch=1,
            grid=(1,),
            in_specs=[
                pl.BlockSpec(
                    (1, 2, per_group, antennas), lambda n, tab, m=m: (tab[m] + index, 0, 0, 0)
                )
                for m in others
            ]
            + [whole for _ in smalls],
            out_specs=[whole for _ in others],
            scratch_shapes=scratch,
        ),
        out_shape=[jax.ShapeDtypeStruct((rows, antennas), jnp.bfloat16) for _ in others],
        cost_estimate=LITTLE,
        name="messages_for",
    )(table, *[beam] * len(others), *smalls)


def slice_kernel(count, tab_ref, *refs):
    for source, target in zip(refs[:count], refs[count:]):
        target[...] = source[...]


def slices_for(array, axis, size, starts, table):
    lead = axis > 0
    shape = array.shape[:axis] + (size,) + array.shape[axis + 1 :]
    block = (1,) + shape[1:] if lead else shape
    rest = (0,) * (array.ndim - axis - 1)
    return pl.pallas_call(
        functools.partial(slice_kernel, len(starts)),
        grid_spec=pltpu.PrefetchScalarGridSpec(
            num_scalar_prefetch=1,
            grid=(shape[0] if lead else 1,),
            in_specs=[
                pl.BlockSpec(
                    block,
                    lambda n, tab, start=start, shift=shift: (
                        *((n,) if lead else ()),
                        tab[start] // size + shift,
                        *rest,
                    ),
                )
                for start, shift in starts
            ],
            out_specs=[
                pl.BlockSpec(block, lambda n, tab: (n,) + (0,) * (array.ndim - 1)) for _ in starts
            ],
        ),
        out_shape=[jax.ShapeDtypeStruct(shape, array.dtype) for _ in starts],
        cost_estimate=LITTLE,
        name="slices_for",
    )(table, *[array] * len(starts))


KIND, ONE, TWO, ONE_AT, TWO_AT = 0, 1, 2, 3, 5
COLUMNS = 7


def unit_kernel(index, offset, pieces, bright_at, homes, tab_ref, *refs):
    arrays = []
    for entries in pieces:
        found = []
        for count, start, number in entries:
            parts = (refs[0].at[0], refs[0].at[1]) if count == 1 else refs[:2]
            found.append((parts, start, number))
            refs = refs[count:]
        arrays.append(found)
    vis_refs, (keep_one_ref, keep_two_ref) = refs[:homes], refs[homes : homes + 2]
    refs = refs[homes + 2 :]
    columns_ref = None
    if bright_at is None:
        columns_ref, refs = refs[0], refs[1:]
    out_refs, grad_ref = refs[:homes], refs[homes]
    refs = refs[homes + 1 :]
    if bright_at is not None:
        columns_ref, refs = refs[0], refs[1:]
    total_ref, one_ref, two_ref, vis_ref = refs
    step = pl.program_id(0)
    slot = tab_ref[0] + index
    sources, span = one_ref.shape[1:]

    def entry(column):
        return tab_ref[offset + step * COLUMNS + column]

    def load(target, at):
        for n, found in enumerate(arrays):

            @pl.when(entry(at) == n)
            def _(found=found):
                place = entry(at + 1)
                for parts, start, number in found:
                    rows = pl.ds(pl.multiple_of(place * number, number), number)
                    for part in (0, 1):
                        target[part, pl.ds(start, number)] = parts[part][rows]

    if bright_at is not None:

        @pl.when(step == 0)
        def _():
            for parts, start, number in arrays[0]:
                lines = parts[0][pl.ds(bright_at * number, BRIGHT_ROWS)].astype(jnp.float32)
                lanes = lax.broadcasted_iota(jnp.int32, (number, span), 1)
                rows = lax.broadcasted_iota(jnp.int32, (number, span), 0)
                for n in range(columns_ref.shape[0]):
                    line = jnp.where(lanes == rows, lines[n : n + 1, :], 0.0)
                    column = jnp.sum(line, axis=1, keepdims=True)
                    columns_ref[n, pl.ds(start, number)] = jnp.broadcast_to(column, (number, 128))

    def dot(a, b):
        return lax.dot_general(a, b, (((1,), (0,)), ((), ())), preferred_element_type=jnp.float32)

    def scaled_of(re, im):
        column = jnp.concatenate([columns_ref[index].astype(jnp.bfloat16)] * (span // 128), 1)
        return re * column, im * column

    def outer(a, b):
        row_ids = lax.broadcasted_iota(jnp.int32, a.shape, 0)
        a = jnp.where(row_ids == slot, a, 0.0)
        return lax.dot_general(a, b, (((0,), (0,)), ((), ())), preferred_element_type=jnp.float32)

    def cross(a_re, a_im, b_re, b_im):
        lhs = jnp.concatenate([a_re, a_im], 0).T
        rhs = jnp.concatenate(
            [jnp.concatenate([b_re, -b_im], 1), jnp.concatenate([b_im, b_re], 1)], 0
        )
        both = dot(lhs, rhs)
        return both[:, :span], both[:, span:]

    def pull(re, im, res_re, res_im, sign):
        lhs = jnp.concatenate([re, im], 1)
        rhs = jnp.concatenate(
            [
                jnp.concatenate([res_re, res_im], 1),
                jnp.concatenate([res_im, -res_re] if sign == 1 else [-res_im, res_re], 1),
            ],
            0,
        )
        both = dot(lhs, rhs)
        return both[:, :span], both[:, span:]

    def add_grad(value):
        folded = value[:, :128]
        for start in range(128, span, 128):
            folded = folded + value[:, start : start + 128]
        total_ref[...] += folded

    each = pl.num_programs(0) // homes

    def put(res_re, res_im):
        for home, out_ref in enumerate(out_refs):

            @pl.when(step // each == home)
            def _(out_ref=out_ref):
                out_ref[0, 0] = res_re
                out_ref[0, 1] = res_im

    @pl.when(step == 0)
    def _():
        total_ref[...] = jnp.zeros_like(total_ref)

    load(one_ref, ONE_AT)
    load(two_ref, TWO_AT)
    for home, home_ref in enumerate(vis_refs):

        @pl.when(step // each == home)
        def _(home_ref=home_ref):
            vis_ref[...] = home_ref[0, 0]

    @pl.when(entry(KIND) == 0)
    def _():
        one_re, one_im, two_re, two_im = one_ref[0], one_ref[1], two_ref[0], two_ref[1]
        pred_re, pred_im = cross(*scaled_of(one_re, one_im), two_re, two_im)
        weights = outer(keep_one_ref[...], keep_two_ref[...])
        res_re = (weights * (vis_ref[0].astype(jnp.float32) - pred_re)).astype(jnp.bfloat16)
        res_im = (weights * (vis_ref[1].astype(jnp.float32) - pred_im)).astype(jnp.bfloat16)
        put(res_re, res_im)
        sum_re, sum_im = pull(one_re, one_im, res_re, res_im, 1)
        add_grad(sum_re * two_re.astype(jnp.float32) - sum_im * two_im.astype(jnp.float32))

    @pl.when(entry(KIND) == 1)
    def _():
        one_re, one_im, two_re, two_im = one_ref[0], one_ref[1], two_ref[0], two_ref[1]
        row_ids = lax.broadcasted_iota(jnp.int32, (span, span), 0)
        col_ids = lax.broadcasted_iota(jnp.int32, (span, span), 1)
        upper = row_ids < col_ids
        lower = row_ids > col_ids
        first_re, first_im = cross(*scaled_of(one_re, one_im), one_re, one_im)
        second_re, second_im = cross(two_re, two_im, *scaled_of(two_re, two_im))
        keep_one = keep_one_ref[...]
        keep_two = keep_two_ref[...]
        weights = jnp.where(upper, outer(keep_one, keep_one), 0.0) + jnp.where(
            lower, outer(keep_two, keep_two), 0.0
        )
        vis_re = vis_ref[0].astype(jnp.float32)
        vis_im = vis_ref[1].astype(jnp.float32)
        res_re = (weights * (vis_re - jnp.where(upper, first_re, second_re))).astype(jnp.bfloat16)
        res_im = (weights * (vis_im - jnp.where(upper, first_im, -second_im))).astype(jnp.bfloat16)
        put(res_re, res_im)
        none = jnp.zeros_like(res_re)
        sum_re, sum_im = pull(
            one_re, one_im, jnp.where(upper, res_re, none), jnp.where(upper, res_im, none), 1
        )
        add_grad(sum_re * one_re.astype(jnp.float32) - sum_im * one_im.astype(jnp.float32))
        sum_re, sum_im = pull(
            two_re, two_im, jnp.where(lower, res_re, none), jnp.where(lower, res_im, none), -1
        )
        add_grad(sum_re * two_re.astype(jnp.float32) + sum_im * two_im.astype(jnp.float32))

    @pl.when(step == pl.num_programs(0) - 1)
    def _():
        grad_ref[...] = jnp.sum(total_ref[...].T, axis=0, keepdims=True)


def unit_work(index, offset, table, pieces, vis, keep, bright):
    units_dev, _, _, span, _ = vis[0].shape
    slots = keep.shape[0]
    sources = sum(number for _, _, number in pieces[0])
    count = units_dev * len(vis)
    whole = pl.BlockSpec(memory_space=pltpu.VMEM)
    arrays = [array for piece in pieces for entry, _, _ in piece for array in entry]

    def at(tab, step, column):
        return tab[offset + step * COLUMNS + column]

    def unit(step, home):
        return jnp.clip(step - home * units_dev, 0, units_dev - 1)

    in_specs = [whole] * len(arrays)
    for home, array in enumerate(vis):
        if array.shape[1] == slots:
            slot = lambda tab: tab[0] + index
        else:
            slot = lambda tab: index
        in_specs.append(
            pl.BlockSpec(
                (1, 1, 2, span, span),
                lambda u, tab, home=home, slot=slot: (unit(u, home), slot(tab), 0, 0, 0),
            )
        )
    in_specs += [
        pl.BlockSpec((slots, span), lambda u, tab: (0, at(tab, u, ONE))),
        pl.BlockSpec((slots, span), lambda u, tab: (0, at(tab, u, TWO))),
    ]
    operands = [table, *arrays, *vis, keep, keep]
    bright_at = None
    if isinstance(bright, int):
        first = pieces[0][0]
        bright_at = (first[0][0].shape[1] - BRIGHT_ROWS) // first[2]
    else:
        in_specs.append(whole)
        operands.append(bright)
    out_specs = [
        pl.BlockSpec((1, 2, span, span), lambda u, tab, home=home: (unit(u, home), 0, 0, 0))
        for home in range(len(vis))
    ]
    out_shapes = [jax.ShapeDtypeStruct((units_dev, 2, span, span), jnp.bfloat16) for _ in vis]
    out_specs.append(pl.BlockSpec((1, sources), lambda u, tab: (0, 0)))
    out_shapes.append(jax.ShapeDtypeStruct((1, sources), jnp.float32))
    if bright_at is not None:
        out_specs.append(pl.BlockSpec((bright, sources, 128), lambda u, tab: (0, 0, 0)))
        out_shapes.append(jax.ShapeDtypeStruct((bright, sources, 128), jnp.float32))
    kinds = [[(len(entry), start, number) for entry, start, number in piece] for piece in pieces]
    return pl.pallas_call(
        functools.partial(unit_kernel, index, offset, kinds, bright_at, len(vis)),
        grid_spec=pltpu.PrefetchScalarGridSpec(
            num_scalar_prefetch=1,
            grid=(count,),
            in_specs=in_specs,
            out_specs=out_specs,
            scratch_shapes=[
                pltpu.VMEM((sources, 128), jnp.float32),
                pltpu.VMEM((2, sources, span), jnp.bfloat16),
                pltpu.VMEM((2, sources, span), jnp.bfloat16),
                pltpu.VMEM((2, span, span), jnp.bfloat16),
            ],
        ),
        out_shape=out_shapes,
        compiler_params=pltpu.CompilerParams(vmem_limit_bytes=16 * 1024 * 1024),
        cost_estimate=LITTLE,
        name="unit_work",
    )(*operands)


def put_kernel(sources, tab_ref, *refs):
    out_ref = refs[-1]
    for step, (which, row) in enumerate(sources):

        @pl.when(pl.program_id(0) == step)
        def _(which=which, row=row):
            out_ref[0, 0] = refs[which][...] if row is None else refs[which][row]


def put_residuals(sources, arrays, offset, table, shape, residual):
    span = shape[-1]
    whole = pl.BlockSpec(memory_space=pltpu.VMEM)
    operands = [table, *arrays]
    in_specs = [whole] * len(arrays)
    aliases = {}
    if residual is not None:
        aliases = {len(operands): 0}
        operands.append(residual)
        in_specs.append(pl.BlockSpec(memory_space=pl.ANY))
    return pl.pallas_call(
        functools.partial(put_kernel, sources),
        grid_spec=pltpu.PrefetchScalarGridSpec(
            num_scalar_prefetch=1,
            grid=(len(sources),),
            in_specs=in_specs,
            out_specs=pl.BlockSpec(
                (1, 1, 2, span, span),
                lambda n, tab: (tab[offset + 2 * n], tab[offset + 2 * n + 1], 0, 0, 0),
            ),
        ),
        out_shape=jax.ShapeDtypeStruct(shape, jnp.bfloat16),
        input_output_aliases=aliases,
        compiler_params=pltpu.CompilerParams(vmem_limit_bytes=16 * 1024 * 1024),
        cost_estimate=LITTLE,
        name="put_residuals",
    )(*operands)


class Routes:
    def __init__(self, planes, width, units, share):
        count = planes * width
        blocks = int(units[:, :2].max()) + 1
        self.width = width
        self.units_dev = units_dev = units.shape[0] // count
        ring = [0] + list(range(1, planes, 2)) + list(range(planes - 2, 0, -2))

        def along(step):
            at = {plane: ring[(n + step) % planes] for n, plane in enumerate(ring)}
            return [(t, at[t // width] * width + t % width) for t in range(count)]

        self.onward = along(1)
        self.backward = along(-1)
        self.opposite = along(2)
        self.partner = [[(t, t ^ m) for t in range(count)] for m in range(width)]

        half = blocks // 2
        self.full = [list(range(blocks))]
        self.pieces = [list(range(half)), list(range(half, blocks))]

        def table_of(pieces, order):
            rows = np.zeros((count, len(order), units_dev, COLUMNS), np.int32)
            for t in range(count):
                for n, m in enumerate(order):
                    for k in range(units_dev):
                        one, two, kind = units[(t ^ m) * units_dev + k].tolist()
                        at = [
                            (p, piece.index(b))
                            for b in (one, two)
                            for p, piece in enumerate(pieces)
                            if b in piece
                        ]
                        rows[t, n, k] = [kind, one, two, *at[0], *at[1]]
            return rows

        def targets(index):
            rows = np.zeros((count, len(self.order), units_dev, 2), np.int32)
            for t in range(count):
                for n, m in enumerate(self.order):
                    for k in range(units_dev):
                        rows[t, n, k] = k, (t % width ^ m) * share + index
            return rows

        self.order = list(range(width // 2, width)) + list(range(width // 2 - 1, -1, -1))
        starts = np.array([[(t % width ^ m) * share for m in range(width)] for t in range(count)])
        parts = [starts, table_of(self.full, self.order), table_of(self.pieces, self.order)]
        parts += [targets(n) for n in range(share)]
        parts = [part.reshape(count, -1) for part in parts]
        ends = np.cumsum([part.shape[1] for part in parts]).tolist()
        self.table = np.concatenate(parts, 1).astype(np.int32)
        self.steps = ends[:2]
        self.targets = ends[2:]
        self.steps_per_home = units_dev * COLUMNS
        self.targets_per_home = units_dev * 2


def plain_program(visibility, beam, antenna_uvw, small, keep):
    units_dev, slots, _, span, _ = visibility.shape
    _, _, per_group, antennas = beam.shape
    blocks = antennas // span
    tile_index = lax.axis_index("tile")
    units = unit_table(blocks)
    none = np.zeros_like(units[:, 0])
    table = np.stack([units[:, 2], units[:, 0], units[:, 1], none, units[:, 0], none, units[:, 1]], 1)
    table = table.astype(np.int32).reshape(-1, units_dev * COLUMNS)
    table = np.pad(table, ((0, 0), (1, 0)))
    table = lax.dynamic_index_in_dim(jnp.asarray(table), tile_index, 0, keepdims=False)
    columns = None
    residuals, grads = [], []
    for slot in range(slots):
        (owned,) = build_factors(
            (slot, slots, per_group),
            table,
            beam,
            [],
            antenna_uvw,
            [small],
            [list(range(blocks))],
            span,
            0 if slot else BRIGHT_ROWS,
            small[0].shape[1],
        )
        everyone = lax.all_gather(owned, "tile", axis=0)
        rows = blocks * per_group
        if columns is None:
            bright = everyone[:, 0, rows : rows + slots, :per_group].astype(jnp.float32)
            bright = jnp.swapaxes(bright, 0, 1).reshape(slots, -1, 1)
            columns = jnp.broadcast_to(bright, bright.shape[:2] + (128,))
        factors = everyone[:, :, :rows].reshape(-1, 2, blocks, per_group, span)
        number = factors.shape[0] * per_group
        factors = factors.transpose(1, 2, 0, 3, 4).reshape(2, blocks * number, span)
        residual, grad = unit_work(
            slot, 1, table, [[((factors,), 0, number)]], [visibility], keep, columns
        )
        residuals.append(residual)
        grads.append(grad)
    summed = lax.psum_scatter(jnp.concatenate(grads, 0), "tile", scatter_dimension=1, tiled=True)
    return jnp.stack(residuals, 1), summed


OWN, OWN_NEAR, OWN_FAR, REST, REST_NEAR, REST_FAR = 0, 1, 3, 5, 6, 8
BEAM, SIDE_BEAMS, LATER_BEAMS, VIS, LATER = 10, 12, 15, 19, 23
PIECE_NEAR, PIECE_FAR = (24, 26), (28, 30)
WORK, HOME, PUT, LATER_WORK, LATER_HOME, PUT_NEAR, PUT_LAST = 32, 35, 38, 40, 43, 46, 47
SUM_PLANES, SUM_PLANE = 48, 51
GATES = {
    1: (0,),
    3: (0, 1),
    5: (0, 2, 13),
    6: (1, 2, 11),
    7: (1, 2),
    14: (13,),
    16: (2,),
    17: (1,),
    19: (18,),
    20: (3, 4, 6, 7, 17),
    21: (3, 4, 5, 13, 14, 16, 17),
    23: (4, 17),
    24: (6, 9, 17),
    25: (6, 9, 17, 23),
    26: (9,),
    27: (8,),
    28: (22,),
    31: (25, 27),
    33: (23, 32),
    34: (33,),
    35: (8, 9, 24, 25),
    40: (28, 34, 36, 37),
    41: (40,),
    42: (29, 41),
    43: (41,),
    45: (28, 32),
    48: (35,),
    49: (44,),
    51: (34,),
    52: (38,),
}


def plane_program(routes, visibility, beam, antenna_uvw, small, keep):
    units_dev, slots, _, span, _ = visibility.shape
    per_group = beam.shape[2]
    width = routes.width
    share = slots // width
    group = width * per_group
    tile_index = lax.axis_index("tile")
    mine = tile_index % width
    table = lax.dynamic_index_in_dim(jnp.asarray(routes.table), tile_index, 0, keepdims=False)
    done = {}

    def gated(step, value):
        earlier = [done[gate] for gate in GATES.get(step, ())]
        return lax.optimization_barrier((value, *earlier))[0] if earlier else value

    def send(step, value, pairs):
        done[step] = lax.ppermute(gated(step, value), "tile", pairs)
        return done[step]

    def near(step, piece):
        return [send(step, piece, routes.onward), send(step + 1, piece, routes.backward)]

    def far(step, sides):
        return [
            send(step, sides[0][0], routes.onward),
            send(step + 1, sides[1][1], routes.backward),
        ]

    def entries(piece, sides, halves, first, number):
        found = [(piece,), (sides[0],), (sides[1],), tuple(halves)]
        return [(arrays, n * group + first, number) for n, arrays in enumerate(found)]

    def build(step, index, own_beam, messages, smalls, pieces, bright_rows):
        built = build_factors(
            (index, share, per_group),
            gated(step, table),
            own_beam,
            messages,
            antenna_uvw,
            smalls,
            pieces,
            span,
            bright_rows,
            small[0].shape[1],
        )
        done[step] = built[0]
        return built

    core, *side = range(1, width)
    (message,) = messages_for(beam, 0, [core], small, gated(BEAM, table))
    message = send(BEAM + 1, message, routes.partner[core])
    (own,) = build(OWN, 0, beam, [message], [small, message], routes.full, BRIGHT_ROWS)
    own_sides = near(OWN_NEAR, own)
    messages = messages_for(beam, 0, side, small, gated(SIDE_BEAMS, table))
    messages = [
        send(SIDE_BEAMS + 1 + n, messages[n], routes.partner[m]) for n, m in enumerate(side)
    ]
    own_far = far(OWN_FAR, own_sides)
    (rest,) = build(REST, 0, None, messages, messages, routes.full, BRIGHT_ROWS)
    rest_sides = near(REST_NEAR, rest)

    later = messages_for(beam, 1, [core, *side], None, gated(LATER_BEAMS, table))
    later = [send(LATER_BEAMS + m, later[m - 1], routes.partner[m]) for m in (core, *side)]
    vis = slices_for(
        visibility, 1, share, [(m, 0) for m in (core, *side)], gated(VIS, table)
    )
    vis = [visibility] + [send(VIS + m, vis[m - 1], routes.partner[m]) for m in (core, *side)]
    later_pieces = build(
        LATER, 1, beam, later, [small, message, *messages], routes.pieces, 0
    )
    rest_far = far(REST_FAR, rest_sides)
    near_0 = near(PIECE_NEAR[0], later_pieces[0])
    near_1 = near(PIECE_NEAR[1], later_pieces[1])
    far_0 = far(PIECE_FAR[0], near_0)

    grads = []

    def work(index, step, home_step, ready, bright):
        arrived, total = [], None
        for n, homes in enumerate([routes.order[:1], routes.order[1:2], routes.order[2:]]):
            made = unit_work(
                index,
                routes.steps[index] + len(arrived) * routes.steps_per_home,
                gated(step + n, table),
                ready,
                [vis[m] for m in homes],
                keep,
                bright,
            )
            results, grad = made[: len(homes)], made[len(homes)]
            if isinstance(bright, int):
                bright = made[-1]
            done[step + n] = grad
            total = grad if total is None else total + grad
            arrived += [
                send(home_step - 1 + m, part, routes.partner[m]) if m else part
                for m, part in zip(homes, results)
            ]
        grads.append(total)
        return arrived, bright

    def put(step, homes, arrays, index, residual):
        rows = [(n, k) for n in range(len(arrays)) for k in range(units_dev)]
        offset = routes.targets[index] + homes * routes.targets_per_home
        done[step] = put_residuals(
            rows, arrays, offset, gated(step, table), visibility.shape, residual
        )
        return done[step]

    number = group // 2
    pieces = entries(own, own_sides, own_far, 0, number)
    pieces += entries(rest, rest_sides, rest_far, number, number)
    arrived, columns = work(0, WORK, HOME, [pieces], share)
    far_1 = far(PIECE_FAR[1], near_1)
    residual = put(PUT, 0, arrived, 0, None)
    ready = [
        entries(piece, sides, halves, 0, group)
        for piece, sides, halves in zip(later_pieces, (near_0, near_1), (far_0, far_1))
    ]
    arrived, _ = work(1, LATER_WORK, LATER_HOME, ready, columns)

    partial = jnp.concatenate(grads, 0)
    parts = [partial[:, n * group : (n + 1) * group] for n in range(4)]
    plane_sum = (parts[0] + send(SUM_PLANES, parts[3], routes.opposite)) + (
        send(SUM_PLANES + 1, parts[1], routes.backward)
        + send(SUM_PLANES + 2, parts[2], routes.onward)
    )
    sums = [plane_sum[:, m * per_group : (m + 1) * per_group] for m in range(width)]
    sums = [sums[0]] + [
        send(SUM_PLANE - 1 + m, sums[m], routes.partner[m]) for m in (core, *side)
    ]
    sums = jnp.stack(sums, 0)
    ids = jnp.arange(width, dtype=jnp.int32)
    here = jnp.bitwise_xor(ids[:, None], mine) == ids[None, :]
    summed = jnp.sum(jnp.where(here[:, :, None, None], sums[None], 0.0), axis=1)
    summed = summed.reshape(slots, per_group)

    residual = put(PUT_NEAR, 2, arrived[2:], 1, residual)
    residual = put(PUT_LAST, 0, arrived[:2], 1, residual)
    return residual, summed


def per_device(
    visibility, station_beam, antenna_uvw, source_dirs, source_flux, visible_list, antenna_flags
):
    span = visibility.shape[4]
    antennas = station_beam.shape[3]
    small = (source_dirs, source_flux.astype(jnp.float32)[None], visible_list)
    keep = 1.0 - antenna_flags.astype(jnp.float32)
    arguments = (visibility, station_beam, antenna_uvw, small, keep)
    if lax.axis_size("tile") == 16:
        routes = Routes(4, 4, unit_table(antennas // span), visibility.shape[1] // 4)
        residual, summed = plane_program(routes, *arguments)
    else:
        residual, summed = plain_program(*arguments)
    return (residual, summed * (-1.0 / (8.0 * antennas)))


def solution(mesh):
    return jax.shard_map(
        per_device,
        mesh=mesh,
        in_specs=(
            P("tile", "grp", None, None, None),
            P("grp", None, "tile", None),
            P("grp", None, None),
            P(None, "tile"),
            P(("grp", "tile")),
            P(None, "tile"),
            P("grp", None),
        ),
        out_specs=(P("tile", "grp", None, None, None), P("grp", "tile")),
        check_vma=False,
    )
```

```python
import functools

import jax
import jax.numpy as jnp
import numpy as np
from jax import lax
from jax.experimental import pallas as pl
from jax.experimental.pallas import tpu as pltpu
from jax.sharding import PartitionSpec as P


def unit_table(block_count):
    first_list = []
    second_list = []
    diag_list = []
    for row_block in range(block_count):
        for col_block in range(row_block + 1, block_count):
            first_list.append(row_block)
            second_list.append(col_block)
            diag_list.append(0)
    for pair_index in range(block_count // 2):
        first_list.append(2 * pair_index)
        second_list.append(2 * pair_index + 1)
        diag_list.append(1)
    return np.stack([first_list, second_list, diag_list], 1).astype(np.int32)


def turn_polynomials():
    nodes = 0.125 + 0.125 * np.cos(np.pi * (np.arange(64) + 0.5) / 64)
    root = np.sqrt(nodes)
    fit = np.polynomial.Polynomial.fit
    sine = fit(nodes, np.sin(2 * np.pi * root) / root, 7, domain=[0, 0.25]).convert()
    cosine = fit(nodes, np.cos(2 * np.pi * root), 8, domain=[0, 0.25]).convert()
    return [float(c) for c in sine.coef], [float(c) for c in cosine.coef]


def horner(coefs, x):
    total = coefs[-1]
    for coef in coefs[-2::-1]:
        total = total * x + coef
    return total


def build_kernel(sets, slot_ids, pieces, bright_rows, width, tab_ref, *refs):
    refs, scratch_ref = refs[:-1], refs[-1]
    uvw_ref, outs = refs[-1 - len(pieces)], refs[-len(pieces) :]
    per_group = sets[0][0]
    span = outs[0].shape[2]
    count = len(sets) * per_group
    sin_coefs, cos_coefs = turn_polynomials()
    brights = []
    for part, (_, beam_at, small_at) in enumerate(sets):
        beam_ref = refs[beam_at]
        if beam_ref.shape[0] == 1:
            beam = [beam_ref.at[0, 0], beam_ref.at[0, 1]]
        else:
            beam = [beam_ref.at[pl.ds(n * per_group, per_group)] for n in (0, 1)]
        if refs[small_at].dtype == jnp.float32:
            small = small_rows(scratch_ref, *refs[small_at : small_at + 3])
        else:
            small = unsplit(refs[small_at], 2 * per_group, width)
        lanes = lax.broadcasted_iota(jnp.int32, (per_group, width), 1)
        rows = lax.broadcasted_iota(jnp.int32, (per_group, width), 0)

        def pick(chosen, row):
            return jnp.sum(jnp.where(chosen, small[row : row + 1, :], 0.0), axis=1, keepdims=True)

        def chosen_at(index):
            here = lax.broadcasted_iota(jnp.int32, small.shape, 0) == LIST_ROW + tab_ref[0] + index
            line = jnp.sum(jnp.where(here, small, 0.0), axis=0, keepdims=True)
            listed = jnp.sum(jnp.where(lanes == rows, line, 0.0), axis=1, keepdims=True)
            return listed.astype(jnp.int32) == lanes

        group = part * per_group
        if bright_rows:
            columns = lax.broadcasted_iota(jnp.int32, (per_group, span), 1)
            numbers = lax.broadcasted_iota(jnp.int32, (per_group, span), 0) + group
            for index in range(slot_ids[1]):
                flux = pick(chosen_at(index), 2)
                line = jnp.sum(jnp.where(columns == numbers, flux, 0.0), axis=0, keepdims=True)
                if part == 0:
                    brights.append(line)
                else:
                    brights[index] += line
        chosen = chosen_at(slot_ids[0])
        east = pick(chosen, 0)
        north = pick(chosen, 1)
        depth = jnp.sqrt(1.0 - east * east - north * north) - 1.0
        for out_ref, piece in zip(outs, pieces):
            for place, block in enumerate(piece):
                cols = pl.ds(block * span, span)
                delay = (
                    uvw_ref[0, 0:1, cols] * east
                    + uvw_ref[0, 1:2, cols] * north
                    + uvw_ref[0, 2:3, cols] * depth
                )
                turn = delay - jnp.floor(delay + 0.5)
                square = turn * turn
                sine = horner(sin_coefs, square) * turn
                cosine = horner(cos_coefs, square)
                real = beam[0][:, cols].astype(jnp.float32)
                imag = beam[1][:, cols].astype(jnp.float32)
                at = pl.ds(place * count + group, per_group)
                out_ref[0, at] = (real * cosine + imag * sine).astype(jnp.bfloat16)
                out_ref[1, at] = (imag * cosine - real * sine).astype(jnp.bfloat16)
    if bright_rows:
        padding = jnp.zeros((bright_rows - len(brights), span), jnp.float32)
        block = jnp.concatenate(brights + [padding], 0).astype(jnp.bfloat16)
        for part in (0, 1):
            outs[0][part, pl.ds(len(pieces[0]) * count, bright_rows)] = block


def small_rows(rows_ref, dirs_ref, flux_ref, list_ref):
    rows_ref[...] = jnp.zeros_like(rows_ref)
    rows_ref[0:2, 0 : dirs_ref.shape[1]] = dirs_ref[...]
    rows_ref[2:3, 0 : flux_ref.shape[1]] = flux_ref[...]
    slots, count = list_ref.shape
    rows_ref[LIST_ROW : LIST_ROW + slots, 0:count] = list_ref[...].astype(jnp.float32)
    return rows_ref[...]


LIST_ROW = 8
SMALL_ROWS = 16


def unsplit(message_ref, start, width):
    rows = pl.ds(start, SMALL_ROWS)
    terms = [message_ref[rows, pl.ds(n * width, width)].astype(jnp.float32) for n in range(3)]
    return (terms[0] + terms[1]) + terms[2]


BRIGHT_ROWS = 16


def full(array):
    return pl.BlockSpec(array.shape, lambda *_: (0,) * len(array.shape))


def build_factors(
    slot_ids, table, beam, messages, antenna_uvw, smalls, pieces, span, bright_rows, small_width
):
    slots, _, antennas = antenna_uvw.shape
    per_group = slot_ids[2]
    index = slot_ids[0]
    operands, in_specs, sets = [], [], []
    if beam is not None:
        operands.append(beam)
        in_specs.append(
            pl.BlockSpec((1, 2, per_group, antennas), lambda n, tab: (tab[0] + index, 0, 0, 0))
        )
    operands += messages
    beams = len(operands)
    for n, small in enumerate(smalls):
        at = next((k for k, known in enumerate(operands) if known is small), len(operands))
        if at == len(operands):
            operands += small if isinstance(small, tuple) else [small]
        sets.append((per_group, n, at))
    in_specs += [full(array) for array in operands[len(in_specs) :]]
    in_specs.append(pl.BlockSpec((1, 3, antennas), lambda n, tab: (tab[0] + index, 0, 0)))
    count = beams * per_group
    made = [
        jax.ShapeDtypeStruct(
            (2, len(piece) * count + (0 if n else bright_rows), span), jnp.bfloat16
        )
        for n, piece in enumerate(pieces)
    ]
    return pl.pallas_call(
        functools.partial(build_kernel, sets, slot_ids, pieces, bright_rows, small_width),
        grid_spec=pltpu.PrefetchScalarGridSpec(
            num_scalar_prefetch=1,
            grid=(1,),
            in_specs=in_specs,
            out_specs=[full(array) for array in made],
            scratch_shapes=[pltpu.VMEM((SMALL_ROWS, small_width), jnp.float32)],
        ),
        out_shape=made,
        compiler_params=pltpu.CompilerParams(vmem_limit_bytes=61 * 1024 * 1024),
        cost_estimate=LITTLE,
        name="build_factors",
    )(table, *operands, antenna_uvw)


LITTLE = pl.CostEstimate(flops=1, bytes_accessed=1, transcendentals=0)


def message_kernel(count, with_small, tab_ref, *refs):
    beams, refs = refs[:count], refs[count:]
    if with_small:
        smalls, outs, scratch_ref = refs[:3], refs[3:-1], refs[-1]
        terms = []
        rest = small_rows(scratch_ref, *smalls)
        width = rest.shape[1]
        for _ in range(3):
            terms.append(rest.astype(jnp.bfloat16))
            rest = rest - terms[-1].astype(jnp.float32)
    else:
        outs = refs
    for beam_ref, out_ref in zip(beams, outs):
        per_group = beam_ref.shape[2]
        for part in (0, 1):
            out_ref[pl.ds(part * per_group, per_group)] = beam_ref[0, part]
        if with_small:
            rows = pl.ds(2 * per_group, SMALL_ROWS)
            out_ref[rows] = jnp.zeros((SMALL_ROWS, out_ref.shape[1]), jnp.bfloat16)
            for n, term in enumerate(terms):
                out_ref[rows, pl.ds(n * width, width)] = term


def messages_for(beam, index, others, small, table):
    _, _, per_group, antennas = beam.shape
    smalls = small or ()
    rows = 2 * per_group + (SMALL_ROWS if smalls else 0)
    made = [jax.ShapeDtypeStruct((rows, antennas), jnp.bfloat16) for _ in others]
    scratch = []
    if smalls:
        scratch.append(pltpu.VMEM((SMALL_ROWS, smalls[0].shape[1]), jnp.float32))
    return pl.pallas_call(
        functools.partial(message_kernel, len(others), bool(smalls)),
        grid_spec=pltpu.PrefetchScalarGridSpec(
            num_scalar_prefetch=1,
            grid=(1,),
            in_specs=[
                pl.BlockSpec(
                    (1, 2, per_group, antennas), lambda n, tab, m=m: (tab[m] + index, 0, 0, 0)
                )
                for m in others
            ]
            + [full(array) for array in smalls],
            out_specs=[full(array) for array in made],
            scratch_shapes=scratch,
        ),
        out_shape=made,
        compiler_params=pltpu.CompilerParams(vmem_limit_bytes=61 * 1024 * 1024),
        cost_estimate=LITTLE,
        name="messages_for",
    )(table, *[beam] * len(others), *smalls)


def slice_kernel(count, tab_ref, *refs):
    for source, target in zip(refs[:count], refs[count:]):
        target[...] = source[...]


def slices_for(array, axis, size, starts, table):
    lead = axis > 0
    shape = array.shape[:axis] + (size,) + array.shape[axis + 1 :]
    block = (1,) + shape[1:] if lead else shape
    rest = (0,) * (array.ndim - axis - 1)
    return pl.pallas_call(
        functools.partial(slice_kernel, len(starts)),
        grid_spec=pltpu.PrefetchScalarGridSpec(
            num_scalar_prefetch=1,
            grid=(shape[0] if lead else 1,),
            in_specs=[
                pl.BlockSpec(
                    block,
                    lambda n, tab, start=start, shift=shift: (
                        *((n,) if lead else ()),
                        tab[start] // size + shift,
                        *rest,
                    ),
                )
                for start, shift in starts
            ],
            out_specs=[
                pl.BlockSpec(block, lambda n, tab: (n,) + (0,) * (array.ndim - 1)) for _ in starts
            ],
        ),
        out_shape=[jax.ShapeDtypeStruct(shape, array.dtype) for _ in starts],
        compiler_params=pltpu.CompilerParams(vmem_limit_bytes=61 * 1024 * 1024),
        cost_estimate=LITTLE,
        name="slices_for",
    )(table, *[array] * len(starts))


KIND, ONE, TWO, ONE_AT, TWO_AT = 0, 1, 2, 3, 5
COLUMNS = 7


def unit_kernel(index, offset, pieces, bright_at, homes, tab_ref, *refs):
    arrays = []
    for entries in pieces:
        found = []
        for count, start, number in entries:
            parts = (refs[0].at[0], refs[0].at[1]) if count == 1 else refs[:2]
            found.append((parts, start, number))
            refs = refs[count:]
        arrays.append(found)
    vis_refs, (keep_one_ref, keep_two_ref) = refs[:homes], refs[homes : homes + 2]
    refs = refs[homes + 2 :]
    columns_ref = None
    if bright_at is None:
        columns_ref, refs = refs[0], refs[1:]
    out_refs, grad_ref = refs[:homes], refs[homes]
    refs = refs[homes + 1 :]
    if bright_at is not None:
        columns_ref, refs = refs[0], refs[1:]
    total_ref, one_ref, two_ref, vis_ref = refs
    step = pl.program_id(0)
    slot = tab_ref[0] + index
    sources, span = one_ref.shape[1:]

    def entry(column):
        return tab_ref[offset + step * COLUMNS + column]

    def load(target, at):
        for n, found in enumerate(arrays):

            @pl.when(entry(at) == n)
            def _(found=found):
                place = entry(at + 1)
                for parts, start, number in found:
                    rows = pl.ds(pl.multiple_of(place * number, number), number)
                    for part in (0, 1):
                        target[part, pl.ds(start, number)] = parts[part][rows]

    if bright_at is not None:

        @pl.when(step == 0)
        def _():
            for parts, start, number in arrays[0]:
                lines = parts[0][pl.ds(bright_at * number, BRIGHT_ROWS)].astype(jnp.float32)
                lanes = lax.broadcasted_iota(jnp.int32, (number, span), 1)
                rows = lax.broadcasted_iota(jnp.int32, (number, span), 0)
                for n in range(columns_ref.shape[0]):
                    line = jnp.where(lanes == rows, lines[n : n + 1, :], 0.0)
                    column = jnp.sum(line, axis=1, keepdims=True)
                    columns_ref[n, pl.ds(start, number)] = jnp.broadcast_to(column, (number, 128))

    def dot(a, b):
        return lax.dot_general(a, b, (((1,), (0,)), ((), ())), preferred_element_type=jnp.float32)

    def scaled_of(re, im):
        column = jnp.concatenate([columns_ref[index].astype(jnp.bfloat16)] * (span // 128), 1)
        return re * column, im * column

    def outer(a, b):
        row_ids = lax.broadcasted_iota(jnp.int32, a.shape, 0)
        a = jnp.where(row_ids == slot, a, 0.0)
        return lax.dot_general(a, b, (((0,), (0,)), ((), ())), preferred_element_type=jnp.float32)

    def cross(a_re, a_im, b_re, b_im):
        lhs = jnp.concatenate([a_re, a_im], 0).T
        rhs = jnp.concatenate(
            [jnp.concatenate([b_re, -b_im], 1), jnp.concatenate([b_im, b_re], 1)], 0
        )
        both = dot(lhs, rhs)
        return both[:, :span], both[:, span:]

    def pull(re, im, res_re, res_im, sign):
        lhs = jnp.concatenate([re, im], 1)
        rhs = jnp.concatenate(
            [
                jnp.concatenate([res_re, res_im], 1),
                jnp.concatenate([res_im, -res_re] if sign == 1 else [-res_im, res_re], 1),
            ],
            0,
        )
        both = dot(lhs, rhs)
        return both[:, :span], both[:, span:]

    def add_grad(value):
        folded = value[:, :128]
        for start in range(128, span, 128):
            folded = folded + value[:, start : start + 128]
        total_ref[...] += folded

    each = pl.num_programs(0) // homes

    def put(res_re, res_im):
        for home, out_ref in enumerate(out_refs):

            @pl.when(step // each == home)
            def _(out_ref=out_ref):
                out_ref[0, 0] = res_re
                out_ref[0, 1] = res_im

    @pl.when(step == 0)
    def _():
        total_ref[...] = jnp.zeros_like(total_ref)

    load(one_ref, ONE_AT)
    load(two_ref, TWO_AT)
    for home, home_ref in enumerate(vis_refs):

        @pl.when(step // each == home)
        def _(home_ref=home_ref):
            vis_ref[...] = home_ref[0, 0]

    @pl.when(entry(KIND) == 0)
    def _():
        one_re, one_im, two_re, two_im = one_ref[0], one_ref[1], two_ref[0], two_ref[1]
        pred_re, pred_im = cross(*scaled_of(one_re, one_im), two_re, two_im)
        weights = outer(keep_one_ref[...], keep_two_ref[...])
        res_re = (weights * (vis_ref[0].astype(jnp.float32) - pred_re)).astype(jnp.bfloat16)
        res_im = (weights * (vis_ref[1].astype(jnp.float32) - pred_im)).astype(jnp.bfloat16)
        put(res_re, res_im)
        sum_re, sum_im = pull(one_re, one_im, res_re, res_im, 1)
        add_grad(sum_re * two_re.astype(jnp.float32) - sum_im * two_im.astype(jnp.float32))

    @pl.when(entry(KIND) == 1)
    def _():
        one_re, one_im, two_re, two_im = one_ref[0], one_ref[1], two_ref[0], two_ref[1]
        row_ids = lax.broadcasted_iota(jnp.int32, (span, span), 0)
        col_ids = lax.broadcasted_iota(jnp.int32, (span, span), 1)
        upper = row_ids < col_ids
        lower = row_ids > col_ids
        first_re, first_im = cross(*scaled_of(one_re, one_im), one_re, one_im)
        second_re, second_im = cross(two_re, two_im, *scaled_of(two_re, two_im))
        keep_one = keep_one_ref[...]
        keep_two = keep_two_ref[...]
        weights = jnp.where(upper, outer(keep_one, keep_one), 0.0) + jnp.where(
            lower, outer(keep_two, keep_two), 0.0
        )
        vis_re = vis_ref[0].astype(jnp.float32)
        vis_im = vis_ref[1].astype(jnp.float32)
        res_re = (weights * (vis_re - jnp.where(upper, first_re, second_re))).astype(jnp.bfloat16)
        res_im = (weights * (vis_im - jnp.where(upper, first_im, -second_im))).astype(jnp.bfloat16)
        put(res_re, res_im)
        none = jnp.zeros_like(res_re)
        sum_re, sum_im = pull(
            one_re, one_im, jnp.where(upper, res_re, none), jnp.where(upper, res_im, none), 1
        )
        add_grad(sum_re * one_re.astype(jnp.float32) - sum_im * one_im.astype(jnp.float32))
        sum_re, sum_im = pull(
            two_re, two_im, jnp.where(lower, res_re, none), jnp.where(lower, res_im, none), -1
        )
        add_grad(sum_re * two_re.astype(jnp.float32) + sum_im * two_im.astype(jnp.float32))

    @pl.when(step == pl.num_programs(0) - 1)
    def _():
        grad_ref[...] = jnp.sum(total_ref[...].T, axis=0, keepdims=True)


def unit_work(index, offset, table, pieces, vis, keep, bright):
    units_dev, _, _, span, _ = vis[0].shape
    slots = keep.shape[0]
    sources = sum(number for _, _, number in pieces[0])
    count = units_dev * len(vis)
    arrays = [array for piece in pieces for entry, _, _ in piece for array in entry]

    def at(tab, step, column):
        return tab[offset + step * COLUMNS + column]

    def unit(step, home):
        return jnp.clip(step - home * units_dev, 0, units_dev - 1)

    in_specs = [full(array) for array in arrays]
    for home, array in enumerate(vis):
        if array.shape[1] == slots:
            slot = lambda tab: tab[0] + index
        else:
            slot = lambda tab: index
        in_specs.append(
            pl.BlockSpec(
                (1, 1, 2, span, span),
                lambda u, tab, home=home, slot=slot: (unit(u, home), slot(tab), 0, 0, 0),
            )
        )
    in_specs += [
        pl.BlockSpec((slots, span), lambda u, tab: (0, at(tab, u, ONE))),
        pl.BlockSpec((slots, span), lambda u, tab: (0, at(tab, u, TWO))),
    ]
    operands = [table, *arrays, *vis, keep, keep]
    bright_at = None
    if isinstance(bright, int):
        first = pieces[0][0]
        bright_at = (first[0][0].shape[1] - BRIGHT_ROWS) // first[2]
    else:
        in_specs.append(full(bright))
        operands.append(bright)
    out_specs = [
        pl.BlockSpec((1, 2, span, span), lambda u, tab, home=home: (unit(u, home), 0, 0, 0))
        for home in range(len(vis))
    ]
    out_shapes = [jax.ShapeDtypeStruct((units_dev, 2, span, span), jnp.bfloat16) for _ in vis]
    out_specs.append(pl.BlockSpec((1, sources), lambda u, tab: (0, 0)))
    out_shapes.append(jax.ShapeDtypeStruct((1, sources), jnp.float32))
    if bright_at is not None:
        out_specs.append(pl.BlockSpec((bright, sources, 128), lambda u, tab: (0, 0, 0)))
        out_shapes.append(jax.ShapeDtypeStruct((bright, sources, 128), jnp.float32))
    kinds = [[(len(entry), start, number) for entry, start, number in piece] for piece in pieces]
    return pl.pallas_call(
        functools.partial(unit_kernel, index, offset, kinds, bright_at, len(vis)),
        grid_spec=pltpu.PrefetchScalarGridSpec(
            num_scalar_prefetch=1,
            grid=(count,),
            in_specs=in_specs,
            out_specs=out_specs,
            scratch_shapes=[
                pltpu.VMEM((sources, 128), jnp.float32),
                pltpu.VMEM((2, sources, span), jnp.bfloat16),
                pltpu.VMEM((2, sources, span), jnp.bfloat16),
                pltpu.VMEM((2, span, span), jnp.bfloat16),
            ],
        ),
        out_shape=out_shapes,
        compiler_params=pltpu.CompilerParams(vmem_limit_bytes=61 * 1024 * 1024),
        cost_estimate=LITTLE,
        name="unit_work",
    )(*operands)


def put_kernel(sources, tab_ref, *refs):
    out_ref = refs[-1]
    for step, (which, row) in enumerate(sources):

        @pl.when(pl.program_id(0) == step)
        def _(which=which, row=row):
            out_ref[0, 0] = refs[which][...] if row is None else refs[which][row]


def put_residuals(sources, arrays, offset, table, shape, residual):
    span = shape[-1]
    operands = [table, *arrays]
    in_specs = [full(array) for array in arrays]
    aliases = {}
    if residual is not None:
        aliases = {len(operands): 0}
        operands.append(residual)
        in_specs.append(pl.BlockSpec(memory_space=pl.ANY))
    return pl.pallas_call(
        functools.partial(put_kernel, sources),
        grid_spec=pltpu.PrefetchScalarGridSpec(
            num_scalar_prefetch=1,
            grid=(len(sources),),
            in_specs=in_specs,
            out_specs=pl.BlockSpec(
                (1, 1, 2, span, span),
                lambda n, tab: (tab[offset + 2 * n], tab[offset + 2 * n + 1], 0, 0, 0),
            ),
        ),
        out_shape=jax.ShapeDtypeStruct(shape, jnp.bfloat16),
        input_output_aliases=aliases,
        compiler_params=pltpu.CompilerParams(vmem_limit_bytes=61 * 1024 * 1024),
        cost_estimate=LITTLE,
        name="put_residuals",
    )(*operands)


class Routes:
    def __init__(self, planes, width, units, share):
        count = planes * width
        blocks = int(units[:, :2].max()) + 1
        self.width = width
        self.units_dev = units_dev = units.shape[0] // count
        ring = [0] + list(range(1, planes, 2)) + list(range(planes - 2, 0, -2))

        def along(step):
            at = {plane: ring[(n + step) % planes] for n, plane in enumerate(ring)}
            return [(t, at[t // width] * width + t % width) for t in range(count)]

        self.onward = along(1)
        self.backward = along(-1)
        self.opposite = along(2)
        self.partner = [[(t, t ^ m) for t in range(count)] for m in range(width)]

        half = blocks // 2
        self.full = [list(range(blocks))]
        self.pieces = [list(range(half)), list(range(half, blocks))]

        def table_of(pieces, order):
            rows = np.zeros((count, len(order), units_dev, COLUMNS), np.int32)
            for t in range(count):
                for n, m in enumerate(order):
                    for k in range(units_dev):
                        one, two, kind = units[(t ^ m) * units_dev + k].tolist()
                        at = [
                            (p, piece.index(b))
                            for b in (one, two)
                            for p, piece in enumerate(pieces)
                            if b in piece
                        ]
                        rows[t, n, k] = [kind, one, two, *at[0], *at[1]]
            return rows

        def targets(index):
            rows = np.zeros((count, len(self.order), units_dev, 2), np.int32)
            for t in range(count):
                for n, m in enumerate(self.order):
                    for k in range(units_dev):
                        rows[t, n, k] = k, (t % width ^ m) * share + index
            return rows

        self.order = list(range(width // 2, width)) + list(range(width // 2 - 1, -1, -1))
        starts = np.array([[(t % width ^ m) * share for m in range(width)] for t in range(count)])
        parts = [starts, table_of(self.full, self.order), table_of(self.pieces, self.order)]
        parts += [targets(n) for n in range(share)]
        parts = [part.reshape(count, -1) for part in parts]
        ends = np.cumsum([part.shape[1] for part in parts]).tolist()
        self.table = np.concatenate(parts, 1).astype(np.int32)
        self.steps = ends[:2]
        self.targets = ends[2:]
        self.steps_per_home = units_dev * COLUMNS
        self.targets_per_home = units_dev * 2


def plain_program(visibility, beam, antenna_uvw, small, keep):
    units_dev, slots, _, span, _ = visibility.shape
    _, _, per_group, antennas = beam.shape
    blocks = antennas // span
    tile_index = lax.axis_index("tile")
    units = unit_table(blocks)
    none = np.zeros_like(units[:, 0])
    table = np.stack([units[:, 2], units[:, 0], units[:, 1], none, units[:, 0], none, units[:, 1]], 1)
    table = table.astype(np.int32).reshape(-1, units_dev * COLUMNS)
    table = np.pad(table, ((0, 0), (1, 0)))
    table = lax.dynamic_index_in_dim(jnp.asarray(table), tile_index, 0, keepdims=False)
    columns = None
    residuals, grads = [], []
    for slot in range(slots):
        (owned,) = build_factors(
            (slot, slots, per_group),
            table,
            beam,
            [],
            antenna_uvw,
            [small],
            [list(range(blocks))],
            span,
            0 if slot else BRIGHT_ROWS,
            small[0].shape[1],
        )
        everyone = lax.all_gather(owned, "tile", axis=0)
        rows = blocks * per_group
        if columns is None:
            bright = everyone[:, 0, rows : rows + slots, :per_group].astype(jnp.float32)
            bright = jnp.swapaxes(bright, 0, 1).reshape(slots, -1, 1)
            columns = jnp.broadcast_to(bright, bright.shape[:2] + (128,))
        factors = everyone[:, :, :rows].reshape(-1, 2, blocks, per_group, span)
        number = factors.shape[0] * per_group
        factors = factors.transpose(1, 2, 0, 3, 4).reshape(2, blocks * number, span)
        residual, grad = unit_work(
            slot, 1, table, [[((factors,), 0, number)]], [visibility], keep, columns
        )
        residuals.append(residual)
        grads.append(grad)
    summed = lax.psum_scatter(jnp.concatenate(grads, 0), "tile", scatter_dimension=1, tiled=True)
    return jnp.stack(residuals, 1), summed


OWN, OWN_NEAR, OWN_FAR, REST, REST_NEAR, REST_FAR = 0, 1, 3, 5, 6, 8
BEAM, SIDE_BEAMS, LATER_BEAMS, VIS, LATER = 10, 12, 15, 19, 23
PIECE_NEAR, PIECE_FAR = (24, 26), (28, 30)
WORK, HOME, PUT, LATER_WORK, LATER_HOME, PUT_NEAR, PUT_LAST = 32, 35, 38, 40, 43, 46, 47
SUM_PLANES, SUM_PLANE = 48, 51
GATES = {
    3: (0,),
    5: (0, 2),
    6: (1,),
    7: (1, 2),
    14: (13,),
    19: (2, 18),
    20: (17, 14, 7),
    21: (3, 4, 5, 13, 14, 16, 17),
    23: (4,),
    24: (16, 9, 17),
    25: (6, 9, 16, 17, 18, 23),
    26: (16, 9),
    27: (8,),
    28: (9, 22),
    31: (8, 25, 27, 37),
    33: (32, 25, 23),
    35: (33, 8, 22, 23, 24, 25, 26, 28, 29),
    40: (32, 33, 36, 37, 27, 28, 29, 30, 31),
    49: (40, 36, 44),
    38: (24, 25),
    30: (8, 26),
    43: (32,),
    44: (26, 30, 31),
    36: (8, 9, 32),
    4: (0,),
    13: (0,),
    41: (40, 33),
    48: (35,),
    51: (49, 31),
    9: (17,),
    50: (35, 30, 31),
    45: (40, 36),
    52: (48,),
    29: (9, 28),
}


def plane_program(routes, visibility, beam, antenna_uvw, small, keep):
    units_dev, slots, _, span, _ = visibility.shape
    per_group = beam.shape[2]
    width = routes.width
    share = slots // width
    group = width * per_group
    tile_index = lax.axis_index("tile")
    mine = tile_index % width
    table = lax.dynamic_index_in_dim(jnp.asarray(routes.table), tile_index, 0, keepdims=False)
    done = {}

    def gated(step, value):
        earlier = [done[gate] for gate in GATES.get(step, ())]
        return lax.optimization_barrier((value, *earlier))[0] if earlier else value

    def send(step, value, pairs):
        done[step] = lax.ppermute(gated(step, value), "tile", pairs)
        return done[step]

    def near(step, piece):
        return [send(step, piece, routes.onward), send(step + 1, piece, routes.backward)]

    def far(step, sides):
        return [
            send(step, sides[0][0], routes.onward),
            send(step + 1, sides[1][1], routes.backward),
        ]

    def entries(piece, sides, halves, first, number):
        found = [(piece,), (sides[0],), (sides[1],), tuple(halves)]
        return [(arrays, n * group + first, number) for n, arrays in enumerate(found)]

    def build(step, index, own_beam, messages, smalls, pieces, bright_rows):
        built = build_factors(
            (index, share, per_group),
            gated(step, table),
            own_beam,
            messages,
            antenna_uvw,
            smalls,
            pieces,
            span,
            bright_rows,
            small[0].shape[1],
        )
        done[step] = built[0]
        return built

    core, *side = range(1, width)
    (message,) = messages_for(beam, 0, [core], small, gated(BEAM, table))
    message = send(BEAM + 1, message, routes.partner[core])
    (own,) = build(OWN, 0, beam, [message], [small, message], routes.full, BRIGHT_ROWS)
    own_sides = near(OWN_NEAR, own)
    messages = messages_for(beam, 0, side, small, gated(SIDE_BEAMS, table))
    messages = [
        send(SIDE_BEAMS + 1 + n, messages[n], routes.partner[m]) for n, m in enumerate(side)
    ]
    own_far = far(OWN_FAR, own_sides)
    (rest,) = build(REST, 0, None, messages, messages, routes.full, BRIGHT_ROWS)
    rest_sides = near(REST_NEAR, rest)

    later = messages_for(beam, 1, [core, *side], None, gated(LATER_BEAMS, table))
    later = [send(LATER_BEAMS + m, later[m - 1], routes.partner[m]) for m in (core, *side)]
    vis = slices_for(
        visibility, 1, share, [(m, 0) for m in (core, *side)], gated(VIS, table)
    )
    vis = [visibility] + [send(VIS + m, vis[m - 1], routes.partner[m]) for m in (core, *side)]
    later_pieces = build(
        LATER, 1, beam, later, [small, message, *messages], routes.pieces, 0
    )
    rest_far = far(REST_FAR, rest_sides)
    near_0 = near(PIECE_NEAR[0], later_pieces[0])
    near_1 = near(PIECE_NEAR[1], later_pieces[1])
    far_0 = far(PIECE_FAR[0], near_0)

    grads = []

    def work(index, step, home_step, ready, bright):
        arrived, total = [], None
        for n, homes in enumerate([routes.order[:1], routes.order[1:]]):
            made = unit_work(
                index,
                routes.steps[index] + len(arrived) * routes.steps_per_home,
                gated(step + n, table),
                ready,
                [vis[m] for m in homes],
                keep,
                bright,
            )
            results, grad = made[: len(homes)], made[len(homes)]
            if isinstance(bright, int):
                bright = made[-1]
            done[step + n] = grad
            total = grad if total is None else total + grad
            arrived += [
                send(home_step - 1 + m, part, routes.partner[m]) if m else part
                for m, part in zip(homes, results)
            ]
        grads.append(total)
        return arrived, bright

    def put(step, homes, arrays, index, residual):
        rows = [(n, k) for n in range(len(arrays)) for k in range(units_dev)]
        offset = routes.targets[index] + homes * routes.targets_per_home
        done[step] = put_residuals(
            rows, arrays, offset, gated(step, table), visibility.shape, residual
        )
        return done[step]

    number = group // 2
    pieces = entries(own, own_sides, own_far, 0, number)
    pieces += entries(rest, rest_sides, rest_far, number, number)
    arrived, columns = work(0, WORK, HOME, [pieces], share)
    far_1 = far(PIECE_FAR[1], near_1)
    residual = put(PUT, 0, arrived, 0, None)
    ready = [
        entries(piece, sides, halves, 0, group)
        for piece, sides, halves in zip(later_pieces, (near_0, near_1), (far_0, far_1))
    ]
    arrived, _ = work(1, LATER_WORK, LATER_HOME, ready, columns)

    partial = jnp.concatenate(grads, 0)
    parts = [partial[:, n * group : (n + 1) * group] for n in range(4)]
    plane_sum = (parts[0] + send(SUM_PLANES, parts[3], routes.opposite)) + (
        send(SUM_PLANES + 1, parts[1], routes.backward)
        + send(SUM_PLANES + 2, parts[2], routes.onward)
    )
    sums = [plane_sum[:, m * per_group : (m + 1) * per_group] for m in range(width)]
    sums = [sums[0]] + [
        send(SUM_PLANE - 1 + m, sums[m], routes.partner[m]) for m in (core, *side)
    ]
    sums = jnp.stack(sums, 0)
    ids = jnp.arange(width, dtype=jnp.int32)
    here = jnp.bitwise_xor(ids[:, None], mine) == ids[None, :]
    summed = jnp.sum(jnp.where(here[:, :, None, None], sums[None], 0.0), axis=1)
    summed = summed.reshape(slots, per_group)

    residual = put(PUT_NEAR, 2, arrived[2:], 1, residual)
    residual = put(PUT_LAST, 0, arrived[:2], 1, residual)
    return residual, summed


def per_device(
    visibility, station_beam, antenna_uvw, source_dirs, source_flux, visible_list, antenna_flags
):
    span = visibility.shape[4]
    antennas = station_beam.shape[3]
    small = (source_dirs, source_flux.astype(jnp.float32)[None], visible_list)
    keep = 1.0 - antenna_flags.astype(jnp.float32)
    arguments = (visibility, station_beam, antenna_uvw, small, keep)
    if lax.axis_size("tile") == 16:
        routes = Routes(4, 4, unit_table(antennas // span), visibility.shape[1] // 4)
        residual, summed = plane_program(routes, *arguments)
    else:
        residual, summed = plain_program(*arguments)
    return (residual, summed * (-1.0 / (8.0 * antennas)))


def solution(mesh):
    return jax.shard_map(
        per_device,
        mesh=mesh,
        in_specs=(
            P("tile", "grp", None, None, None),
            P("grp", None, "tile", None),
            P("grp", None, None),
            P(None, "tile"),
            P(("grp", "tile")),
            P(None, "tile"),
            P("grp", None),
        ),
        out_specs=(P("tile", "grp", None, None, None), P("grp", "tile")),
        check_vma=False,
    )
```

```python
import functools

import jax
import jax.numpy as jnp
import numpy as np
from jax import lax
from jax.experimental import pallas as pl
from jax.experimental.pallas import tpu as pltpu
from jax.sharding import PartitionSpec as P


def unit_table(block_count):
    first_list = []
    second_list = []
    diag_list = []
    for row_block in range(block_count):
        for col_block in range(row_block + 1, block_count):
            first_list.append(row_block)
            second_list.append(col_block)
            diag_list.append(0)
    for pair_index in range(block_count // 2):
        first_list.append(2 * pair_index)
        second_list.append(2 * pair_index + 1)
        diag_list.append(1)
    return np.stack([first_list, second_list, diag_list], 1).astype(np.int32)


def turn_polynomials():
    nodes = 0.125 + 0.125 * np.cos(np.pi * (np.arange(64) + 0.5) / 64)
    root = np.sqrt(nodes)
    fit = np.polynomial.Polynomial.fit
    sine = fit(nodes, np.sin(2 * np.pi * root) / root, 7, domain=[0, 0.25]).convert()
    cosine = fit(nodes, np.cos(2 * np.pi * root), 8, domain=[0, 0.25]).convert()
    return [float(c) for c in sine.coef], [float(c) for c in cosine.coef]


def horner(coefs, x):
    total = coefs[-1]
    for coef in coefs[-2::-1]:
        total = total * x + coef
    return total


def build_kernel(sets, slot_ids, pieces, bright_rows, width, tab_ref, *refs):
    refs, scratch_ref = refs[:-1], refs[-1]
    uvw_ref, outs = refs[-1 - len(pieces)], refs[-len(pieces) :]
    per_group = sets[0][0]
    span = outs[0].shape[2]
    count = len(sets) * per_group
    sin_coefs, cos_coefs = turn_polynomials()
    brights = []
    for part, (_, beam_at, small_at) in enumerate(sets):
        beam_ref = refs[beam_at]
        if beam_ref.shape[0] == 1:
            beam = [beam_ref.at[0, 0], beam_ref.at[0, 1]]
        else:
            beam = [beam_ref.at[pl.ds(n * per_group, per_group)] for n in (0, 1)]
        if refs[small_at].dtype == jnp.float32:
            small = small_rows(scratch_ref, *refs[small_at : small_at + 3])
        else:
            small = unsplit(refs[small_at], 2 * per_group, width)
        lanes = lax.broadcasted_iota(jnp.int32, (per_group, width), 1)
        rows = lax.broadcasted_iota(jnp.int32, (per_group, width), 0)

        def pick(chosen, row):
            return jnp.sum(jnp.where(chosen, small[row : row + 1, :], 0.0), axis=1, keepdims=True)

        def chosen_at(index):
            here = lax.broadcasted_iota(jnp.int32, small.shape, 0) == LIST_ROW + tab_ref[0] + index
            line = jnp.sum(jnp.where(here, small, 0.0), axis=0, keepdims=True)
            listed = jnp.sum(jnp.where(lanes == rows, line, 0.0), axis=1, keepdims=True)
            return listed.astype(jnp.int32) == lanes

        group = part * per_group
        if bright_rows:
            columns = lax.broadcasted_iota(jnp.int32, (per_group, span), 1)
            numbers = lax.broadcasted_iota(jnp.int32, (per_group, span), 0) + group
            for index in range(slot_ids[1]):
                flux = pick(chosen_at(index), 2)
                line = jnp.sum(jnp.where(columns == numbers, flux, 0.0), axis=0, keepdims=True)
                if part == 0:
                    brights.append(line)
                else:
                    brights[index] += line
        chosen = chosen_at(slot_ids[0])
        east = pick(chosen, 0)
        north = pick(chosen, 1)
        depth = jnp.sqrt(1.0 - east * east - north * north) - 1.0
        for out_ref, piece in zip(outs, pieces):
            for place, block in enumerate(piece):
                cols = pl.ds(block * span, span)
                delay = (
                    uvw_ref[0, 0:1, cols] * east
                    + uvw_ref[0, 1:2, cols] * north
                    + uvw_ref[0, 2:3, cols] * depth
                )
                turn = delay - jnp.floor(delay + 0.5)
                square = turn * turn
                sine = horner(sin_coefs, square) * turn
                cosine = horner(cos_coefs, square)
                real = beam[0][:, cols].astype(jnp.float32)
                imag = beam[1][:, cols].astype(jnp.float32)
                at = pl.ds(place * count + group, per_group)
                out_ref[0, at] = (real * cosine + imag * sine).astype(jnp.bfloat16)
                out_ref[1, at] = (imag * cosine - real * sine).astype(jnp.bfloat16)
    if bright_rows:
        padding = jnp.zeros((bright_rows - len(brights), span), jnp.float32)
        block = jnp.concatenate(brights + [padding], 0).astype(jnp.bfloat16)
        for part in (0, 1):
            outs[0][part, pl.ds(len(pieces[0]) * count, bright_rows)] = block


def small_rows(rows_ref, dirs_ref, flux_ref, list_ref):
    rows_ref[...] = jnp.zeros_like(rows_ref)
    rows_ref[0:2, 0 : dirs_ref.shape[1]] = dirs_ref[...]
    rows_ref[2:3, 0 : flux_ref.shape[1]] = flux_ref[...]
    slots, count = list_ref.shape
    rows_ref[LIST_ROW : LIST_ROW + slots, 0:count] = list_ref[...].astype(jnp.float32)
    return rows_ref[...]


LIST_ROW = 8
SMALL_ROWS = 16


def unsplit(message_ref, start, width):
    rows = pl.ds(start, SMALL_ROWS)
    terms = [message_ref[rows, pl.ds(n * width, width)].astype(jnp.float32) for n in range(3)]
    return (terms[0] + terms[1]) + terms[2]


BRIGHT_ROWS = 16


def build_factors(
    slot_ids, table, beam, messages, antenna_uvw, smalls, pieces, span, bright_rows, small_width
):
    slots, _, antennas = antenna_uvw.shape
    per_group = slot_ids[2]
    index = slot_ids[0]
    whole = pl.BlockSpec(memory_space=pltpu.VMEM)
    operands, in_specs, sets = [], [], []
    if beam is not None:
        operands.append(beam)
        in_specs.append(
            pl.BlockSpec((1, 2, per_group, antennas), lambda n, tab: (tab[0] + index, 0, 0, 0))
        )
    operands += messages
    beams = len(operands)
    for n, small in enumerate(smalls):
        at = next((k for k, known in enumerate(operands) if known is small), len(operands))
        if at == len(operands):
            operands += small if isinstance(small, tuple) else [small]
        sets.append((per_group, n, at))
    in_specs += [whole] * (len(operands) - len(in_specs))
    in_specs.append(pl.BlockSpec((1, 3, antennas), lambda n, tab: (tab[0] + index, 0, 0)))
    count = beams * per_group
    shapes = [
        (2, len(piece) * count + (0 if n else bright_rows), span) for n, piece in enumerate(pieces)
    ]
    return pl.pallas_call(
        functools.partial(build_kernel, sets, slot_ids, pieces, bright_rows, small_width),
        grid_spec=pltpu.PrefetchScalarGridSpec(
            num_scalar_prefetch=1,
            grid=(1,),
            in_specs=in_specs,
            out_specs=[whole] * len(pieces),
            scratch_shapes=[pltpu.VMEM((SMALL_ROWS, small_width), jnp.float32)],
        ),
        out_shape=[jax.ShapeDtypeStruct(shape, jnp.bfloat16) for shape in shapes],
        compiler_params=pltpu.CompilerParams(vmem_limit_bytes=16 * 1024 * 1024),
        cost_estimate=LITTLE,
        name="build_factors",
    )(table, *operands, antenna_uvw)


LITTLE = pl.CostEstimate(flops=1, bytes_accessed=1, transcendentals=0)


def message_kernel(count, with_small, tab_ref, *refs):
    beams, refs = refs[:count], refs[count:]
    if with_small:
        smalls, outs, scratch_ref = refs[:3], refs[3:-1], refs[-1]
        terms = []
        rest = small_rows(scratch_ref, *smalls)
        width = rest.shape[1]
        for _ in range(3):
            terms.append(rest.astype(jnp.bfloat16))
            rest = rest - terms[-1].astype(jnp.float32)
    else:
        outs = refs
    for beam_ref, out_ref in zip(beams, outs):
        per_group = beam_ref.shape[2]
        for part in (0, 1):
            out_ref[pl.ds(part * per_group, per_group)] = beam_ref[0, part]
        if with_small:
            rows = pl.ds(2 * per_group, SMALL_ROWS)
            out_ref[rows] = jnp.zeros((SMALL_ROWS, out_ref.shape[1]), jnp.bfloat16)
            for n, term in enumerate(terms):
                out_ref[rows, pl.ds(n * width, width)] = term


def messages_for(beam, index, others, small, table):
    _, _, per_group, antennas = beam.shape
    smalls = small or ()
    rows = 2 * per_group + (SMALL_ROWS if smalls else 0)
    whole = pl.BlockSpec(memory_space=pltpu.VMEM)
    scratch = []
    if smalls:
        scratch.append(pltpu.VMEM((SMALL_ROWS, smalls[0].shape[1]), jnp.float32))
    return pl.pallas_call(
        functools.partial(message_kernel, len(others), bool(smalls)),
        grid_spec=pltpu.PrefetchScalarGridSpec(
            num_scalar_prefetch=1,
            grid=(1,),
            in_specs=[
                pl.BlockSpec(
                    (1, 2, per_group, antennas), lambda n, tab, m=m: (tab[m] + index, 0, 0, 0)
                )
                for m in others
            ]
            + [whole for _ in smalls],
            out_specs=[whole for _ in others],
            scratch_shapes=scratch,
        ),
        out_shape=[jax.ShapeDtypeStruct((rows, antennas), jnp.bfloat16) for _ in others],
        cost_estimate=LITTLE,
        name="messages_for",
    )(table, *[beam] * len(others), *smalls)


def slice_kernel(count, tab_ref, *refs):
    for source, target in zip(refs[:count], refs[count:]):
        target[...] = source[...]


def slices_for(array, axis, size, starts, table):
    lead = axis > 0
    shape = array.shape[:axis] + (size,) + array.shape[axis + 1 :]
    block = (1,) + shape[1:] if lead else shape
    rest = (0,) * (array.ndim - axis - 1)
    return pl.pallas_call(
        functools.partial(slice_kernel, len(starts)),
        grid_spec=pltpu.PrefetchScalarGridSpec(
            num_scalar_prefetch=1,
            grid=(shape[0] if lead else 1,),
            in_specs=[
                pl.BlockSpec(
                    block,
                    lambda n, tab, start=start, shift=shift: (
                        *((n,) if lead else ()),
                        tab[start] // size + shift,
                        *rest,
                    ),
                )
                for start, shift in starts
            ],
            out_specs=[
                pl.BlockSpec(block, lambda n, tab: (n,) + (0,) * (array.ndim - 1)) for _ in starts
            ],
        ),
        out_shape=[jax.ShapeDtypeStruct(shape, array.dtype) for _ in starts],
        cost_estimate=LITTLE,
        name="slices_for",
    )(table, *[array] * len(starts))


KIND, ONE, TWO, ONE_AT, TWO_AT = 0, 1, 2, 3, 5
COLUMNS = 7


def unit_kernel(index, offset, pieces, bright_at, homes, tab_ref, *refs):
    arrays = []
    for entries in pieces:
        found = []
        for count, start, number in entries:
            parts = (refs[0].at[0], refs[0].at[1]) if count == 1 else refs[:2]
            found.append((parts, start, number))
            refs = refs[count:]
        arrays.append(found)
    vis_refs, (keep_one_ref, keep_two_ref) = refs[:homes], refs[homes : homes + 2]
    refs = refs[homes + 2 :]
    columns_ref = None
    if bright_at is None:
        columns_ref, refs = refs[0], refs[1:]
    out_refs, grad_ref = refs[:homes], refs[homes]
    refs = refs[homes + 1 :]
    if bright_at is not None:
        columns_ref, refs = refs[0], refs[1:]
    total_ref, one_ref, two_ref, vis_ref = refs
    step = pl.program_id(0)
    slot = tab_ref[0] + index
    sources, span = one_ref.shape[1:]

    def entry(column):
        return tab_ref[offset + step * COLUMNS + column]

    def load(target, at):
        for n, found in enumerate(arrays):

            @pl.when(entry(at) == n)
            def _(found=found):
                place = entry(at + 1)
                for parts, start, number in found:
                    rows = pl.ds(pl.multiple_of(place * number, number), number)
                    for part in (0, 1):
                        target[part, pl.ds(start, number)] = parts[part][rows]

    if bright_at is not None:

        @pl.when(step == 0)
        def _():
            for parts, start, number in arrays[0]:
                lines = parts[0][pl.ds(bright_at * number, BRIGHT_ROWS)].astype(jnp.float32)
                lanes = lax.broadcasted_iota(jnp.int32, (number, span), 1)
                rows = lax.broadcasted_iota(jnp.int32, (number, span), 0)
                for n in range(columns_ref.shape[0]):
                    line = jnp.where(lanes == rows, lines[n : n + 1, :], 0.0)
                    column = jnp.sum(line, axis=1, keepdims=True)
                    columns_ref[n, pl.ds(start, number)] = jnp.broadcast_to(column, (number, 128))

    def dot(a, b):
        return lax.dot_general(a, b, (((1,), (0,)), ((), ())), preferred_element_type=jnp.float32)

    def scaled_of(re, im):
        column = jnp.concatenate([columns_ref[index].astype(jnp.bfloat16)] * (span // 128), 1)
        return re * column, im * column

    def outer(a, b):
        row_ids = lax.broadcasted_iota(jnp.int32, a.shape, 0)
        a = jnp.where(row_ids == slot, a, 0.0)
        return lax.dot_general(a, b, (((0,), (0,)), ((), ())), preferred_element_type=jnp.float32)

    def cross(a_re, a_im, b_re, b_im):
        lhs = jnp.concatenate([a_re, a_im], 0).T
        rhs = jnp.concatenate(
            [jnp.concatenate([b_re, -b_im], 1), jnp.concatenate([b_im, b_re], 1)], 0
        )
        both = dot(lhs, rhs)
        return both[:, :span], both[:, span:]

    def pull(re, im, res_re, res_im, sign):
        lhs = jnp.concatenate([re, im], 1)
        rhs = jnp.concatenate(
            [
                jnp.concatenate([res_re, res_im], 1),
                jnp.concatenate([res_im, -res_re] if sign == 1 else [-res_im, res_re], 1),
            ],
            0,
        )
        both = dot(lhs, rhs)
        return both[:, :span], both[:, span:]

    def add_grad(value):
        folded = value[:, :128]
        for start in range(128, span, 128):
            folded = folded + value[:, start : start + 128]
        total_ref[...] += folded

    each = pl.num_programs(0) // homes

    def put(res_re, res_im):
        for home, out_ref in enumerate(out_refs):

            @pl.when(step // each == home)
            def _(out_ref=out_ref):
                out_ref[0, 0] = res_re
                out_ref[0, 1] = res_im

    @pl.when(step == 0)
    def _():
        total_ref[...] = jnp.zeros_like(total_ref)

    load(one_ref, ONE_AT)
    load(two_ref, TWO_AT)
    for home, home_ref in enumerate(vis_refs):

        @pl.when(step // each == home)
        def _(home_ref=home_ref):
            vis_ref[...] = home_ref[0, 0]

    @pl.when(entry(KIND) == 0)
    def _():
        one_re, one_im, two_re, two_im = one_ref[0], one_ref[1], two_ref[0], two_ref[1]
        pred_re, pred_im = cross(*scaled_of(one_re, one_im), two_re, two_im)
        weights = outer(keep_one_ref[...], keep_two_ref[...])
        res_re = (weights * (vis_ref[0].astype(jnp.float32) - pred_re)).astype(jnp.bfloat16)
        res_im = (weights * (vis_ref[1].astype(jnp.float32) - pred_im)).astype(jnp.bfloat16)
        put(res_re, res_im)
        sum_re, sum_im = pull(one_re, one_im, res_re, res_im, 1)
        add_grad(sum_re * two_re.astype(jnp.float32) - sum_im * two_im.astype(jnp.float32))

    @pl.when(entry(KIND) == 1)
    def _():
        one_re, one_im, two_re, two_im = one_ref[0], one_ref[1], two_ref[0], two_ref[1]
        row_ids = lax.broadcasted_iota(jnp.int32, (span, span), 0)
        col_ids = lax.broadcasted_iota(jnp.int32, (span, span), 1)
        upper = row_ids < col_ids
        lower = row_ids > col_ids
        first_re, first_im = cross(*scaled_of(one_re, one_im), one_re, one_im)
        second_re, second_im = cross(two_re, two_im, *scaled_of(two_re, two_im))
        keep_one = keep_one_ref[...]
        keep_two = keep_two_ref[...]
        weights = jnp.where(upper, outer(keep_one, keep_one), 0.0) + jnp.where(
            lower, outer(keep_two, keep_two), 0.0
        )
        vis_re = vis_ref[0].astype(jnp.float32)
        vis_im = vis_ref[1].astype(jnp.float32)
        res_re = (weights * (vis_re - jnp.where(upper, first_re, second_re))).astype(jnp.bfloat16)
        res_im = (weights * (vis_im - jnp.where(upper, first_im, -second_im))).astype(jnp.bfloat16)
        put(res_re, res_im)
        none = jnp.zeros_like(res_re)
        sum_re, sum_im = pull(
            one_re, one_im, jnp.where(upper, res_re, none), jnp.where(upper, res_im, none), 1
        )
        add_grad(sum_re * one_re.astype(jnp.float32) - sum_im * one_im.astype(jnp.float32))
        sum_re, sum_im = pull(
            two_re, two_im, jnp.where(lower, res_re, none), jnp.where(lower, res_im, none), -1
        )
        add_grad(sum_re * two_re.astype(jnp.float32) + sum_im * two_im.astype(jnp.float32))

    @pl.when(step == pl.num_programs(0) - 1)
    def _():
        grad_ref[...] = jnp.sum(total_ref[...].T, axis=0, keepdims=True)


def unit_work(index, offset, table, pieces, vis, keep, bright):
    units_dev, _, _, span, _ = vis[0].shape
    slots = keep.shape[0]
    sources = sum(number for _, _, number in pieces[0])
    count = units_dev * len(vis)
    whole = pl.BlockSpec(memory_space=pltpu.VMEM)
    arrays = [array for piece in pieces for entry, _, _ in piece for array in entry]

    def at(tab, step, column):
        return tab[offset + step * COLUMNS + column]

    def unit(step, home):
        return jnp.clip(step - home * units_dev, 0, units_dev - 1)

    in_specs = [whole] * len(arrays)
    for home, array in enumerate(vis):
        if array.shape[1] == slots:
            slot = lambda tab: tab[0] + index
        else:
            slot = lambda tab: index
        in_specs.append(
            pl.BlockSpec(
                (1, 1, 2, span, span),
                lambda u, tab, home=home, slot=slot: (unit(u, home), slot(tab), 0, 0, 0),
            )
        )
    in_specs += [
        pl.BlockSpec((slots, span), lambda u, tab: (0, at(tab, u, ONE))),
        pl.BlockSpec((slots, span), lambda u, tab: (0, at(tab, u, TWO))),
    ]
    operands = [table, *arrays, *vis, keep, keep]
    bright_at = None
    if isinstance(bright, int):
        first = pieces[0][0]
        bright_at = (first[0][0].shape[1] - BRIGHT_ROWS) // first[2]
    else:
        in_specs.append(whole)
        operands.append(bright)
    out_specs = [
        pl.BlockSpec((1, 2, span, span), lambda u, tab, home=home: (unit(u, home), 0, 0, 0))
        for home in range(len(vis))
    ]
    out_shapes = [jax.ShapeDtypeStruct((units_dev, 2, span, span), jnp.bfloat16) for _ in vis]
    out_specs.append(pl.BlockSpec((1, sources), lambda u, tab: (0, 0)))
    out_shapes.append(jax.ShapeDtypeStruct((1, sources), jnp.float32))
    if bright_at is not None:
        out_specs.append(pl.BlockSpec((bright, sources, 128), lambda u, tab: (0, 0, 0)))
        out_shapes.append(jax.ShapeDtypeStruct((bright, sources, 128), jnp.float32))
    kinds = [[(len(entry), start, number) for entry, start, number in piece] for piece in pieces]
    return pl.pallas_call(
        functools.partial(unit_kernel, index, offset, kinds, bright_at, len(vis)),
        grid_spec=pltpu.PrefetchScalarGridSpec(
            num_scalar_prefetch=1,
            grid=(count,),
            in_specs=in_specs,
            out_specs=out_specs,
            scratch_shapes=[
                pltpu.VMEM((sources, 128), jnp.float32),
                pltpu.VMEM((2, sources, span), jnp.bfloat16),
                pltpu.VMEM((2, sources, span), jnp.bfloat16),
                pltpu.VMEM((2, span, span), jnp.bfloat16),
            ],
        ),
        out_shape=out_shapes,
        compiler_params=pltpu.CompilerParams(vmem_limit_bytes=16 * 1024 * 1024),
        cost_estimate=LITTLE,
        name="unit_work",
    )(*operands)


def put_kernel(sources, tab_ref, *refs):
    out_ref = refs[-1]
    for step, (which, row) in enumerate(sources):

        @pl.when(pl.program_id(0) == step)
        def _(which=which, row=row):
            out_ref[0, 0] = refs[which][...] if row is None else refs[which][row]


def put_residuals(sources, arrays, offset, table, shape, residual):
    span = shape[-1]
    whole = pl.BlockSpec(memory_space=pltpu.VMEM)
    operands = [table, *arrays]
    in_specs = [whole] * len(arrays)
    aliases = {}
    if residual is not None:
        aliases = {len(operands): 0}
        operands.append(residual)
        in_specs.append(pl.BlockSpec(memory_space=pl.ANY))
    return pl.pallas_call(
        functools.partial(put_kernel, sources),
        grid_spec=pltpu.PrefetchScalarGridSpec(
            num_scalar_prefetch=1,
            grid=(len(sources),),
            in_specs=in_specs,
            out_specs=pl.BlockSpec(
                (1, 1, 2, span, span),
                lambda n, tab: (tab[offset + 2 * n], tab[offset + 2 * n + 1], 0, 0, 0),
            ),
        ),
        out_shape=jax.ShapeDtypeStruct(shape, jnp.bfloat16),
        input_output_aliases=aliases,
        compiler_params=pltpu.CompilerParams(vmem_limit_bytes=16 * 1024 * 1024),
        cost_estimate=LITTLE,
        name="put_residuals",
    )(*operands)


class Routes:
    def __init__(self, planes, width, units, share):
        count = planes * width
        blocks = int(units[:, :2].max()) + 1
        self.width = width
        self.units_dev = units_dev = units.shape[0] // count
        ring = [0] + list(range(1, planes, 2)) + list(range(planes - 2, 0, -2))

        def along(step):
            at = {plane: ring[(n + step) % planes] for n, plane in enumerate(ring)}
            return [(t, at[t // width] * width + t % width) for t in range(count)]

        self.onward = along(1)
        self.backward = along(-1)
        self.opposite = along(2)
        self.partner = [[(t, t ^ m) for t in range(count)] for m in range(width)]

        half = blocks // 2
        self.full = [list(range(blocks))]
        self.pieces = [list(range(half)), list(range(half, blocks))]

        def table_of(pieces, order):
            rows = np.zeros((count, len(order), units_dev, COLUMNS), np.int32)
            for t in range(count):
                for n, m in enumerate(order):
                    for k in range(units_dev):
                        one, two, kind = units[(t ^ m) * units_dev + k].tolist()
                        at = [
                            (p, piece.index(b))
                            for b in (one, two)
                            for p, piece in enumerate(pieces)
                            if b in piece
                        ]
                        rows[t, n, k] = [kind, one, two, *at[0], *at[1]]
            return rows

        def targets(index):
            rows = np.zeros((count, len(self.order), units_dev, 2), np.int32)
            for t in range(count):
                for n, m in enumerate(self.order):
                    for k in range(units_dev):
                        rows[t, n, k] = k, (t % width ^ m) * share + index
            return rows

        self.order = list(range(width // 2, width)) + list(range(width // 2 - 1, -1, -1))
        starts = np.array([[(t % width ^ m) * share for m in range(width)] for t in range(count)])
        parts = [starts, table_of(self.full, self.order), table_of(self.pieces, self.order)]
        parts += [targets(n) for n in range(share)]
        parts = [part.reshape(count, -1) for part in parts]
        ends = np.cumsum([part.shape[1] for part in parts]).tolist()
        self.table = np.concatenate(parts, 1).astype(np.int32)
        self.steps = ends[:2]
        self.targets = ends[2:]
        self.steps_per_home = units_dev * COLUMNS
        self.targets_per_home = units_dev * 2


def plain_program(visibility, beam, antenna_uvw, small, keep):
    units_dev, slots, _, span, _ = visibility.shape
    _, _, per_group, antennas = beam.shape
    blocks = antennas // span
    tile_index = lax.axis_index("tile")
    units = unit_table(blocks)
    none = np.zeros_like(units[:, 0])
    table = np.stack([units[:, 2], units[:, 0], units[:, 1], none, units[:, 0], none, units[:, 1]], 1)
    table = table.astype(np.int32).reshape(-1, units_dev * COLUMNS)
    table = np.pad(table, ((0, 0), (1, 0)))
    table = lax.dynamic_index_in_dim(jnp.asarray(table), tile_index, 0, keepdims=False)
    columns = None
    residuals, grads = [], []
    for slot in range(slots):
        (owned,) = build_factors(
            (slot, slots, per_group),
            table,
            beam,
            [],
            antenna_uvw,
            [small],
            [list(range(blocks))],
            span,
            0 if slot else BRIGHT_ROWS,
            small[0].shape[1],
        )
        everyone = lax.all_gather(owned, "tile", axis=0)
        rows = blocks * per_group
        if columns is None:
            bright = everyone[:, 0, rows : rows + slots, :per_group].astype(jnp.float32)
            bright = jnp.swapaxes(bright, 0, 1).reshape(slots, -1, 1)
            columns = jnp.broadcast_to(bright, bright.shape[:2] + (128,))
        factors = everyone[:, :, :rows].reshape(-1, 2, blocks, per_group, span)
        number = factors.shape[0] * per_group
        factors = factors.transpose(1, 2, 0, 3, 4).reshape(2, blocks * number, span)
        residual, grad = unit_work(
            slot, 1, table, [[((factors,), 0, number)]], [visibility], keep, columns
        )
        residuals.append(residual)
        grads.append(grad)
    summed = lax.psum_scatter(jnp.concatenate(grads, 0), "tile", scatter_dimension=1, tiled=True)
    return jnp.stack(residuals, 1), summed


OWN, OWN_NEAR, OWN_FAR, REST, REST_NEAR, REST_FAR = 0, 1, 3, 5, 6, 8
BEAM, SIDE_BEAMS, LATER_BEAMS, VIS, LATER = 10, 12, 15, 19, 23
PIECE_NEAR, PIECE_FAR = (24, 26), (28, 30)
WORK, HOME, PUT, LATER_WORK, LATER_HOME, PUT_NEAR, PUT_LAST = 32, 35, 38, 40, 43, 46, 47
SUM_PLANES, SUM_PLANE = 48, 51
GATES = {
    1: (0,),
    3: (0, 1),
    5: (0, 2, 13),
    6: (1, 2, 11),
    7: (1, 2),
    14: (13,),
    16: (2,),
    17: (1,),
    19: (18,),
    20: (3, 4, 6, 7, 17),
    21: (3, 4, 5, 13, 14, 16, 17),
    23: (4, 17),
    24: (6, 9, 17),
    25: (6, 9, 17, 23),
    26: (9,),
    27: (8,),
    28: (22,),
    31: (25, 27),
    33: (23, 32, 20),
    34: (33,),
    35: (8, 9, 24, 25),
    40: (28, 34, 36, 37),
    41: (40,),
    42: (29, 41),
    43: (41,),
    45: (28, 32),
    48: (35,),
    49: (44,),
    51: (34,),
    52: (38,),
    8: (23,),
    9: (23,),
    47: (51, 52, 53),
}


def plane_program(routes, visibility, beam, antenna_uvw, small, keep):
    units_dev, slots, _, span, _ = visibility.shape
    per_group = beam.shape[2]
    width = routes.width
    share = slots // width
    group = width * per_group
    tile_index = lax.axis_index("tile")
    mine = tile_index % width
    table = lax.dynamic_index_in_dim(jnp.asarray(routes.table), tile_index, 0, keepdims=False)
    done = {}

    def gated(step, value):
        earlier = [done[gate] for gate in GATES.get(step, ())]
        return lax.optimization_barrier((value, *earlier))[0] if earlier else value

    def send(step, value, pairs):
        done[step] = lax.ppermute(gated(step, value), "tile", pairs)
        return done[step]

    def near(step, piece):
        return [send(step, piece, routes.onward), send(step + 1, piece, routes.backward)]

    def far(step, sides):
        return [
            send(step, sides[0][0], routes.onward),
            send(step + 1, sides[1][1], routes.backward),
        ]

    def entries(piece, sides, halves, first, number):
        found = [(piece,), (sides[0],), (sides[1],), tuple(halves)]
        return [(arrays, n * group + first, number) for n, arrays in enumerate(found)]

    def build(step, index, own_beam, messages, smalls, pieces, bright_rows):
        built = build_factors(
            (index, share, per_group),
            gated(step, table),
            own_beam,
            messages,
            antenna_uvw,
            smalls,
            pieces,
            span,
            bright_rows,
            small[0].shape[1],
        )
        done[step] = built[0]
        return built

    core, *side = range(1, width)
    (message,) = messages_for(beam, 0, [core], small, gated(BEAM, table))
    message = send(BEAM + 1, message, routes.partner[core])
    (own,) = build(OWN, 0, beam, [message], [small, message], routes.full, BRIGHT_ROWS)
    own_sides = near(OWN_NEAR, own)
    messages = messages_for(beam, 0, side, small, gated(SIDE_BEAMS, table))
    messages = [
        send(SIDE_BEAMS + 1 + n, messages[n], routes.partner[m]) for n, m in enumerate(side)
    ]
    own_far = far(OWN_FAR, own_sides)
    (rest,) = build(REST, 0, None, messages, messages, routes.full, BRIGHT_ROWS)
    rest_sides = near(REST_NEAR, rest)

    later = messages_for(beam, 1, [core, *side], None, gated(LATER_BEAMS, table))
    later = [send(LATER_BEAMS + m, later[m - 1], routes.partner[m]) for m in (core, *side)]
    vis = slices_for(
        visibility, 1, share, [(m, 0) for m in (core, *side)], gated(VIS, table)
    )
    vis = [visibility] + [send(VIS + m, vis[m - 1], routes.partner[m]) for m in (core, *side)]
    later_pieces = build(
        LATER, 1, beam, later, [small, message, *messages], routes.pieces, 0
    )
    rest_far = far(REST_FAR, rest_sides)
    near_0 = near(PIECE_NEAR[0], later_pieces[0])
    near_1 = near(PIECE_NEAR[1], later_pieces[1])
    far_0 = far(PIECE_FAR[0], near_0)

    grads = []

    def work(index, step, home_step, ready, bright):
        arrived, total = [], None
        for n, homes in enumerate([routes.order[:1], routes.order[1:2], routes.order[2:]]):
            made = unit_work(
                index,
                routes.steps[index] + len(arrived) * routes.steps_per_home,
                gated(step + n, table),
                ready,
                [vis[m] for m in homes],
                keep,
                bright,
            )
            results, grad = made[: len(homes)], made[len(homes)]
            if isinstance(bright, int):
                bright = made[-1]
            done[step + n] = grad
            total = grad if total is None else total + grad
            arrived += [
                send(home_step - 1 + m, part, routes.partner[m]) if m else part
                for m, part in zip(homes, results)
            ]
        grads.append(total)
        return arrived, bright

    def put(step, homes, arrays, index, residual):
        rows = [(n, k) for n in range(len(arrays)) for k in range(units_dev)]
        offset = routes.targets[index] + homes * routes.targets_per_home
        done[step] = put_residuals(
            rows, arrays, offset, gated(step, table), visibility.shape, residual
        )
        return done[step]

    number = group // 2
    pieces = entries(own, own_sides, own_far, 0, number)
    pieces += entries(rest, rest_sides, rest_far, number, number)
    arrived, columns = work(0, WORK, HOME, [pieces], share)
    far_1 = far(PIECE_FAR[1], near_1)
    residual = put(PUT, 0, arrived, 0, None)
    ready = [
        entries(piece, sides, halves, 0, group)
        for piece, sides, halves in zip(later_pieces, (near_0, near_1), (far_0, far_1))
    ]
    arrived, _ = work(1, LATER_WORK, LATER_HOME, ready, columns)

    partial = jnp.concatenate(grads, 0)
    parts = [partial[:, n * group : (n + 1) * group] for n in range(4)]
    plane_sum = (parts[0] + send(SUM_PLANES, parts[3], routes.opposite)) + (
        send(SUM_PLANES + 1, parts[1], routes.backward)
        + send(SUM_PLANES + 2, parts[2], routes.onward)
    )
    sums = [plane_sum[:, m * per_group : (m + 1) * per_group] for m in range(width)]
    sums = [sums[0]] + [
        send(SUM_PLANE - 1 + m, sums[m], routes.partner[m]) for m in (core, *side)
    ]
    sums = jnp.stack(sums, 0)
    ids = jnp.arange(width, dtype=jnp.int32)
    here = jnp.bitwise_xor(ids[:, None], mine) == ids[None, :]
    summed = jnp.sum(jnp.where(here[:, :, None, None], sums[None], 0.0), axis=1)
    summed = summed.reshape(slots, per_group)

    residual = put(PUT_NEAR, 2, arrived[2:], 1, residual)
    residual = put(PUT_LAST, 0, arrived[:2], 1, residual)
    return residual, summed


def per_device(
    visibility, station_beam, antenna_uvw, source_dirs, source_flux, visible_list, antenna_flags
):
    span = visibility.shape[4]
    antennas = station_beam.shape[3]
    small = (source_dirs, source_flux.astype(jnp.float32)[None], visible_list)
    keep = 1.0 - antenna_flags.astype(jnp.float32)
    arguments = (visibility, station_beam, antenna_uvw, small, keep)
    if lax.axis_size("tile") == 16:
        routes = Routes(4, 4, unit_table(antennas // span), visibility.shape[1] // 4)
        residual, summed = plane_program(routes, *arguments)
    else:
        residual, summed = plain_program(*arguments)
    return (residual, summed * (-1.0 / (8.0 * antennas)))


def solution(mesh):
    return jax.shard_map(
        per_device,
        mesh=mesh,
        in_specs=(
            P("tile", "grp", None, None, None),
            P("grp", None, "tile", None),
            P("grp", None, None),
            P(None, "tile"),
            P(("grp", "tile")),
            P(None, "tile"),
            P("grp", None),
        ),
        out_specs=(P("tile", "grp", None, None, None), P("grp", "tile")),
        check_vma=False,
    )
```

```python
import functools

import jax
import jax.numpy as jnp
import numpy as np
from jax import lax
from jax.experimental import pallas as pl
from jax.experimental.pallas import tpu as pltpu
from jax.sharding import PartitionSpec as P


def unit_table(block_count):
    first_list = []
    second_list = []
    diag_list = []
    for row_block in range(block_count):
        for col_block in range(row_block + 1, block_count):
            first_list.append(row_block)
            second_list.append(col_block)
            diag_list.append(0)
    for pair_index in range(block_count // 2):
        first_list.append(2 * pair_index)
        second_list.append(2 * pair_index + 1)
        diag_list.append(1)
    return np.stack([first_list, second_list, diag_list], 1).astype(np.int32)


def turn_polynomials():
    nodes = 0.125 + 0.125 * np.cos(np.pi * (np.arange(64) + 0.5) / 64)
    root = np.sqrt(nodes)
    fit = np.polynomial.Polynomial.fit
    sine = fit(nodes, np.sin(2 * np.pi * root) / root, 7, domain=[0, 0.25]).convert()
    cosine = fit(nodes, np.cos(2 * np.pi * root), 8, domain=[0, 0.25]).convert()
    return [float(c) for c in sine.coef], [float(c) for c in cosine.coef]


def horner(coefs, x):
    total = coefs[-1]
    for coef in coefs[-2::-1]:
        total = total * x + coef
    return total


def build_kernel(sets, slot_ids, pieces, bright_rows, width, tab_ref, *refs):
    refs, scratch_ref = refs[:-1], refs[-1]
    uvw_ref, outs = refs[-1 - len(pieces)], refs[-len(pieces) :]
    per_group = sets[0][0]
    span = outs[0].shape[2]
    count = len(sets) * per_group
    sin_coefs, cos_coefs = turn_polynomials()
    brights = []
    for part, (_, beam_at, small_at) in enumerate(sets):
        beam_ref = refs[beam_at]
        if beam_ref.shape[0] == 1:
            beam = [beam_ref.at[0, 0], beam_ref.at[0, 1]]
        else:
            beam = [beam_ref.at[pl.ds(n * per_group, per_group)] for n in (0, 1)]
        if refs[small_at].dtype == jnp.float32:
            small = small_rows(scratch_ref, *refs[small_at : small_at + 3])
        else:
            small = unsplit(refs[small_at], 2 * per_group, width)
        lanes = lax.broadcasted_iota(jnp.int32, (per_group, width), 1)
        rows = lax.broadcasted_iota(jnp.int32, (per_group, width), 0)

        def pick(chosen, row):
            return jnp.sum(jnp.where(chosen, small[row : row + 1, :], 0.0), axis=1, keepdims=True)

        def chosen_at(index):
            here = lax.broadcasted_iota(jnp.int32, small.shape, 0) == LIST_ROW + tab_ref[0] + index
            line = jnp.sum(jnp.where(here, small, 0.0), axis=0, keepdims=True)
            listed = jnp.sum(jnp.where(lanes == rows, line, 0.0), axis=1, keepdims=True)
            return listed.astype(jnp.int32) == lanes

        group = part * per_group
        if bright_rows:
            columns = lax.broadcasted_iota(jnp.int32, (per_group, span), 1)
            numbers = lax.broadcasted_iota(jnp.int32, (per_group, span), 0) + group
            for index in range(slot_ids[1]):
                flux = pick(chosen_at(index), 2)
                line = jnp.sum(jnp.where(columns == numbers, flux, 0.0), axis=0, keepdims=True)
                if part == 0:
                    brights.append(line)
                else:
                    brights[index] += line
        chosen = chosen_at(slot_ids[0])
        east = pick(chosen, 0)
        north = pick(chosen, 1)
        depth = jnp.sqrt(1.0 - east * east - north * north) - 1.0
        for out_ref, piece in zip(outs, pieces):
            for place, block in enumerate(piece):
                cols = pl.ds(block * span, span)
                delay = (
                    uvw_ref[0, 0:1, cols] * east
                    + uvw_ref[0, 1:2, cols] * north
                    + uvw_ref[0, 2:3, cols] * depth
                )
                turn = delay - jnp.floor(delay + 0.5)
                square = turn * turn
                sine = horner(sin_coefs, square) * turn
                cosine = horner(cos_coefs, square)
                real = beam[0][:, cols].astype(jnp.float32)
                imag = beam[1][:, cols].astype(jnp.float32)
                at = pl.ds(place * count + group, per_group)
                out_ref[0, at] = (real * cosine + imag * sine).astype(jnp.bfloat16)
                out_ref[1, at] = (imag * cosine - real * sine).astype(jnp.bfloat16)
    if bright_rows:
        padding = jnp.zeros((bright_rows - len(brights), span), jnp.float32)
        block = jnp.concatenate(brights + [padding], 0).astype(jnp.bfloat16)
        for part in (0, 1):
            outs[0][part, pl.ds(len(pieces[0]) * count, bright_rows)] = block


def small_rows(rows_ref, dirs_ref, flux_ref, list_ref):
    rows_ref[...] = jnp.zeros_like(rows_ref)
    rows_ref[0:2, 0 : dirs_ref.shape[1]] = dirs_ref[...]
    rows_ref[2:3, 0 : flux_ref.shape[1]] = flux_ref[...]
    slots, count = list_ref.shape
    rows_ref[LIST_ROW : LIST_ROW + slots, 0:count] = list_ref[...].astype(jnp.float32)
    return rows_ref[...]


LIST_ROW = 8
SMALL_ROWS = 16


def unsplit(message_ref, start, width):
    rows = pl.ds(start, SMALL_ROWS)
    terms = [message_ref[rows, pl.ds(n * width, width)].astype(jnp.float32) for n in range(3)]
    return (terms[0] + terms[1]) + terms[2]


BRIGHT_ROWS = 16


def build_factors(
    slot_ids, table, beam, messages, antenna_uvw, smalls, pieces, span, bright_rows, small_width
):
    slots, _, antennas = antenna_uvw.shape
    per_group = slot_ids[2]
    index = slot_ids[0]
    whole = pl.BlockSpec(memory_space=pltpu.VMEM)
    operands, in_specs, sets = [], [], []
    if beam is not None:
        operands.append(beam)
        in_specs.append(
            pl.BlockSpec((1, 2, per_group, antennas), lambda n, tab: (tab[0] + index, 0, 0, 0))
        )
    operands += messages
    beams = len(operands)
    for n, small in enumerate(smalls):
        at = next((k for k, known in enumerate(operands) if known is small), len(operands))
        if at == len(operands):
            operands += small if isinstance(small, tuple) else [small]
        sets.append((per_group, n, at))
    in_specs += [whole] * (len(operands) - len(in_specs))
    in_specs.append(pl.BlockSpec((1, 3, antennas), lambda n, tab: (tab[0] + index, 0, 0)))
    count = beams * per_group
    shapes = [
        (2, len(piece) * count + (0 if n else bright_rows), span) for n, piece in enumerate(pieces)
    ]
    return pl.pallas_call(
        functools.partial(build_kernel, sets, slot_ids, pieces, bright_rows, small_width),
        grid_spec=pltpu.PrefetchScalarGridSpec(
            num_scalar_prefetch=1,
            grid=(1,),
            in_specs=in_specs,
            out_specs=[whole] * len(pieces),
            scratch_shapes=[pltpu.VMEM((SMALL_ROWS, small_width), jnp.float32)],
        ),
        out_shape=[jax.ShapeDtypeStruct(shape, jnp.bfloat16) for shape in shapes],
        compiler_params=pltpu.CompilerParams(vmem_limit_bytes=16 * 1024 * 1024),
        cost_estimate=LITTLE,
        name="build_factors",
    )(table, *operands, antenna_uvw)


LITTLE = pl.CostEstimate(flops=1, bytes_accessed=1, transcendentals=0)


def message_kernel(count, with_small, tab_ref, *refs):
    beams, refs = refs[:count], refs[count:]
    if with_small:
        smalls, outs, scratch_ref = refs[:3], refs[3:-1], refs[-1]
        terms = []
        rest = small_rows(scratch_ref, *smalls)
        width = rest.shape[1]
        for _ in range(3):
            terms.append(rest.astype(jnp.bfloat16))
            rest = rest - terms[-1].astype(jnp.float32)
    else:
        outs = refs
    for beam_ref, out_ref in zip(beams, outs):
        per_group = beam_ref.shape[2]
        for part in (0, 1):
            out_ref[pl.ds(part * per_group, per_group)] = beam_ref[0, part]
        if with_small:
            rows = pl.ds(2 * per_group, SMALL_ROWS)
            out_ref[rows] = jnp.zeros((SMALL_ROWS, out_ref.shape[1]), jnp.bfloat16)
            for n, term in enumerate(terms):
                out_ref[rows, pl.ds(n * width, width)] = term


def messages_for(beam, index, others, small, table):
    _, _, per_group, antennas = beam.shape
    smalls = small or ()
    rows = 2 * per_group + (SMALL_ROWS if smalls else 0)
    whole = pl.BlockSpec(memory_space=pltpu.VMEM)
    scratch = []
    if smalls:
        scratch.append(pltpu.VMEM((SMALL_ROWS, smalls[0].shape[1]), jnp.float32))
    return pl.pallas_call(
        functools.partial(message_kernel, len(others), bool(smalls)),
        grid_spec=pltpu.PrefetchScalarGridSpec(
            num_scalar_prefetch=1,
            grid=(1,),
            in_specs=[
                pl.BlockSpec(
                    (1, 2, per_group, antennas), lambda n, tab, m=m: (tab[m] + index, 0, 0, 0)
                )
                for m in others
            ]
            + [whole for _ in smalls],
            out_specs=[whole for _ in others],
            scratch_shapes=scratch,
        ),
        out_shape=[jax.ShapeDtypeStruct((rows, antennas), jnp.bfloat16) for _ in others],
        cost_estimate=LITTLE,
        name="messages_for",
    )(table, *[beam] * len(others), *smalls)


def slice_kernel(count, tab_ref, *refs):
    for source, target in zip(refs[:count], refs[count:]):
        target[...] = source[...]


def slices_for(array, axis, size, starts, table):
    lead = axis > 0
    shape = array.shape[:axis] + (size,) + array.shape[axis + 1 :]
    block = (1,) + shape[1:] if lead else shape
    rest = (0,) * (array.ndim - axis - 1)
    return pl.pallas_call(
        functools.partial(slice_kernel, len(starts)),
        grid_spec=pltpu.PrefetchScalarGridSpec(
            num_scalar_prefetch=1,
            grid=(shape[0] if lead else 1,),
            in_specs=[
                pl.BlockSpec(
                    block,
                    lambda n, tab, start=start, shift=shift: (
                        *((n,) if lead else ()),
                        tab[start] // size + shift,
                        *rest,
                    ),
                )
                for start, shift in starts
            ],
            out_specs=[
                pl.BlockSpec(block, lambda n, tab: (n,) + (0,) * (array.ndim - 1)) for _ in starts
            ],
        ),
        out_shape=[jax.ShapeDtypeStruct(shape, array.dtype) for _ in starts],
        cost_estimate=LITTLE,
        name="slices_for",
    )(table, *[array] * len(starts))


KIND, ONE, TWO, ONE_AT, TWO_AT = 0, 1, 2, 3, 5
COLUMNS = 7


def unit_kernel(index, offset, pieces, bright_at, homes, tab_ref, *refs):
    arrays = []
    for entries in pieces:
        found = []
        for count, start, number in entries:
            parts = (refs[0].at[0], refs[0].at[1]) if count == 1 else refs[:2]
            found.append((parts, start, number))
            refs = refs[count:]
        arrays.append(found)
    vis_refs, (keep_one_ref, keep_two_ref) = refs[:homes], refs[homes : homes + 2]
    refs = refs[homes + 2 :]
    columns_ref = None
    if bright_at is None:
        columns_ref, refs = refs[0], refs[1:]
    out_refs, grad_ref = refs[:homes], refs[homes]
    refs = refs[homes + 1 :]
    if bright_at is not None:
        columns_ref, refs = refs[0], refs[1:]
    total_ref, one_ref, two_ref, vis_ref = refs
    step = pl.program_id(0)
    slot = tab_ref[0] + index
    sources, span = one_ref.shape[1:]

    def entry(column):
        return tab_ref[offset + step * COLUMNS + column]

    def load(target, at):
        for n, found in enumerate(arrays):

            @pl.when(entry(at) == n)
            def _(found=found):
                place = entry(at + 1)
                for parts, start, number in found:
                    rows = pl.ds(pl.multiple_of(place * number, number), number)
                    for part in (0, 1):
                        target[part, pl.ds(start, number)] = parts[part][rows]

    if bright_at is not None:

        @pl.when(step == 0)
        def _():
            for parts, start, number in arrays[0]:
                lines = parts[0][pl.ds(bright_at * number, BRIGHT_ROWS)].astype(jnp.float32)
                lanes = lax.broadcasted_iota(jnp.int32, (number, span), 1)
                rows = lax.broadcasted_iota(jnp.int32, (number, span), 0)
                for n in range(columns_ref.shape[0]):
                    line = jnp.where(lanes == rows, lines[n : n + 1, :], 0.0)
                    column = jnp.sum(line, axis=1, keepdims=True)
                    columns_ref[n, pl.ds(start, number)] = jnp.broadcast_to(column, (number, 128))

    def dot(a, b):
        return lax.dot_general(a, b, (((1,), (0,)), ((), ())), preferred_element_type=jnp.float32)

    def scaled_of(re, im):
        column = jnp.concatenate([columns_ref[index].astype(jnp.bfloat16)] * (span // 128), 1)
        return re * column, im * column

    def outer(a, b):
        row_ids = lax.broadcasted_iota(jnp.int32, a.shape, 0)
        a = jnp.where(row_ids == slot, a, 0.0)
        return lax.dot_general(a, b, (((0,), (0,)), ((), ())), preferred_element_type=jnp.float32)

    def cross(a_re, a_im, b_re, b_im):
        lhs = jnp.concatenate([a_re, a_im], 0).T
        rhs = jnp.concatenate(
            [jnp.concatenate([b_re, -b_im], 1), jnp.concatenate([b_im, b_re], 1)], 0
        )
        both = dot(lhs, rhs)
        return both[:, :span], both[:, span:]

    def pull(re, im, res_re, res_im, sign):
        lhs = jnp.concatenate([re, im], 1)
        rhs = jnp.concatenate(
            [
                jnp.concatenate([res_re, res_im], 1),
                jnp.concatenate([res_im, -res_re] if sign == 1 else [-res_im, res_re], 1),
            ],
            0,
        )
        both = dot(lhs, rhs)
        return both[:, :span], both[:, span:]

    def add_grad(value):
        folded = value[:, :128]
        for start in range(128, span, 128):
            folded = folded + value[:, start : start + 128]
        total_ref[...] += folded

    each = pl.num_programs(0) // homes

    def put(res_re, res_im):
        for home, out_ref in enumerate(out_refs):

            @pl.when(step // each == home)
            def _(out_ref=out_ref):
                out_ref[0, 0] = res_re
                out_ref[0, 1] = res_im

    @pl.when(step == 0)
    def _():
        total_ref[...] = jnp.zeros_like(total_ref)

    load(one_ref, ONE_AT)
    load(two_ref, TWO_AT)
    for home, home_ref in enumerate(vis_refs):

        @pl.when(step // each == home)
        def _(home_ref=home_ref):
            vis_ref[...] = home_ref[0, 0]

    @pl.when(entry(KIND) == 0)
    def _():
        one_re, one_im, two_re, two_im = one_ref[0], one_ref[1], two_ref[0], two_ref[1]
        pred_re, pred_im = cross(*scaled_of(one_re, one_im), two_re, two_im)
        weights = outer(keep_one_ref[...], keep_two_ref[...])
        res_re = (weights * (vis_ref[0].astype(jnp.float32) - pred_re)).astype(jnp.bfloat16)
        res_im = (weights * (vis_ref[1].astype(jnp.float32) - pred_im)).astype(jnp.bfloat16)
        put(res_re, res_im)
        sum_re, sum_im = pull(one_re, one_im, res_re, res_im, 1)
        add_grad(sum_re * two_re.astype(jnp.float32) - sum_im * two_im.astype(jnp.float32))

    @pl.when(entry(KIND) == 1)
    def _():
        one_re, one_im, two_re, two_im = one_ref[0], one_ref[1], two_ref[0], two_ref[1]
        row_ids = lax.broadcasted_iota(jnp.int32, (span, span), 0)
        col_ids = lax.broadcasted_iota(jnp.int32, (span, span), 1)
        upper = row_ids < col_ids
        lower = row_ids > col_ids
        first_re, first_im = cross(*scaled_of(one_re, one_im), one_re, one_im)
        second_re, second_im = cross(two_re, two_im, *scaled_of(two_re, two_im))
        keep_one = keep_one_ref[...]
        keep_two = keep_two_ref[...]
        weights = jnp.where(upper, outer(keep_one, keep_one), 0.0) + jnp.where(
            lower, outer(keep_two, keep_two), 0.0
        )
        vis_re = vis_ref[0].astype(jnp.float32)
        vis_im = vis_ref[1].astype(jnp.float32)
        res_re = (weights * (vis_re - jnp.where(upper, first_re, second_re))).astype(jnp.bfloat16)
        res_im = (weights * (vis_im - jnp.where(upper, first_im, -second_im))).astype(jnp.bfloat16)
        put(res_re, res_im)
        none = jnp.zeros_like(res_re)
        sum_re, sum_im = pull(
            one_re, one_im, jnp.where(upper, res_re, none), jnp.where(upper, res_im, none), 1
        )
        add_grad(sum_re * one_re.astype(jnp.float32) - sum_im * one_im.astype(jnp.float32))
        sum_re, sum_im = pull(
            two_re, two_im, jnp.where(lower, res_re, none), jnp.where(lower, res_im, none), -1
        )
        add_grad(sum_re * two_re.astype(jnp.float32) + sum_im * two_im.astype(jnp.float32))

    @pl.when(step == pl.num_programs(0) - 1)
    def _():
        grad_ref[...] = jnp.sum(total_ref[...].T, axis=0, keepdims=True)


def unit_work(index, offset, table, pieces, vis, keep, bright):
    units_dev, _, _, span, _ = vis[0].shape
    slots = keep.shape[0]
    sources = sum(number for _, _, number in pieces[0])
    count = units_dev * len(vis)
    whole = pl.BlockSpec(memory_space=pltpu.VMEM)
    arrays = [array for piece in pieces for entry, _, _ in piece for array in entry]

    def at(tab, step, column):
        return tab[offset + step * COLUMNS + column]

    def unit(step, home):
        return jnp.clip(step - home * units_dev, 0, units_dev - 1)

    in_specs = [whole] * len(arrays)
    for home, array in enumerate(vis):
        if array.shape[1] == slots:
            slot = lambda tab: tab[0] + index
        else:
            slot = lambda tab: index
        in_specs.append(
            pl.BlockSpec(
                (1, 1, 2, span, span),
                lambda u, tab, home=home, slot=slot: (unit(u, home), slot(tab), 0, 0, 0),
            )
        )
    in_specs += [
        pl.BlockSpec((slots, span), lambda u, tab: (0, at(tab, u, ONE))),
        pl.BlockSpec((slots, span), lambda u, tab: (0, at(tab, u, TWO))),
    ]
    operands = [table, *arrays, *vis, keep, keep]
    bright_at = None
    if isinstance(bright, int):
        first = pieces[0][0]
        bright_at = (first[0][0].shape[1] - BRIGHT_ROWS) // first[2]
    else:
        in_specs.append(whole)
        operands.append(bright)
    out_specs = [
        pl.BlockSpec((1, 2, span, span), lambda u, tab, home=home: (unit(u, home), 0, 0, 0))
        for home in range(len(vis))
    ]
    out_shapes = [jax.ShapeDtypeStruct((units_dev, 2, span, span), jnp.bfloat16) for _ in vis]
    out_specs.append(pl.BlockSpec((1, sources), lambda u, tab: (0, 0)))
    out_shapes.append(jax.ShapeDtypeStruct((1, sources), jnp.float32))
    if bright_at is not None:
        out_specs.append(pl.BlockSpec((bright, sources, 128), lambda u, tab: (0, 0, 0)))
        out_shapes.append(jax.ShapeDtypeStruct((bright, sources, 128), jnp.float32))
    kinds = [[(len(entry), start, number) for entry, start, number in piece] for piece in pieces]
    return pl.pallas_call(
        functools.partial(unit_kernel, index, offset, kinds, bright_at, len(vis)),
        grid_spec=pltpu.PrefetchScalarGridSpec(
            num_scalar_prefetch=1,
            grid=(count,),
            in_specs=in_specs,
            out_specs=out_specs,
            scratch_shapes=[
                pltpu.VMEM((sources, 128), jnp.float32),
                pltpu.VMEM((2, sources, span), jnp.bfloat16),
                pltpu.VMEM((2, sources, span), jnp.bfloat16),
                pltpu.VMEM((2, span, span), jnp.bfloat16),
            ],
        ),
        out_shape=out_shapes,
        compiler_params=pltpu.CompilerParams(vmem_limit_bytes=16 * 1024 * 1024),
        cost_estimate=LITTLE,
        name="unit_work",
    )(*operands)


def put_kernel(sources, tab_ref, *refs):
    out_ref = refs[-1]
    for step, (which, row) in enumerate(sources):

        @pl.when(pl.program_id(0) == step)
        def _(which=which, row=row):
            out_ref[0, 0] = refs[which][...] if row is None else refs[which][row]


def put_residuals(sources, arrays, offset, table, shape, residual):
    span = shape[-1]
    whole = pl.BlockSpec(memory_space=pltpu.VMEM)
    operands = [table, *arrays]
    in_specs = [whole] * len(arrays)
    aliases = {}
    if residual is not None:
        aliases = {len(operands): 0}
        operands.append(residual)
        in_specs.append(pl.BlockSpec(memory_space=pl.ANY))
    return pl.pallas_call(
        functools.partial(put_kernel, sources),
        grid_spec=pltpu.PrefetchScalarGridSpec(
            num_scalar_prefetch=1,
            grid=(len(sources),),
            in_specs=in_specs,
            out_specs=pl.BlockSpec(
                (1, 1, 2, span, span),
                lambda n, tab: (tab[offset + 2 * n], tab[offset + 2 * n + 1], 0, 0, 0),
            ),
        ),
        out_shape=jax.ShapeDtypeStruct(shape, jnp.bfloat16),
        input_output_aliases=aliases,
        compiler_params=pltpu.CompilerParams(vmem_limit_bytes=16 * 1024 * 1024),
        cost_estimate=LITTLE,
        name="put_residuals",
    )(*operands)


class Routes:
    def __init__(self, planes, width, units, share):
        count = planes * width
        blocks = int(units[:, :2].max()) + 1
        self.width = width
        self.units_dev = units_dev = units.shape[0] // count
        ring = [0] + list(range(1, planes, 2)) + list(range(planes - 2, 0, -2))

        def along(step):
            at = {plane: ring[(n + step) % planes] for n, plane in enumerate(ring)}
            return [(t, at[t // width] * width + t % width) for t in range(count)]

        self.onward = along(1)
        self.backward = along(-1)
        self.opposite = along(2)
        self.partner = [[(t, t ^ m) for t in range(count)] for m in range(width)]

        half = blocks // 2
        self.full = [list(range(blocks))]
        self.pieces = [list(range(half)), list(range(half, blocks))]

        def table_of(pieces, order):
            rows = np.zeros((count, len(order), units_dev, COLUMNS), np.int32)
            for t in range(count):
                for n, m in enumerate(order):
                    for k in range(units_dev):
                        one, two, kind = units[(t ^ m) * units_dev + k].tolist()
                        at = [
                            (p, piece.index(b))
                            for b in (one, two)
                            for p, piece in enumerate(pieces)
                            if b in piece
                        ]
                        rows[t, n, k] = [kind, one, two, *at[0], *at[1]]
            return rows

        def targets(index):
            rows = np.zeros((count, len(self.order), units_dev, 2), np.int32)
            for t in range(count):
                for n, m in enumerate(self.order):
                    for k in range(units_dev):
                        rows[t, n, k] = k, (t % width ^ m) * share + index
            return rows

        self.order = list(range(width // 2, width)) + list(range(width // 2 - 1, -1, -1))
        starts = np.array([[(t % width ^ m) * share for m in range(width)] for t in range(count)])
        parts = [starts, table_of(self.full, self.order), table_of(self.pieces, self.order)]
        parts += [targets(n) for n in range(share)]
        parts = [part.reshape(count, -1) for part in parts]
        ends = np.cumsum([part.shape[1] for part in parts]).tolist()
        self.table = np.concatenate(parts, 1).astype(np.int32)
        self.steps = ends[:2]
        self.targets = ends[2:]
        self.steps_per_home = units_dev * COLUMNS
        self.targets_per_home = units_dev * 2


def plain_program(visibility, beam, antenna_uvw, small, keep):
    units_dev, slots, _, span, _ = visibility.shape
    _, _, per_group, antennas = beam.shape
    blocks = antennas // span
    tile_index = lax.axis_index("tile")
    units = unit_table(blocks)
    none = np.zeros_like(units[:, 0])
    table = np.stack([units[:, 2], units[:, 0], units[:, 1], none, units[:, 0], none, units[:, 1]], 1)
    table = table.astype(np.int32).reshape(-1, units_dev * COLUMNS)
    table = np.pad(table, ((0, 0), (1, 0)))
    table = lax.dynamic_index_in_dim(jnp.asarray(table), tile_index, 0, keepdims=False)
    columns = None
    residuals, grads = [], []
    for slot in range(slots):
        (owned,) = build_factors(
            (slot, slots, per_group),
            table,
            beam,
            [],
            antenna_uvw,
            [small],
            [list(range(blocks))],
            span,
            0 if slot else BRIGHT_ROWS,
            small[0].shape[1],
        )
        everyone = lax.all_gather(owned, "tile", axis=0)
        rows = blocks * per_group
        if columns is None:
            bright = everyone[:, 0, rows : rows + slots, :per_group].astype(jnp.float32)
            bright = jnp.swapaxes(bright, 0, 1).reshape(slots, -1, 1)
            columns = jnp.broadcast_to(bright, bright.shape[:2] + (128,))
        factors = everyone[:, :, :rows].reshape(-1, 2, blocks, per_group, span)
        number = factors.shape[0] * per_group
        factors = factors.transpose(1, 2, 0, 3, 4).reshape(2, blocks * number, span)
        residual, grad = unit_work(
            slot, 1, table, [[((factors,), 0, number)]], [visibility], keep, columns
        )
        residuals.append(residual)
        grads.append(grad)
    summed = lax.psum_scatter(jnp.concatenate(grads, 0), "tile", scatter_dimension=1, tiled=True)
    return jnp.stack(residuals, 1), summed


OWN, OWN_NEAR, OWN_FAR, REST, REST_NEAR, REST_FAR = 0, 1, 3, 5, 6, 8
BEAM, SIDE_BEAMS, LATER_BEAMS, VIS, LATER = 10, 12, 15, 19, 23
PIECE_NEAR, PIECE_FAR = (24, 26), (28, 30)
WORK, HOME, PUT, LATER_WORK, LATER_HOME, PUT_NEAR, PUT_LAST = 32, 35, 38, 40, 43, 46, 47
SUM_PLANES, SUM_PLANE = 48, 51
GATES = {
    1: (0,),
    3: (0, 1),
    5: (0, 2, 13),
    6: (1, 2, 11),
    7: (1, 2),
    14: (13,),
    16: (2,),
    17: (1,),
    19: (18,),
    20: (3, 4, 6, 7, 17),
    21: (3, 4, 5, 13, 14, 16, 17),
    23: (4, 17),
    24: (6, 9, 17),
    25: (6, 9, 17, 23),
    26: (9,),
    27: (8,),
    28: (22,),
    31: (25, 27),
    33: (23, 32),
    34: (33,),
    35: (8, 9, 24, 25),
    40: (28, 34, 36, 37),
    41: (29, 40),
    45: (28, 32),
    48: (35,),
    49: (44,),
    51: (34,),
    52: (38,),
}


def plane_program(routes, visibility, beam, antenna_uvw, small, keep):
    units_dev, slots, _, span, _ = visibility.shape
    per_group = beam.shape[2]
    width = routes.width
    share = slots // width
    group = width * per_group
    tile_index = lax.axis_index("tile")
    mine = tile_index % width
    table = lax.dynamic_index_in_dim(jnp.asarray(routes.table), tile_index, 0, keepdims=False)
    done = {}

    def gated(step, value):
        earlier = [done[gate] for gate in GATES.get(step, ())]
        return lax.optimization_barrier((value, *earlier))[0] if earlier else value

    def send(step, value, pairs):
        done[step] = lax.ppermute(gated(step, value), "tile", pairs)
        return done[step]

    def near(step, piece):
        return [send(step, piece, routes.onward), send(step + 1, piece, routes.backward)]

    def far(step, sides):
        return [
            send(step, sides[0][0], routes.onward),
            send(step + 1, sides[1][1], routes.backward),
        ]

    def entries(piece, sides, halves, first, number):
        found = [(piece,), (sides[0],), (sides[1],), tuple(halves)]
        return [(arrays, n * group + first, number) for n, arrays in enumerate(found)]

    def build(step, index, own_beam, messages, smalls, pieces, bright_rows):
        built = build_factors(
            (index, share, per_group),
            gated(step, table),
            own_beam,
            messages,
            antenna_uvw,
            smalls,
            pieces,
            span,
            bright_rows,
            small[0].shape[1],
        )
        done[step] = built[0]
        return built

    core, *side = range(1, width)
    (message,) = messages_for(beam, 0, [core], small, gated(BEAM, table))
    message = send(BEAM + 1, message, routes.partner[core])
    (own,) = build(OWN, 0, beam, [message], [small, message], routes.full, BRIGHT_ROWS)
    own_sides = near(OWN_NEAR, own)
    messages = messages_for(beam, 0, side, small, gated(SIDE_BEAMS, table))
    messages = [
        send(SIDE_BEAMS + 1 + n, messages[n], routes.partner[m]) for n, m in enumerate(side)
    ]
    own_far = far(OWN_FAR, own_sides)
    (rest,) = build(REST, 0, None, messages, messages, routes.full, BRIGHT_ROWS)
    rest_sides = near(REST_NEAR, rest)

    later = messages_for(beam, 1, [core, *side], None, gated(LATER_BEAMS, table))
    later = [send(LATER_BEAMS + m, later[m - 1], routes.partner[m]) for m in (core, *side)]
    vis = slices_for(
        visibility, 1, share, [(m, 0) for m in (core, *side)], gated(VIS, table)
    )
    vis = [visibility] + [send(VIS + m, vis[m - 1], routes.partner[m]) for m in (core, *side)]
    later_pieces = build(
        LATER, 1, beam, later, [small, message, *messages], routes.pieces, 0
    )
    rest_far = far(REST_FAR, rest_sides)
    near_0 = near(PIECE_NEAR[0], later_pieces[0])
    near_1 = near(PIECE_NEAR[1], later_pieces[1])
    far_0 = far(PIECE_FAR[0], near_0)

    grads = []

    def work(index, step, home_step, ready, bright, calls):
        arrived, total = [], None
        for n, homes in enumerate(calls):
            made = unit_work(
                index,
                routes.steps[index] + len(arrived) * routes.steps_per_home,
                gated(step + n, table),
                ready,
                [vis[m] for m in homes],
                keep,
                bright,
            )
            results, grad = made[: len(homes)], made[len(homes)]
            if isinstance(bright, int):
                bright = made[-1]
            done[step + n] = grad
            total = grad if total is None else total + grad
            arrived += [
                send(home_step - 1 + m, part, routes.partner[m]) if m else part
                for m, part in zip(homes, results)
            ]
        grads.append(total)
        return arrived, bright

    def put(step, homes, arrays, index, residual):
        rows = [(n, k) for n in range(len(arrays)) for k in range(units_dev)]
        offset = routes.targets[index] + homes * routes.targets_per_home
        done[step] = put_residuals(
            rows, arrays, offset, gated(step, table), visibility.shape, residual
        )
        return done[step]

    number = group // 2
    pieces = entries(own, own_sides, own_far, 0, number)
    pieces += entries(rest, rest_sides, rest_far, number, number)
    order = routes.order
    arrived, columns = work(
        0, WORK, HOME, [pieces], share, [order[:1], order[1:2], order[2:]]
    )
    far_1 = far(PIECE_FAR[1], near_1)
    residual = put(PUT, 0, arrived, 0, None)
    ready = [
        entries(piece, sides, halves, 0, group)
        for piece, sides, halves in zip(later_pieces, (near_0, near_1), (far_0, far_1))
    ]
    arrived, _ = work(1, LATER_WORK, LATER_HOME, ready, columns, [order[:1], order[1:]])

    partial = jnp.concatenate(grads, 0)
    parts = [partial[:, n * group : (n + 1) * group] for n in range(4)]
    plane_sum = (parts[0] + send(SUM_PLANES, parts[3], routes.opposite)) + (
        send(SUM_PLANES + 1, parts[1], routes.backward)
        + send(SUM_PLANES + 2, parts[2], routes.onward)
    )
    sums = [plane_sum[:, m * per_group : (m + 1) * per_group] for m in range(width)]
    sums = [sums[0]] + [
        send(SUM_PLANE - 1 + m, sums[m], routes.partner[m]) for m in (core, *side)
    ]
    sums = jnp.stack(sums, 0)
    ids = jnp.arange(width, dtype=jnp.int32)
    here = jnp.bitwise_xor(ids[:, None], mine) == ids[None, :]
    summed = jnp.sum(jnp.where(here[:, :, None, None], sums[None], 0.0), axis=1)
    summed = summed.reshape(slots, per_group)

    residual = put(PUT_NEAR, 2, arrived[2:], 1, residual)
    residual = put(PUT_LAST, 0, arrived[:2], 1, residual)
    return residual, summed


def per_device(
    visibility, station_beam, antenna_uvw, source_dirs, source_flux, visible_list, antenna_flags
):
    span = visibility.shape[4]
    antennas = station_beam.shape[3]
    small = (source_dirs, source_flux.astype(jnp.float32)[None], visible_list)
    keep = 1.0 - antenna_flags.astype(jnp.float32)
    arguments = (visibility, station_beam, antenna_uvw, small, keep)
    if lax.axis_size("tile") == 16:
        routes = Routes(4, 4, unit_table(antennas // span), visibility.shape[1] // 4)
        residual, summed = plane_program(routes, *arguments)
    else:
        residual, summed = plain_program(*arguments)
    return (residual, summed * (-1.0 / (8.0 * antennas)))


def solution(mesh):
    return jax.shard_map(
        per_device,
        mesh=mesh,
        in_specs=(
            P("tile", "grp", None, None, None),
            P("grp", None, "tile", None),
            P("grp", None, None),
            P(None, "tile"),
            P(("grp", "tile")),
            P(None, "tile"),
            P("grp", None),
        ),
        out_specs=(P("tile", "grp", None, None, None), P("grp", "tile")),
        check_vma=False,
    )
```

```python
import functools

import jax
import jax.numpy as jnp
import numpy as np
from jax import lax
from jax.experimental import pallas as pl
from jax.experimental.pallas import tpu as pltpu
from jax.sharding import PartitionSpec as P


def unit_table(block_count):
    first_list = []
    second_list = []
    diag_list = []
    for row_block in range(block_count):
        for col_block in range(row_block + 1, block_count):
            first_list.append(row_block)
            second_list.append(col_block)
            diag_list.append(0)
    for pair_index in range(block_count // 2):
        first_list.append(2 * pair_index)
        second_list.append(2 * pair_index + 1)
        diag_list.append(1)
    return np.stack([first_list, second_list, diag_list], 1).astype(np.int32)


def turn_polynomials():
    nodes = 0.125 + 0.125 * np.cos(np.pi * (np.arange(64) + 0.5) / 64)
    root = np.sqrt(nodes)
    fit = np.polynomial.Polynomial.fit
    sine = fit(nodes, np.sin(2 * np.pi * root) / root, 7, domain=[0, 0.25]).convert()
    cosine = fit(nodes, np.cos(2 * np.pi * root), 8, domain=[0, 0.25]).convert()
    return [float(c) for c in sine.coef], [float(c) for c in cosine.coef]


def horner(coefs, x):
    total = coefs[-1]
    for coef in coefs[-2::-1]:
        total = total * x + coef
    return total


def build_kernel(sets, slot_ids, pieces, bright_rows, width, tab_ref, *refs):
    refs, scratch_ref = refs[:-1], refs[-1]
    uvw_ref, outs = refs[-1 - len(pieces)], refs[-len(pieces) :]
    per_group = sets[0][0]
    span = outs[0].shape[2]
    count = len(sets) * per_group
    sin_coefs, cos_coefs = turn_polynomials()
    brights = []
    for part, (_, beam_at, small_at) in enumerate(sets):
        beam_ref = refs[beam_at]
        if beam_ref.shape[0] == 1:
            beam = [beam_ref.at[0, 0], beam_ref.at[0, 1]]
        else:
            beam = [beam_ref.at[pl.ds(n * per_group, per_group)] for n in (0, 1)]
        if refs[small_at].dtype == jnp.float32:
            small = small_rows(scratch_ref, *refs[small_at : small_at + 3])
        else:
            small = unsplit(refs[small_at], 2 * per_group, width)
        lanes = lax.broadcasted_iota(jnp.int32, (per_group, width), 1)
        rows = lax.broadcasted_iota(jnp.int32, (per_group, width), 0)

        def pick(chosen, row):
            return jnp.sum(jnp.where(chosen, small[row : row + 1, :], 0.0), axis=1, keepdims=True)

        def chosen_at(index):
            here = lax.broadcasted_iota(jnp.int32, small.shape, 0) == LIST_ROW + tab_ref[0] + index
            line = jnp.sum(jnp.where(here, small, 0.0), axis=0, keepdims=True)
            listed = jnp.sum(jnp.where(lanes == rows, line, 0.0), axis=1, keepdims=True)
            return listed.astype(jnp.int32) == lanes

        group = part * per_group
        if bright_rows:
            columns = lax.broadcasted_iota(jnp.int32, (per_group, span), 1)
            numbers = lax.broadcasted_iota(jnp.int32, (per_group, span), 0) + group
            for index in range(slot_ids[1]):
                flux = pick(chosen_at(index), 2)
                line = jnp.sum(jnp.where(columns == numbers, flux, 0.0), axis=0, keepdims=True)
                if part == 0:
                    brights.append(line)
                else:
                    brights[index] += line
        chosen = chosen_at(slot_ids[0])
        east = pick(chosen, 0)
        north = pick(chosen, 1)
        depth = jnp.sqrt(1.0 - east * east - north * north) - 1.0
        for out_ref, piece in zip(outs, pieces):
            for place, block in enumerate(piece):
                cols = pl.ds(block * span, span)
                delay = (
                    uvw_ref[0, 0:1, cols] * east
                    + uvw_ref[0, 1:2, cols] * north
                    + uvw_ref[0, 2:3, cols] * depth
                )
                turn = delay - jnp.floor(delay + 0.5)
                square = turn * turn
                sine = horner(sin_coefs, square) * turn
                cosine = horner(cos_coefs, square)
                real = beam[0][:, cols].astype(jnp.float32)
                imag = beam[1][:, cols].astype(jnp.float32)
                at = pl.ds(place * count + group, per_group)
                out_ref[0, at] = (real * cosine + imag * sine).astype(jnp.bfloat16)
                out_ref[1, at] = (imag * cosine - real * sine).astype(jnp.bfloat16)
    if bright_rows:
        padding = jnp.zeros((bright_rows - len(brights), span), jnp.float32)
        block = jnp.concatenate(brights + [padding], 0).astype(jnp.bfloat16)
        for part in (0, 1):
            outs[0][part, pl.ds(len(pieces[0]) * count, bright_rows)] = block


def small_rows(rows_ref, dirs_ref, flux_ref, list_ref):
    rows_ref[...] = jnp.zeros_like(rows_ref)
    rows_ref[0:2, 0 : dirs_ref.shape[1]] = dirs_ref[...]
    rows_ref[2:3, 0 : flux_ref.shape[1]] = flux_ref[...]
    slots, count = list_ref.shape
    rows_ref[LIST_ROW : LIST_ROW + slots, 0:count] = list_ref[...].astype(jnp.float32)
    return rows_ref[...]


LIST_ROW = 8
SMALL_ROWS = 16


def unsplit(message_ref, start, width):
    rows = pl.ds(start, SMALL_ROWS)
    terms = [message_ref[rows, pl.ds(n * width, width)].astype(jnp.float32) for n in range(3)]
    return (terms[0] + terms[1]) + terms[2]


BRIGHT_ROWS = 16


def build_factors(
    slot_ids, table, beam, messages, antenna_uvw, smalls, pieces, span, bright_rows, small_width
):
    slots, _, antennas = antenna_uvw.shape
    per_group = slot_ids[2]
    index = slot_ids[0]
    whole = pl.BlockSpec(memory_space=pltpu.VMEM)
    operands, in_specs, sets = [], [], []
    if beam is not None:
        operands.append(beam)
        in_specs.append(
            pl.BlockSpec((1, 2, per_group, antennas), lambda n, tab: (tab[0] + index, 0, 0, 0))
        )
    operands += messages
    beams = len(operands)
    for n, small in enumerate(smalls):
        at = next((k for k, known in enumerate(operands) if known is small), len(operands))
        if at == len(operands):
            operands += small if isinstance(small, tuple) else [small]
        sets.append((per_group, n, at))
    in_specs += [whole] * (len(operands) - len(in_specs))
    in_specs.append(pl.BlockSpec((1, 3, antennas), lambda n, tab: (tab[0] + index, 0, 0)))
    count = beams * per_group
    shapes = [
        (2, len(piece) * count + (0 if n else bright_rows), span) for n, piece in enumerate(pieces)
    ]
    return pl.pallas_call(
        functools.partial(build_kernel, sets, slot_ids, pieces, bright_rows, small_width),
        grid_spec=pltpu.PrefetchScalarGridSpec(
            num_scalar_prefetch=1,
            grid=(1,),
            in_specs=in_specs,
            out_specs=[whole] * len(pieces),
            scratch_shapes=[pltpu.VMEM((SMALL_ROWS, small_width), jnp.float32)],
        ),
        out_shape=[jax.ShapeDtypeStruct(shape, jnp.bfloat16) for shape in shapes],
        compiler_params=pltpu.CompilerParams(vmem_limit_bytes=16 * 1024 * 1024),
        cost_estimate=LITTLE,
        name="build_factors",
    )(table, *operands, antenna_uvw)


LITTLE = pl.CostEstimate(flops=1, bytes_accessed=1, transcendentals=0)


def message_kernel(count, with_small, tab_ref, *refs):
    beams, refs = refs[:count], refs[count:]
    if with_small:
        smalls, outs, scratch_ref = refs[:3], refs[3:-1], refs[-1]
        terms = []
        rest = small_rows(scratch_ref, *smalls)
        width = rest.shape[1]
        for _ in range(3):
            terms.append(rest.astype(jnp.bfloat16))
            rest = rest - terms[-1].astype(jnp.float32)
    else:
        outs = refs
    for beam_ref, out_ref in zip(beams, outs):
        per_group = beam_ref.shape[2]
        for part in (0, 1):
            out_ref[pl.ds(part * per_group, per_group)] = beam_ref[0, part]
        if with_small:
            rows = pl.ds(2 * per_group, SMALL_ROWS)
            out_ref[rows] = jnp.zeros((SMALL_ROWS, out_ref.shape[1]), jnp.bfloat16)
            for n, term in enumerate(terms):
                out_ref[rows, pl.ds(n * width, width)] = term


def messages_for(beam, index, others, small, table):
    _, _, per_group, antennas = beam.shape
    smalls = small or ()
    rows = 2 * per_group + (SMALL_ROWS if smalls else 0)
    whole = pl.BlockSpec(memory_space=pltpu.VMEM)
    scratch = []
    if smalls:
        scratch.append(pltpu.VMEM((SMALL_ROWS, smalls[0].shape[1]), jnp.float32))
    return pl.pallas_call(
        functools.partial(message_kernel, len(others), bool(smalls)),
        grid_spec=pltpu.PrefetchScalarGridSpec(
            num_scalar_prefetch=1,
            grid=(1,),
            in_specs=[
                pl.BlockSpec(
                    (1, 2, per_group, antennas), lambda n, tab, m=m: (tab[m] + index, 0, 0, 0)
                )
                for m in others
            ]
            + [whole for _ in smalls],
            out_specs=[whole for _ in others],
            scratch_shapes=scratch,
        ),
        out_shape=[jax.ShapeDtypeStruct((rows, antennas), jnp.bfloat16) for _ in others],
        cost_estimate=LITTLE,
        name="messages_for",
    )(table, *[beam] * len(others), *smalls)


def slice_kernel(count, tab_ref, *refs):
    for source, target in zip(refs[:count], refs[count:]):
        target[...] = source[...]


def slices_for(array, axis, size, starts, table):
    lead = axis > 0
    shape = array.shape[:axis] + (size,) + array.shape[axis + 1 :]
    block = (1,) + shape[1:] if lead else shape
    rest = (0,) * (array.ndim - axis - 1)
    return pl.pallas_call(
        functools.partial(slice_kernel, len(starts)),
        grid_spec=pltpu.PrefetchScalarGridSpec(
            num_scalar_prefetch=1,
            grid=(shape[0] if lead else 1,),
            in_specs=[
                pl.BlockSpec(
                    block,
                    lambda n, tab, start=start, shift=shift: (
                        *((n,) if lead else ()),
                        tab[start] // size + shift,
                        *rest,
                    ),
                )
                for start, shift in starts
            ],
            out_specs=[
                pl.BlockSpec(block, lambda n, tab: (n,) + (0,) * (array.ndim - 1)) for _ in starts
            ],
        ),
        out_shape=[jax.ShapeDtypeStruct(shape, array.dtype) for _ in starts],
        cost_estimate=LITTLE,
        name="slices_for",
    )(table, *[array] * len(starts))


KIND, ONE, TWO, ONE_AT, TWO_AT = 0, 1, 2, 3, 5
COLUMNS = 7


def unit_kernel(index, offset, pieces, bright_at, homes, tab_ref, *refs):
    arrays = []
    for entries in pieces:
        found = []
        for count, start, number in entries:
            parts = (refs[0].at[0], refs[0].at[1]) if count == 1 else refs[:2]
            found.append((parts, start, number))
            refs = refs[count:]
        arrays.append(found)
    vis_refs, (keep_one_ref, keep_two_ref) = refs[:homes], refs[homes : homes + 2]
    refs = refs[homes + 2 :]
    columns_ref = None
    if bright_at is None:
        columns_ref, refs = refs[0], refs[1:]
    out_refs, grad_ref = refs[:homes], refs[homes]
    refs = refs[homes + 1 :]
    if bright_at is not None:
        columns_ref, refs = refs[0], refs[1:]
    total_ref, one_ref, two_ref, vis_ref = refs
    step = pl.program_id(0)
    slot = tab_ref[0] + index
    sources, span = one_ref.shape[1:]

    def entry(column):
        return tab_ref[offset + step * COLUMNS + column]

    def load(target, at):
        for n, found in enumerate(arrays):

            @pl.when(entry(at) == n)
            def _(found=found):
                place = entry(at + 1)
                for parts, start, number in found:
                    rows = pl.ds(pl.multiple_of(place * number, number), number)
                    for part in (0, 1):
                        target[part, pl.ds(start, number)] = parts[part][rows]

    if bright_at is not None:

        @pl.when(step == 0)
        def _():
            for parts, start, number in arrays[0]:
                lines = parts[0][pl.ds(bright_at * number, BRIGHT_ROWS)].astype(jnp.float32)
                lanes = lax.broadcasted_iota(jnp.int32, (number, span), 1)
                rows = lax.broadcasted_iota(jnp.int32, (number, span), 0)
                for n in range(columns_ref.shape[0]):
                    line = jnp.where(lanes == rows, lines[n : n + 1, :], 0.0)
                    column = jnp.sum(line, axis=1, keepdims=True)
                    columns_ref[n, pl.ds(start, number)] = jnp.broadcast_to(column, (number, 128))

    def dot(a, b):
        return lax.dot_general(a, b, (((1,), (0,)), ((), ())), preferred_element_type=jnp.float32)

    def scaled_of(re, im):
        column = jnp.concatenate([columns_ref[index].astype(jnp.bfloat16)] * (span // 128), 1)
        return re * column, im * column

    def outer(a, b):
        row_ids = lax.broadcasted_iota(jnp.int32, a.shape, 0)
        a = jnp.where(row_ids == slot, a, 0.0)
        return lax.dot_general(a, b, (((0,), (0,)), ((), ())), preferred_element_type=jnp.float32)

    def cross(a_re, a_im, b_re, b_im):
        lhs = jnp.concatenate([a_re, a_im], 0).T
        rhs = jnp.concatenate(
            [jnp.concatenate([b_re, -b_im], 1), jnp.concatenate([b_im, b_re], 1)], 0
        )
        both = dot(lhs, rhs)
        return both[:, :span], both[:, span:]

    def pull(re, im, res_re, res_im, sign):
        lhs = jnp.concatenate([re, im], 1)
        rhs = jnp.concatenate(
            [
                jnp.concatenate([res_re, res_im], 1),
                jnp.concatenate([res_im, -res_re] if sign == 1 else [-res_im, res_re], 1),
            ],
            0,
        )
        both = dot(lhs, rhs)
        return both[:, :span], both[:, span:]

    def add_grad(value):
        folded = value[:, :128]
        for start in range(128, span, 128):
            folded = folded + value[:, start : start + 128]
        total_ref[...] += folded

    each = pl.num_programs(0) // homes

    def put(res_re, res_im):
        for home, out_ref in enumerate(out_refs):

            @pl.when(step // each == home)
            def _(out_ref=out_ref):
                out_ref[0, 0] = res_re
                out_ref[0, 1] = res_im

    @pl.when(step == 0)
    def _():
        total_ref[...] = jnp.zeros_like(total_ref)

    load(one_ref, ONE_AT)
    load(two_ref, TWO_AT)
    for home, home_ref in enumerate(vis_refs):

        @pl.when(step // each == home)
        def _(home_ref=home_ref):
            vis_ref[...] = home_ref[0, 0]

    @pl.when(entry(KIND) == 0)
    def _():
        one_re, one_im, two_re, two_im = one_ref[0], one_ref[1], two_ref[0], two_ref[1]
        pred_re, pred_im = cross(*scaled_of(one_re, one_im), two_re, two_im)
        weights = outer(keep_one_ref[...], keep_two_ref[...])
        res_re = (weights * (vis_ref[0].astype(jnp.float32) - pred_re)).astype(jnp.bfloat16)
        res_im = (weights * (vis_ref[1].astype(jnp.float32) - pred_im)).astype(jnp.bfloat16)
        put(res_re, res_im)
        sum_re, sum_im = pull(one_re, one_im, res_re, res_im, 1)
        add_grad(sum_re * two_re.astype(jnp.float32) - sum_im * two_im.astype(jnp.float32))

    @pl.when(entry(KIND) == 1)
    def _():
        one_re, one_im, two_re, two_im = one_ref[0], one_ref[1], two_ref[0], two_ref[1]
        row_ids = lax.broadcasted_iota(jnp.int32, (span, span), 0)
        col_ids = lax.broadcasted_iota(jnp.int32, (span, span), 1)
        upper = row_ids < col_ids
        lower = row_ids > col_ids
        first_re, first_im = cross(*scaled_of(one_re, one_im), one_re, one_im)
        second_re, second_im = cross(two_re, two_im, *scaled_of(two_re, two_im))
        keep_one = keep_one_ref[...]
        keep_two = keep_two_ref[...]
        weights = jnp.where(upper, outer(keep_one, keep_one), 0.0) + jnp.where(
            lower, outer(keep_two, keep_two), 0.0
        )
        vis_re = vis_ref[0].astype(jnp.float32)
        vis_im = vis_ref[1].astype(jnp.float32)
        res_re = (weights * (vis_re - jnp.where(upper, first_re, second_re))).astype(jnp.bfloat16)
        res_im = (weights * (vis_im - jnp.where(upper, first_im, -second_im))).astype(jnp.bfloat16)
        put(res_re, res_im)
        none = jnp.zeros_like(res_re)
        sum_re, sum_im = pull(
            one_re, one_im, jnp.where(upper, res_re, none), jnp.where(upper, res_im, none), 1
        )
        add_grad(sum_re * one_re.astype(jnp.float32) - sum_im * one_im.astype(jnp.float32))
        sum_re, sum_im = pull(
            two_re, two_im, jnp.where(lower, res_re, none), jnp.where(lower, res_im, none), -1
        )
        add_grad(sum_re * two_re.astype(jnp.float32) + sum_im * two_im.astype(jnp.float32))

    @pl.when(step == pl.num_programs(0) - 1)
    def _():
        grad_ref[...] = jnp.sum(total_ref[...].T, axis=0, keepdims=True)


def unit_work(index, offset, table, pieces, vis, keep, bright):
    units_dev, _, _, span, _ = vis[0].shape
    slots = keep.shape[0]
    sources = sum(number for _, _, number in pieces[0])
    count = units_dev * len(vis)
    whole = pl.BlockSpec(memory_space=pltpu.VMEM)
    arrays = [array for piece in pieces for entry, _, _ in piece for array in entry]

    def at(tab, step, column):
        return tab[offset + step * COLUMNS + column]

    def unit(step, home):
        return jnp.clip(step - home * units_dev, 0, units_dev - 1)

    in_specs = [whole] * len(arrays)
    for home, array in enumerate(vis):
        if array.shape[1] == slots:
            slot = lambda tab: tab[0] + index
        else:
            slot = lambda tab: index
        in_specs.append(
            pl.BlockSpec(
                (1, 1, 2, span, span),
                lambda u, tab, home=home, slot=slot: (unit(u, home), slot(tab), 0, 0, 0),
            )
        )
    in_specs += [
        pl.BlockSpec((slots, span), lambda u, tab: (0, at(tab, u, ONE))),
        pl.BlockSpec((slots, span), lambda u, tab: (0, at(tab, u, TWO))),
    ]
    operands = [table, *arrays, *vis, keep, keep]
    bright_at = None
    if isinstance(bright, int):
        first = pieces[0][0]
        bright_at = (first[0][0].shape[1] - BRIGHT_ROWS) // first[2]
    else:
        in_specs.append(whole)
        operands.append(bright)
    out_specs = [
        pl.BlockSpec((1, 2, span, span), lambda u, tab, home=home: (unit(u, home), 0, 0, 0))
        for home in range(len(vis))
    ]
    out_shapes = [jax.ShapeDtypeStruct((units_dev, 2, span, span), jnp.bfloat16) for _ in vis]
    out_specs.append(pl.BlockSpec((1, sources), lambda u, tab: (0, 0)))
    out_shapes.append(jax.ShapeDtypeStruct((1, sources), jnp.float32))
    if bright_at is not None:
        out_specs.append(pl.BlockSpec((bright, sources, 128), lambda u, tab: (0, 0, 0)))
        out_shapes.append(jax.ShapeDtypeStruct((bright, sources, 128), jnp.float32))
    kinds = [[(len(entry), start, number) for entry, start, number in piece] for piece in pieces]
    return pl.pallas_call(
        functools.partial(unit_kernel, index, offset, kinds, bright_at, len(vis)),
        grid_spec=pltpu.PrefetchScalarGridSpec(
            num_scalar_prefetch=1,
            grid=(count,),
            in_specs=in_specs,
            out_specs=out_specs,
            scratch_shapes=[
                pltpu.VMEM((sources, 128), jnp.float32),
                pltpu.VMEM((2, sources, span), jnp.bfloat16),
                pltpu.VMEM((2, sources, span), jnp.bfloat16),
                pltpu.VMEM((2, span, span), jnp.bfloat16),
            ],
        ),
        out_shape=out_shapes,
        compiler_params=pltpu.CompilerParams(vmem_limit_bytes=16 * 1024 * 1024),
        cost_estimate=LITTLE,
        name="unit_work",
    )(*operands)


def put_kernel(count, tab_ref, *refs):
    out_ref = refs[-1]
    for step in range(count):

        @pl.when(pl.program_id(0) == step)
        def _(step=step):
            out_ref[:, 0] = refs[step][...]


def put_residuals(arrays, offset, stride, table, shape, residual):
    units_dev, span = shape[0], shape[-1]
    whole = pl.BlockSpec(memory_space=pltpu.VMEM)
    operands = [table, *arrays]
    in_specs = [whole] * len(arrays)
    aliases = {}
    if residual is not None:
        aliases = {len(operands): 0}
        operands.append(residual)
        in_specs.append(pl.BlockSpec(memory_space=pl.ANY))
    return pl.pallas_call(
        functools.partial(put_kernel, len(arrays)),
        grid_spec=pltpu.PrefetchScalarGridSpec(
            num_scalar_prefetch=1,
            grid=(len(arrays),),
            in_specs=in_specs,
            out_specs=pl.BlockSpec(
                (units_dev, 1, 2, span, span),
                lambda n, tab: (0, tab[offset + stride * n], 0, 0, 0),
            ),
        ),
        out_shape=jax.ShapeDtypeStruct(shape, jnp.bfloat16),
        input_output_aliases=aliases,
        compiler_params=pltpu.CompilerParams(vmem_limit_bytes=16 * 1024 * 1024),
        cost_estimate=LITTLE,
        name="put_residuals",
    )(*operands)


class Routes:
    def __init__(self, planes, width, units, share):
        count = planes * width
        blocks = int(units[:, :2].max()) + 1
        self.width = width
        self.units_dev = units_dev = units.shape[0] // count
        ring = [0] + list(range(1, planes, 2)) + list(range(planes - 2, 0, -2))

        def along(step):
            at = {plane: ring[(n + step) % planes] for n, plane in enumerate(ring)}
            return [(t, at[t // width] * width + t % width) for t in range(count)]

        self.onward = along(1)
        self.backward = along(-1)
        self.opposite = along(2)
        self.partner = [[(t, t ^ m) for t in range(count)] for m in range(width)]

        half = blocks // 2
        self.full = [list(range(blocks))]
        self.pieces = [list(range(half)), list(range(half, blocks))]

        def table_of(pieces, order):
            rows = np.zeros((count, len(order), units_dev, COLUMNS), np.int32)
            for t in range(count):
                for n, m in enumerate(order):
                    for k in range(units_dev):
                        one, two, kind = units[(t ^ m) * units_dev + k].tolist()
                        at = [
                            (p, piece.index(b))
                            for b in (one, two)
                            for p, piece in enumerate(pieces)
                            if b in piece
                        ]
                        rows[t, n, k] = [kind, one, two, *at[0], *at[1]]
            return rows

        def targets(index):
            rows = np.zeros((count, len(self.order)), np.int32)
            for t in range(count):
                for n, m in enumerate(self.order):
                    rows[t, n] = (t % width ^ m) * share + index
            return rows

        self.order = list(range(width // 2, width)) + list(range(width // 2 - 1, -1, -1))
        starts = np.array([[(t % width ^ m) * share for m in range(width)] for t in range(count)])
        parts = [starts, table_of(self.full, self.order), table_of(self.pieces, self.order)]
        parts += [targets(n) for n in range(share)]
        parts = [part.reshape(count, -1) for part in parts]
        ends = np.cumsum([part.shape[1] for part in parts]).tolist()
        self.table = np.concatenate(parts, 1).astype(np.int32)
        self.steps = ends[:2]
        self.targets = ends[2:]
        self.steps_per_home = units_dev * COLUMNS
        self.targets_per_home = 1


def plain_program(visibility, beam, antenna_uvw, small, keep):
    units_dev, slots, _, span, _ = visibility.shape
    _, _, per_group, antennas = beam.shape
    blocks = antennas // span
    tile_index = lax.axis_index("tile")
    units = unit_table(blocks)
    none = np.zeros_like(units[:, 0])
    table = np.stack([units[:, 2], units[:, 0], units[:, 1], none, units[:, 0], none, units[:, 1]], 1)
    table = table.astype(np.int32).reshape(-1, units_dev * COLUMNS)
    table = np.pad(table, ((0, 0), (1, 0)))
    table = lax.dynamic_index_in_dim(jnp.asarray(table), tile_index, 0, keepdims=False)
    columns = None
    residuals, grads = [], []
    for slot in range(slots):
        (owned,) = build_factors(
            (slot, slots, per_group),
            table,
            beam,
            [],
            antenna_uvw,
            [small],
            [list(range(blocks))],
            span,
            0 if slot else BRIGHT_ROWS,
            small[0].shape[1],
        )
        everyone = lax.all_gather(owned, "tile", axis=0)
        rows = blocks * per_group
        if columns is None:
            bright = everyone[:, 0, rows : rows + slots, :per_group].astype(jnp.float32)
            bright = jnp.swapaxes(bright, 0, 1).reshape(slots, -1, 1)
            columns = jnp.broadcast_to(bright, bright.shape[:2] + (128,))
        factors = everyone[:, :, :rows].reshape(-1, 2, blocks, per_group, span)
        number = factors.shape[0] * per_group
        factors = factors.transpose(1, 2, 0, 3, 4).reshape(2, blocks * number, span)
        residual, grad = unit_work(
            slot, 1, table, [[((factors,), 0, number)]], [visibility], keep, columns
        )
        residuals.append(residual)
        grads.append(grad)
    summed = lax.psum_scatter(jnp.concatenate(grads, 0), "tile", scatter_dimension=1, tiled=True)
    return jnp.stack(residuals, 1), summed


OWN, OWN_NEAR, OWN_FAR, REST, REST_NEAR, REST_FAR = 0, 1, 3, 5, 6, 8
BEAM, SIDE_BEAMS, LATER_BEAMS, VIS, LATER = 10, 12, 15, 19, 23
PIECE_NEAR, PIECE_FAR = (24, 26), (28, 30)
WORK, HOME, PUT, LATER_WORK, LATER_HOME, PUT_NEAR, PUT_LAST = 32, 35, 38, 40, 43, 46, 47
SUM_PLANES, SUM_PLANE = 48, 51
GATES = {
    1: (0,),
    3: (0, 1),
    5: (0, 2, 13),
    6: (1, 2, 11),
    7: (1, 2),
    14: (13,),
    16: (2,),
    17: (1,),
    19: (18,),
    20: (3, 4, 6, 7, 17),
    21: (3, 4, 5, 13, 14, 16, 17),
    23: (4, 17),
    24: (6, 9, 17),
    25: (6, 9, 17, 23),
    26: (9,),
    27: (8,),
    28: (22,),
    31: (25, 27),
    33: (23, 32),
    34: (33,),
    35: (8, 9, 24, 25),
    40: (28, 34, 36, 37),
    41: (40,),
    42: (29, 41),
    43: (41,),
    45: (28, 32),
    48: (35,),
    49: (44,),
    51: (34,),
    52: (38,),
}


def plane_program(routes, visibility, beam, antenna_uvw, small, keep):
    units_dev, slots, _, span, _ = visibility.shape
    per_group = beam.shape[2]
    width = routes.width
    share = slots // width
    group = width * per_group
    tile_index = lax.axis_index("tile")
    mine = tile_index % width
    table = lax.dynamic_index_in_dim(jnp.asarray(routes.table), tile_index, 0, keepdims=False)
    done = {}

    def gated(step, value):
        earlier = [done[gate] for gate in GATES.get(step, ())]
        return lax.optimization_barrier((value, *earlier))[0] if earlier else value

    def send(step, value, pairs):
        done[step] = lax.ppermute(gated(step, value), "tile", pairs)
        return done[step]

    def near(step, piece):
        return [send(step, piece, routes.onward), send(step + 1, piece, routes.backward)]

    def far(step, sides):
        return [
            send(step, sides[0][0], routes.onward),
            send(step + 1, sides[1][1], routes.backward),
        ]

    def entries(piece, sides, halves, first, number):
        found = [(piece,), (sides[0],), (sides[1],), tuple(halves)]
        return [(arrays, n * group + first, number) for n, arrays in enumerate(found)]

    def build(step, index, own_beam, messages, smalls, pieces, bright_rows):
        built = build_factors(
            (index, share, per_group),
            gated(step, table),
            own_beam,
            messages,
            antenna_uvw,
            smalls,
            pieces,
            span,
            bright_rows,
            small[0].shape[1],
        )
        done[step] = built[0]
        return built

    core, *side = range(1, width)
    (message,) = messages_for(beam, 0, [core], small, gated(BEAM, table))
    message = send(BEAM + 1, message, routes.partner[core])
    (own,) = build(OWN, 0, beam, [message], [small, message], routes.full, BRIGHT_ROWS)
    own_sides = near(OWN_NEAR, own)
    messages = messages_for(beam, 0, side, small, gated(SIDE_BEAMS, table))
    messages = [
        send(SIDE_BEAMS + 1 + n, messages[n], routes.partner[m]) for n, m in enumerate(side)
    ]
    own_far = far(OWN_FAR, own_sides)
    (rest,) = build(REST, 0, None, messages, messages, routes.full, BRIGHT_ROWS)
    rest_sides = near(REST_NEAR, rest)

    later = messages_for(beam, 1, [core, *side], None, gated(LATER_BEAMS, table))
    later = [send(LATER_BEAMS + m, later[m - 1], routes.partner[m]) for m in (core, *side)]
    vis = slices_for(
        visibility, 1, share, [(m, 0) for m in (core, *side)], gated(VIS, table)
    )
    vis = [visibility] + [send(VIS + m, vis[m - 1], routes.partner[m]) for m in (core, *side)]
    later_pieces = build(
        LATER, 1, beam, later, [small, message, *messages], routes.pieces, 0
    )
    rest_far = far(REST_FAR, rest_sides)
    near_0 = near(PIECE_NEAR[0], later_pieces[0])
    near_1 = near(PIECE_NEAR[1], later_pieces[1])
    far_0 = far(PIECE_FAR[0], near_0)

    grads = []

    def work(index, step, home_step, ready, bright):
        arrived, total = [], None
        for n, homes in enumerate([routes.order[:1], routes.order[1:2], routes.order[2:]]):
            made = unit_work(
                index,
                routes.steps[index] + len(arrived) * routes.steps_per_home,
                gated(step + n, table),
                ready,
                [vis[m] for m in homes],
                keep,
                bright,
            )
            results, grad = made[: len(homes)], made[len(homes)]
            if isinstance(bright, int):
                bright = made[-1]
            done[step + n] = grad
            total = grad if total is None else total + grad
            arrived += [
                send(home_step - 1 + m, part, routes.partner[m]) if m else part
                for m, part in zip(homes, results)
            ]
        grads.append(total)
        return arrived, bright

    def put(step, homes, arrays, index, residual):
        stride = routes.targets_per_home
        offset = routes.targets[index] + homes * stride
        done[step] = put_residuals(
            arrays, offset, stride, gated(step, table), visibility.shape, residual
        )
        return done[step]

    number = group // 2
    pieces = entries(own, own_sides, own_far, 0, number)
    pieces += entries(rest, rest_sides, rest_far, number, number)
    arrived, columns = work(0, WORK, HOME, [pieces], share)
    far_1 = far(PIECE_FAR[1], near_1)
    residual = put(PUT, 0, arrived, 0, None)
    ready = [
        entries(piece, sides, halves, 0, group)
        for piece, sides, halves in zip(later_pieces, (near_0, near_1), (far_0, far_1))
    ]
    arrived, _ = work(1, LATER_WORK, LATER_HOME, ready, columns)

    partial = jnp.concatenate(grads, 0)
    parts = [partial[:, n * group : (n + 1) * group] for n in range(4)]
    plane_sum = (parts[0] + send(SUM_PLANES, parts[3], routes.opposite)) + (
        send(SUM_PLANES + 1, parts[1], routes.backward)
        + send(SUM_PLANES + 2, parts[2], routes.onward)
    )
    sums = [plane_sum[:, m * per_group : (m + 1) * per_group] for m in range(width)]
    sums = [sums[0]] + [
        send(SUM_PLANE - 1 + m, sums[m], routes.partner[m]) for m in (core, *side)
    ]
    sums = jnp.stack(sums, 0)
    ids = jnp.arange(width, dtype=jnp.int32)
    here = jnp.bitwise_xor(ids[:, None], mine) == ids[None, :]
    summed = jnp.sum(jnp.where(here[:, :, None, None], sums[None], 0.0), axis=1)
    summed = summed.reshape(slots, per_group)

    residual = put(PUT_NEAR, 2, arrived[2:], 1, residual)
    residual = put(PUT_LAST, 0, arrived[:2], 1, residual)
    return residual, summed


def per_device(
    visibility, station_beam, antenna_uvw, source_dirs, source_flux, visible_list, antenna_flags
):
    span = visibility.shape[4]
    antennas = station_beam.shape[3]
    small = (source_dirs, source_flux.astype(jnp.float32)[None], visible_list)
    keep = 1.0 - antenna_flags.astype(jnp.float32)
    arguments = (visibility, station_beam, antenna_uvw, small, keep)
    if lax.axis_size("tile") == 16:
        routes = Routes(4, 4, unit_table(antennas // span), visibility.shape[1] // 4)
        residual, summed = plane_program(routes, *arguments)
    else:
        residual, summed = plain_program(*arguments)
    return (residual, summed * (-1.0 / (8.0 * antennas)))


def solution(mesh):
    return jax.shard_map(
        per_device,
        mesh=mesh,
        in_specs=(
            P("tile", "grp", None, None, None),
            P("grp", None, "tile", None),
            P("grp", None, None),
            P(None, "tile"),
            P(("grp", "tile")),
            P(None, "tile"),
            P("grp", None),
        ),
        out_specs=(P("tile", "grp", None, None, None), P("grp", "tile")),
        check_vma=False,
    )
```

```python
import functools

import jax
import jax.numpy as jnp
import numpy as np
from jax import lax
from jax.experimental import pallas as pl
from jax.experimental.pallas import tpu as pltpu
from jax.sharding import PartitionSpec as P


def unit_table(block_count):
    first_list = []
    second_list = []
    diag_list = []
    for row_block in range(block_count):
        for col_block in range(row_block + 1, block_count):
            first_list.append(row_block)
            second_list.append(col_block)
            diag_list.append(0)
    for pair_index in range(block_count // 2):
        first_list.append(2 * pair_index)
        second_list.append(2 * pair_index + 1)
        diag_list.append(1)
    return np.stack([first_list, second_list, diag_list], 1).astype(np.int32)


def turn_polynomials():
    nodes = 0.125 + 0.125 * np.cos(np.pi * (np.arange(64) + 0.5) / 64)
    root = np.sqrt(nodes)
    fit = np.polynomial.Polynomial.fit
    sine = fit(nodes, np.sin(2 * np.pi * root) / root, 7, domain=[0, 0.25]).convert()
    cosine = fit(nodes, np.cos(2 * np.pi * root), 8, domain=[0, 0.25]).convert()
    return [float(c) for c in sine.coef], [float(c) for c in cosine.coef]


def horner(coefs, x):
    total = coefs[-1]
    for coef in coefs[-2::-1]:
        total = total * x + coef
    return total


def build_kernel(sets, slot_ids, pieces, bright_rows, width, tab_ref, *refs):
    refs, scratch_ref = refs[:-1], refs[-1]
    uvw_ref, outs = refs[-1 - len(pieces)], refs[-len(pieces) :]
    per_group = sets[0][0]
    span = outs[0].shape[2]
    count = len(sets) * per_group
    sin_coefs, cos_coefs = turn_polynomials()
    brights = []
    for part, (_, beam_at, small_at) in enumerate(sets):
        beam_ref = refs[beam_at]
        if beam_ref.shape[0] == 1:
            beam = [beam_ref.at[0, 0], beam_ref.at[0, 1]]
        else:
            beam = [beam_ref.at[pl.ds(n * per_group, per_group)] for n in (0, 1)]
        if refs[small_at].dtype == jnp.float32:
            small = small_rows(scratch_ref, *refs[small_at : small_at + 3])
        else:
            small = unsplit(refs[small_at], 2 * per_group, width)
        lanes = lax.broadcasted_iota(jnp.int32, (per_group, width), 1)
        rows = lax.broadcasted_iota(jnp.int32, (per_group, width), 0)

        def pick(chosen, row):
            return jnp.sum(jnp.where(chosen, small[row : row + 1, :], 0.0), axis=1, keepdims=True)

        def chosen_at(index):
            here = lax.broadcasted_iota(jnp.int32, small.shape, 0) == LIST_ROW + tab_ref[0] + index
            line = jnp.sum(jnp.where(here, small, 0.0), axis=0, keepdims=True)
            listed = jnp.sum(jnp.where(lanes == rows, line, 0.0), axis=1, keepdims=True)
            return listed.astype(jnp.int32) == lanes

        group = part * per_group
        if bright_rows:
            columns = lax.broadcasted_iota(jnp.int32, (per_group, span), 1)
            numbers = lax.broadcasted_iota(jnp.int32, (per_group, span), 0) + group
            for index in range(slot_ids[1]):
                flux = pick(chosen_at(index), 2)
                line = jnp.sum(jnp.where(columns == numbers, flux, 0.0), axis=0, keepdims=True)
                if part == 0:
                    brights.append(line)
                else:
                    brights[index] += line
        chosen = chosen_at(slot_ids[0])
        east = pick(chosen, 0)
        north = pick(chosen, 1)
        depth = jnp.sqrt(1.0 - east * east - north * north) - 1.0
        for out_ref, piece in zip(outs, pieces):
            for place, block in enumerate(piece):
                cols = pl.ds(block * span, span)
                delay = (
                    uvw_ref[0, 0:1, cols] * east
                    + uvw_ref[0, 1:2, cols] * north
                    + uvw_ref[0, 2:3, cols] * depth
                )
                turn = delay - jnp.floor(delay + 0.5)
                square = turn * turn
                sine = horner(sin_coefs, square) * turn
                cosine = horner(cos_coefs, square)
                real = beam[0][:, cols].astype(jnp.float32)
                imag = beam[1][:, cols].astype(jnp.float32)
                at = pl.ds(place * count + group, per_group)
                out_ref[0, at] = (real * cosine + imag * sine).astype(jnp.bfloat16)
                out_ref[1, at] = (imag * cosine - real * sine).astype(jnp.bfloat16)
    if bright_rows:
        padding = jnp.zeros((bright_rows - len(brights), span), jnp.float32)
        block = jnp.concatenate(brights + [padding], 0).astype(jnp.bfloat16)
        for part in (0, 1):
            outs[0][part, pl.ds(len(pieces[0]) * count, bright_rows)] = block


def small_rows(rows_ref, dirs_ref, flux_ref, list_ref):
    rows_ref[...] = jnp.zeros_like(rows_ref)
    rows_ref[0:2, 0 : dirs_ref.shape[1]] = dirs_ref[...]
    rows_ref[2:3, 0 : flux_ref.shape[1]] = flux_ref[...]
    slots, count = list_ref.shape
    rows_ref[LIST_ROW : LIST_ROW + slots, 0:count] = list_ref[...].astype(jnp.float32)
    return rows_ref[...]


LIST_ROW = 8
SMALL_ROWS = 16


def unsplit(message_ref, start, width):
    rows = pl.ds(start, SMALL_ROWS)
    terms = [message_ref[rows, pl.ds(n * width, width)].astype(jnp.float32) for n in range(3)]
    return (terms[0] + terms[1]) + terms[2]


BRIGHT_ROWS = 16


def build_factors(
    slot_ids, table, beam, messages, antenna_uvw, smalls, pieces, span, bright_rows, small_width
):
    slots, _, antennas = antenna_uvw.shape
    per_group = slot_ids[2]
    index = slot_ids[0]
    whole = pl.BlockSpec(memory_space=pltpu.VMEM)
    operands, in_specs, sets = [], [], []
    if beam is not None:
        operands.append(beam)
        in_specs.append(
            pl.BlockSpec((1, 2, per_group, antennas), lambda n, tab: (tab[0] + index, 0, 0, 0))
        )
    operands += messages
    beams = len(operands)
    for n, small in enumerate(smalls):
        at = next((k for k, known in enumerate(operands) if known is small), len(operands))
        if at == len(operands):
            operands += small if isinstance(small, tuple) else [small]
        sets.append((per_group, n, at))
    in_specs += [whole] * (len(operands) - len(in_specs))
    in_specs.append(pl.BlockSpec((1, 3, antennas), lambda n, tab: (tab[0] + index, 0, 0)))
    count = beams * per_group
    shapes = [
        (2, len(piece) * count + (0 if n else bright_rows), span) for n, piece in enumerate(pieces)
    ]
    return pl.pallas_call(
        functools.partial(build_kernel, sets, slot_ids, pieces, bright_rows, small_width),
        grid_spec=pltpu.PrefetchScalarGridSpec(
            num_scalar_prefetch=1,
            grid=(1,),
            in_specs=in_specs,
            out_specs=[whole] * len(pieces),
            scratch_shapes=[pltpu.VMEM((SMALL_ROWS, small_width), jnp.float32)],
        ),
        out_shape=[jax.ShapeDtypeStruct(shape, jnp.bfloat16) for shape in shapes],
        compiler_params=pltpu.CompilerParams(vmem_limit_bytes=16 * 1024 * 1024),
        cost_estimate=LITTLE,
        name="build_factors",
    )(table, *operands, antenna_uvw)


LITTLE = pl.CostEstimate(flops=1, bytes_accessed=1, transcendentals=0)


def message_kernel(count, with_small, tab_ref, *refs):
    beams, refs = refs[:count], refs[count:]
    if with_small:
        smalls, outs, scratch_ref = refs[:3], refs[3:-1], refs[-1]
        terms = []
        rest = small_rows(scratch_ref, *smalls)
        width = rest.shape[1]
        for _ in range(3):
            terms.append(rest.astype(jnp.bfloat16))
            rest = rest - terms[-1].astype(jnp.float32)
    else:
        outs = refs
    for beam_ref, out_ref in zip(beams, outs):
        per_group = beam_ref.shape[2]
        for part in (0, 1):
            out_ref[pl.ds(part * per_group, per_group)] = beam_ref[0, part]
        if with_small:
            rows = pl.ds(2 * per_group, SMALL_ROWS)
            out_ref[rows] = jnp.zeros((SMALL_ROWS, out_ref.shape[1]), jnp.bfloat16)
            for n, term in enumerate(terms):
                out_ref[rows, pl.ds(n * width, width)] = term


def messages_for(beam, index, others, small, table):
    _, _, per_group, antennas = beam.shape
    smalls = small or ()
    rows = 2 * per_group + (SMALL_ROWS if smalls else 0)
    whole = pl.BlockSpec(memory_space=pltpu.VMEM)
    scratch = []
    if smalls:
        scratch.append(pltpu.VMEM((SMALL_ROWS, smalls[0].shape[1]), jnp.float32))
    return pl.pallas_call(
        functools.partial(message_kernel, len(others), bool(smalls)),
        grid_spec=pltpu.PrefetchScalarGridSpec(
            num_scalar_prefetch=1,
            grid=(1,),
            in_specs=[
                pl.BlockSpec(
                    (1, 2, per_group, antennas), lambda n, tab, m=m: (tab[m] + index, 0, 0, 0)
                )
                for m in others
            ]
            + [whole for _ in smalls],
            out_specs=[whole for _ in others],
            scratch_shapes=scratch,
        ),
        out_shape=[jax.ShapeDtypeStruct((rows, antennas), jnp.bfloat16) for _ in others],
        cost_estimate=LITTLE,
        name="messages_for",
    )(table, *[beam] * len(others), *smalls)


def slice_kernel(count, tab_ref, *refs):
    for source, target in zip(refs[:count], refs[count:]):
        target[...] = source[...]


def slices_for(array, axis, size, starts, table):
    lead = axis > 0
    shape = array.shape[:axis] + (size,) + array.shape[axis + 1 :]
    block = (1,) + shape[1:] if lead else shape
    rest = (0,) * (array.ndim - axis - 1)
    return pl.pallas_call(
        functools.partial(slice_kernel, len(starts)),
        grid_spec=pltpu.PrefetchScalarGridSpec(
            num_scalar_prefetch=1,
            grid=(shape[0] if lead else 1,),
            in_specs=[
                pl.BlockSpec(
                    block,
                    lambda n, tab, start=start, shift=shift: (
                        *((n,) if lead else ()),
                        tab[start] // size + shift,
                        *rest,
                    ),
                )
                for start, shift in starts
            ],
            out_specs=[
                pl.BlockSpec(block, lambda n, tab: (n,) + (0,) * (array.ndim - 1)) for _ in starts
            ],
        ),
        out_shape=[jax.ShapeDtypeStruct(shape, array.dtype) for _ in starts],
        cost_estimate=LITTLE,
        name="slices_for",
    )(table, *[array] * len(starts))


KIND, ONE, TWO, ONE_AT, TWO_AT = 0, 1, 2, 3, 5
COLUMNS = 7


def unit_kernel(index, offset, pieces, bright_at, homes, tab_ref, *refs):
    arrays = []
    for entries in pieces:
        found = []
        for count, start, number in entries:
            parts = (refs[0].at[0], refs[0].at[1]) if count == 1 else refs[:2]
            found.append((parts, start, number))
            refs = refs[count:]
        arrays.append(found)
    vis_refs, (keep_one_ref, keep_two_ref) = refs[:homes], refs[homes : homes + 2]
    refs = refs[homes + 2 :]
    columns_ref = None
    if bright_at is None:
        columns_ref, refs = refs[0], refs[1:]
    out_refs, grad_ref = refs[:homes], refs[homes]
    refs = refs[homes + 1 :]
    if bright_at is not None:
        columns_ref, refs = refs[0], refs[1:]
    total_ref, one_ref, two_ref, vis_ref = refs
    step = pl.program_id(0)
    slot = tab_ref[0] + index
    sources, span = one_ref.shape[1:]

    def entry(column):
        return tab_ref[offset + step * COLUMNS + column]

    def load(target, at):
        for n, found in enumerate(arrays):

            @pl.when(entry(at) == n)
            def _(found=found):
                place = entry(at + 1)
                for parts, start, number in found:
                    rows = pl.ds(pl.multiple_of(place * number, number), number)
                    for part in (0, 1):
                        target[part, pl.ds(start, number)] = parts[part][rows]

    if bright_at is not None:

        @pl.when(step == 0)
        def _():
            for parts, start, number in arrays[0]:
                lines = parts[0][pl.ds(bright_at * number, BRIGHT_ROWS)].astype(jnp.float32)
                lanes = lax.broadcasted_iota(jnp.int32, (number, span), 1)
                rows = lax.broadcasted_iota(jnp.int32, (number, span), 0)
                for n in range(columns_ref.shape[0]):
                    line = jnp.where(lanes == rows, lines[n : n + 1, :], 0.0)
                    column = jnp.sum(line, axis=1, keepdims=True)
                    columns_ref[n, pl.ds(start, number)] = jnp.broadcast_to(column, (number, 128))

    def dot(a, b):
        return lax.dot_general(a, b, (((1,), (0,)), ((), ())), preferred_element_type=jnp.float32)

    def scaled_of(re, im):
        column = jnp.concatenate([columns_ref[index].astype(jnp.bfloat16)] * (span // 128), 1)
        return re * column, im * column

    def outer(a, b):
        row_ids = lax.broadcasted_iota(jnp.int32, a.shape, 0)
        a = jnp.where(row_ids == slot, a, 0.0)
        return lax.dot_general(a, b, (((0,), (0,)), ((), ())), preferred_element_type=jnp.float32)

    def cross(a_re, a_im, b_re, b_im):
        lhs = jnp.concatenate([a_re, a_im], 0).T
        rhs = jnp.concatenate(
            [jnp.concatenate([b_re, -b_im], 1), jnp.concatenate([b_im, b_re], 1)], 0
        )
        both = dot(lhs, rhs)
        return both[:, :span], both[:, span:]

    def pull(re, im, res_re, res_im, sign):
        lhs = jnp.concatenate([re, im], 1)
        rhs = jnp.concatenate(
            [
                jnp.concatenate([res_re, res_im], 1),
                jnp.concatenate([res_im, -res_re] if sign == 1 else [-res_im, res_re], 1),
            ],
            0,
        )
        both = dot(lhs, rhs)
        return both[:, :span], both[:, span:]

    def add_grad(value):
        folded = value[:, :128]
        for start in range(128, span, 128):
            folded = folded + value[:, start : start + 128]
        total_ref[...] += folded

    each = pl.num_programs(0) // homes

    def put(res_re, res_im):
        for home, out_ref in enumerate(out_refs):

            @pl.when(step // each == home)
            def _(out_ref=out_ref):
                out_ref[0, 0] = res_re
                out_ref[0, 1] = res_im

    @pl.when(step == 0)
    def _():
        total_ref[...] = jnp.zeros_like(total_ref)

    load(one_ref, ONE_AT)
    load(two_ref, TWO_AT)
    for home, home_ref in enumerate(vis_refs):

        @pl.when(step // each == home)
        def _(home_ref=home_ref):
            vis_ref[...] = home_ref[0, 0]

    @pl.when(entry(KIND) == 0)
    def _():
        one_re, one_im, two_re, two_im = one_ref[0], one_ref[1], two_ref[0], two_ref[1]
        pred_re, pred_im = cross(*scaled_of(one_re, one_im), two_re, two_im)
        weights = outer(keep_one_ref[...], keep_two_ref[...])
        res_re = (weights * (vis_ref[0].astype(jnp.float32) - pred_re)).astype(jnp.bfloat16)
        res_im = (weights * (vis_ref[1].astype(jnp.float32) - pred_im)).astype(jnp.bfloat16)
        put(res_re, res_im)
        sum_re, sum_im = pull(one_re, one_im, res_re, res_im, 1)
        add_grad(sum_re * two_re.astype(jnp.float32) - sum_im * two_im.astype(jnp.float32))

    @pl.when(entry(KIND) == 1)
    def _():
        one_re, one_im, two_re, two_im = one_ref[0], one_ref[1], two_ref[0], two_ref[1]
        row_ids = lax.broadcasted_iota(jnp.int32, (span, span), 0)
        col_ids = lax.broadcasted_iota(jnp.int32, (span, span), 1)
        upper = row_ids < col_ids
        lower = row_ids > col_ids
        first_re, first_im = cross(*scaled_of(one_re, one_im), one_re, one_im)
        second_re, second_im = cross(two_re, two_im, *scaled_of(two_re, two_im))
        keep_one = keep_one_ref[...]
        keep_two = keep_two_ref[...]
        weights = jnp.where(upper, outer(keep_one, keep_one), 0.0) + jnp.where(
            lower, outer(keep_two, keep_two), 0.0
        )
        vis_re = vis_ref[0].astype(jnp.float32)
        vis_im = vis_ref[1].astype(jnp.float32)
        res_re = (weights * (vis_re - jnp.where(upper, first_re, second_re))).astype(jnp.bfloat16)
        res_im = (weights * (vis_im - jnp.where(upper, first_im, -second_im))).astype(jnp.bfloat16)
        put(res_re, res_im)
        none = jnp.zeros_like(res_re)
        sum_re, sum_im = pull(
            one_re, one_im, jnp.where(upper, res_re, none), jnp.where(upper, res_im, none), 1
        )
        add_grad(sum_re * one_re.astype(jnp.float32) - sum_im * one_im.astype(jnp.float32))
        sum_re, sum_im = pull(
            two_re, two_im, jnp.where(lower, res_re, none), jnp.where(lower, res_im, none), -1
        )
        add_grad(sum_re * two_re.astype(jnp.float32) + sum_im * two_im.astype(jnp.float32))

    @pl.when(step == pl.num_programs(0) - 1)
    def _():
        grad_ref[...] = jnp.sum(total_ref[...].T, axis=0, keepdims=True)


def unit_work(index, offset, table, pieces, vis, keep, bright):
    units_dev, _, _, span, _ = vis[0].shape
    slots = keep.shape[0]
    sources = sum(number for _, _, number in pieces[0])
    count = units_dev * len(vis)
    whole = pl.BlockSpec(memory_space=pltpu.VMEM)
    arrays = [array for piece in pieces for entry, _, _ in piece for array in entry]

    def at(tab, step, column):
        return tab[offset + step * COLUMNS + column]

    def unit(step, home):
        return jnp.clip(step - home * units_dev, 0, units_dev - 1)

    in_specs = [whole] * len(arrays)
    for home, array in enumerate(vis):
        if array.shape[1] == slots:
            slot = lambda tab: tab[0] + index
        else:
            slot = lambda tab: index
        in_specs.append(
            pl.BlockSpec(
                (1, 1, 2, span, span),
                lambda u, tab, home=home, slot=slot: (unit(u, home), slot(tab), 0, 0, 0),
            )
        )
    in_specs += [
        pl.BlockSpec((slots, span), lambda u, tab: (0, at(tab, u, ONE))),
        pl.BlockSpec((slots, span), lambda u, tab: (0, at(tab, u, TWO))),
    ]
    operands = [table, *arrays, *vis, keep, keep]
    bright_at = None
    if isinstance(bright, int):
        first = pieces[0][0]
        bright_at = (first[0][0].shape[1] - BRIGHT_ROWS) // first[2]
    else:
        in_specs.append(whole)
        operands.append(bright)
    out_specs = [
        pl.BlockSpec((1, 2, span, span), lambda u, tab, home=home: (unit(u, home), 0, 0, 0))
        for home in range(len(vis))
    ]
    out_shapes = [jax.ShapeDtypeStruct((units_dev, 2, span, span), jnp.bfloat16) for _ in vis]
    out_specs.append(pl.BlockSpec((1, sources), lambda u, tab: (0, 0)))
    out_shapes.append(jax.ShapeDtypeStruct((1, sources), jnp.float32))
    if bright_at is not None:
        out_specs.append(pl.BlockSpec((bright, sources, 128), lambda u, tab: (0, 0, 0)))
        out_shapes.append(jax.ShapeDtypeStruct((bright, sources, 128), jnp.float32))
    kinds = [[(len(entry), start, number) for entry, start, number in piece] for piece in pieces]
    return pl.pallas_call(
        functools.partial(unit_kernel, index, offset, kinds, bright_at, len(vis)),
        grid_spec=pltpu.PrefetchScalarGridSpec(
            num_scalar_prefetch=1,
            grid=(count,),
            in_specs=in_specs,
            out_specs=out_specs,
            scratch_shapes=[
                pltpu.VMEM((sources, 128), jnp.float32),
                pltpu.VMEM((2, sources, span), jnp.bfloat16),
                pltpu.VMEM((2, sources, span), jnp.bfloat16),
                pltpu.VMEM((2, span, span), jnp.bfloat16),
            ],
        ),
        out_shape=out_shapes,
        compiler_params=pltpu.CompilerParams(vmem_limit_bytes=16 * 1024 * 1024),
        cost_estimate=LITTLE,
        name="unit_work",
    )(*operands)


def put_kernel(count, tab_ref, *refs):
    out_ref = refs[-1]
    for step in range(count):

        @pl.when(pl.program_id(0) == step)
        def _(step=step):
            out_ref[:, 0] = refs[step][...]


def put_residuals(arrays, offset, stride, table, shape, residual):
    units_dev, span = shape[0], shape[-1]
    whole = pl.BlockSpec(memory_space=pltpu.VMEM)
    operands = [table, *arrays]
    in_specs = [whole] * len(arrays)
    aliases = {}
    if residual is not None:
        aliases = {len(operands): 0}
        operands.append(residual)
        in_specs.append(pl.BlockSpec(memory_space=pl.ANY))
    return pl.pallas_call(
        functools.partial(put_kernel, len(arrays)),
        grid_spec=pltpu.PrefetchScalarGridSpec(
            num_scalar_prefetch=1,
            grid=(len(arrays),),
            in_specs=in_specs,
            out_specs=pl.BlockSpec(
                (units_dev, 1, 2, span, span),
                lambda n, tab: (0, tab[offset + stride * n], 0, 0, 0),
            ),
        ),
        out_shape=jax.ShapeDtypeStruct(shape, jnp.bfloat16),
        input_output_aliases=aliases,
        compiler_params=pltpu.CompilerParams(vmem_limit_bytes=16 * 1024 * 1024),
        cost_estimate=LITTLE,
        name="put_residuals",
    )(*operands)


class Routes:
    def __init__(self, planes, width, units, share):
        count = planes * width
        blocks = int(units[:, :2].max()) + 1
        self.width = width
        self.units_dev = units_dev = units.shape[0] // count
        ring = [0] + list(range(1, planes, 2)) + list(range(planes - 2, 0, -2))

        def along(step):
            at = {plane: ring[(n + step) % planes] for n, plane in enumerate(ring)}
            return [(t, at[t // width] * width + t % width) for t in range(count)]

        self.onward = along(1)
        self.backward = along(-1)
        self.opposite = along(2)
        self.partner = [[(t, t ^ m) for t in range(count)] for m in range(width)]

        half = blocks // 2
        self.full = [list(range(blocks))]
        self.pieces = [list(range(half)), list(range(half, blocks))]

        def table_of(pieces, order):
            rows = np.zeros((count, len(order), units_dev, COLUMNS), np.int32)
            for t in range(count):
                for n, m in enumerate(order):
                    for k in range(units_dev):
                        one, two, kind = units[(t ^ m) * units_dev + k].tolist()
                        at = [
                            (p, piece.index(b))
                            for b in (one, two)
                            for p, piece in enumerate(pieces)
                            if b in piece
                        ]
                        rows[t, n, k] = [kind, one, two, *at[0], *at[1]]
            return rows

        def targets(index):
            rows = np.zeros((count, len(self.order)), np.int32)
            for t in range(count):
                for n, m in enumerate(self.order):
                    rows[t, n] = (t % width ^ m) * share + index
            return rows

        self.order = list(range(width // 2, width)) + list(range(width // 2 - 1, -1, -1))
        starts = np.array([[(t % width ^ m) * share for m in range(width)] for t in range(count)])
        parts = [starts, table_of(self.full, self.order), table_of(self.pieces, self.order)]
        parts += [targets(n) for n in range(share)]
        parts = [part.reshape(count, -1) for part in parts]
        ends = np.cumsum([part.shape[1] for part in parts]).tolist()
        self.table = np.concatenate(parts, 1).astype(np.int32)
        self.steps = ends[:2]
        self.targets = ends[2:]
        self.steps_per_home = units_dev * COLUMNS
        self.targets_per_home = 1


def plain_program(visibility, beam, antenna_uvw, small, keep):
    units_dev, slots, _, span, _ = visibility.shape
    _, _, per_group, antennas = beam.shape
    blocks = antennas // span
    tile_index = lax.axis_index("tile")
    units = unit_table(blocks)
    none = np.zeros_like(units[:, 0])
    table = np.stack([units[:, 2], units[:, 0], units[:, 1], none, units[:, 0], none, units[:, 1]], 1)
    table = table.astype(np.int32).reshape(-1, units_dev * COLUMNS)
    table = np.pad(table, ((0, 0), (1, 0)))
    table = lax.dynamic_index_in_dim(jnp.asarray(table), tile_index, 0, keepdims=False)
    columns = None
    residuals, grads = [], []
    for slot in range(slots):
        (owned,) = build_factors(
            (slot, slots, per_group),
            table,
            beam,
            [],
            antenna_uvw,
            [small],
            [list(range(blocks))],
            span,
            0 if slot else BRIGHT_ROWS,
            small[0].shape[1],
        )
        everyone = lax.all_gather(owned, "tile", axis=0)
        rows = blocks * per_group
        if columns is None:
            bright = everyone[:, 0, rows : rows + slots, :per_group].astype(jnp.float32)
            bright = jnp.swapaxes(bright, 0, 1).reshape(slots, -1, 1)
            columns = jnp.broadcast_to(bright, bright.shape[:2] + (128,))
        factors = everyone[:, :, :rows].reshape(-1, 2, blocks, per_group, span)
        number = factors.shape[0] * per_group
        factors = factors.transpose(1, 2, 0, 3, 4).reshape(2, blocks * number, span)
        residual, grad = unit_work(
            slot, 1, table, [[((factors,), 0, number)]], [visibility], keep, columns
        )
        residuals.append(residual)
        grads.append(grad)
    summed = lax.psum_scatter(jnp.concatenate(grads, 0), "tile", scatter_dimension=1, tiled=True)
    return jnp.stack(residuals, 1), summed


OWN, OWN_NEAR, OWN_FAR, REST, REST_NEAR, REST_FAR = 0, 1, 3, 5, 6, 8
BEAM, SIDE_BEAMS, LATER_BEAMS, VIS, LATER = 10, 12, 15, 19, 23
PIECE_NEAR, PIECE_FAR = (24, 26), (28, 30)
WORK, HOME, PUT, LATER_WORK, LATER_HOME, PUT_NEAR, PUT_LAST = 32, 35, 38, 40, 43, 46, 47
SUM_PLANES, SUM_PLANE = 48, 51
GATES = {
    1: (0,),
    3: (0, 1),
    5: (0, 2, 13),
    6: (1, 2, 11),
    7: (1, 2),
    14: (13,),
    16: (2,),
    17: (1,),
    19: (18,),
    20: (3, 4, 6, 7, 17),
    21: (3, 4, 5, 13, 14, 16, 17),
    23: (4, 17),
    24: (6, 9, 17),
    25: (6, 9, 17, 23),
    26: (9,),
    27: (8,),
    28: (22,),
    31: (25, 27),
    33: (23, 32),
    34: (33,),
    35: (8, 9, 24, 25),
    40: (28, 34, 36, 37),
    41: (40,),
    42: (29, 41),
    43: (41,),
    45: (28, 32),
    48: (35,),
    49: (44,),
    51: (34,),
    52: (38,),
}


def plane_program(routes, visibility, beam, antenna_uvw, small, keep):
    units_dev, slots, _, span, _ = visibility.shape
    per_group = beam.shape[2]
    width = routes.width
    share = slots // width
    group = width * per_group
    tile_index = lax.axis_index("tile")
    mine = tile_index % width
    table = lax.dynamic_index_in_dim(jnp.asarray(routes.table), tile_index, 0, keepdims=False)
    done = {}

    def gated(step, value):
        earlier = [done[gate] for gate in GATES.get(step, ())]
        return lax.optimization_barrier((value, *earlier))[0] if earlier else value

    def send(step, value, pairs):
        done[step] = lax.ppermute(gated(step, value), "tile", pairs)
        return done[step]

    def near(step, piece):
        return [send(step, piece, routes.onward), send(step + 1, piece, routes.backward)]

    def far(step, sides):
        return [
            send(step, sides[0][0], routes.onward),
            send(step + 1, sides[1][1], routes.backward),
        ]

    def entries(piece, sides, halves, first, number):
        found = [(piece,), (sides[0],), (sides[1],), tuple(halves)]
        return [(arrays, n * group + first, number) for n, arrays in enumerate(found)]

    def build(step, index, own_beam, messages, smalls, pieces, bright_rows):
        built = build_factors(
            (index, share, per_group),
            gated(step, table),
            own_beam,
            messages,
            antenna_uvw,
            smalls,
            pieces,
            span,
            bright_rows,
            small[0].shape[1],
        )
        done[step] = built[0]
        return built

    core, *side = range(1, width)
    (message,) = messages_for(beam, 0, [core], small, gated(BEAM, table))
    message = send(BEAM + 1, message, routes.partner[core])
    (own,) = build(OWN, 0, beam, [message], [small, message], routes.full, BRIGHT_ROWS)
    own_sides = near(OWN_NEAR, own)
    messages = messages_for(beam, 0, side, small, gated(SIDE_BEAMS, table))
    messages = [
        send(SIDE_BEAMS + 1 + n, messages[n], routes.partner[m]) for n, m in enumerate(side)
    ]
    own_far = far(OWN_FAR, own_sides)
    (rest,) = build(REST, 0, None, messages, messages, routes.full, BRIGHT_ROWS)
    rest_sides = near(REST_NEAR, rest)

    later = messages_for(beam, 1, [core, *side], None, gated(LATER_BEAMS, table))
    later = [send(LATER_BEAMS + m, later[m - 1], routes.partner[m]) for m in (core, *side)]
    vis = slices_for(
        visibility, 1, share, [(m, 0) for m in (core, *side)], gated(VIS, table)
    )
    vis = [visibility] + [send(VIS + m, vis[m - 1], routes.partner[m]) for m in (core, *side)]
    later_pieces = build(
        LATER, 1, beam, later, [small, message, *messages], routes.pieces, 0
    )
    rest_far = far(REST_FAR, rest_sides)
    near_0 = near(PIECE_NEAR[0], later_pieces[0])
    near_1 = near(PIECE_NEAR[1], later_pieces[1])
    far_0 = far(PIECE_FAR[0], near_0)

    grads = []

    def work(index, step, home_step, ready, bright):
        arrived, total = [], None
        for n, homes in enumerate([routes.order[:1], routes.order[1:2], routes.order[2:]]):
            made = unit_work(
                index,
                routes.steps[index] + len(arrived) * routes.steps_per_home,
                gated(step + n, table),
                ready,
                [vis[m] for m in homes],
                keep,
                bright,
            )
            results, grad = made[: len(homes)], made[len(homes)]
            if isinstance(bright, int):
                bright = made[-1]
            done[step + n] = grad
            total = grad if total is None else total + grad
            arrived += [
                send(home_step - 1 + m, part, routes.partner[m]) if m else part
                for m, part in zip(homes, results)
            ]
        grads.append(total)
        return arrived, bright

    def put(step, homes, arrays, index, residual):
        stride = routes.targets_per_home
        offset = routes.targets[index] + homes * stride
        done[step] = put_residuals(
            arrays, offset, stride, gated(step, table), visibility.shape, residual
        )
        return done[step]

    number = group // 2
    pieces = entries(own, own_sides, own_far, 0, number)
    pieces += entries(rest, rest_sides, rest_far, number, number)
    arrived, columns = work(0, WORK, HOME, [pieces], share)
    far_1 = far(PIECE_FAR[1], near_1)
    first_arrived = arrived
    ready = [
        entries(piece, sides, halves, 0, group)
        for piece, sides, halves in zip(later_pieces, (near_0, near_1), (far_0, far_1))
    ]
    arrived, _ = work(1, LATER_WORK, LATER_HOME, ready, columns)

    residual = put(PUT, 0, [*first_arrived, arrived[0]], 0, None)

    partial = jnp.concatenate(grads, 0)
    parts = [partial[:, n * group : (n + 1) * group] for n in range(4)]
    plane_sum = (parts[0] + send(SUM_PLANES, parts[3], routes.opposite)) + (
        send(SUM_PLANES + 1, parts[1], routes.backward)
        + send(SUM_PLANES + 2, parts[2], routes.onward)
    )
    sums = [plane_sum[:, m * per_group : (m + 1) * per_group] for m in range(width)]
    sums = [sums[0]] + [
        send(SUM_PLANE - 1 + m, sums[m], routes.partner[m]) for m in (core, *side)
    ]
    sums = jnp.stack(sums, 0)
    ids = jnp.arange(width, dtype=jnp.int32)
    here = jnp.bitwise_xor(ids[:, None], mine) == ids[None, :]
    summed = jnp.sum(jnp.where(here[:, :, None, None], sums[None], 0.0), axis=1)
    summed = summed.reshape(slots, per_group)

    residual = put(PUT_NEAR, 2, arrived[2:], 1, residual)
    residual = put(PUT_LAST, 1, arrived[1:2], 1, residual)
    return residual, summed


def per_device(
    visibility, station_beam, antenna_uvw, source_dirs, source_flux, visible_list, antenna_flags
):
    span = visibility.shape[4]
    antennas = station_beam.shape[3]
    small = (source_dirs, source_flux.astype(jnp.float32)[None], visible_list)
    keep = 1.0 - antenna_flags.astype(jnp.float32)
    arguments = (visibility, station_beam, antenna_uvw, small, keep)
    if lax.axis_size("tile") == 16:
        routes = Routes(4, 4, unit_table(antennas // span), visibility.shape[1] // 4)
        residual, summed = plane_program(routes, *arguments)
    else:
        residual, summed = plain_program(*arguments)
    return (residual, summed * (-1.0 / (8.0 * antennas)))


def solution(mesh):
    return jax.shard_map(
        per_device,
        mesh=mesh,
        in_specs=(
            P("tile", "grp", None, None, None),
            P("grp", None, "tile", None),
            P("grp", None, None),
            P(None, "tile"),
            P(("grp", "tile")),
            P(None, "tile"),
            P("grp", None),
        ),
        out_specs=(P("tile", "grp", None, None, None), P("grp", "tile")),
        check_vma=False,
    )
```
